32 devices in a mesh: dp: 8 (over z, x), seq: 4 (over y, core).
Axes of the slice: x: 2, y: 2, z: 4, core: 2. Of those that a mesh axis runs over, the one named last changes fastest.
Arguments:
- tokens: bfloat16 [48, 512, 768], P('dp', 'seq'), may hold values from -6 to 6
- grad_out: bfloat16 [48, 512, 768], P('dp', 'seq'), may hold values from -6 to 6
- lengths: int32 [48], P('dp'), may hold values from 1 to 512, as said below
- members: int32 [24, 6], P('dp'), may hold values from -1 to 47, as said below
- owners: int32 [8], replicated, may hold values from 0 to 7, as said below
- mat_master: float32 [9216, 768], P('dp'), may hold values from -0.4330127 to 0.4330127
- mat_moment1: float32 [9216, 768], P('dp'), may hold values from -0.00061035156 to 0.00061035156
- mat_moment2: float32 [9216, 768], P('dp'), may hold values from 7.0550676e-11 to 1.1288108e-09
- vec_master: float32 [12, 768], replicated, may hold values from -1.5 to 1.5
- vec_moment1: float32 [12, 768], replicated, may hold values from -0.0024414062 to 0.0024414062
- vec_moment2: float32 [12, 768], replicated, may hold values from 1.1288108e-09 to 1.8060973e-08
Outputs:
- output: bfloat16 [48, 512, 768], P('dp', 'seq')
- input_grad: bfloat16 [48, 512, 768], P('dp', 'seq')
- group_embeddings: float32 [24, 768], P('dp')
- grad_norm: float32 [], replicated
- mat_moment1_new: float32 [9216, 768], P('dp')
- mat_moment2_new: float32 [9216, 768], P('dp')
- mat_master_new: float32 [9216, 768], P('dp')
- mat_weight_low: bfloat16 [9216, 768], P('dp')
- vec_moment1_new: float32 [12, 768], replicated
- vec_moment2_new: float32 [12, 768], replicated
- vec_master_new: float32 [12, 768], replicated
- vec_weight_low: bfloat16 [12, 768], replicated
The draws below stay inside these ranges and needn't reach their ends.
Inputs may be any that keep to these rules, and one draw needn't show every extreme that they name: Among the 6 sentences of each index of dp, one has length 512; sentence s holds tokens at positions below lengths[s], the rest is padding. Row g lists distinct sentences held by the same index of dp as the group (indices g // 3 * 6 to that plus 6 - 1) first, then -1; each group has 1 to 6 members. `owners`: A permutation of the dp indices.
All inputs are finite; a program needn't handle non-finite values.
Results may differ from the reference program's by a relative error of at most 0.014.
Values may be sent and summed in bfloat16 or wider, within the bound.
A program may use at most 256 MiB of HBM per device.

```python
import math
import jax
import jax.numpy as jnp
from jax import lax

D = 768
HEADS = 12
HEAD_DIM = 64
FEEDFWD_UNITS = 3072
LEN = 512
SENT_DEV = 6
GRP_DEV = 3
GMAX = 6
STEP = 10
SENT = 48
GROUPS = 24
ROWS = 9216
VROWS = 12
N_DP = 8


def owner_perm(key):
    devices = GROUPS // GRP_DEV
    return jax.random.permutation(jax.random.fold_in(key, 7), devices)


def draw_owners(key, part):
    owner_order = owner_perm(key)
    return owner_order.astype(jnp.int32)


def draw_lengths(key, part):
    key = jax.random.fold_in(key, 21)
    devices = SENT // SENT_DEV
    first_key, second_key = jax.random.split(key)
    drawn = jax.random.randint(first_key, (devices, SENT_DEV), 1, LEN + 1)
    longest = jax.random.randint(second_key, (devices, 1), 0, SENT_DEV)
    drawn = jnp.where(jnp.arange(SENT_DEV)[None, :] == longest, LEN, drawn)
    return drawn.reshape(SENT).astype(jnp.int32)


def draw_members(key, part):
    key = jax.random.fold_in(key, 31)
    devices = GROUPS // GRP_DEV
    size_key, full_key, score_key = jax.random.split(key, 3)
    group_sizes = jax.random.randint(size_key, (devices, GRP_DEV), 1, GMAX + 1)
    full_group = jax.random.randint(full_key, (devices, 1), 0, GRP_DEV)
    group_slot = jnp.arange(GRP_DEV)[None, :]
    short_group = (full_group + 1) % GRP_DEV
    group_sizes = jnp.where(group_slot == full_group, GMAX, group_sizes)
    group_sizes = jnp.where(group_slot == short_group, jnp.minimum(group_sizes, GMAX - 1), group_sizes)
    sentence_slot = jnp.arange(SENT_DEV)
    scores = jax.random.randint(score_key, (devices, GRP_DEV, SENT_DEV), 0, 2 ** 20) * SENT_DEV + sentence_slot[None, None, :]
    first_pick = (group_slot == full_group)[:, :, None] & (sentence_slot == SENT_DEV - 1)[None, None, :]
    scores = jnp.where(first_pick, -1, scores)
    ranked = jnp.argsort(scores, axis=-1)[:, :, :GMAX].astype(jnp.int32)
    sentence_ids = ranked + (jnp.arange(devices) * SENT_DEV)[:, None, None]
    listed = jnp.where(jnp.arange(GMAX)[None, None, :] < group_sizes[:, :, None], sentence_ids, -1)
    return listed.reshape(GROUPS, GMAX).astype(jnp.int32)


def draw_mat_master(key, part):
    owner_order = owner_perm(key)
    key = jax.random.fold_in(key, 41)
    devices = GROUPS // GRP_DEV
    block_rows = ROWS // devices
    inverse = jnp.argsort(owner_order).astype(jnp.int32)
    row_ids = (inverse[:, None] * block_rows + jnp.arange(block_rows)[None, :]).reshape(ROWS, 1)
    row_scale = jnp.where(row_ids < 2 * D, 1.3 * D ** (-0.5), jnp.where(row_ids < 3 * D, D ** (-0.5), jnp.where(row_ids < 4 * D, 4.0 * D ** (-0.5), jnp.where(row_ids < 4 * D + FEEDFWD_UNITS, D ** (-0.5), FEEDFWD_UNITS ** (-0.5)))))
    base_noise = jnp.clip(jax.random.normal(key, (ROWS, D), jnp.float32), -3.0, 3.0)
    return (base_noise * row_scale).astype(jnp.float32)


def draw_vec_master(key, part):
    key = jax.random.fold_in(key, 61)
    base_noise = jnp.clip(jax.random.normal(key, (VROWS, D), jnp.float32), -3.0, 3.0)
    row_ids = jnp.arange(VROWS)[:, None]
    gain_rows = (row_ids == 4) | (row_ids == 6)
    shift_rows = (row_ids == 5) | (row_ids == 7)
    drawn = jnp.where(gain_rows, 1.0 + 0.1 * base_noise, jnp.where(shift_rows, 0.5 * base_noise, 0.3 * base_noise))
    return drawn.astype(jnp.float32)


def levels(key, shape, cuts, least, top_value):
    def one(position, blocks):
        steps = jax.random.uniform(jax.random.fold_in(jax.random.fold_in(key, 6), position), (blocks,), jnp.float32, least / len(cuts), top_value / len(cuts))
        return jnp.repeat(jnp.exp(steps), shape[position] // blocks).reshape((-1,) + (1,) * (len(shape) - position - 1))

    factor_of = one(*cuts[0])
    for cut in cuts[1:]:
        factor_of = factor_of * one(*cut)
    return factor_of


def gaussian(stream_key, shape, spread, limit, pieces=(), dtype=jnp.bfloat16):
    array = jax.random.normal(stream_key, shape, jnp.float32) * spread
    if len(pieces) > 0:
        array = levels(stream_key, shape, pieces, -0.22, 0.18) * array
    return jnp.clip(array, min=-limit, max=limit).astype(dtype)


def setup_inputs(seed: int = 0) -> dict:
    keys = jax.random.split(jax.random.key(seed), 12)
    return {
        "tokens": gaussian(keys[0], (SENT, LEN, D), 1.0, 6.0, ((0, 8), (1, 4))),
        "grad_out": gaussian(keys[1], (SENT, LEN, D), 1.0, 6.0, ((0, 8), (1, 4))),
        "lengths": draw_lengths(jax.random.fold_in(keys[11], 71), 0),
        "members": draw_members(jax.random.fold_in(keys[11], 71), 0),
        "owners": draw_owners(jax.random.fold_in(keys[11], 71), 0),
        "mat_master": draw_mat_master(jax.random.fold_in(keys[11], 71), 0),
        "mat_moment1": gaussian(keys[6], (ROWS, D), (0.111 * (ROWS * D + VROWS * D) ** -0.5), 0.00061035156, ((0, 8),), jnp.float32),
        "mat_moment2": jnp.clip(jnp.exp(math.log(1.1288108225926408e-09) - 2.7725887 * jax.random.uniform(keys[7], (ROWS, D), jnp.float32) ** levels(keys[7], (ROWS, D), ((0, 8),), -0.2, 0.2)), 7.055067641204005e-11, 1.1288108225926408e-09),
        "vec_master": draw_vec_master(jax.random.fold_in(keys[11], 71), 0),
        "vec_moment1": gaussian(keys[9], (VROWS, D), (0.444 * (ROWS * D + VROWS * D) ** -0.5), 0.0024414062, (), jnp.float32),
        "vec_moment2": jnp.clip(jnp.exp(jax.random.uniform(keys[10], (VROWS, D), jnp.float32, math.log(1.1288108225926408e-09), math.log(1.8060973161482252e-08))), 1.1288108225926408e-09, 1.8060973161482252e-08),
    }


NORM_EPS = 1e-06
MASK_FILL = -1e+30
MAX_NORM = 1.0
ADAM_ONE = 0.9
ADAM_TWO = 0.999
ADAM_EPS = 1e-08
WEIGHT_DECAY = 0.01
RATE_MATRIX = 0.04
RATE_VECTOR = 0.5

@jax.custom_vjp
def lowered_value(v):
    return lax.optimization_barrier(v.astype(jnp.bfloat16)).astype(jnp.float32)

@jax.custom_vjp
def lowered_backward(v):
    return v

def low_keep(v):
    return (lowered_value(v), None)

def low_pass(kept, grad):
    return (grad,)

def back_keep(v):
    return (v, None)

def back_low(kept, grad):
    return (lowered_value(grad),)
lowered_value.defvjp(low_keep, low_pass)
lowered_backward.defvjp(back_keep, back_low)

def round_both(tensor_value):
    return lowered_value(lowered_backward(tensor_value))

def layer_norm(tensor_value, norm_gain, norm_shift):
    row_mean = lax.optimization_barrier(jnp.mean(tensor_value, -1, keepdims=True))
    centered = tensor_value - row_mean
    row_var = lax.optimization_barrier(jnp.mean(centered * centered, -1, keepdims=True))
    return centered * lax.rsqrt(row_var + NORM_EPS) * norm_gain + norm_shift

def block_forward(inputs, seq_lengths, matrices, vector_list):
    highest_precision = lax.Precision.HIGHEST
    sentences = inputs.shape[0]
    query_w = matrices[0:D]
    key_w = matrices[D:2 * D]
    value_w = matrices[2 * D:3 * D]
    out_w = matrices[3 * D:4 * D]
    inner_weight = matrices[4 * D:4 * D + FEEDFWD_UNITS]
    outer_weight = matrices[4 * D + FEEDFWD_UNITS:]

    def project(tensor_value, weight_matrix):
        return jnp.einsum('qfr,ro->qfo', tensor_value, weight_matrix, precision=highest_precision)
    queries = round_both(project(inputs, query_w) + vector_list[0]).reshape(sentences, LEN, HEADS, HEAD_DIM)
    key_vals = round_both(project(inputs, key_w)).reshape(sentences, LEN, HEADS, HEAD_DIM)
    value_vals = round_both(project(inputs, value_w) + vector_list[1]).reshape(sentences, LEN, HEADS, HEAD_DIM)
    scores = lowered_backward(jnp.einsum('sqhd,skhd->shqk', queries, key_vals, precision=highest_precision) * HEAD_DIM ** (-0.5))
    key_mask = jnp.arange(LEN)[None, :] < seq_lengths[:, None]
    scores = jnp.where(key_mask[:, None, None, :], scores, MASK_FILL)
    shifted = jnp.exp(scores - lax.optimization_barrier(jnp.max(scores, -1, keepdims=True)))
    softmax_probs = lowered_value(shifted / lax.optimization_barrier(jnp.sum(shifted, -1, keepdims=True)))
    attended = round_both(jnp.einsum('shqk,skhd->sqhd', softmax_probs, value_vals, precision=highest_precision).reshape(sentences, LEN, D))
    branch = lowered_backward(project(attended, out_w) + vector_list[2])
    first_normed = layer_norm(inputs + branch, vector_list[4], vector_list[5])
    inner_activation = lowered_backward(jnp.einsum('joq,tq->jot', lowered_value(first_normed), inner_weight, precision=highest_precision) + vector_list[8:].reshape(FEEDFWD_UNITS))
    active_values = lowered_value(jax.nn.gelu(inner_activation, approximate=False))
    outer_output = lowered_backward(jnp.einsum('ivp,pm->ivm', active_values, outer_weight, precision=highest_precision) + vector_list[3])
    return layer_norm(first_normed + outer_output, vector_list[6], vector_list[7])

def adam_step(master, moment_one, moment_two, gradient, learn_rate, decay_rate):
    moment_one = ADAM_ONE * moment_one + (1.0 - ADAM_ONE) * gradient
    moment_two = ADAM_TWO * moment_two + (1.0 - ADAM_TWO) * gradient * gradient
    scaled_one = moment_one / (1.0 - ADAM_ONE ** STEP)
    scaled_two = moment_two / (1.0 - ADAM_TWO ** STEP)
    master = master - learn_rate * (scaled_one / (jnp.sqrt(scaled_two) + ADAM_EPS) + decay_rate * master)
    return (moment_one, moment_two, master)

def reference(tokens, grad_out, lengths, members, owners, mat_master, mat_moment1, mat_moment2, vec_master, vec_moment1, vec_moment2):
    block_rows = ROWS // N_DP
    standard = mat_master.reshape(N_DP, block_rows, D)[owners].reshape(ROWS, D)
    weights = lowered_value(standard)
    inputs = tokens.astype(jnp.float32).reshape(N_DP, SENT_DEV, LEN, D)
    cotangent = grad_out.astype(jnp.float32).reshape(N_DP, SENT_DEV, LEN, D)
    seq_lengths = lengths.reshape(N_DP, SENT_DEV)

    def scan_step(running, operands):
        block_in, block_len, block_cot = operands

        def forward(tensor_value, matrices, vector_list):
            return block_forward(tensor_value, block_len, matrices, vector_list)
        output, pull_back = jax.vjp(forward, block_in, weights, vec_master)
        grad_in, grad_mats, grad_vecs = pull_back(block_cot)
        valid_mask = (jnp.arange(LEN)[None, :] < block_len[:, None]).astype(jnp.float32)
        pooled = lax.optimization_barrier(jnp.sum(output * valid_mask[:, :, None], axis=1)) / block_len.astype(jnp.float32)[:, None]
        return ((running[0] + grad_mats, running[1] + grad_vecs), (output.astype(jnp.bfloat16), grad_in.astype(jnp.bfloat16), pooled))
    start_value = (jnp.zeros((ROWS, D), jnp.float32), jnp.zeros((VROWS, D), jnp.float32))
    (mat_grad, vec_grad), (outputs, grads_in, pooled) = lax.scan(scan_step, start_value, (inputs, seq_lengths, cotangent))
    pooled = pooled.reshape(SENT, D)
    listed = members >= 0
    picked = pooled[jnp.where(listed, members, 0)] * listed[:, :, None].astype(jnp.float32)
    group_embeddings = lax.optimization_barrier(jnp.sum(picked, axis=1)) / lax.optimization_barrier(jnp.sum(listed.astype(jnp.float32), axis=1))[:, None]
    grad_norm = jnp.sqrt(jnp.sum(mat_grad * mat_grad) + jnp.sum(vec_grad * vec_grad))
    clip_factor = MAX_NORM / jnp.maximum(grad_norm, MAX_NORM)
    inverse = jnp.argsort(owners).astype(jnp.int32)
    owner_grad = (mat_grad * clip_factor).reshape(N_DP, block_rows, D)[inverse].reshape(ROWS, D)
    matrix_new = adam_step(mat_master, mat_moment1, mat_moment2, owner_grad, RATE_MATRIX, WEIGHT_DECAY)
    vector_new = adam_step(vec_master, vec_moment1, vec_moment2, vec_grad * clip_factor, RATE_VECTOR, 0.0)
    return (outputs.reshape(SENT, LEN, D), grads_in.reshape(SENT, LEN, D), group_embeddings, grad_norm, matrix_new[0], matrix_new[1], matrix_new[2], matrix_new[2].astype(jnp.bfloat16), vector_new[0], vector_new[1], vector_new[2], vector_new[2].astype(jnp.bfloat16))
```

```python
import functools

import jax
import jax.numpy as jnp
from jax import lax
from jax.experimental import pallas as pl
from jax.experimental.pallas import tpu as pltpu
from jax.sharding import PartitionSpec as P

HEADS = 12
HEAD_DIM = 64
FEEDFWD_UNITS = 3072
STEP = 10


NORM_EPS = 1e-06
MASK_FILL = -1e30
MAX_NORM = 1.0
ADAM_ONE = 0.9
ADAM_TWO = 0.999
ADAM_EPS = 1e-08
WEIGHT_DECAY = 0.01
RATE_MATRIX = 0.04
RATE_VECTOR = 0.5

TILE = 384
VMEM_LIMIT = 60 * 1024 * 1024
MESH_ID = pl.DeviceIdType.MESH
LOW = jnp.bfloat16
WIDE = jnp.float32


def adam_step(master, moment_one, moment_two, gradient, learn_rate, decay_rate):
    moment_one = ADAM_ONE * moment_one + (1.0 - ADAM_ONE) * gradient
    moment_two = ADAM_TWO * moment_two + (1.0 - ADAM_TWO) * gradient * gradient
    scaled_one = moment_one / (1.0 - ADAM_ONE**STEP)
    scaled_two = moment_two / (1.0 - ADAM_TWO**STEP)
    master = master - learn_rate * (
        scaled_one / (jnp.sqrt(scaled_two) + ADAM_EPS) + decay_rate * master
    )
    return (moment_one, moment_two, master)


def dot_nn(left, right):
    return jnp.dot(left, right, preferred_element_type=WIDE)


def dot_nt(left, right):
    return lax.dot_general(
        left, right, (((1,), (1,)), ((), ())), preferred_element_type=WIDE
    )


def dot_tn(left, right):
    return lax.dot_general(
        left, right, (((0,), (0,)), ((), ())), preferred_element_type=WIDE
    )


def params(**kwargs):
    return pltpu.CompilerParams(vmem_limit_bytes=VMEM_LIMIT, **kwargs)


def gather_body(w_ref, x_ref, out_ref, xo_ref, send_sem, recv_sem, tok_recv, local_sem):
    dp, sq = lax.axis_index("dp"), lax.axis_index("seq")
    z, x = dp // 2, dp % 2
    y, c = sq // 2, sq % 2
    q, qc, qy, qyc = sq, sq ^ 1, sq ^ 2, sq ^ 3
    dev_c, dev_y, dev_yc, dev_x = (dp, sq ^ 1), (dp, sq ^ 2), (dp, sq ^ 3), (dp ^ 1, sq)
    has_up, has_down, inner = z < 3, z > 0, (z > 0) & (z < 3)
    dev_up = (jnp.minimum(dp + 2, dp % 2 + 6), sq)
    dev_down = (jnp.maximum(dp - 2, dp % 2), sq)
    first = jnp.where(z > 0, z - 1, 1)
    second = jnp.where(z < 2, 2, jnp.where(z == 2, 3, 1))
    third = jnp.where(z < 2, 3, 0)

    barrier = pltpu.get_barrier_semaphore()

    def greet(device):
        pl.semaphore_signal(barrier, inc=1, device_id=device, device_id_type=MESH_ID)

    for device in (dev_c, dev_y, dev_yc, dev_x):
        greet(device)
    pl.when(has_up)(lambda: greet(dev_up))
    pl.when(has_down)(lambda: greet(dev_down))
    pl.semaphore_wait(barrier, 4 + jnp.where(inner, 2, 1))

    count = [0]
    started = []

    def remote(src, dst, recv, device):
        copy = pltpu.make_async_remote_copy(
            src_ref=src,
            dst_ref=dst,
            send_sem=send_sem.at[count[0]],
            recv_sem=recv,
            device_id=device,
            device_id_type=MESH_ID,
        )
        count[0] += 1
        return copy

    def send(src, dst, recv, device):
        copy = remote(src, dst, recv, device)
        copy.start()
        started.append((copy, None))

    def send_if(pred, src, dst, recv, device):
        copy = remote(src, dst, recv, device)
        pl.when(pred)(lambda: copy.start())
        started.append((copy, pred))

    def piece(slot, quarter, device, src=None):
        at = out_ref.at[slot, quarter]
        send(at if src is None else src, at, recv_sem.at[slot, quarter], device)

    def arrived(slot, quarter):
        at = out_ref.at[slot, quarter]
        pltpu.make_async_copy(at, at, recv_sem.at[slot, quarter]).wait()

    locals_ = [pltpu.make_async_copy(w_ref, out_ref.at[dp], local_sem.at[0])]
    oy = 1 - y
    full_own, full_sib = 3 * y + 2 * c, 3 * y + 2 * (1 - c)
    full_far, full_cross = 3 * oy + 2 * c, 3 * oy + 2 * (1 - c)

    def full_rows(j):
        return xo_ref.at[pl.ds(128 * j, 128)]

    def half_rows(part, j, core):
        return xo_ref.at[pl.ds(512 + 256 * (part ^ core) + 64 * j, 64)]

    locals_.append(pltpu.make_async_copy(x_ref.at[full_own], full_rows(sq), local_sem.at[1]))
    for part in range(2):
        locals_.append(
            pltpu.make_async_copy(
                x_ref.at[3 * y + 1, pl.ds(64 * part, 64)],
                half_rows(part, sq, c),
                local_sem.at[2 + part],
            )
        )
    send(x_ref.at[full_far], full_rows(sq), tok_recv.at[sq, 0], dev_y)
    for part in range(2):
        send(
            x_ref.at[3 * oy + 1, pl.ds(64 * part, 64)],
            half_rows(part, sq, c),
            tok_recv.at[sq, 1 + part],
            dev_y,
        )
    send(x_ref.at[full_cross], full_rows(sq), tok_recv.at[sq, 0], dev_yc)
    own = w_ref.at[q]
    piece(dp, q, dev_x, own)
    at = out_ref.at[dp, q]
    send_if(has_up, own, at, recv_sem.at[dp, q], dev_up)
    send_if(has_down, own, at, recv_sem.at[dp, q], dev_down)
    send(x_ref.at[full_sib], full_rows(sq), tok_recv.at[sq, 0], dev_c)
    for part in range(2):
        send(
            x_ref.at[3 * y + 1, pl.ds(64 * part, 64)],
            half_rows(part, sq, 1 - c),
            tok_recv.at[sq, 1 + part],
            dev_c,
        )
    for copy in locals_:
        copy.start()

    def line_step(source):
        slot = 2 * source + x
        arrived(slot, q)
        at = out_ref.at[slot, q]
        onward = (jnp.where(source < z, dev_up[0], dev_down[0]), sq)
        send_if(inner, at, at, recv_sem.at[slot, q], onward)
        piece(slot, q, dev_x)
        piece(slot, q, dev_y)
        piece(slot, q, dev_c)

    far = lambda source: 2 * source + (1 - x)
    line_step(first)
    arrived(dp ^ 1, q)
    piece(dp ^ 1, q, dev_c)
    line_step(second)
    arrived(far(first), q)
    piece(far(first), q, dev_c)
    for part in range(2):
        at = half_rows(part, sq ^ 2, c)
        pltpu.make_async_copy(at, at, tok_recv.at[sq ^ 2, 1 + part]).wait()
        send(at, half_rows(part, sq ^ 2, 1 - c), tok_recv.at[sq ^ 2, 1 + part], dev_c)
    line_step(third)
    arrived(far(second), q)
    piece(far(second), q, dev_y)
    piece(far(second), q, dev_c)
    arrived(2 * first + x, qy)
    piece(2 * first + x, qy, dev_x)
    piece(2 * first + x, qy, dev_c)
    piece(dp, qy, dev_x, w_ref.at[qy])
    arrived(2 * second + x, qy)
    piece(2 * second + x, qy, dev_c)
    arrived(far(third), q)
    piece(far(third), q, dev_y)
    piece(far(third), q, dev_c)
    for slot in (2 * third + x, far(second), far(first), dp ^ 1, far(third)):
        arrived(slot, qy)
        piece(slot, qy, dev_c)
    for step in range(1, 8):
        slot = (dp + step) % 8
        arrived(slot, qc)
        arrived(slot, qyc)
    for other in (sq ^ 1, sq ^ 2, sq ^ 3):
        at = full_rows(other)
        pltpu.make_async_copy(at, at, tok_recv.at[other, 0]).wait()
    for other in (sq ^ 1, sq ^ 3):
        for part in range(2):
            at = half_rows(part, other, c)
            pltpu.make_async_copy(at, at, tok_recv.at[other, 1 + part]).wait()
    for copy in locals_:
        copy.wait()
    for copy, pred in started:
        if pred is None:
            copy.wait_send()
        else:
            pl.when(pred)(lambda copy=copy: copy.wait_send())


def gather_all(block_low, tokens):
    block_rows, width = block_low.shape
    quarter = block_rows // 4
    out, spread = pl.pallas_call(
        gather_body,
        out_shape=(
            jax.ShapeDtypeStruct((8, 4, quarter, width), LOW),
            jax.ShapeDtypeStruct((1024, width), LOW),
        ),
        in_specs=[pl.BlockSpec(memory_space=pl.ANY)] * 2,
        out_specs=(pl.BlockSpec(memory_space=pl.ANY),) * 2,
        scratch_shapes=[
            pltpu.SemaphoreType.DMA((64,)),
            pltpu.SemaphoreType.DMA((8, 4)),
            pltpu.SemaphoreType.DMA((4, 3)),
            pltpu.SemaphoreType.DMA((4,)),
        ],
        compiler_params=params(collective_id=1, has_side_effects=True),
        name="gather_weights",
    )(block_low.reshape(4, quarter, width), tokens)
    return out.reshape(8 * block_rows // TILE, TILE, width), spread


def qkv_body(map_ref, x_ref, top_ref, low_ref, bias_ref, out_ref):
    part = pl.program_id(0)
    scale = jnp.where(part == 0, HEAD_DIM ** (-0.5), 1.0)
    value = dot_nn(x_ref[:, :TILE], top_ref[0]) + dot_nn(x_ref[:, TILE:], low_ref[0])
    value = (value + bias_ref[0]).astype(LOW).astype(WIDE)
    out_ref[0] = (value * scale).astype(LOW)


def qkv_project(tile_map, rows, weights, bias):
    count, width = rows.shape
    return pl.pallas_call(
        qkv_body,
        grid_spec=pltpu.PrefetchScalarGridSpec(
            num_scalar_prefetch=1,
            grid=(3,),
            in_specs=[
                pl.BlockSpec((count, width), lambda i, m: (0, 0)),
                pl.BlockSpec((1, TILE, width), lambda i, m: (m[2 * i], 0, 0)),
                pl.BlockSpec((1, TILE, width), lambda i, m: (m[2 * i + 1], 0, 0)),
                pl.BlockSpec((1, 1, width), lambda i, m: (i, 0, 0)),
            ],
            out_specs=pl.BlockSpec((1, count, width), lambda i, m: (i, 0, 0)),
        ),
        out_shape=jax.ShapeDtypeStruct((3, count, width), LOW),
        compiler_params=params(),
        name="qkv",
    )(tile_map, rows, weights, weights, bias)


def head_masks(shape):
    lane = lax.broadcasted_iota(jnp.int32, shape, 1)
    return (lane < HEAD_DIM, lane >= HEAD_DIM)


def attend_body(q_ref, k_ref, v_ref, bias_ref, o_ref, lse_ref):
    queries, keys = q_ref[0], k_ref[0]
    value_t = v_ref[0].T
    bias = jnp.concatenate([bias_ref[0], bias_ref[0]], axis=1)
    outs = []
    for head, mask in enumerate(head_masks(queries.shape)):
        scores = dot_nt(keys, jnp.where(mask, queries, jnp.zeros_like(queries))) + bias
        top = jnp.max(scores, axis=0, keepdims=True)
        shifted = jnp.exp(scores - top)
        total = jnp.sum(shifted, axis=0, keepdims=True)
        part = value_t[HEAD_DIM * head : HEAD_DIM * (head + 1)]
        outs.append(dot_nn(part, shifted.astype(LOW)) * (1.0 / total))
        lse_ref[0, head : head + 1, :] = top + jnp.log(total)
    o_ref[...] = jnp.concatenate(outs, axis=0).T.astype(LOW)


def attend(qkv, bias):
    width = qkv.shape[-1]
    pairs = width // 128
    return pl.pallas_call(
        attend_body,
        grid=(3, pairs),
        in_specs=[
            pl.BlockSpec((1, 256, 128), lambda i, h: (0, i, h)),
            pl.BlockSpec((1, 512, 128), lambda i, h: (1, i // 2, h)),
            pl.BlockSpec((1, 512, 128), lambda i, h: (2, i // 2, h)),
            pl.BlockSpec((1, 512, 128), lambda i, h: (i // 2, 0, 0)),
        ],
        out_specs=(
            pl.BlockSpec((256, 128), lambda i, h: (i, h)),
            pl.BlockSpec((1, 2, 256), lambda i, h: (h, 0, i)),
        ),
        out_shape=(
            jax.ShapeDtypeStruct((768, width), LOW),
            jax.ShapeDtypeStruct((pairs, 2, 768), WIDE),
        ),
        compiler_params=params(),
        name="attend",
    )(qkv, qkv, qkv, bias)


def attend_back_body(
    q_ref, k_ref, v_ref, bias_ref, lse_ref, do_ref, o_ref, dq_ref, dk_ref, dv_ref, dk_acc, dv_acc
):
    block = pl.program_id(1)

    @pl.when(block == 3)
    def _():
        dq_ref[...] = jnp.zeros_like(dq_ref)

    @pl.when(block < 3)
    def _():
        queries, keys, values, grads = q_ref[0], k_ref[0], v_ref[0], do_ref[...]
        keys_t = keys.T
        inner = (grads.astype(WIDE) * o_ref[...].astype(WIDE)).T
        bias = jnp.concatenate([bias_ref[0], bias_ref[0]], axis=1)
        d_query = []
        d_key = d_value = 0.0
        for head, mask in enumerate(head_masks(queries.shape)):
            query = jnp.where(mask, queries, jnp.zeros_like(queries))
            grad = jnp.where(mask, grads, jnp.zeros_like(grads))
            rows = slice(HEAD_DIM * head, HEAD_DIM * (head + 1))
            inner_sum = jnp.sum(inner[rows], axis=0, keepdims=True)
            scores = dot_nt(keys, query) + bias
            probs = jnp.exp(scores - lse_ref[0, head : head + 1, :])
            d_probs = dot_nt(values, grad)
            d_scores = (probs * (d_probs - inner_sum)).astype(LOW)
            d_value = d_value + dot_nn(probs.astype(LOW), grad)
            d_key = d_key + dot_nn(d_scores, query)
            d_query.append(dot_nn(keys_t[rows], d_scores))
        d_query = jnp.concatenate(d_query, axis=0) * HEAD_DIM ** (-0.5)
        dq_ref[...] = d_query.T.astype(LOW)

        @pl.when(block == 0)
        def _():
            dk_acc[...] = d_key
            dv_acc[...] = d_value

        @pl.when(block == 1)
        def _():
            dk_ref[...] = (dk_acc[...] + d_key).astype(LOW)
            dv_ref[...] = (dv_acc[...] + d_value).astype(LOW)

        @pl.when(block == 2)
        def _():
            dk_ref[...] = d_key.astype(LOW)
            dv_ref[...] = d_value.astype(LOW)


def attend_back(qkv, bias, lse, d_out, out):
    width = qkv.shape[-1]
    pairs = width // 128
    query_at = lambda h, i: (jnp.minimum(i, 2), h)
    full = jax.ShapeDtypeStruct((1024, width), LOW)
    return pl.pallas_call(
        attend_back_body,
        grid=(pairs, 4),
        in_specs=[
            pl.BlockSpec((1, 256, 128), lambda h, i: (0, jnp.minimum(i, 2), h)),
            pl.BlockSpec((1, 512, 128), lambda h, i: (1, i // 2, h)),
            pl.BlockSpec((1, 512, 128), lambda h, i: (2, i // 2, h)),
            pl.BlockSpec((1, 512, 128), lambda h, i: (i // 2, 0, 0)),
            pl.BlockSpec((1, 2, 256), lambda h, i: (h, 0, jnp.minimum(i, 2))),
            pl.BlockSpec((256, 128), query_at),
            pl.BlockSpec((256, 128), query_at),
        ],
        out_specs=(
            pl.BlockSpec((256, 128), lambda h, i: (i, h)),
            pl.BlockSpec((512, 128), lambda h, i: (i // 2, h)),
            pl.BlockSpec((512, 128), lambda h, i: (i // 2, h)),
        ),
        out_shape=(full, full, full),
        scratch_shapes=[pltpu.VMEM((512, 128), WIDE), pltpu.VMEM((512, 128), WIDE)],
        compiler_params=params(),
        name="attend_back",
    )(qkv, qkv, qkv, bias, lse, d_out, out)


def row_mean(value):
    return jnp.mean(value, axis=-1, keepdims=True)


def col_sum(value):
    return jnp.sum(value, axis=0, keepdims=True)


def middle_body(
    map_ref, o_ref, x_ref, gy_ref, valid_ref, w_ref, vec_ref,
    y_ref, left_ref, right_ref, do_ref, da_ref, dh_ref, sums_ref,
    w_buf, slope, total, hat_one, rstd_one, sem,
):
    step = pl.program_id(0)
    tiles = w_buf.shape[0]
    chunks = FEEDFWD_UNITS // 768

    def fetch(t):
        return pltpu.make_async_copy(w_ref.at[map_ref[6 + t]], w_buf.at[t], sem.at[t])

    def ready(first, count):
        @pl.when(step == 0)
        def _():
            for t in range(first, first + count):
                fetch(t).wait()

    @pl.when(step == 0)
    def _():
        for t in range(tiles):
            fetch(t).start()
        sums_ref[...] = jnp.zeros_like(sums_ref)

    def add_row(row, value):
        sums_ref[row : row + 1, :] += value

    def vec(row):
        return vec_ref[row : row + 1, :]

    ready(0, 2)
    branch = dot_nn(o_ref[:, :TILE], w_buf[0]) + dot_nn(o_ref[:, TILE:], w_buf[1]) + vec(2)
    resid = x_ref[...].astype(WIDE) + branch
    centered = resid - row_mean(resid)
    rstd = lax.rsqrt(row_mean(centered * centered) + NORM_EPS)
    rstd_one[...] = rstd
    hat = centered * rstd
    hat_one[...] = hat
    first = hat * vec(4) + vec(5)
    total[...] = first + vec(3)
    first_low = first.astype(LOW)
    right_ref[0] = first_low

    for c in range(chunks):
        ready(2 + 2 * c, 2)
        ready(10 + 2 * c, 2)
        for u in range(2):
            t = 2 * c + u
            cols = slice(TILE * t, TILE * (t + 1))
            act = dot_nt(first_low, w_buf[2 + t]) + vec_ref[
                8 + c : 9 + c, TILE * u : TILE * (u + 1)
            ]
            cdf = 0.5 + 0.5 * lax.erf(act * (0.5**0.5))
            pdf = jnp.exp(-0.5 * act * act) * 0.3989422804014327
            slope[:, cols] = cdf + act * pdf
            active = (act * cdf).astype(LOW)
            left_ref[1, :, cols] = active
            total[...] += dot_nn(active, w_buf[10 + t])

    resid = total[...]
    centered = resid - row_mean(resid)
    rstd = lax.rsqrt(row_mean(centered * centered) + NORM_EPS)
    hat = centered * rstd
    result = hat * vec(6) + vec(7)
    y_ref[...] = result.astype(LOW)
    pooled = col_sum(result * valid_ref[...])
    sums_ref[pl.ds(10 + step // 2, 1), :] += pooled
    grad = gy_ref[...].astype(WIDE)
    add_row(4, col_sum(grad * hat))
    add_row(5, col_sum(grad))
    grad = grad * vec(6)
    d_resid = rstd * (grad - row_mean(grad) - hat * row_mean(grad * hat))
    total[...] = d_resid
    grad_low = d_resid.astype(LOW)
    right_ref[1] = grad_low
    add_row(1, col_sum(grad_low.astype(WIDE)))

    for c in range(chunks):
        for u in range(2):
            t = 2 * c + u
            cols = slice(TILE * t, TILE * (t + 1))
            d_active = dot_nt(grad_low, w_buf[10 + t])
            d_act = (d_active * slope[:, cols]).astype(LOW)
            left_ref[0, :, cols] = d_act
            sums_ref[6 + c : 7 + c, TILE * u : TILE * (u + 1)] += col_sum(d_act.astype(WIDE))
            total[...] += dot_nn(d_act, w_buf[2 + t])

    grad = total[...]
    hat = hat_one[...]
    add_row(2, col_sum(grad * hat))
    add_row(3, col_sum(grad))
    grad = grad * vec(4)
    d_resid = rstd_one[...] * (grad - row_mean(grad) - hat * row_mean(grad * hat))
    dh_ref[...] = d_resid
    grad_low = d_resid.astype(LOW)
    da_ref[...] = grad_low
    add_row(0, col_sum(grad_low.astype(WIDE)))
    do_ref[:, :TILE] = dot_nt(grad_low, w_buf[0]).astype(LOW)
    do_ref[:, TILE:] = dot_nt(grad_low, w_buf[1]).astype(LOW)


def middle(tile_map, attended, rows, out_grad, valid, weights, vectors):
    width = attended.shape[1]
    tiles = 2 + 2 * FEEDFWD_UNITS // TILE
    block = pl.BlockSpec((256, width), lambda i, m: (i, 0))
    flat = jax.ShapeDtypeStruct((768, width), LOW)
    return pl.pallas_call(
        middle_body,
        grid_spec=pltpu.PrefetchScalarGridSpec(
            num_scalar_prefetch=1,
            grid=(3,),
            in_specs=[
                block,
                block,
                block,
                pl.BlockSpec((256, 1), lambda i, m: (i, 0)),
                pl.BlockSpec(memory_space=pl.ANY),
                pl.BlockSpec(vectors.shape, lambda i, m: (0, 0)),
            ],
            out_specs=(
                block,
                pl.BlockSpec((2, 256, FEEDFWD_UNITS), lambda i, m: (0, i, 0)),
                pl.BlockSpec((2, 256, width), lambda i, m: (0, i, 0)),
                block,
                block,
                block,
                pl.BlockSpec((16, width), lambda i, m: (0, 0)),
            ),
            scratch_shapes=[
                pltpu.VMEM((tiles, TILE, width), LOW),
                pltpu.VMEM((256, FEEDFWD_UNITS), WIDE),
                pltpu.VMEM((256, width), WIDE),
                pltpu.VMEM((256, width), WIDE),
                pltpu.VMEM((256, 1), WIDE),
                pltpu.SemaphoreType.DMA((tiles,)),
            ],
        ),
        out_shape=(
            flat,
            jax.ShapeDtypeStruct((2, 768, FEEDFWD_UNITS), LOW),
            jax.ShapeDtypeStruct((2, 768, width), LOW),
            flat,
            flat,
            jax.ShapeDtypeStruct((768, width), WIDE),
            jax.ShapeDtypeStruct((16, width), WIDE),
        ),
        compiler_params=params(),
        name="feed_forward",
    )(tile_map, attended, rows, out_grad, valid, weights, vectors)


def grad_ff_body(map_ref, left_ref, right_ref, out_ref):
    out_ref[0] = dot_tn(left_ref[0], right_ref[0]).astype(LOW)


def grad_ff(tile_map, left, right):
    per = FEEDFWD_UNITS // TILE
    count, width = right.shape[1:]
    return pl.pallas_call(
        grad_ff_body,
        grid_spec=pltpu.PrefetchScalarGridSpec(
            num_scalar_prefetch=1,
            grid=(2 * per,),
            in_specs=[
                pl.BlockSpec((1, count, TILE), lambda i, m: (i // per, 0, i % per)),
                pl.BlockSpec((1, count, width), lambda i, m: (i // per, 0, 0)),
            ],
            out_specs=pl.BlockSpec((1, TILE, width), lambda i, m: (m[8 + i], 0, 0)),
        ),
        out_shape=jax.ShapeDtypeStruct((8 + 2 * per, TILE, width), LOW),
        compiler_params=params(),
        name="grad_ff",
    )(tile_map, left, right)


def grad_attn_body(
    map_ref, x_ref, dq_ref, dk_ref, dv_ref, o_ref, da_ref, into_ref, out_ref, sums_ref
):
    step = pl.program_id(0)
    for part, grad_ref in enumerate((dq_ref, dk_ref, dv_ref)):

        @pl.when(step // 2 == part)
        def _(grad_ref=grad_ref):
            out_ref[0] = dot_tn(x_ref[...], grad_ref[...]).astype(LOW)

    @pl.when(step // 2 == 3)
    def _():
        out_ref[0] = dot_tn(o_ref[...], da_ref[...]).astype(LOW)

    @pl.when(step == 0)
    def _():
        sums_ref[...] = jnp.zeros_like(sums_ref)
        sums_ref[0:1, :] = col_sum(dq_ref[...].astype(WIDE))
        sums_ref[1:2, :] = col_sum(dv_ref[...].astype(WIDE))


def grad_attn(tile_map, rows, dq, dk, dv, attended, da, into):
    count, width = rows.shape
    whole = pl.BlockSpec((count, width), lambda i, m: (0, 0))
    return pl.pallas_call(
        grad_attn_body,
        grid_spec=pltpu.PrefetchScalarGridSpec(
            num_scalar_prefetch=1,
            grid=(8,),
            in_specs=[
                pl.BlockSpec((count, TILE), lambda i, m: (0, i % 2)),
                whole,
                whole,
                whole,
                pl.BlockSpec((768, TILE), lambda i, m: (0, i % 2)),
                pl.BlockSpec((768, width), lambda i, m: (0, 0)),
                pl.BlockSpec(memory_space=pl.ANY),
            ],
            out_specs=(
                pl.BlockSpec((1, TILE, width), lambda i, m: (m[i], 0, 0)),
                pl.BlockSpec((8, width), lambda i, m: (0, 0)),
            ),
        ),
        out_shape=(
            jax.ShapeDtypeStruct(into.shape, LOW),
            jax.ShapeDtypeStruct((8, width), WIDE),
        ),
        input_output_aliases={7: 0},
        compiler_params=params(),
        name="grad_attn",
    )(tile_map, rows, dq, dk, dv, attended, da, into)


def grad_in_body(map_ref, dq_ref, dk_ref, dv_ref, dh_ref, *refs):
    w_refs, out_ref = refs[:6], refs[6]
    keep = (pl.program_id(0) < 3).astype(WIDE)
    for half in range(2):
        cols = slice(TILE * half, TILE * (half + 1))
        value = dh_ref[:, cols] * keep
        for part, grad_ref in enumerate((dq_ref, dk_ref, dv_ref)):
            value = value + dot_nt(grad_ref[...], w_refs[2 * part + half][0])
        out_ref[:, cols] = value.astype(LOW)


def grad_in(tile_map, dq, dk, dv, dh, weights):
    count, width = dq.shape
    block = pl.BlockSpec((256, width), lambda i, m: (i, 0))
    return pl.pallas_call(
        grad_in_body,
        grid_spec=pltpu.PrefetchScalarGridSpec(
            num_scalar_prefetch=1,
            grid=(count // 256,),
            in_specs=[
                block,
                block,
                block,
                pl.BlockSpec((256, width), lambda i, m: (jnp.minimum(i, 2), 0)),
            ]
            + [
                pl.BlockSpec((1, TILE, width), lambda i, m, t=t: (m[t], 0, 0)) for t in range(6)
            ],
            out_specs=block,
        ),
        out_shape=jax.ShapeDtypeStruct((count, width), LOW),
        compiler_params=params(),
        name="grad_in",
    )(tile_map, dq, dk, dv, dh, *([weights] * 6))


def to_sentences(value):
    sent_dev, local_len, width = value.shape
    pieces = []
    for j in range(4):
        y, c = j // 2, j % 2
        pieces.append(value[3 * y + 2 * c])
        pieces.append(value[3 * y + 1, 64 * c : 64 * c + 64])
    moved = jnp.concatenate(pieces, axis=0).reshape(4, 192, width)
    moved = lax.all_to_all(moved, "seq", split_axis=0, concat_axis=0, tiled=True)
    return jnp.concatenate(
        [moved[:, :128].reshape(512, width), moved[:, 128:].reshape(256, width)], axis=0
    )


def to_positions(value):
    width = value.shape[1]
    moved = jnp.concatenate(
        [value[:512].reshape(4, 128, width), value[512:].reshape(4, 64, width)], axis=1
    )
    moved = lax.all_to_all(moved, "seq", split_axis=0, concat_axis=0, tiled=True)
    rows = []
    for y in range(2):
        rows.append(moved[2 * y, :128])
        rows.append(jnp.concatenate([moved[2 * y, 128:], moved[2 * y + 1, 128:]], axis=0))
        rows.append(moved[2 * y + 1, :128])
    return jnp.stack(rows)


def to_rows(tokens):
    width = tokens.shape[-1]
    core = lax.axis_index("seq") % 2
    pieces = []
    for j in range(4):
        y, c = j // 2, j % 2
        pieces += [tokens[3 * y + 2 * c], tokens[3 * y + 1]]
    moved = jnp.concatenate(pieces, axis=0).reshape(4, 256, width)
    moved = lax.all_to_all(moved, "seq", split_axis=0, concat_axis=0, tiled=True)
    shared = moved[:, 128:].reshape(4, 2, 64, width)
    own = lax.dynamic_index_in_dim(shared, core, 1, keepdims=False)
    other = lax.dynamic_index_in_dim(shared, 1 - core, 1, keepdims=False)
    return jnp.concatenate(
        [moved[:, :128].reshape(512, width), own.reshape(256, width), other.reshape(256, width)],
        axis=0,
    )


def local(
    tokens,
    grad_out,
    lengths,
    members,
    owners,
    mat_master,
    mat_moment1,
    mat_moment2,
    vec_master,
    vec_moment1,
    vec_moment2,
):
    sent_dev, local_len, model_width = tokens.shape
    dp_count = lax.axis_size("dp")
    block_rows = mat_master.shape[0]
    seq_at = lax.axis_index("seq")
    group, core = seq_at // 2, seq_at % 2
    tiles = dp_count * block_rows // TILE
    direct = dp_count == 8 and block_rows % TILE == 0

    block_low = mat_master.astype(LOW)
    if direct:
        weights, rows = gather_all(block_low, tokens)
        per = block_rows // TILE
        tile_map = (owners[:, None] * per + jnp.arange(per)[None, :]).reshape(-1)
    else:
        gathered = lax.all_gather(block_low, "dp", axis=0, tiled=True)
        weights = gathered.reshape(dp_count, block_rows, model_width)[owners]
        weights = weights.reshape(tiles, TILE, model_width)
        rows = to_rows(tokens)
        tile_map = jnp.arange(tiles)
    tile_map = tile_map.astype(jnp.int32)
    out_grad = to_sentences(grad_out)

    full_at = jnp.arange(512)
    half_at = jnp.arange(256)
    half_at = (half_at // 64) * 128 + half_at % 64
    shared_at = jnp.concatenate([half_at + 64 * core, half_at + 64 * (1 - core)])
    full_id, shared_id = 3 * group + 2 * core, 3 * group + 1
    full_ok = full_at < lengths[full_id]
    shared_ok = shared_at < lengths[shared_id]
    bias = jnp.where(jnp.stack([full_ok, shared_ok]), 0.0, MASK_FILL).astype(WIDE)
    bias = jnp.broadcast_to(bias[:, :, None], (2, 512, 128))
    valid = jnp.concatenate([full_ok, shared_ok[:256]]).astype(WIDE)[:, None]

    qkv_bias = jnp.stack([vec_master[0], jnp.zeros_like(vec_master[0]), vec_master[1]])[:, None, :]
    qkv = qkv_project(tile_map, rows, weights, qkv_bias)
    attended, lse = attend(qkv, bias)
    result, left, right, d_attended, d_branch, d_resid, sums = middle(
        tile_map, attended, rows, out_grad, valid, weights, vec_master
    )
    output = to_positions(result)
    grads = grad_ff(tile_map, left, right)
    dq, dk, dv = attend_back(qkv, bias, lse, d_attended, attended)
    grads, sums_qv = grad_attn(tile_map, rows, dq, dk, dv, attended, d_branch, grads)
    grad_rows = grad_in(tile_map, dq, dk, dv, d_resid, weights)
    swap = [(j, j ^ 1) for j in range(4)]
    from_other = lax.ppermute(grad_rows[768:], "seq", swap)
    shared = (grad_rows[512:768].astype(WIDE) + from_other.astype(WIDE)).astype(LOW)
    input_grad = to_positions(jnp.concatenate([grad_rows[:512], shared], axis=0))

    place = jnp.arange(sent_dev)[:, None]
    pooled = jnp.where(place == full_id, sums[10:11], 0.0) + jnp.where(
        place == shared_id, sums[11:12], 0.0
    )
    pooled = lax.psum(pooled, "seq") / lengths.astype(WIDE)[:, None]
    local_ids = members - lax.axis_index("dp") * sent_dev
    listed = members >= 0
    member_table = jnp.sum(
        (
            (local_ids[:, :, None] == jnp.arange(sent_dev)[None, None, :]) & listed[:, :, None]
        ).astype(WIDE),
        axis=1,
    )
    group_emb = (
        jnp.dot(member_table, pooled, precision=lax.Precision.HIGHEST)
        / jnp.sum(listed.astype(WIDE), axis=1)[:, None]
    )

    if not direct:
        inverse = jnp.argsort(owners)
        grads = grads.reshape(dp_count, block_rows, model_width)[inverse]
    grads = grads.reshape(dp_count * block_rows, model_width)
    owned_quarter = lax.psum_scatter(grads, ("dp", "seq"), scatter_dimension=0, tiled=True)
    owned_rows = lax.all_gather(owned_quarter, "seq", axis=0, tiled=True).astype(WIDE)
    local_vec = jnp.concatenate([sums_qv[0:2], sums[0:10]], axis=0)
    quarter_wide = owned_quarter.astype(WIDE)
    square_sum, vec_total = lax.psum(
        (jnp.sum(quarter_wide * quarter_wide), local_vec), ("dp", "seq")
    )
    grad_norm = jnp.sqrt(square_sum + jnp.sum(vec_total * vec_total))
    clip_factor = MAX_NORM / jnp.maximum(grad_norm, MAX_NORM)
    matrix_new = adam_step(
        mat_master, mat_moment1, mat_moment2, owned_rows * clip_factor, RATE_MATRIX, WEIGHT_DECAY
    )
    vector_new = adam_step(
        vec_master, vec_moment1, vec_moment2, vec_total * clip_factor, RATE_VECTOR, 0.0
    )
    return (
        output,
        input_grad,
        group_emb,
        grad_norm,
        matrix_new[0],
        matrix_new[1],
        matrix_new[2],
        matrix_new[2].astype(LOW),
        vector_new[0],
        vector_new[1],
        vector_new[2],
        vector_new[2].astype(LOW),
    )


def solution(mesh):
    placed = (
        P("dp", "seq", None),
        P("dp", "seq", None),
        P("dp"),
        P("dp", None),
        P(),
        P("dp", None),
        P("dp", None),
        P("dp", None),
        P(),
        P(),
        P(),
    )
    return jax.shard_map(
        local,
        mesh=mesh,
        in_specs=placed,
        out_specs=(
            P("dp", "seq", None),
            P("dp", "seq", None),
            P("dp", None),
            P(),
            P("dp", None),
            P("dp", None),
            P("dp", None),
            P("dp", None),
            P(),
            P(),
            P(),
            P(),
        ),
        check_vma=False,
    )
```

```python
import functools

import jax
import jax.numpy as jnp
from jax import lax
from jax.experimental import pallas as pl
from jax.experimental.pallas import tpu as pltpu
from jax.sharding import PartitionSpec as P

HEADS = 12
HEAD_DIM = 64
FEEDFWD_UNITS = 3072
STEP = 10


NORM_EPS = 1e-06
MASK_FILL = -1e30
MAX_NORM = 1.0
ADAM_ONE = 0.9
ADAM_TWO = 0.999
ADAM_EPS = 1e-08
WEIGHT_DECAY = 0.01
RATE_MATRIX = 0.04
RATE_VECTOR = 0.5

TILE = 384
VMEM_LIMIT = 60 * 1024 * 1024
MESH_ID = pl.DeviceIdType.MESH
LOW = jnp.bfloat16
WIDE = jnp.float32


def adam_step(master, moment_one, moment_two, gradient, learn_rate, decay_rate):
    moment_one = ADAM_ONE * moment_one + (1.0 - ADAM_ONE) * gradient
    moment_two = ADAM_TWO * moment_two + (1.0 - ADAM_TWO) * gradient * gradient
    scaled_one = moment_one / (1.0 - ADAM_ONE**STEP)
    scaled_two = moment_two / (1.0 - ADAM_TWO**STEP)
    master = master - learn_rate * (
        scaled_one / (jnp.sqrt(scaled_two) + ADAM_EPS) + decay_rate * master
    )
    return (moment_one, moment_two, master)


def dot_nn(left, right):
    return jnp.dot(left, right, preferred_element_type=WIDE)


def dot_nt(left, right):
    return lax.dot_general(
        left, right, (((1,), (1,)), ((), ())), preferred_element_type=WIDE
    )


def dot_tn(left, right):
    return lax.dot_general(
        left, right, (((0,), (0,)), ((), ())), preferred_element_type=WIDE
    )


def params(**kwargs):
    return pltpu.CompilerParams(vmem_limit_bytes=VMEM_LIMIT, **kwargs)


def gather_body(w_ref, x_ref, out_ref, xo_ref, send_sem, recv_sem, tok_recv, local_sem):
    dp, sq = lax.axis_index("dp"), lax.axis_index("seq")
    z, x = dp // 2, dp % 2
    y, c = sq // 2, sq % 2
    q, qc, qy, qyc = sq, sq ^ 1, sq ^ 2, sq ^ 3
    dev_c, dev_y, dev_yc, dev_x = (dp, sq ^ 1), (dp, sq ^ 2), (dp, sq ^ 3), (dp ^ 1, sq)
    has_up, has_down, inner = z < 3, z > 0, (z > 0) & (z < 3)
    dev_up = (jnp.minimum(dp + 2, dp % 2 + 6), sq)
    dev_down = (jnp.maximum(dp - 2, dp % 2), sq)
    first = jnp.where(z > 0, z - 1, 1)
    second = jnp.where(z < 2, 2, jnp.where(z == 2, 3, 1))
    third = jnp.where(z < 2, 3, 0)

    barrier = pltpu.get_barrier_semaphore()

    def greet(device):
        pl.semaphore_signal(barrier, inc=1, device_id=device, device_id_type=MESH_ID)

    for device in (dev_c, dev_y, dev_yc, dev_x):
        greet(device)
    pl.when(has_up)(lambda: greet(dev_up))
    pl.when(has_down)(lambda: greet(dev_down))
    pl.semaphore_wait(barrier, 4 + jnp.where(inner, 2, 1))

    count = [0]
    started = []

    def remote(src, dst, recv, device):
        copy = pltpu.make_async_remote_copy(
            src_ref=src,
            dst_ref=dst,
            send_sem=send_sem.at[count[0]],
            recv_sem=recv,
            device_id=device,
            device_id_type=MESH_ID,
        )
        count[0] += 1
        return copy

    def send(src, dst, recv, device):
        copy = remote(src, dst, recv, device)
        copy.start()
        started.append((copy, None))

    def send_if(pred, src, dst, recv, device):
        copy = remote(src, dst, recv, device)
        pl.when(pred)(lambda: copy.start())
        started.append((copy, pred))

    def piece(slot, quarter, device, src=None):
        at = out_ref.at[slot, quarter]
        send(at if src is None else src, at, recv_sem.at[slot, quarter], device)

    def arrived(slot, quarter):
        at = out_ref.at[slot, quarter]
        pltpu.make_async_copy(at, at, recv_sem.at[slot, quarter]).wait()

    locals_ = [pltpu.make_async_copy(w_ref, out_ref.at[dp], local_sem.at[0])]
    oy = 1 - y
    full_own, full_sib = 3 * y + 2 * c, 3 * y + 2 * (1 - c)
    full_far, full_cross = 3 * oy + 2 * c, 3 * oy + 2 * (1 - c)

    def full_rows(j):
        return xo_ref.at[pl.ds(128 * j, 128)]

    def half_rows(part, j, core):
        return xo_ref.at[pl.ds(512 + 256 * (part ^ core) + 64 * j, 64)]

    locals_.append(pltpu.make_async_copy(x_ref.at[full_own], full_rows(sq), local_sem.at[1]))
    for part in range(2):
        locals_.append(
            pltpu.make_async_copy(
                x_ref.at[3 * y + 1, pl.ds(64 * part, 64)],
                half_rows(part, sq, c),
                local_sem.at[2 + part],
            )
        )
    send(x_ref.at[full_far], full_rows(sq), tok_recv.at[sq, 0], dev_y)
    for part in range(2):
        send(
            x_ref.at[3 * oy + 1, pl.ds(64 * part, 64)],
            half_rows(part, sq, c),
            tok_recv.at[sq, 1 + part],
            dev_y,
        )
    send(x_ref.at[full_cross], full_rows(sq), tok_recv.at[sq, 0], dev_yc)
    own = w_ref.at[q]
    piece(dp, q, dev_x, own)
    at = out_ref.at[dp, q]
    send_if(has_up, own, at, recv_sem.at[dp, q], dev_up)
    send_if(has_down, own, at, recv_sem.at[dp, q], dev_down)
    send(x_ref.at[full_sib], full_rows(sq), tok_recv.at[sq, 0], dev_c)
    for part in range(2):
        send(
            x_ref.at[3 * y + 1, pl.ds(64 * part, 64)],
            half_rows(part, sq, 1 - c),
            tok_recv.at[sq, 1 + part],
            dev_c,
        )
    for copy in locals_:
        copy.start()

    def line_step(source):
        slot = 2 * source + x
        arrived(slot, q)
        at = out_ref.at[slot, q]
        onward = (jnp.where(source < z, dev_up[0], dev_down[0]), sq)
        send_if(inner, at, at, recv_sem.at[slot, q], onward)
        piece(slot, q, dev_x)
        piece(slot, q, dev_y)
        piece(slot, q, dev_c)

    far = lambda source: 2 * source + (1 - x)
    line_step(first)
    arrived(dp ^ 1, q)
    piece(dp ^ 1, q, dev_c)
    line_step(second)
    arrived(far(first), q)
    piece(far(first), q, dev_c)
    for part in range(2):
        at = half_rows(part, sq ^ 2, c)
        pltpu.make_async_copy(at, at, tok_recv.at[sq ^ 2, 1 + part]).wait()
        send(at, half_rows(part, sq ^ 2, 1 - c), tok_recv.at[sq ^ 2, 1 + part], dev_c)
    line_step(third)
    arrived(far(second), q)
    piece(far(second), q, dev_y)
    piece(far(second), q, dev_c)
    arrived(2 * first + x, qy)
    piece(2 * first + x, qy, dev_x)
    piece(2 * first + x, qy, dev_c)
    piece(dp, qy, dev_x, w_ref.at[qy])
    arrived(2 * second + x, qy)
    piece(2 * second + x, qy, dev_c)
    arrived(far(third), q)
    piece(far(third), q, dev_y)
    piece(far(third), q, dev_c)
    for slot in (2 * third + x, far(second), far(first), dp ^ 1, far(third)):
        arrived(slot, qy)
        piece(slot, qy, dev_c)
    for step in range(1, 8):
        slot = (dp + step) % 8
        arrived(slot, qc)
        arrived(slot, qyc)
    for other in (sq ^ 1, sq ^ 2, sq ^ 3):
        at = full_rows(other)
        pltpu.make_async_copy(at, at, tok_recv.at[other, 0]).wait()
    for other in (sq ^ 1, sq ^ 3):
        for part in range(2):
            at = half_rows(part, other, c)
            pltpu.make_async_copy(at, at, tok_recv.at[other, 1 + part]).wait()
    for copy in locals_:
        copy.wait()
    for copy, pred in started:
        if pred is None:
            copy.wait_send()
        else:
            pl.when(pred)(lambda copy=copy: copy.wait_send())


def gather_all(block_low, tokens):
    block_rows, width = block_low.shape
    quarter = block_rows // 4
    out, spread = pl.pallas_call(
        gather_body,
        out_shape=(
            jax.ShapeDtypeStruct((8, 4, quarter, width), LOW),
            jax.ShapeDtypeStruct((1024, width), LOW),
        ),
        in_specs=[pl.BlockSpec(memory_space=pl.ANY)] * 2,
        out_specs=(pl.BlockSpec(memory_space=pl.ANY),) * 2,
        scratch_shapes=[
            pltpu.SemaphoreType.DMA((64,)),
            pltpu.SemaphoreType.DMA((8, 4)),
            pltpu.SemaphoreType.DMA((4, 3)),
            pltpu.SemaphoreType.DMA((4,)),
        ],
        compiler_params=params(collective_id=1, has_side_effects=True),
        name="gather_weights",
    )(block_low.reshape(4, quarter, width), tokens)
    return out.reshape(8 * block_rows // TILE, TILE, width), spread


def qkv_body(map_ref, x_ref, top_ref, low_ref, bias_ref, out_ref):
    part = pl.program_id(0)
    scale = jnp.where(part == 0, HEAD_DIM ** (-0.5), 1.0)
    value = dot_nn(x_ref[:, :TILE], top_ref[0]) + dot_nn(x_ref[:, TILE:], low_ref[0])
    value = (value + bias_ref[0]).astype(LOW).astype(WIDE)
    out_ref[0] = (value * scale).astype(LOW)


def qkv_project(tile_map, rows, weights, bias):
    count, width = rows.shape
    return pl.pallas_call(
        qkv_body,
        grid_spec=pltpu.PrefetchScalarGridSpec(
            num_scalar_prefetch=1,
            grid=(3,),
            in_specs=[
                pl.BlockSpec((count, width), lambda i, m: (0, 0)),
                pl.BlockSpec((1, TILE, width), lambda i, m: (m[2 * i], 0, 0)),
                pl.BlockSpec((1, TILE, width), lambda i, m: (m[2 * i + 1], 0, 0)),
                pl.BlockSpec((1, 1, width), lambda i, m: (i, 0, 0)),
            ],
            out_specs=pl.BlockSpec((1, count, width), lambda i, m: (i, 0, 0)),
        ),
        out_shape=jax.ShapeDtypeStruct((3, count, width), LOW),
        compiler_params=params(),
        name="qkv",
    )(tile_map, rows, weights, weights, bias)


def head_masks(shape):
    lane = lax.broadcasted_iota(jnp.int32, shape, 1)
    return (lane < HEAD_DIM, lane >= HEAD_DIM)


def attend_body(q_ref, k_ref, v_ref, bias_ref, o_ref, lse_ref):
    queries, keys = q_ref[0], k_ref[0]
    value_t = v_ref[0].T
    bias = jnp.concatenate([bias_ref[0], bias_ref[0]], axis=1)
    outs = []
    for head, mask in enumerate(head_masks(queries.shape)):
        scores = dot_nt(keys, jnp.where(mask, queries, jnp.zeros_like(queries))) + bias
        top = jnp.max(scores, axis=0, keepdims=True)
        shifted = jnp.exp(scores - top)
        total = jnp.sum(shifted, axis=0, keepdims=True)
        part = value_t[HEAD_DIM * head : HEAD_DIM * (head + 1)]
        outs.append(dot_nn(part, shifted.astype(LOW)) * (1.0 / total))
        lse_ref[0, head : head + 1, :] = top + jnp.log(total)
    o_ref[...] = jnp.concatenate(outs, axis=0).T.astype(LOW)


def attend(qkv, bias):
    width = qkv.shape[-1]
    pairs = width // 128
    return pl.pallas_call(
        attend_body,
        grid=(3, pairs),
        in_specs=[
            pl.BlockSpec((1, 256, 128), lambda i, h: (0, i, h)),
            pl.BlockSpec((1, 512, 128), lambda i, h: (1, i // 2, h)),
            pl.BlockSpec((1, 512, 128), lambda i, h: (2, i // 2, h)),
            pl.BlockSpec((1, 512, 128), lambda i, h: (i // 2, 0, 0)),
        ],
        out_specs=(
            pl.BlockSpec((256, 128), lambda i, h: (i, h)),
            pl.BlockSpec((1, 2, 256), lambda i, h: (h, 0, i)),
        ),
        out_shape=(
            jax.ShapeDtypeStruct((768, width), LOW),
            jax.ShapeDtypeStruct((pairs, 2, 768), WIDE),
        ),
        compiler_params=params(),
        name="attend",
    )(qkv, qkv, qkv, bias)


def attend_back_body(
    q_ref, k_ref, v_ref, bias_ref, lse_ref, do_ref, o_ref, dq_ref, dk_ref, dv_ref, dk_acc, dv_acc
):
    block = pl.program_id(1)
    queries, keys, values, grads = q_ref[0], k_ref[0], v_ref[0], do_ref[...]
    keys_t = keys.T
    inner = (grads.astype(WIDE) * o_ref[...].astype(WIDE)).T
    bias = jnp.concatenate([bias_ref[0], bias_ref[0]], axis=1)
    d_query = []
    d_key = d_value = 0.0
    for head, mask in enumerate(head_masks(queries.shape)):
        query = jnp.where(mask, queries, jnp.zeros_like(queries))
        grad = jnp.where(mask, grads, jnp.zeros_like(grads))
        rows = slice(HEAD_DIM * head, HEAD_DIM * (head + 1))
        inner_sum = jnp.sum(inner[rows], axis=0, keepdims=True)
        scores = dot_nt(keys, query) + bias
        probs = jnp.exp(scores - lse_ref[0, head : head + 1, :])
        d_probs = dot_nt(values, grad)
        d_scores = (probs * (d_probs - inner_sum)).astype(LOW)
        d_value = d_value + dot_nn(probs.astype(LOW), grad)
        d_key = d_key + dot_nn(d_scores, query)
        d_query.append(dot_nn(keys_t[rows], d_scores))
    d_query = jnp.concatenate(d_query, axis=0) * HEAD_DIM ** (-0.5)
    dq_ref[...] = d_query.T.astype(LOW)

    @pl.when(block == 0)
    def _():
        dk_acc[...] = d_key
        dv_acc[...] = d_value

    @pl.when(block > 0)
    def _():
        dk_acc[...] += d_key
        dv_acc[...] += d_value

    @pl.when(block == pl.num_programs(1) - 1)
    def _():
        dk_ref[...] = dk_acc[...].astype(LOW)
        dv_ref[...] = dv_acc[...].astype(LOW)


def attend_back(sentence, qkv, bias, lse, d_out, out):
    width = qkv.shape[-1]
    pairs = width // 128
    first, count = 2 * sentence, 2 - sentence
    query = pl.BlockSpec((256, 128), lambda h, i: (first + i, h))
    keys = jax.ShapeDtypeStruct((512, width), LOW)
    return pl.pallas_call(
        attend_back_body,
        grid=(pairs, count),
        in_specs=[
            pl.BlockSpec((1, 256, 128), lambda h, i: (0, first + i, h)),
            pl.BlockSpec((1, 512, 128), lambda h, i: (1, sentence, h)),
            pl.BlockSpec((1, 512, 128), lambda h, i: (2, sentence, h)),
            pl.BlockSpec((1, 512, 128), lambda h, i: (sentence, 0, 0)),
            pl.BlockSpec((1, 2, 256), lambda h, i: (h, 0, first + i)),
            query,
            query,
        ],
        out_specs=(
            pl.BlockSpec((256, 128), lambda h, i: (i, h)),
            pl.BlockSpec((512, 128), lambda h, i: (0, h)),
            pl.BlockSpec((512, 128), lambda h, i: (0, h)),
        ),
        out_shape=(jax.ShapeDtypeStruct((256 * count, width), LOW), keys, keys),
        scratch_shapes=[pltpu.VMEM((512, 128), WIDE), pltpu.VMEM((512, 128), WIDE)],
        compiler_params=params(),
        name="attend_back",
    )(qkv, qkv, qkv, bias, lse, d_out, out)


def row_mean(value):
    return jnp.mean(value, axis=-1, keepdims=True)


def col_sum(value):
    return jnp.sum(value, axis=0, keepdims=True)


def middle_body(
    map_ref, o_ref, x_ref, gy_ref, valid_ref, w_ref, vec_ref,
    y_ref, left_ref, right_ref, do_ref, da_ref, dh_ref, sums_ref,
    w_buf, slope, total, hat_one, rstd_one, sem,
):
    step = pl.program_id(0)
    tiles = w_buf.shape[0]
    chunks = FEEDFWD_UNITS // 768

    def fetch(t):
        return pltpu.make_async_copy(w_ref.at[map_ref[6 + t]], w_buf.at[t], sem.at[t])

    def ready(first, count):
        @pl.when(step == 0)
        def _():
            for t in range(first, first + count):
                fetch(t).wait()

    @pl.when(step == 0)
    def _():
        for t in range(tiles):
            fetch(t).start()
        sums_ref[...] = jnp.zeros_like(sums_ref)

    def add_row(row, value):
        sums_ref[row : row + 1, :] += value

    def vec(row):
        return vec_ref[row : row + 1, :]

    ready(0, 2)
    branch = dot_nn(o_ref[:, :TILE], w_buf[0]) + dot_nn(o_ref[:, TILE:], w_buf[1]) + vec(2)
    resid = x_ref[...].astype(WIDE) + branch
    centered = resid - row_mean(resid)
    rstd = lax.rsqrt(row_mean(centered * centered) + NORM_EPS)
    rstd_one[...] = rstd
    hat = centered * rstd
    hat_one[...] = hat
    first = hat * vec(4) + vec(5)
    total[...] = first + vec(3)
    first_low = first.astype(LOW)
    right_ref[0] = first_low

    for c in range(chunks):
        ready(2 + 2 * c, 2)
        ready(10 + 2 * c, 2)
        for u in range(2):
            t = 2 * c + u
            cols = slice(TILE * t, TILE * (t + 1))
            act = dot_nt(first_low, w_buf[2 + t]) + vec_ref[
                8 + c : 9 + c, TILE * u : TILE * (u + 1)
            ]
            cdf = 0.5 + 0.5 * lax.erf(act * (0.5**0.5))
            pdf = jnp.exp(-0.5 * act * act) * 0.3989422804014327
            slope[:, cols] = cdf + act * pdf
            active = (act * cdf).astype(LOW)
            left_ref[8 + t] = active.T
            total[...] += dot_nn(active, w_buf[10 + t])

    resid = total[...]
    centered = resid - row_mean(resid)
    rstd = lax.rsqrt(row_mean(centered * centered) + NORM_EPS)
    hat = centered * rstd
    result = hat * vec(6) + vec(7)
    y_ref[...] = result.astype(LOW)
    pooled = col_sum(result * valid_ref[...])
    sums_ref[pl.ds(10 + step // 2, 1), :] += pooled
    grad = gy_ref[...].astype(WIDE)
    add_row(4, col_sum(grad * hat))
    add_row(5, col_sum(grad))
    grad = grad * vec(6)
    d_resid = rstd * (grad - row_mean(grad) - hat * row_mean(grad * hat))
    total[...] = d_resid
    grad_low = d_resid.astype(LOW)
    right_ref[1] = grad_low
    add_row(1, col_sum(grad_low.astype(WIDE)))

    for c in range(chunks):
        for u in range(2):
            t = 2 * c + u
            cols = slice(TILE * t, TILE * (t + 1))
            d_active = dot_nt(grad_low, w_buf[10 + t])
            d_act = (d_active * slope[:, cols]).astype(LOW)
            left_ref[t] = d_act.T
            sums_ref[6 + c : 7 + c, TILE * u : TILE * (u + 1)] += col_sum(d_act.astype(WIDE))
            total[...] += dot_nn(d_act, w_buf[2 + t])

    grad = total[...]
    hat = hat_one[...]
    add_row(2, col_sum(grad * hat))
    add_row(3, col_sum(grad))
    grad = grad * vec(4)
    d_resid = rstd_one[...] * (grad - row_mean(grad) - hat * row_mean(grad * hat))
    dh_ref[...] = d_resid
    grad_low = d_resid.astype(LOW)
    da_ref[...] = grad_low
    add_row(0, col_sum(grad_low.astype(WIDE)))
    do_ref[:, :TILE] = dot_nt(grad_low, w_buf[0]).astype(LOW)
    do_ref[:, TILE:] = dot_nt(grad_low, w_buf[1]).astype(LOW)


def middle(tile_map, attended, rows, out_grad, valid, weights, vectors):
    width = attended.shape[1]
    tiles = 2 + 2 * FEEDFWD_UNITS // TILE
    block = pl.BlockSpec((256, width), lambda i, m: (i, 0))
    flat = jax.ShapeDtypeStruct((768, width), LOW)
    return pl.pallas_call(
        middle_body,
        grid_spec=pltpu.PrefetchScalarGridSpec(
            num_scalar_prefetch=1,
            grid=(3,),
            in_specs=[
                block,
                block,
                block,
                pl.BlockSpec((256, 1), lambda i, m: (i, 0)),
                pl.BlockSpec(memory_space=pl.ANY),
                pl.BlockSpec(vectors.shape, lambda i, m: (0, 0)),
            ],
            out_specs=(
                block,
                pl.BlockSpec((tiles - 2, TILE, 256), lambda i, m: (0, 0, i)),
                pl.BlockSpec((2, 256, width), lambda i, m: (0, i, 0)),
                block,
                block,
                block,
                pl.BlockSpec((16, width), lambda i, m: (0, 0)),
            ),
            scratch_shapes=[
                pltpu.VMEM((tiles, TILE, width), LOW),
                pltpu.VMEM((256, FEEDFWD_UNITS), WIDE),
                pltpu.VMEM((256, width), WIDE),
                pltpu.VMEM((256, width), WIDE),
                pltpu.VMEM((256, 1), WIDE),
                pltpu.SemaphoreType.DMA((tiles,)),
            ],
        ),
        out_shape=(
            flat,
            jax.ShapeDtypeStruct((tiles - 2, TILE, 768), LOW),
            jax.ShapeDtypeStruct((2, 768, width), LOW),
            flat,
            flat,
            jax.ShapeDtypeStruct((768, width), WIDE),
            jax.ShapeDtypeStruct((16, width), WIDE),
        ),
        compiler_params=params(),
        name="feed_forward",
    )(tile_map, attended, rows, out_grad, valid, weights, vectors)


def grad_ff_body(map_ref, left_ref, right_ref, out_ref):
    out_ref[0] = dot_nn(left_ref[0], right_ref[0]).astype(LOW)


def grad_ff(tile_map, left, right):
    per = FEEDFWD_UNITS // TILE
    count, width = right.shape[1:]
    return pl.pallas_call(
        grad_ff_body,
        grid_spec=pltpu.PrefetchScalarGridSpec(
            num_scalar_prefetch=1,
            grid=(2 * per,),
            in_specs=[
                pl.BlockSpec((1, TILE, count), lambda i, m: (i, 0, 0)),
                pl.BlockSpec((1, count, width), lambda i, m: (i // per, 0, 0)),
            ],
            out_specs=pl.BlockSpec((1, TILE, width), lambda i, m: (m[8 + i], 0, 0)),
        ),
        out_shape=jax.ShapeDtypeStruct((8 + 2 * per, TILE, width), LOW),
        compiler_params=params(),
        name="grad_ff",
    )(tile_map, left, right)


def grad_attn_body(
    map_ref, x_ref, dq_ref, dk_ref, dv_ref, o_ref, da_ref, into_ref, out_ref, sums_ref
):
    step = pl.program_id(0)
    for part, grad_ref in enumerate((dq_ref, dk_ref, dv_ref)):

        @pl.when(step // 2 == part)
        def _(grad_ref=grad_ref):
            out_ref[0] = dot_tn(x_ref[...], grad_ref[...]).astype(LOW)

    @pl.when(step // 2 == 3)
    def _():
        out_ref[0] = dot_tn(o_ref[...], da_ref[...]).astype(LOW)

    @pl.when(step == 0)
    def _():
        sums_ref[...] = jnp.zeros_like(sums_ref)
        sums_ref[0:1, :] = col_sum(dq_ref[...].astype(WIDE))
        sums_ref[1:2, :] = col_sum(dv_ref[...].astype(WIDE))


def grad_attn(tile_map, rows, dq, dk, dv, attended, da, into):
    count, width = dq.shape
    whole = pl.BlockSpec((count, width), lambda i, m: (0, 0))
    return pl.pallas_call(
        grad_attn_body,
        grid_spec=pltpu.PrefetchScalarGridSpec(
            num_scalar_prefetch=1,
            grid=(8,),
            in_specs=[
                pl.BlockSpec((count, TILE), lambda i, m: (0, i % 2)),
                whole,
                whole,
                whole,
                pl.BlockSpec((768, TILE), lambda i, m: (0, i % 2)),
                pl.BlockSpec((768, width), lambda i, m: (0, 0)),
                pl.BlockSpec(memory_space=pl.ANY),
            ],
            out_specs=(
                pl.BlockSpec((1, TILE, width), lambda i, m: (m[i], 0, 0)),
                pl.BlockSpec((8, width), lambda i, m: (0, 0)),
            ),
        ),
        out_shape=(
            jax.ShapeDtypeStruct(into.shape, LOW),
            jax.ShapeDtypeStruct((8, width), WIDE),
        ),
        input_output_aliases={7: 0},
        compiler_params=params(),
        name="grad_attn",
    )(tile_map, rows, dq, dk, dv, attended, da, into)


def grad_in_body(map_ref, dq_ref, dk_ref, dv_ref, dh_ref, *refs):
    w_refs, out_ref = refs[:6], refs[6]
    for half in range(2):
        cols = slice(TILE * half, TILE * (half + 1))
        value = dh_ref[:, cols]
        for part, grad_ref in enumerate((dq_ref, dk_ref, dv_ref)):
            value = value + dot_nt(grad_ref[...], w_refs[2 * part + half][0])
        out_ref[:, cols] = value.astype(LOW)


def grad_in(tile_map, dq, dk, dv, dh, weights):
    count, width = dq.shape
    block = pl.BlockSpec((256, width), lambda i, m: (i, 0))
    return pl.pallas_call(
        grad_in_body,
        grid_spec=pltpu.PrefetchScalarGridSpec(
            num_scalar_prefetch=1,
            grid=(count // 256,),
            in_specs=[block] * 4
            + [
                pl.BlockSpec((1, TILE, width), lambda i, m, t=t: (m[t], 0, 0)) for t in range(6)
            ],
            out_specs=block,
        ),
        out_shape=jax.ShapeDtypeStruct((count, width), LOW),
        compiler_params=params(),
        name="grad_in",
    )(tile_map, dq, dk, dv, dh, *([weights] * 6))


def reduce_body(
    p_ref, v_ref, g_ref, own_ref, vt_ref, sq_ref, gi_ref,
    cbuf, core_in, x_in, y_in, y_pair, z_in, ebuf, tbuf, tlow, vbuf, v_in, s_own, s_seq, s_dp,
    send_sem, local_sem, core_sem, x_sem, y_sem, ypair_sem, z_sem, v_sem, out_sem, seq_sem,
    dp_sem, in_sem,
):
    dp, sq = lax.axis_index("dp"), lax.axis_index("seq")
    z, x = dp // 2, dp % 2
    y, c = sq // 2, sq % 2
    dev_c, dev_y, dev_yc, dev_x = (dp, sq ^ 1), (dp, sq ^ 2), (dp, sq ^ 3), (dp ^ 1, sq)
    has_up, has_down, inner = z < 3, z > 0, (z > 0) & (z < 3)
    order = (
        jnp.where(z < 2, 3, 0),
        jnp.where(z == 0, 2, jnp.where(z == 1, 0, jnp.where(z == 2, 3, 1))),
        jnp.where(z == 0, 1, jnp.where(z == 1, 2, jnp.where(z == 2, 1, 2))),
        z,
    )

    barrier = pltpu.get_barrier_semaphore()
    for step in range(1, 4):
        pl.semaphore_signal(
            barrier, inc=1, device_id=(dp, sq ^ step), device_id_type=MESH_ID
        )
    for step in range(1, 8):
        pl.semaphore_signal(
            barrier, inc=1, device_id=(dp ^ step, sq), device_id_type=MESH_ID
        )
    pl.semaphore_wait(barrier, 10)

    used = [0, 0]
    remotes, locals_ = [], []

    def send(src, dst, recv, device, pred=None):
        copy = pltpu.make_async_remote_copy(
            src_ref=src,
            dst_ref=dst,
            send_sem=send_sem.at[used[0]],
            recv_sem=recv,
            device_id=device,
            device_id_type=MESH_ID,
        )
        used[0] += 1
        if pred is None:
            copy.start()
        else:
            pl.when(pred)(lambda: copy.start())
        remotes.append((copy, pred))

    def move(src, dst):
        copy = pltpu.make_async_copy(src, dst, local_sem.at[used[1]])
        used[1] += 1
        copy.start()
        return copy

    def arrived(at, sem):
        pltpu.make_async_copy(at, at, sem).wait()

    def wide(ref, *at):
        return ref[at].astype(WIDE)

    partners = (dev_c, dev_y, dev_x, (dp ^ 2, sq), (dp ^ 4, sq))

    def vec_send(step):
        send(vbuf.at[step], v_in.at[step], v_sem.at[step], partners[step])

    def vec_add(step):
        arrived(v_in.at[step], v_sem.at[step])
        vbuf[step + 1] = vbuf[step] + v_in[step]

    vbuf[0] = v_ref[...]
    vec_send(0)

    def in_full(j):
        return g_ref.at[pl.ds(128 * j, 128)], gi_ref.at[3 * y + 2 * c]

    def in_half(j):
        return g_ref.at[pl.ds(512 + 64 * j, 64)], gi_ref.at[3 * y + 1, pl.ds(64 * c, 64)]

    for device in (dev_y, dev_yc):
        for kind, pair in enumerate((in_full(device[1]), in_half(device[1]))):
            send(pair[0], pair[1], in_sem.at[sq, kind], device)

    order_of = []
    for t in range(3):
        order_of += [(2 * order[0] + 1 - x, t), (2 * order[1] + x, t)]
        order_of += [(2 * order[k] + 1 - x, t) for k in (1, 2, 3)]
        order_of += [(2 * order[k] + x, t) for k in (0, 2, 3)]
    kept = []
    for index, (slot, t) in enumerate(order_of):
        send(p_ref.at[slot, t, :, 1 - c], core_in.at[slot, t], core_sem.at[slot, t], dev_c)
        kept.append(move(p_ref.at[slot, t, :, c], cbuf.at[slot, t]))
    for kind, pair in enumerate((in_full(sq ^ 1), in_half(sq ^ 1))):
        send(pair[0], pair[1], in_sem.at[sq, kind], dev_c)
    own_moves = [move(*in_full(sq)), move(*in_half(sq))]

    def combine(index):
        slot, t = order_of[index]
        kept[index].wait()
        arrived(core_in.at[slot, t], core_sem.at[slot, t])
        cbuf[slot, t] = (wide(cbuf, slot, t) + wide(core_in, slot, t)).astype(LOW)

    def start_third(t):
        base = 8 * t
        combine(base)
        d = order[0]
        send(cbuf.at[2 * d + 1 - x, t], x_in.at[d, t], x_sem.at[d, t], dev_x)
        combine(base + 1)
        combine(base + 2)
        d = order[1]
        send(cbuf.at[2 * d + x, t, 1 - y], y_pair.at[t, 0], ypair_sem.at[t, 0], dev_y)
        send(cbuf.at[2 * d + 1 - x, t, 1 - y], y_pair.at[t, 1], ypair_sem.at[t, 1], dev_y)
        for k in (2, 3):
            combine(base + k + 1)
            d = order[k]
            send(cbuf.at[2 * d + 1 - x, t], x_in.at[d, t], x_sem.at[d, t], dev_x)
        for k in (5, 6, 7):
            combine(base + k)

    def turn(k, t):
        d = order[k]
        near, far = 2 * d + x, 2 * d + 1 - x
        if k == 1:
            for half in range(2):
                arrived(y_pair.at[t, half], ypair_sem.at[t, half])
            cbuf[far, t, y] = (wide(cbuf, far, t, y) + wide(y_pair, t, 1)).astype(LOW)
            send(cbuf.at[far, t, y], x_in.at[d, t, 0], x_sem.at[d, t], dev_x)
        else:
            arrived(x_in.at[d, t], x_sem.at[d, t])
            cbuf[near, t] = (wide(cbuf, near, t) + wide(x_in, d, t)).astype(LOW)
            send(cbuf.at[near, t, 1 - y], y_in.at[d, t], y_sem.at[d, t], dev_y)

    def plane_sum(k, t):
        d = order[k]
        near = 2 * d + x
        if k == 1:
            arrived(x_in.at[d, t, 0], x_sem.at[d, t])
            return wide(cbuf, near, t, y) + wide(y_pair, t, 0) + wide(x_in, d, t, 0)
        arrived(y_in.at[d, t], y_sem.at[d, t])
        return wide(cbuf, near, t, y) + wide(y_in, d, t)

    def onward(k, t):
        d = order[k]
        tbuf[...] = plane_sum(k, t)

        @pl.when(inner)
        def _():
            arrived(z_in.at[d, t], z_sem.at[d, t])
            tbuf[...] += wide(z_in, d, t)

        ebuf[k, t] = tbuf[...].astype(LOW)
        up = d > z
        step = jnp.where(up, 1, -1)
        index = jnp.where(z + step == d, jnp.where(up, 4, 5), d)
        send(ebuf.at[k, t], z_in.at[index, t], z_sem.at[index, t], (dp + 2 * step, sq))

    def finish(t):
        tbuf[...] = plane_sum(3, t)
        for index, there in ((4, has_down), (5, has_up)):

            @pl.when(there)
            def _(index=index):
                arrived(z_in.at[index, t], z_sem.at[index, t])
                tbuf[...] += wide(z_in, index, t)

        total = tbuf[...].astype(LOW)
        tlow[t] = total
        wide_total = total.astype(WIDE)
        squares = (wide_total * wide_total).reshape(-1, 8, wide_total.shape[-1])
        at = own_ref.at[t, sq]
        for device in (dev_y, dev_c):
            send(tlow.at[t], at, out_sem.at[t, sq], device)
        own_moves.append(move(tlow.at[t], at))
        return jnp.sum(squares, axis=0)

    start_third(0)
    vec_add(0)
    vec_send(1)
    start_third(1)
    for k in range(4):
        turn(k, 0)
    vec_add(1)
    vec_send(2)
    start_third(2)
    squares = 0.0
    for t in range(3):
        if t < 2:
            for k in range(4):
                turn(k, t + 1)
        for k in range(3):
            onward(k, t)
        vec_add(2 + t)
        if t < 2:
            vec_send(3 + t)
        squares = squares + finish(t)

    folded = squares[:, :128]
    for lane in range(1, squares.shape[-1] // 128):
        folded = folded + squares[:, 128 * lane : 128 * (lane + 1)]
    s_own[...] = folded
    for step in range(1, 4):
        send(s_own, s_seq.at[sq], seq_sem.at[sq], (dp, sq ^ step))
    s_seq[sq] = folded
    for t in range(3):
        arrived(own_ref.at[t, sq ^ 2], out_sem.at[t, sq ^ 2])
        send(own_ref.at[t, sq ^ 2], own_ref.at[t, sq ^ 2], out_sem.at[t, sq ^ 2], dev_c)
    for step in range(1, 4):
        arrived(s_seq.at[sq ^ step], seq_sem.at[sq ^ step])
    group = s_seq[0] + s_seq[1] + s_seq[2] + s_seq[3]
    s_dp[dp] = group
    for step in range(1, 8):
        send(s_dp.at[dp], s_dp.at[dp], dp_sem.at[dp], (dp ^ step, sq))
    for step in range(1, 8):
        arrived(s_dp.at[dp ^ step], dp_sem.at[dp ^ step])
    everyone = s_dp[0]
    for index in range(1, 8):
        everyone = everyone + s_dp[index]
    sq_ref[...] = everyone
    vt_ref[0:16] = vbuf[5][0:16]
    vt_ref[16:24] = vbuf[2][16:24]

    for t in range(3):
        arrived(own_ref.at[t, sq ^ 1], out_sem.at[t, sq ^ 1])
        arrived(own_ref.at[t, sq ^ 3], out_sem.at[t, sq ^ 3])
    for step in range(1, 4):
        other = sq ^ step
        there, member = other // 2, other % 2
        arrived(gi_ref.at[3 * there + 2 * member], in_sem.at[other, 0])
        arrived(gi_ref.at[3 * there + 1, pl.ds(64 * member, 64)], in_sem.at[other, 1])
    for copy in own_moves:
        copy.wait()
    for copy, pred in remotes:
        if pred is None:
            copy.wait_send()
        else:
            pl.when(pred)(lambda copy=copy: copy.wait_send())


def reduce_all(grads, payload, grad_rows, sent_dev):
    width = grads.shape[-1]
    part = TILE // 4
    hbm = pl.BlockSpec(memory_space=pl.ANY)
    vmem = pl.BlockSpec(memory_space=pltpu.VMEM)
    owned, totals, squares, input_grad = pl.pallas_call(
        reduce_body,
        out_shape=(
            jax.ShapeDtypeStruct((3, 4, part, width), LOW),
            jax.ShapeDtypeStruct((24, width), WIDE),
            jax.ShapeDtypeStruct((8, 128), WIDE),
            jax.ShapeDtypeStruct((sent_dev, 128, width), LOW),
        ),
        in_specs=[hbm, vmem, hbm],
        out_specs=(hbm, vmem, vmem, hbm),
        scratch_shapes=[
            pltpu.VMEM((8, 3, 2, part, width), LOW),
            pltpu.VMEM((8, 3, 2, part, width), LOW),
            pltpu.VMEM((4, 3, 2, part, width), LOW),
            pltpu.VMEM((4, 3, part, width), LOW),
            pltpu.VMEM((3, 2, part, width), LOW),
            pltpu.VMEM((6, 3, part, width), LOW),
            pltpu.VMEM((3, 3, part, width), LOW),
            pltpu.VMEM((part, width), WIDE),
            pltpu.VMEM((3, part, width), LOW),
            pltpu.VMEM((6, 24, width), WIDE),
            pltpu.VMEM((5, 24, width), WIDE),
            pltpu.VMEM((8, 128), WIDE),
            pltpu.VMEM((4, 8, 128), WIDE),
            pltpu.VMEM((8, 8, 128), WIDE),
            pltpu.SemaphoreType.DMA((96,)),
            pltpu.SemaphoreType.DMA((32,)),
            pltpu.SemaphoreType.DMA((8, 3)),
            pltpu.SemaphoreType.DMA((4, 3)),
            pltpu.SemaphoreType.DMA((4, 3)),
            pltpu.SemaphoreType.DMA((3, 2)),
            pltpu.SemaphoreType.DMA((6, 3)),
            pltpu.SemaphoreType.DMA((5,)),
            pltpu.SemaphoreType.DMA((3, 4)),
            pltpu.SemaphoreType.DMA((4,)),
            pltpu.SemaphoreType.DMA((8,)),
            pltpu.SemaphoreType.DMA((4, 2)),
        ],
        compiler_params=params(collective_id=2, has_side_effects=True),
        name="reduce_gradients",
    )(grads.reshape(8, 3, 2, 2, part, width), payload, grad_rows)
    return owned.reshape(3 * TILE, width), totals, jnp.sum(squares), input_grad


def to_sentences(value):
    sent_dev, local_len, width = value.shape
    pieces = []
    for j in range(4):
        y, c = j // 2, j % 2
        pieces.append(value[3 * y + 2 * c])
        pieces.append(value[3 * y + 1, 64 * c : 64 * c + 64])
    moved = jnp.concatenate(pieces, axis=0).reshape(4, 192, width)
    moved = lax.all_to_all(moved, "seq", split_axis=0, concat_axis=0, tiled=True)
    return jnp.concatenate(
        [moved[:, :128].reshape(512, width), moved[:, 128:].reshape(256, width)], axis=0
    )


def to_positions(value):
    width = value.shape[1]
    moved = jnp.concatenate(
        [value[:512].reshape(4, 128, width), value[512:].reshape(4, 64, width)], axis=1
    )
    moved = lax.all_to_all(moved, "seq", split_axis=0, concat_axis=0, tiled=True)
    rows = []
    for y in range(2):
        rows.append(moved[2 * y, :128])
        rows.append(jnp.concatenate([moved[2 * y, 128:], moved[2 * y + 1, 128:]], axis=0))
        rows.append(moved[2 * y + 1, :128])
    return jnp.stack(rows)


def to_rows(tokens):
    width = tokens.shape[-1]
    core = lax.axis_index("seq") % 2
    pieces = []
    for j in range(4):
        y, c = j // 2, j % 2
        pieces += [tokens[3 * y + 2 * c], tokens[3 * y + 1]]
    moved = jnp.concatenate(pieces, axis=0).reshape(4, 256, width)
    moved = lax.all_to_all(moved, "seq", split_axis=0, concat_axis=0, tiled=True)
    shared = moved[:, 128:].reshape(4, 2, 64, width)
    own = lax.dynamic_index_in_dim(shared, core, 1, keepdims=False)
    other = lax.dynamic_index_in_dim(shared, 1 - core, 1, keepdims=False)
    return jnp.concatenate(
        [moved[:, :128].reshape(512, width), own.reshape(256, width), other.reshape(256, width)],
        axis=0,
    )


def local(
    tokens,
    grad_out,
    lengths,
    members,
    owners,
    mat_master,
    mat_moment1,
    mat_moment2,
    vec_master,
    vec_moment1,
    vec_moment2,
):
    sent_dev, local_len, model_width = tokens.shape
    dp_count = lax.axis_size("dp")
    block_rows = mat_master.shape[0]
    seq_at = lax.axis_index("seq")
    group, core = seq_at // 2, seq_at % 2
    tiles = dp_count * block_rows // TILE
    direct = dp_count == 8 and block_rows % TILE == 0

    block_low = mat_master.astype(LOW)
    if direct:
        weights, rows = gather_all(block_low, tokens)
        per = block_rows // TILE
        tile_map = (owners[:, None] * per + jnp.arange(per)[None, :]).reshape(-1)
    else:
        gathered = lax.all_gather(block_low, "dp", axis=0, tiled=True)
        weights = gathered.reshape(dp_count, block_rows, model_width)[owners]
        weights = weights.reshape(tiles, TILE, model_width)
        rows = to_rows(tokens)
        tile_map = jnp.arange(tiles)
    tile_map = tile_map.astype(jnp.int32)
    out_grad = to_sentences(grad_out)

    full_at = jnp.arange(512)
    half_at = jnp.arange(256)
    half_at = (half_at // 64) * 128 + half_at % 64
    shared_at = jnp.concatenate([half_at + 64 * core, half_at + 64 * (1 - core)])
    full_id, shared_id = 3 * group + 2 * core, 3 * group + 1
    full_ok = full_at < lengths[full_id]
    shared_ok = shared_at < lengths[shared_id]
    bias = jnp.where(jnp.stack([full_ok, shared_ok]), 0.0, MASK_FILL).astype(WIDE)
    bias = jnp.broadcast_to(bias[:, :, None], (2, 512, 128))
    valid = jnp.concatenate([full_ok, shared_ok[:256]]).astype(WIDE)[:, None]

    qkv_bias = jnp.stack([vec_master[0], jnp.zeros_like(vec_master[0]), vec_master[1]])[:, None, :]
    qkv = qkv_project(tile_map, rows, weights, qkv_bias)
    attended, lse = attend(qkv, bias)
    result, left, right, d_attended, d_branch, d_resid, sums = middle(
        tile_map, attended, rows, out_grad, valid, weights, vec_master
    )
    output = to_positions(result)
    grads = grad_ff(tile_map, left, right)
    dq_shared, dk_shared, dv_shared = attend_back(1, qkv, bias, lse, d_attended, attended)
    swap = [(j, j ^ 1) for j in range(4)]
    dk_other = lax.ppermute(dk_shared[256:], "seq", swap)
    dv_other = lax.ppermute(dv_shared[256:], "seq", swap)
    dq, dk, dv = attend_back(0, qkv, bias, lse, d_attended, attended)

    def both(full, own, other):
        return jnp.concatenate([full, (own.astype(WIDE) + other.astype(WIDE)).astype(LOW)], axis=0)

    dq = jnp.concatenate([dq, dq_shared], axis=0)
    dk = both(dk, dk_shared[:256], dk_other)
    dv = both(dv, dv_shared[:256], dv_other)
    grads, sums_qv = grad_attn(tile_map, rows, dq, dk, dv, attended, d_branch, grads)
    grad_rows = grad_in(tile_map, dq, dk, dv, d_resid, weights)

    place = jnp.arange(sent_dev)[:, None]
    pooled = jnp.where(place == full_id, sums[10:11], 0.0) + jnp.where(
        place == shared_id, sums[11:12], 0.0
    )
    local_vec = jnp.concatenate([sums_qv[0:2], sums[0:10]], axis=0)
    if direct:
        pad = jnp.zeros((4, model_width), WIDE)
        payload = jnp.concatenate([local_vec, pad, pooled, pad[:2]], axis=0)
        owned_rows, totals, square_sum, input_grad = reduce_all(
            grads, payload, grad_rows, sent_dev
        )
        owned_rows = owned_rows.astype(WIDE)
        vec_total, pooled = totals[:12], totals[16 : 16 + sent_dev]
    else:
        input_grad = to_positions(grad_rows)
        inverse = jnp.argsort(owners)
        grads = grads.reshape(dp_count, block_rows, model_width)[inverse]
        grads = grads.reshape(dp_count * block_rows, model_width)
        owned_quarter = lax.psum_scatter(grads, ("dp", "seq"), scatter_dimension=0, tiled=True)
        owned_rows = lax.all_gather(owned_quarter, "seq", axis=0, tiled=True).astype(WIDE)
        quarter_wide = owned_quarter.astype(WIDE)
        pooled = lax.psum(pooled, "seq")
        square_sum, vec_total = lax.psum(
            (jnp.sum(quarter_wide * quarter_wide), local_vec), ("dp", "seq")
        )

    pooled = pooled / lengths.astype(WIDE)[:, None]
    local_ids = members - lax.axis_index("dp") * sent_dev
    listed = members >= 0
    member_table = jnp.sum(
        (
            (local_ids[:, :, None] == jnp.arange(sent_dev)[None, None, :]) & listed[:, :, None]
        ).astype(WIDE),
        axis=1,
    )
    group_emb = (
        jnp.dot(member_table, pooled, precision=lax.Precision.HIGHEST)
        / jnp.sum(listed.astype(WIDE), axis=1)[:, None]
    )

    grad_norm = jnp.sqrt(square_sum + jnp.sum(vec_total * vec_total))
    clip_factor = MAX_NORM / jnp.maximum(grad_norm, MAX_NORM)
    matrix_new = adam_step(
        mat_master, mat_moment1, mat_moment2, owned_rows * clip_factor, RATE_MATRIX, WEIGHT_DECAY
    )
    vector_new = adam_step(
        vec_master, vec_moment1, vec_moment2, vec_total * clip_factor, RATE_VECTOR, 0.0
    )
    return (
        output,
        input_grad,
        group_emb,
        grad_norm,
        matrix_new[0],
        matrix_new[1],
        matrix_new[2],
        matrix_new[2].astype(LOW),
        vector_new[0],
        vector_new[1],
        vector_new[2],
        vector_new[2].astype(LOW),
    )


def solution(mesh):
    placed = (
        P("dp", "seq", None),
        P("dp", "seq", None),
        P("dp"),
        P("dp", None),
        P(),
        P("dp", None),
        P("dp", None),
        P("dp", None),
        P(),
        P(),
        P(),
    )
    return jax.shard_map(
        local,
        mesh=mesh,
        in_specs=placed,
        out_specs=(
            P("dp", "seq", None),
            P("dp", "seq", None),
            P("dp", None),
            P(),
            P("dp", None),
            P("dp", None),
            P("dp", None),
            P("dp", None),
            P(),
            P(),
            P(),
            P(),
        ),
        check_vma=False,
    )
```

```python
import functools

import jax
import jax.numpy as jnp
from jax import lax
from jax.experimental import pallas as pl
from jax.experimental.pallas import tpu as pltpu
from jax.sharding import PartitionSpec as P

HEADS = 12
HEAD_DIM = 64
FEEDFWD_UNITS = 3072
STEP = 10


NORM_EPS = 1e-06
MASK_FILL = -1e30
MAX_NORM = 1.0
ADAM_ONE = 0.9
ADAM_TWO = 0.999
ADAM_EPS = 1e-08
WEIGHT_DECAY = 0.01
RATE_MATRIX = 0.04
RATE_VECTOR = 0.5

FWD_PAIRS = 3
BACK_PAIRS = 1
TILE = 384
VMEM_LIMIT = 60 * 1024 * 1024
MESH_ID = pl.DeviceIdType.MESH
LOW = jnp.bfloat16
WIDE = jnp.float32


def adam_step(master, moment_one, moment_two, gradient, learn_rate, decay_rate):
    moment_one = ADAM_ONE * moment_one + (1.0 - ADAM_ONE) * gradient
    moment_two = ADAM_TWO * moment_two + (1.0 - ADAM_TWO) * gradient * gradient
    scaled_one = moment_one / (1.0 - ADAM_ONE**STEP)
    scaled_two = moment_two / (1.0 - ADAM_TWO**STEP)
    master = master - learn_rate * (
        scaled_one / (jnp.sqrt(scaled_two) + ADAM_EPS) + decay_rate * master
    )
    return (moment_one, moment_two, master)


def dot_nn(left, right):
    return jnp.dot(left, right, preferred_element_type=WIDE)


def dot_nt(left, right):
    return lax.dot_general(
        left, right, (((1,), (1,)), ((), ())), preferred_element_type=WIDE
    )


def dot_tn(left, right):
    return lax.dot_general(
        left, right, (((0,), (0,)), ((), ())), preferred_element_type=WIDE
    )


def tile_at(owners, tile):
    return 3 * owners[tile // 3] + tile % 3


def params(**kwargs):
    return pltpu.CompilerParams(vmem_limit_bytes=VMEM_LIMIT, **kwargs)


def gather_body(w_ref, x_ref, out_ref, xo_ref, send_sem, recv_sem, tok_recv, local_sem):
    dp, sq = lax.axis_index("dp"), lax.axis_index("seq")
    z, x = dp // 2, dp % 2
    y, c = sq // 2, sq % 2
    q, qc, qy, qyc = sq, sq ^ 1, sq ^ 2, sq ^ 3
    dev_c, dev_y, dev_yc, dev_x = (dp, sq ^ 1), (dp, sq ^ 2), (dp, sq ^ 3), (dp ^ 1, sq)
    has_up, has_down, inner = z < 3, z > 0, (z > 0) & (z < 3)
    dev_up = (jnp.minimum(dp + 2, dp % 2 + 6), sq)
    dev_down = (jnp.maximum(dp - 2, dp % 2), sq)
    first = jnp.where(z > 0, z - 1, 1)
    second = jnp.where(z < 2, 2, jnp.where(z == 2, 3, 1))
    third = jnp.where(z < 2, 3, 0)

    barrier = pltpu.get_barrier_semaphore()

    def greet(device):
        pl.semaphore_signal(barrier, inc=1, device_id=device, device_id_type=MESH_ID)

    for device in (dev_c, dev_y, dev_yc, dev_x):
        greet(device)
    pl.when(has_up)(lambda: greet(dev_up))
    pl.when(has_down)(lambda: greet(dev_down))
    pl.semaphore_wait(barrier, 4 + jnp.where(inner, 2, 1))

    count = [0]
    started = []

    def remote(src, dst, recv, device):
        copy = pltpu.make_async_remote_copy(
            src_ref=src,
            dst_ref=dst,
            send_sem=send_sem.at[count[0]],
            recv_sem=recv,
            device_id=device,
            device_id_type=MESH_ID,
        )
        count[0] += 1
        return copy

    def send(src, dst, recv, device):
        copy = remote(src, dst, recv, device)
        copy.start()
        started.append((copy, None))

    def send_if(pred, src, dst, recv, device):
        copy = remote(src, dst, recv, device)
        pl.when(pred)(lambda: copy.start())
        started.append((copy, pred))

    def piece(slot, quarter, device, src=None):
        at = out_ref.at[slot, quarter]
        send(at if src is None else src, at, recv_sem.at[slot, quarter], device)

    def arrived(slot, quarter):
        at = out_ref.at[slot, quarter]
        pltpu.make_async_copy(at, at, recv_sem.at[slot, quarter]).wait()

    locals_ = [pltpu.make_async_copy(w_ref, out_ref.at[dp], local_sem.at[0])]
    oy = 1 - y
    full_own, full_sib = 3 * y + 2 * c, 3 * y + 2 * (1 - c)
    full_far, full_cross = 3 * oy + 2 * c, 3 * oy + 2 * (1 - c)

    def full_rows(j):
        return xo_ref.at[pl.ds(128 * j, 128)]

    def half_rows(part, j, core):
        return xo_ref.at[pl.ds(512 + 256 * (part ^ core) + 64 * j, 64)]

    locals_.append(pltpu.make_async_copy(x_ref.at[full_own], full_rows(sq), local_sem.at[1]))
    for part in range(2):
        locals_.append(
            pltpu.make_async_copy(
                x_ref.at[3 * y + 1, pl.ds(64 * part, 64)],
                half_rows(part, sq, c),
                local_sem.at[2 + part],
            )
        )
    send(x_ref.at[full_far], full_rows(sq), tok_recv.at[sq, 0], dev_y)
    for part in range(2):
        send(
            x_ref.at[3 * oy + 1, pl.ds(64 * part, 64)],
            half_rows(part, sq, c),
            tok_recv.at[sq, 1 + part],
            dev_y,
        )
    send(x_ref.at[full_cross], full_rows(sq), tok_recv.at[sq, 0], dev_yc)
    own = w_ref.at[q]
    piece(dp, q, dev_x, own)
    at = out_ref.at[dp, q]
    send_if(has_up, own, at, recv_sem.at[dp, q], dev_up)
    send_if(has_down, own, at, recv_sem.at[dp, q], dev_down)
    send(x_ref.at[full_sib], full_rows(sq), tok_recv.at[sq, 0], dev_c)
    for part in range(2):
        send(
            x_ref.at[3 * y + 1, pl.ds(64 * part, 64)],
            half_rows(part, sq, 1 - c),
            tok_recv.at[sq, 1 + part],
            dev_c,
        )
    for copy in locals_:
        copy.start()

    def line_step(source):
        slot = 2 * source + x
        arrived(slot, q)
        at = out_ref.at[slot, q]
        onward = (jnp.where(source < z, dev_up[0], dev_down[0]), sq)
        send_if(inner, at, at, recv_sem.at[slot, q], onward)
        piece(slot, q, dev_x)
        piece(slot, q, dev_y)
        piece(slot, q, dev_c)

    far = lambda source: 2 * source + (1 - x)
    line_step(first)
    arrived(dp ^ 1, q)
    piece(dp ^ 1, q, dev_c)
    line_step(second)
    arrived(far(first), q)
    piece(far(first), q, dev_c)
    for part in range(2):
        at = half_rows(part, sq ^ 2, c)
        pltpu.make_async_copy(at, at, tok_recv.at[sq ^ 2, 1 + part]).wait()
        send(at, half_rows(part, sq ^ 2, 1 - c), tok_recv.at[sq ^ 2, 1 + part], dev_c)
    line_step(third)
    arrived(far(second), q)
    piece(far(second), q, dev_y)
    piece(far(second), q, dev_c)
    arrived(2 * first + x, qy)
    piece(2 * first + x, qy, dev_x)
    piece(2 * first + x, qy, dev_c)
    piece(dp, qy, dev_x, w_ref.at[qy])
    arrived(2 * second + x, qy)
    piece(2 * second + x, qy, dev_c)
    arrived(far(third), q)
    piece(far(third), q, dev_y)
    piece(far(third), q, dev_c)
    for slot in (2 * third + x, far(second), far(first), dp ^ 1, far(third)):
        arrived(slot, qy)
        piece(slot, qy, dev_c)
    for step in range(1, 8):
        slot = (dp + step) % 8
        arrived(slot, qc)
        arrived(slot, qyc)
    for other in (sq ^ 1, sq ^ 2, sq ^ 3):
        at = full_rows(other)
        pltpu.make_async_copy(at, at, tok_recv.at[other, 0]).wait()
    for other in (sq ^ 1, sq ^ 3):
        for part in range(2):
            at = half_rows(part, other, c)
            pltpu.make_async_copy(at, at, tok_recv.at[other, 1 + part]).wait()
    for copy in locals_:
        copy.wait()
    for copy, pred in started:
        if pred is None:
            copy.wait_send()
        else:
            pl.when(pred)(lambda copy=copy: copy.wait_send())


def gather_all(block_low, tokens):
    block_rows, width = block_low.shape
    quarter = block_rows // 4
    out, spread = pl.pallas_call(
        gather_body,
        out_shape=(
            jax.ShapeDtypeStruct((8, 4, quarter, width), LOW),
            jax.ShapeDtypeStruct((1024, width), LOW),
        ),
        in_specs=[pl.BlockSpec(memory_space=pl.ANY)] * 2,
        out_specs=(pl.BlockSpec(memory_space=pl.ANY),) * 2,
        scratch_shapes=[
            pltpu.SemaphoreType.DMA((64,)),
            pltpu.SemaphoreType.DMA((8, 4)),
            pltpu.SemaphoreType.DMA((4, 3)),
            pltpu.SemaphoreType.DMA((4,)),
        ],
        compiler_params=params(collective_id=1, has_side_effects=True),
        name="gather_weights",
    )(block_low.reshape(4, quarter, width), tokens)
    return out.reshape(8 * block_rows // TILE, TILE, width), spread


def qkv_body(map_ref, x_ref, top_ref, low_ref, vec_ref, out_ref):
    part = pl.program_id(0)
    scale = jnp.where(part == 0, HEAD_DIM ** (-0.5), 1.0)
    value = dot_nn(x_ref[:, :TILE], top_ref[0]) + dot_nn(x_ref[:, TILE:], low_ref[0])
    bias = jnp.where(part == 0, vec_ref[0:1], jnp.where(part == 2, vec_ref[1:2], 0.0))
    out_ref[0] = ((value + bias) * scale).astype(LOW)


def qkv_project(owners, rows, weights, vectors):
    count, width = rows.shape
    return pl.pallas_call(
        qkv_body,
        grid_spec=pltpu.PrefetchScalarGridSpec(
            num_scalar_prefetch=1,
            grid=(3,),
            in_specs=[
                pl.BlockSpec((count, width), lambda i, m: (0, 0)),
                pl.BlockSpec((1, TILE, width), lambda i, m: (tile_at(m, 2 * i), 0, 0)),
                pl.BlockSpec((1, TILE, width), lambda i, m: (tile_at(m, 2 * i + 1), 0, 0)),
                pl.BlockSpec(vectors.shape, lambda i, m: (0, 0)),
            ],
            out_specs=pl.BlockSpec((1, count, width), lambda i, m: (i, 0, 0)),
        ),
        out_shape=jax.ShapeDtypeStruct((3, count, width), LOW),
        compiler_params=params(),
        name="qkv",
    )(owners, rows, weights, weights, vectors)


def group_barrier(dp, sq):
    barrier = pltpu.get_barrier_semaphore()
    for step in range(1, 4):
        pl.semaphore_signal(
            barrier, inc=1, device_id=(dp, sq ^ step), device_id_type=MESH_ID
        )
    pl.semaphore_wait(barrier, 3)


class Exchange:
    def __init__(self, pieces, send_sem, recv_sem, local_sem):
        self.dp, self.sq = lax.axis_index("dp"), lax.axis_index("seq")
        self.pieces = pieces
        self.sems = (send_sem, recv_sem, local_sem)

    def copies(self):
        send_sem, recv_sem, local_sem = self.sems
        out = []
        for step in (2, 3, 1):
            target = self.sq ^ step
            for kind, (src, dst) in enumerate(self.pieces(self.sq, target)):
                out.append(
                    pltpu.make_async_remote_copy(
                        src_ref=src,
                        dst_ref=dst,
                        send_sem=send_sem.at[step - 1, kind],
                        recv_sem=recv_sem.at[self.sq, kind],
                        device_id=(self.dp, target),
                        device_id_type=MESH_ID,
                    )
                )
        for kind, (src, dst) in enumerate(self.pieces(self.sq, self.sq)):
            out.append(pltpu.make_async_copy(src, dst, local_sem.at[kind]))
        return out

    def start(self):
        for copy in self.copies():
            copy.start()

    def finish(self):
        copies = self.copies()
        for copy in copies[:6]:
            copy.wait_send()
        for copy in copies[6:]:
            copy.wait()
        for step in range(1, 4):
            source = self.sq ^ step
            for kind, (_, dst) in enumerate(self.pieces(source, self.sq)):
                pltpu.make_async_copy(dst, dst, self.sems[1].at[source, kind]).wait()


EXCHANGE_SEMS = [
    pltpu.SemaphoreType.DMA((3, 2)),
    pltpu.SemaphoreType.DMA((4, 2)),
    pltpu.SemaphoreType.DMA((2,)),
]


def by_sentence(src, dst):
    def pieces(source, target):
        y, c = target // 2, target % 2
        return (
            (src.at[3 * y + 2 * c], dst.at[pl.ds(128 * source, 128)]),
            (src.at[3 * y + 1, pl.ds(64 * c, 64)], dst.at[pl.ds(512 + 64 * source, 64)]),
        )

    return pieces


def by_position(src, dst):
    def pieces(source, target):
        y, c = source // 2, source % 2
        return (
            (src.at[pl.ds(128 * target, 128)], dst.at[3 * y + 2 * c]),
            (src.at[pl.ds(512 + 64 * target, 64)], dst.at[3 * y + 1, pl.ds(64 * c, 64)]),
        )

    return pieces


def sentence_length(lengths_ref, shared):
    sq = lax.axis_index("seq")
    group, core = sq // 2, sq % 2
    return jnp.where(shared, lengths_ref[3 * group + 1], lengths_ref[3 * group + 2 * core])


def positions(shape, shared):
    row = lax.broadcasted_iota(jnp.int32, shape, 0)
    own = lax.axis_index("seq") % 2
    half = row // 256
    part = row - 256 * half
    core = own + half - 2 * own * half
    mixed = (part // 64) * 128 + part % 64 + 64 * core
    return jnp.where(shared, mixed, row)


def key_bias(lengths_ref, shared):
    inside = positions((512, 128), shared) < sentence_length(lengths_ref, shared)
    bias = jnp.where(inside, 0.0, MASK_FILL)
    return jnp.concatenate([bias, bias], axis=1)


def head_masks(shape):
    lane = lax.broadcasted_iota(jnp.int32, shape, 1)
    return (lane < HEAD_DIM, lane >= HEAD_DIM)


def attend_body(
    len_ref, q_ref, k_ref, v_ref, g_ref, o_ref, lse_ref, gy_ref, send_sem, recv_sem, local_sem
):
    block, group = pl.program_id(0), pl.program_id(1)
    exchange = Exchange(by_sentence(g_ref, gy_ref), send_sem, recv_sem, local_sem)

    @pl.when((block == 0) & (group == 0))
    def _():
        group_barrier(exchange.dp, exchange.sq)
        exchange.start()

    bias = key_bias(len_ref, block == 2)
    for pair in range(q_ref.shape[-1] // 128):
        lanes = slice(128 * pair, 128 * (pair + 1))
        queries, keys = q_ref[0, :, lanes], k_ref[0, :, lanes]
        value_t = v_ref[0, :, lanes].T
        outs = []
        for head, mask in enumerate(head_masks(queries.shape)):
            scores = dot_nt(keys, jnp.where(mask, queries, jnp.zeros_like(queries))) + bias
            top = jnp.max(scores, axis=0, keepdims=True)
            shifted = jnp.exp(scores - top)
            total = jnp.sum(shifted, axis=0, keepdims=True)
            part = value_t[HEAD_DIM * head : HEAD_DIM * (head + 1)]
            outs.append(dot_nn(part, shifted.astype(LOW)) * (1.0 / total))
            lse_ref[0, 2 * pair + head : 2 * pair + head + 1, :] = top + jnp.log(total)
        o_ref[:, lanes] = jnp.concatenate(outs, axis=0).T.astype(LOW)

    @pl.when((block == 2) & (group == pl.num_programs(1) - 1))
    def _():
        exchange.finish()


def attend(lengths, qkv, grad_out):
    width = qkv.shape[-1]
    groups = width // 128 // FWD_PAIRS
    lanes = 128 * FWD_PAIRS
    hbm = pl.BlockSpec(memory_space=pl.ANY)
    return pl.pallas_call(
        attend_body,
        grid=(3, groups),
        in_specs=[
            pl.BlockSpec(memory_space=pltpu.SMEM),
            pl.BlockSpec((1, 256, lanes), lambda i, h: (0, i, h)),
            pl.BlockSpec((1, 512, lanes), lambda i, h: (1, i // 2, h)),
            pl.BlockSpec((1, 512, lanes), lambda i, h: (2, i // 2, h)),
            hbm,
        ],
        out_specs=(
            pl.BlockSpec((256, lanes), lambda i, h: (i, h)),
            pl.BlockSpec((1, 2 * FWD_PAIRS, 256), lambda i, h: (h, 0, i)),
            hbm,
        ),
        out_shape=(
            jax.ShapeDtypeStruct((768, width), LOW),
            jax.ShapeDtypeStruct((groups, 2 * FWD_PAIRS, 768), WIDE),
            jax.ShapeDtypeStruct((768, width), LOW),
        ),
        scratch_shapes=EXCHANGE_SEMS,
        compiler_params=params(collective_id=3, has_side_effects=True),
        name="attend",
    )(lengths, qkv, qkv, qkv, grad_out)


def attend_back_body(
    len_ref, q_ref, k_ref, v_ref, lse_ref, do_ref, o_ref, y_ref,
    dq_ref, dk_ref, dv_ref, out_ref,
    acc, keep, give, take, send_sem, recv_sem, local_sem, give_sem, take_sem,
):
    group, block = pl.program_id(0), pl.program_id(1)
    exchange = Exchange(by_position(y_ref, out_ref), send_sem, recv_sem, local_sem)
    dp, sq = exchange.dp, exchange.sq

    @pl.when((block == 0) & (group == 0))
    def _():
        group_barrier(dp, sq)
        exchange.start()

    bias = key_bias(len_ref, block == 0)
    d_keys, d_values = [], []
    for pair in range(q_ref.shape[-1] // 128):
        lanes = slice(128 * pair, 128 * (pair + 1))
        queries, keys, values = q_ref[0, :, lanes], k_ref[0, :, lanes], v_ref[0, :, lanes]
        grads = do_ref[:, lanes]
        keys_t = keys.T
        inner = (grads.astype(WIDE) * o_ref[:, lanes].astype(WIDE)).T
        d_query = []
        d_key = d_value = 0.0
        for head, mask in enumerate(head_masks(queries.shape)):
            query = jnp.where(mask, queries, jnp.zeros_like(queries))
            grad = jnp.where(mask, grads, jnp.zeros_like(grads))
            rows = slice(HEAD_DIM * head, HEAD_DIM * (head + 1))
            inner_sum = jnp.sum(inner[rows], axis=0, keepdims=True)
            scores = dot_nt(keys, query) + bias
            probs = jnp.exp(scores - lse_ref[0, 2 * pair + head : 2 * pair + head + 1, :])
            d_probs = dot_nt(values, grad)
            d_scores = (probs * (d_probs - inner_sum)).astype(LOW)
            d_value = d_value + dot_nn(probs.astype(LOW), grad)
            d_key = d_key + dot_nn(d_scores, query)
            d_query.append(dot_nn(keys_t[rows], d_scores))
        d_query = jnp.concatenate(d_query, axis=0) * HEAD_DIM ** (-0.5)
        dq_ref[:, lanes] = d_query.T.astype(LOW)
        d_keys.append((lanes, d_key))
        d_values.append((lanes, d_value))
    pairs = ((0, d_keys), (1, d_values))

    def swap(kind):
        return pltpu.make_async_remote_copy(
            src_ref=give.at[group, kind],
            dst_ref=take.at[group, kind],
            send_sem=give_sem.at[group, kind],
            recv_sem=take_sem.at[group, kind],
            device_id=(dp, sq ^ 1),
            device_id_type=MESH_ID,
        )

    @pl.when(block == 0)
    def _():
        for kind, parts in pairs:
            for lanes, part in parts:
                keep[kind, :, lanes] = part[:256]
                give[group, kind, :, lanes] = part[256:].astype(LOW)
            swap(kind).start()

    @pl.when(block == 1)
    def _():
        for kind, parts in pairs:
            for lanes, part in parts:
                acc[kind, :, lanes] = part

    @pl.when(block == 2)
    def _():
        for (kind, parts), ref in zip(pairs, (dk_ref, dv_ref)):
            swap(kind).wait()
            for lanes, part in parts:
                ref[:512, lanes] = (acc[kind, :, lanes] + part).astype(LOW)
                other = take[group, kind, :, lanes].astype(WIDE)
                ref[512:, lanes] = (keep[kind, :, lanes] + other).astype(LOW)

    @pl.when((block == 2) & (group == pl.num_programs(0) - 1))
    def _():
        exchange.finish()


def attend_back(lengths, qkv, lse, d_out, out, result, sent_dev):
    width = qkv.shape[-1]
    groups = width // 128 // BACK_PAIRS
    lanes = 128 * BACK_PAIRS
    hbm = pl.BlockSpec(memory_space=pl.ANY)
    query = pl.BlockSpec((256, lanes), lambda h, i: ((i + 2) % 3, h))
    keys = pl.BlockSpec((768, lanes), lambda h, i: (0, h))
    flat = jax.ShapeDtypeStruct((768, width), LOW)
    shared = lambda i: jnp.where(i == 0, 1, 0)
    return pl.pallas_call(
        attend_back_body,
        grid=(groups, 3),
        in_specs=[
            pl.BlockSpec(memory_space=pltpu.SMEM),
            pl.BlockSpec((1, 256, lanes), lambda h, i: (0, (i + 2) % 3, h)),
            pl.BlockSpec((1, 512, lanes), lambda h, i: (1, shared(i), h)),
            pl.BlockSpec((1, 512, lanes), lambda h, i: (2, shared(i), h)),
            pl.BlockSpec((1, 2 * BACK_PAIRS, 256), lambda h, i: (h, 0, (i + 2) % 3)),
            query,
            query,
            hbm,
        ],
        out_specs=(query, keys, keys, hbm),
        out_shape=(flat, flat, flat, jax.ShapeDtypeStruct((sent_dev, 128, width), LOW)),
        scratch_shapes=[
            pltpu.VMEM((2, 512, lanes), WIDE),
            pltpu.VMEM((2, 256, lanes), WIDE),
            pltpu.VMEM((groups, 2, 256, lanes), LOW),
            pltpu.VMEM((groups, 2, 256, lanes), LOW),
        ]
        + EXCHANGE_SEMS
        + [pltpu.SemaphoreType.DMA((groups, 2)), pltpu.SemaphoreType.DMA((groups, 2))],
        compiler_params=params(collective_id=4, has_side_effects=True),
        name="attend_back",
    )(lengths, qkv, qkv, qkv, lse.reshape(groups, 2 * BACK_PAIRS, 768), d_out, out, result)


def row_mean(value):
    return jnp.mean(value, axis=-1, keepdims=True)


def col_sum(value):
    return jnp.sum(value, axis=0, keepdims=True)


def middle_body(
    map_ref, len_ref, o_ref, x_ref, gy_ref, w_ref, vec_ref,
    y_ref, left_ref, right_ref, do_ref, da_ref, dh_ref, sums_ref,
    w_buf, slope, total, hat_one, rstd_one, sem,
):
    step = pl.program_id(0)
    tiles = w_buf.shape[0]
    chunks = FEEDFWD_UNITS // 768

    def fetch(t):
        return pltpu.make_async_copy(w_ref.at[tile_at(map_ref, 6 + t)], w_buf.at[t], sem.at[t])

    def ready(first, count):
        @pl.when(step == 0)
        def _():
            for t in range(first, first + count):
                fetch(t).wait()

    @pl.when(step == 0)
    def _():
        for t in range(tiles):
            fetch(t).start()
        sums_ref[...] = jnp.zeros_like(sums_ref)

    def add_row(row, value):
        sums_ref[row : row + 1, :] += value

    def vec(row):
        return vec_ref[row : row + 1, :]

    ready(0, 2)
    branch = dot_nn(o_ref[:, :TILE], w_buf[0]) + dot_nn(o_ref[:, TILE:], w_buf[1]) + vec(2)
    resid = x_ref[...].astype(WIDE) + branch
    centered = resid - row_mean(resid)
    rstd = lax.rsqrt(row_mean(centered * centered) + NORM_EPS)
    rstd_one[...] = rstd
    hat = centered * rstd
    hat_one[...] = hat
    first = hat * vec(4) + vec(5)
    total[...] = first + vec(3)
    first_low = first.astype(LOW)
    right_ref[0] = first_low

    for c in range(chunks):
        ready(2 + 2 * c, 2)
        ready(10 + 2 * c, 2)
        for u in range(2):
            t = 2 * c + u
            cols = slice(TILE * t, TILE * (t + 1))
            act = dot_nt(first_low, w_buf[2 + t]) + vec_ref[
                8 + c : 9 + c, TILE * u : TILE * (u + 1)
            ]
            cdf = 0.5 + 0.5 * lax.erf(act * (0.5**0.5))
            pdf = jnp.exp(-0.5 * act * act) * 0.3989422804014327
            slope[:, cols] = cdf + act * pdf
            active = (act * cdf).astype(LOW)
            left_ref[8 + t] = active.T
            total[...] += dot_nn(active, w_buf[10 + t])

    resid = total[...]
    centered = resid - row_mean(resid)
    rstd = lax.rsqrt(row_mean(centered * centered) + NORM_EPS)
    hat = centered * rstd
    result = hat * vec(6) + vec(7)
    y_ref[...] = result.astype(LOW)
    shared = step == 2
    row = positions((256, 128), shared) + jnp.where(shared, 0, 256 * step)
    valid = jnp.where(row < sentence_length(len_ref, shared), 1.0, 0.0)
    valid = jnp.concatenate([valid] * (result.shape[1] // 128), axis=1)
    pooled = col_sum(result * valid)
    sums_ref[pl.ds(10 + step // 2, 1), :] += pooled
    grad = gy_ref[...].astype(WIDE)
    add_row(4, col_sum(grad * hat))
    add_row(5, col_sum(grad))
    grad = grad * vec(6)
    d_resid = rstd * (grad - row_mean(grad) - hat * row_mean(grad * hat))
    total[...] = d_resid
    grad_low = d_resid.astype(LOW)
    right_ref[1] = grad_low
    add_row(1, col_sum(grad_low.astype(WIDE)))

    for c in range(chunks):
        for u in range(2):
            t = 2 * c + u
            cols = slice(TILE * t, TILE * (t + 1))
            d_active = dot_nt(grad_low, w_buf[10 + t])
            d_act = (d_active * slope[:, cols]).astype(LOW)
            left_ref[t] = d_act.T
            sums_ref[6 + c : 7 + c, TILE * u : TILE * (u + 1)] += col_sum(d_act.astype(WIDE))
            total[...] += dot_nn(d_act, w_buf[2 + t])

    grad = total[...]
    hat = hat_one[...]
    add_row(2, col_sum(grad * hat))
    add_row(3, col_sum(grad))
    grad = grad * vec(4)
    d_resid = rstd_one[...] * (grad - row_mean(grad) - hat * row_mean(grad * hat))
    dh_ref[...] = d_resid
    grad_low = d_resid.astype(LOW)
    da_ref[...] = grad_low
    add_row(0, col_sum(grad_low.astype(WIDE)))
    do_ref[:, :TILE] = dot_nt(grad_low, w_buf[0]).astype(LOW)
    do_ref[:, TILE:] = dot_nt(grad_low, w_buf[1]).astype(LOW)


def middle(owners, lengths, attended, rows, out_grad, weights, vectors):
    width = attended.shape[1]
    tiles = 2 + 2 * FEEDFWD_UNITS // TILE
    block = pl.BlockSpec((256, width), lambda i, m: (i, 0))
    flat = jax.ShapeDtypeStruct((768, width), LOW)
    return pl.pallas_call(
        middle_body,
        grid_spec=pltpu.PrefetchScalarGridSpec(
            num_scalar_prefetch=1,
            grid=(3,),
            in_specs=[
                pl.BlockSpec(memory_space=pltpu.SMEM),
                block,
                block,
                block,
                pl.BlockSpec(memory_space=pl.ANY),
                pl.BlockSpec(vectors.shape, lambda i, m: (0, 0)),
            ],
            out_specs=(
                block,
                pl.BlockSpec((tiles - 2, TILE, 256), lambda i, m: (0, 0, i)),
                pl.BlockSpec((2, 256, width), lambda i, m: (0, i, 0)),
                block,
                block,
                block,
                pl.BlockSpec((16, width), lambda i, m: (0, 0)),
            ),
            scratch_shapes=[
                pltpu.VMEM((tiles, TILE, width), LOW),
                pltpu.VMEM((256, FEEDFWD_UNITS), WIDE),
                pltpu.VMEM((256, width), WIDE),
                pltpu.VMEM((256, width), WIDE),
                pltpu.VMEM((256, 1), WIDE),
                pltpu.SemaphoreType.DMA((tiles,)),
            ],
        ),
        out_shape=(
            flat,
            jax.ShapeDtypeStruct((tiles - 2, TILE, 768), LOW),
            jax.ShapeDtypeStruct((2, 768, width), LOW),
            flat,
            flat,
            jax.ShapeDtypeStruct((768, width), WIDE),
            jax.ShapeDtypeStruct((16, width), WIDE),
        ),
        compiler_params=params(),
        name="feed_forward",
    )(owners, lengths, attended, rows, out_grad, weights, vectors)


def grad_ff_body(map_ref, left_ref, right_ref, out_ref):
    out_ref[0] = dot_nn(left_ref[0], right_ref[0]).astype(LOW)


def grad_ff(owners, left, right):
    per = FEEDFWD_UNITS // TILE
    count, width = right.shape[1:]
    return pl.pallas_call(
        grad_ff_body,
        grid_spec=pltpu.PrefetchScalarGridSpec(
            num_scalar_prefetch=1,
            grid=(2 * per,),
            in_specs=[
                pl.BlockSpec((1, TILE, count), lambda i, m: (i, 0, 0)),
                pl.BlockSpec((1, count, width), lambda i, m: (i // per, 0, 0)),
            ],
            out_specs=pl.BlockSpec((1, TILE, width), lambda i, m: (tile_at(m, 8 + i), 0, 0)),
        ),
        out_shape=jax.ShapeDtypeStruct((8 + 2 * per, TILE, width), LOW),
        compiler_params=params(),
        name="grad_ff",
    )(owners, left, right)


def grad_attn_body(
    map_ref, x_ref, dq_ref, dk_ref, dv_ref, o_ref, da_ref, into_ref, out_ref, sums_ref
):
    step = pl.program_id(0)
    for part, grad_ref in enumerate((dq_ref, dk_ref, dv_ref)):

        @pl.when(step // 2 == part)
        def _(grad_ref=grad_ref):
            out_ref[0] = dot_tn(x_ref[...], grad_ref[...]).astype(LOW)

    @pl.when(step // 2 == 3)
    def _():
        out_ref[0] = dot_tn(o_ref[...], da_ref[...]).astype(LOW)

    @pl.when(step == 0)
    def _():
        sums_ref[...] = jnp.zeros_like(sums_ref)
        sums_ref[0:1, :] = col_sum(dq_ref[...].astype(WIDE))
        sums_ref[1:2, :] = col_sum(dv_ref[...].astype(WIDE))


def grad_attn(owners, rows, dq, dk, dv, attended, da, into):
    count, width = dq.shape
    whole = pl.BlockSpec((count, width), lambda i, m: (0, 0))
    return pl.pallas_call(
        grad_attn_body,
        grid_spec=pltpu.PrefetchScalarGridSpec(
            num_scalar_prefetch=1,
            grid=(8,),
            in_specs=[
                pl.BlockSpec((count, TILE), lambda i, m: (0, i % 2)),
                whole,
                whole,
                whole,
                pl.BlockSpec((768, TILE), lambda i, m: (0, i % 2)),
                pl.BlockSpec((768, width), lambda i, m: (0, 0)),
                pl.BlockSpec(memory_space=pl.ANY),
            ],
            out_specs=(
                pl.BlockSpec((1, TILE, width), lambda i, m: (tile_at(m, i), 0, 0)),
                pl.BlockSpec((8, width), lambda i, m: (0, 0)),
            ),
        ),
        out_shape=(
            jax.ShapeDtypeStruct(into.shape, LOW),
            jax.ShapeDtypeStruct((8, width), WIDE),
        ),
        input_output_aliases={7: 0},
        compiler_params=params(),
        name="grad_attn",
    )(owners, rows, dq, dk, dv, attended, da, into)


def grad_in_body(map_ref, dq_ref, dk_ref, dv_ref, dh_ref, *refs):
    w_refs, out_ref = refs[:6], refs[6]
    for half in range(2):
        cols = slice(TILE * half, TILE * (half + 1))
        value = dh_ref[:, cols]
        for part, grad_ref in enumerate((dq_ref, dk_ref, dv_ref)):
            value = value + dot_nt(grad_ref[...], w_refs[2 * part + half][0])
        out_ref[:, cols] = value.astype(LOW)


def grad_in(owners, dq, dk, dv, dh, weights):
    count, width = dq.shape
    block = pl.BlockSpec((256, width), lambda i, m: (i, 0))
    return pl.pallas_call(
        grad_in_body,
        grid_spec=pltpu.PrefetchScalarGridSpec(
            num_scalar_prefetch=1,
            grid=(count // 256,),
            in_specs=[block] * 4
            + [
                pl.BlockSpec((1, TILE, width), lambda i, m, t=t: (tile_at(m, t), 0, 0)) for t in range(6)
            ],
            out_specs=block,
        ),
        out_shape=jax.ShapeDtypeStruct((count, width), LOW),
        compiler_params=params(),
        name="grad_in",
    )(owners, dq, dk, dv, dh, *([weights] * 6))


def reduce_body(
    p_ref, qv_ref, sums_ref, g_ref, own_ref, vt_ref, sq_ref, gi_ref,
    cbuf, core_in, x_in, y_in, y_pair, z_in, ebuf, tbuf, tlow, vbuf, v_in, s_own, s_seq, s_dp,
    send_sem, local_sem, core_sem, x_sem, y_sem, ypair_sem, z_sem, v_sem, out_sem, seq_sem,
    dp_sem, in_sem,
):
    dp, sq = lax.axis_index("dp"), lax.axis_index("seq")
    z, x = dp // 2, dp % 2
    y, c = sq // 2, sq % 2
    dev_c, dev_y, dev_yc, dev_x = (dp, sq ^ 1), (dp, sq ^ 2), (dp, sq ^ 3), (dp ^ 1, sq)
    has_up, has_down, inner = z < 3, z > 0, (z > 0) & (z < 3)
    order = (
        jnp.where(z < 2, 3, 0),
        jnp.where(z == 0, 2, jnp.where(z == 1, 0, jnp.where(z == 2, 3, 1))),
        jnp.where(z == 0, 1, jnp.where(z == 1, 2, jnp.where(z == 2, 1, 2))),
        z,
    )

    barrier = pltpu.get_barrier_semaphore()
    for step in range(1, 4):
        pl.semaphore_signal(
            barrier, inc=1, device_id=(dp, sq ^ step), device_id_type=MESH_ID
        )
    for step in range(1, 8):
        pl.semaphore_signal(
            barrier, inc=1, device_id=(dp ^ step, sq), device_id_type=MESH_ID
        )
    pl.semaphore_wait(barrier, 10)

    used = [0, 0]
    remotes, locals_ = [], []

    def send(src, dst, recv, device, pred=None):
        copy = pltpu.make_async_remote_copy(
            src_ref=src,
            dst_ref=dst,
            send_sem=send_sem.at[used[0]],
            recv_sem=recv,
            device_id=device,
            device_id_type=MESH_ID,
        )
        used[0] += 1
        if pred is None:
            copy.start()
        else:
            pl.when(pred)(lambda: copy.start())
        remotes.append((copy, pred))

    def move(src, dst):
        copy = pltpu.make_async_copy(src, dst, local_sem.at[used[1]])
        used[1] += 1
        copy.start()
        return copy

    def arrived(at, sem):
        pltpu.make_async_copy(at, at, sem).wait()

    def wide(ref, *at):
        return ref[at].astype(WIDE)

    partners = (dev_c, dev_y, dev_x, (dp ^ 2, sq), (dp ^ 4, sq))

    def vec_send(step):
        send(vbuf.at[step], v_in.at[step], v_sem.at[step], partners[step])

    def vec_add(step):
        arrived(v_in.at[step], v_sem.at[step])
        vbuf[step + 1] = vbuf[step] + v_in[step]

    vbuf[0, 0:2] = qv_ref[0:2]
    vbuf[0, 2:12] = sums_ref[0:10]
    vbuf[0, 12:24] = jnp.zeros((12, vbuf.shape[-1]), WIDE)
    vbuf[0, pl.ds(16 + 3 * y + 2 * c, 1)] = sums_ref[10:11]
    vbuf[0, pl.ds(16 + 3 * y + 1, 1)] = sums_ref[11:12]
    vec_send(0)

    def in_full(j):
        return g_ref.at[pl.ds(128 * j, 128)], gi_ref.at[3 * y + 2 * c]

    def in_half(j):
        return g_ref.at[pl.ds(512 + 64 * j, 64)], gi_ref.at[3 * y + 1, pl.ds(64 * c, 64)]

    for device in (dev_y, dev_yc):
        for kind, pair in enumerate((in_full(device[1]), in_half(device[1]))):
            send(pair[0], pair[1], in_sem.at[sq, kind], device)

    order_of = []
    for t in range(3):
        order_of += [(2 * order[0] + 1 - x, t), (2 * order[1] + x, t)]
        order_of += [(2 * order[k] + 1 - x, t) for k in (1, 2, 3)]
        order_of += [(2 * order[k] + x, t) for k in (0, 2, 3)]
    kept = []
    for index, (slot, t) in enumerate(order_of):
        send(p_ref.at[slot, t, :, 1 - c], core_in.at[slot, t], core_sem.at[slot, t], dev_c)
        kept.append(move(p_ref.at[slot, t, :, c], cbuf.at[slot, t]))
    for kind, pair in enumerate((in_full(sq ^ 1), in_half(sq ^ 1))):
        send(pair[0], pair[1], in_sem.at[sq, kind], dev_c)
    own_moves = [move(*in_full(sq)), move(*in_half(sq))]

    def combine(index):
        slot, t = order_of[index]
        kept[index].wait()
        arrived(core_in.at[slot, t], core_sem.at[slot, t])
        cbuf[slot, t] = (wide(cbuf, slot, t) + wide(core_in, slot, t)).astype(LOW)

    def start_third(t):
        base = 8 * t
        combine(base)
        d = order[0]
        send(cbuf.at[2 * d + 1 - x, t], x_in.at[d, t], x_sem.at[d, t], dev_x)
        combine(base + 1)
        combine(base + 2)
        d = order[1]
        send(cbuf.at[2 * d + x, t, 1 - y], y_pair.at[t, 0], ypair_sem.at[t, 0], dev_y)
        send(cbuf.at[2 * d + 1 - x, t, 1 - y], y_pair.at[t, 1], ypair_sem.at[t, 1], dev_y)
        for k in (2, 3):
            combine(base + k + 1)
            d = order[k]
            send(cbuf.at[2 * d + 1 - x, t], x_in.at[d, t], x_sem.at[d, t], dev_x)
        for k in (5, 6, 7):
            combine(base + k)

    def turn(k, t):
        d = order[k]
        near, far = 2 * d + x, 2 * d + 1 - x
        if k == 1:
            for half in range(2):
                arrived(y_pair.at[t, half], ypair_sem.at[t, half])
            cbuf[far, t, y] = (wide(cbuf, far, t, y) + wide(y_pair, t, 1)).astype(LOW)
            send(cbuf.at[far, t, y], x_in.at[d, t, 0], x_sem.at[d, t], dev_x)
        else:
            arrived(x_in.at[d, t], x_sem.at[d, t])
            cbuf[near, t] = (wide(cbuf, near, t) + wide(x_in, d, t)).astype(LOW)
            send(cbuf.at[near, t, 1 - y], y_in.at[d, t], y_sem.at[d, t], dev_y)

    def plane_sum(k, t):
        d = order[k]
        near = 2 * d + x
        if k == 1:
            arrived(x_in.at[d, t, 0], x_sem.at[d, t])
            return wide(cbuf, near, t, y) + wide(y_pair, t, 0) + wide(x_in, d, t, 0)
        arrived(y_in.at[d, t], y_sem.at[d, t])
        return wide(cbuf, near, t, y) + wide(y_in, d, t)

    def onward(k, t):
        d = order[k]
        tbuf[...] = plane_sum(k, t)

        @pl.when(inner)
        def _():
            arrived(z_in.at[d, t], z_sem.at[d, t])
            tbuf[...] += wide(z_in, d, t)

        ebuf[k, t] = tbuf[...].astype(LOW)
        up = d > z
        step = jnp.where(up, 1, -1)
        index = jnp.where(z + step == d, jnp.where(up, 4, 5), d)
        send(ebuf.at[k, t], z_in.at[index, t], z_sem.at[index, t], (dp + 2 * step, sq))

    def finish(t):
        tbuf[...] = plane_sum(3, t)
        for index, there in ((4, has_down), (5, has_up)):

            @pl.when(there)
            def _(index=index):
                arrived(z_in.at[index, t], z_sem.at[index, t])
                tbuf[...] += wide(z_in, index, t)

        total = tbuf[...].astype(LOW)
        tlow[t] = total
        wide_total = total.astype(WIDE)
        squares = (wide_total * wide_total).reshape(-1, 8, wide_total.shape[-1])
        at = own_ref.at[t, sq]
        for device in (dev_y, dev_c):
            send(tlow.at[t], at, out_sem.at[t, sq], device)
        own_moves.append(move(tlow.at[t], at))
        return jnp.sum(squares, axis=0)

    start_third(0)
    vec_add(0)
    vec_send(1)
    start_third(1)
    for k in range(4):
        turn(k, 0)
    vec_add(1)
    vec_send(2)
    start_third(2)
    squares = 0.0
    for t in range(3):
        if t < 2:
            for k in range(4):
                turn(k, t + 1)
        for k in range(3):
            onward(k, t)
        vec_add(2 + t)
        if t < 2:
            vec_send(3 + t)
        squares = squares + finish(t)

    folded = squares[:, :128]
    for lane in range(1, squares.shape[-1] // 128):
        folded = folded + squares[:, 128 * lane : 128 * (lane + 1)]
    s_own[...] = folded
    for step in range(1, 4):
        send(s_own, s_seq.at[sq], seq_sem.at[sq], (dp, sq ^ step))
    s_seq[sq] = folded
    for t in range(3):
        arrived(own_ref.at[t, sq ^ 2], out_sem.at[t, sq ^ 2])
        send(own_ref.at[t, sq ^ 2], own_ref.at[t, sq ^ 2], out_sem.at[t, sq ^ 2], dev_c)
    for step in range(1, 4):
        arrived(s_seq.at[sq ^ step], seq_sem.at[sq ^ step])
    group = s_seq[0] + s_seq[1] + s_seq[2] + s_seq[3]
    s_dp[dp] = group
    for step in range(1, 8):
        send(s_dp.at[dp], s_dp.at[dp], dp_sem.at[dp], (dp ^ step, sq))
    for step in range(1, 8):
        arrived(s_dp.at[dp ^ step], dp_sem.at[dp ^ step])
    everyone = s_dp[0]
    for index in range(1, 8):
        everyone = everyone + s_dp[index]
    sq_ref[...] = everyone
    vt_ref[0:16] = vbuf[5][0:16]
    vt_ref[16:24] = vbuf[2][16:24]

    for t in range(3):
        arrived(own_ref.at[t, sq ^ 1], out_sem.at[t, sq ^ 1])
        arrived(own_ref.at[t, sq ^ 3], out_sem.at[t, sq ^ 3])
    for step in range(1, 4):
        other = sq ^ step
        there, member = other // 2, other % 2
        arrived(gi_ref.at[3 * there + 2 * member], in_sem.at[other, 0])
        arrived(gi_ref.at[3 * there + 1, pl.ds(64 * member, 64)], in_sem.at[other, 1])
    for copy in own_moves:
        copy.wait()
    for copy, pred in remotes:
        if pred is None:
            copy.wait_send()
        else:
            pl.when(pred)(lambda copy=copy: copy.wait_send())


def reduce_all(grads, sums_qv, sums, grad_rows, sent_dev):
    width = grads.shape[-1]
    part = TILE // 4
    hbm = pl.BlockSpec(memory_space=pl.ANY)
    vmem = pl.BlockSpec(memory_space=pltpu.VMEM)
    owned, totals, squares, input_grad = pl.pallas_call(
        reduce_body,
        out_shape=(
            jax.ShapeDtypeStruct((3, 4, part, width), LOW),
            jax.ShapeDtypeStruct((24, width), WIDE),
            jax.ShapeDtypeStruct((8, 128), WIDE),
            jax.ShapeDtypeStruct((sent_dev, 128, width), LOW),
        ),
        in_specs=[hbm, vmem, vmem, hbm],
        out_specs=(hbm, vmem, vmem, hbm),
        scratch_shapes=[
            pltpu.VMEM((8, 3, 2, part, width), LOW),
            pltpu.VMEM((8, 3, 2, part, width), LOW),
            pltpu.VMEM((4, 3, 2, part, width), LOW),
            pltpu.VMEM((4, 3, part, width), LOW),
            pltpu.VMEM((3, 2, part, width), LOW),
            pltpu.VMEM((6, 3, part, width), LOW),
            pltpu.VMEM((3, 3, part, width), LOW),
            pltpu.VMEM((part, width), WIDE),
            pltpu.VMEM((3, part, width), LOW),
            pltpu.VMEM((6, 24, width), WIDE),
            pltpu.VMEM((5, 24, width), WIDE),
            pltpu.VMEM((8, 128), WIDE),
            pltpu.VMEM((4, 8, 128), WIDE),
            pltpu.VMEM((8, 8, 128), WIDE),
            pltpu.SemaphoreType.DMA((96,)),
            pltpu.SemaphoreType.DMA((32,)),
            pltpu.SemaphoreType.DMA((8, 3)),
            pltpu.SemaphoreType.DMA((4, 3)),
            pltpu.SemaphoreType.DMA((4, 3)),
            pltpu.SemaphoreType.DMA((3, 2)),
            pltpu.SemaphoreType.DMA((6, 3)),
            pltpu.SemaphoreType.DMA((5,)),
            pltpu.SemaphoreType.DMA((3, 4)),
            pltpu.SemaphoreType.DMA((4,)),
            pltpu.SemaphoreType.DMA((8,)),
            pltpu.SemaphoreType.DMA((4, 2)),
        ],
        compiler_params=params(collective_id=2, has_side_effects=True),
        name="reduce_gradients",
    )(grads.reshape(8, 3, 2, 2, part, width), sums_qv, sums, grad_rows)
    return owned.reshape(3 * TILE, width), totals, squares, input_grad


def optimizer_body(
    len_ref, mem_ref, g_ref, sq_ref, tot_ref, w_ref, one_ref, two_ref, vw_ref, vone_ref, vtwo_ref,
    norm_ref, emb_ref, *outs,
):
    count = vw_ref.shape[0]
    gradient = tot_ref[:count]
    norm = jnp.sqrt(jnp.sum(sq_ref[...]) + jnp.sum(gradient * gradient))
    clip = MAX_NORM / jnp.maximum(norm, MAX_NORM)

    def update(refs, outs, gradient, rate, decay):
        new = adam_step(refs[2][...], refs[0][...], refs[1][...], gradient, rate, decay)
        for ref, value in zip(outs, new + (new[2].astype(LOW),)):
            ref[...] = value

    update(
        (one_ref, two_ref, w_ref), outs[:4], g_ref[...].astype(WIDE) * clip,
        RATE_MATRIX, WEIGHT_DECAY,
    )

    @pl.when(pl.program_id(0) == 0)
    def _():
        norm_ref[0, 0] = norm
        update((vone_ref, vtwo_ref, vw_ref), outs[4:], gradient * clip, RATE_VECTOR, 0.0)
        groups, most = mem_ref.shape
        sentences = len_ref.shape[0]
        first = lax.axis_index("dp") * sentences
        pooled = [
            tot_ref[16 + s : 17 + s] / len_ref[s].astype(WIDE) for s in range(sentences)
        ]
        for g in range(groups):
            listed = jnp.int32(0)
            total = jnp.zeros_like(pooled[0])
            for m in range(most):
                listed += jnp.where(mem_ref[g, m] >= 0, 1, 0)
            for s in range(sentences):
                times = jnp.int32(0)
                for m in range(most):
                    times += jnp.where(mem_ref[g, m] == first + s, 1, 0)
                total = total + pooled[s] * times.astype(WIDE)
            emb_ref[g : g + 1] = total / listed.astype(WIDE)


def optimizer(lengths, members, owned, squares, totals, matrices, vectors):
    block_rows, width = owned.shape
    steps = 6 if block_rows % 96 == 0 else 3
    smem = pl.BlockSpec(memory_space=pltpu.SMEM)
    mat = pl.BlockSpec((block_rows // steps, width), lambda i: (i, 0))

    def whole(shape):
        return pl.BlockSpec(shape, lambda i: (0, 0))

    vec = whole(vectors[0].shape)
    embeddings = (members.shape[0], width)
    return pl.pallas_call(
        optimizer_body,
        grid=(steps,),
        in_specs=[smem, smem, mat, whole(squares.shape), whole(totals.shape)]
        + [mat] * 3
        + [vec] * 3,
        out_specs=(smem, whole(embeddings)) + (mat,) * 4 + (vec,) * 4,
        out_shape=(
            jax.ShapeDtypeStruct((1, 1), WIDE),
            jax.ShapeDtypeStruct(embeddings, WIDE),
        )
        + tuple(
            jax.ShapeDtypeStruct(like.shape, dtype)
            for like in (owned, vectors[0])
            for dtype in (WIDE, WIDE, WIDE, LOW)
        ),
        compiler_params=params(),
        name="optimizer",
    )(lengths, members, owned, squares, totals, *matrices, *vectors)


def to_positions(value):
    width = value.shape[1]
    moved = jnp.concatenate(
        [value[:512].reshape(4, 128, width), value[512:].reshape(4, 64, width)], axis=1
    )
    moved = lax.all_to_all(moved, "seq", split_axis=0, concat_axis=0, tiled=True)
    rows = []
    for y in range(2):
        rows.append(moved[2 * y, :128])
        rows.append(jnp.concatenate([moved[2 * y, 128:], moved[2 * y + 1, 128:]], axis=0))
        rows.append(moved[2 * y + 1, :128])
    return jnp.stack(rows)


def to_rows(tokens):
    width = tokens.shape[-1]
    core = lax.axis_index("seq") % 2
    pieces = []
    for j in range(4):
        y, c = j // 2, j % 2
        pieces += [tokens[3 * y + 2 * c], tokens[3 * y + 1]]
    moved = jnp.concatenate(pieces, axis=0).reshape(4, 256, width)
    moved = lax.all_to_all(moved, "seq", split_axis=0, concat_axis=0, tiled=True)
    shared = moved[:, 128:].reshape(4, 2, 64, width)
    own = lax.dynamic_index_in_dim(shared, core, 1, keepdims=False)
    other = lax.dynamic_index_in_dim(shared, 1 - core, 1, keepdims=False)
    return jnp.concatenate(
        [moved[:, :128].reshape(512, width), own.reshape(256, width), other.reshape(256, width)],
        axis=0,
    )


def local(
    tokens,
    grad_out,
    lengths,
    members,
    owners,
    mat_master,
    mat_moment1,
    mat_moment2,
    vec_master,
    vec_moment1,
    vec_moment2,
):
    sent_dev, local_len, model_width = tokens.shape
    dp_count = lax.axis_size("dp")
    block_rows = mat_master.shape[0]
    direct = dp_count == 8 and block_rows == 3 * TILE

    block_low = mat_master.astype(LOW)
    if direct:
        weights, rows = gather_all(block_low, tokens)
        blocks = owners
    else:
        gathered = lax.all_gather(block_low, "dp", axis=0, tiled=True)
        weights = gathered.reshape(dp_count, block_rows, model_width)[owners]
        weights = weights.reshape(-1, TILE, model_width)
        rows = to_rows(tokens)
        blocks = jnp.arange(weights.shape[0] // 3, dtype=jnp.int32)

    qkv = qkv_project(blocks, rows, weights, vec_master)
    attended, lse, out_grad = attend(lengths, qkv, grad_out)
    result, left, right, d_attended, d_branch, d_resid, sums = middle(
        blocks, lengths, attended, rows, out_grad, weights, vec_master
    )
    dq, dk, dv, output = attend_back(
        lengths, qkv, lse, d_attended, attended, result, sent_dev
    )
    grads = grad_ff(blocks, left, right)
    grads, sums_qv = grad_attn(blocks, rows, dq, dk, dv, attended, d_branch, grads)
    grad_rows = grad_in(blocks, dq, dk, dv, d_resid, weights)

    if direct:
        owned, totals, squares, input_grad = reduce_all(
            grads, sums_qv, sums, grad_rows, sent_dev
        )
    else:
        input_grad = to_positions(grad_rows)
        inverse = jnp.argsort(owners)
        grads = grads.reshape(dp_count, block_rows, model_width)[inverse]
        grads = grads.reshape(dp_count * block_rows, model_width)
        quarter = lax.psum_scatter(grads, ("dp", "seq"), scatter_dimension=0, tiled=True)
        owned = lax.all_gather(quarter, "seq", axis=0, tiled=True)
        quarter = quarter.astype(WIDE)
        group = lax.axis_index("seq") // 2
        core = lax.axis_index("seq") % 2
        place = jnp.arange(8)[:, None]
        pooled = jnp.where(place == 3 * group + 2 * core, sums[10:11], 0.0) + jnp.where(
            place == 3 * group + 1, sums[11:12], 0.0
        )
        pooled = lax.psum(pooled, "seq")
        local_vec = jnp.concatenate([sums_qv[0:2], sums[0:14]], axis=0)
        squares, vec_total = lax.psum(
            (jnp.sum(quarter * quarter), local_vec), ("dp", "seq")
        )
        squares = jnp.full((8, 128), squares / 1024.0)
        totals = jnp.concatenate([vec_total, pooled], axis=0)

    norm, embeddings, *new = optimizer(
        lengths,
        members,
        owned,
        squares,
        totals,
        (mat_master, mat_moment1, mat_moment2),
        (vec_master, vec_moment1, vec_moment2),
    )
    return (output, input_grad, embeddings, norm.reshape(()), *new)


def solution(mesh):
    placed = (
        P("dp", "seq", None),
        P("dp", "seq", None),
        P("dp"),
        P("dp", None),
        P(),
        P("dp", None),
        P("dp", None),
        P("dp", None),
        P(),
        P(),
        P(),
    )
    return jax.shard_map(
        local,
        mesh=mesh,
        in_specs=placed,
        out_specs=(
            P("dp", "seq", None),
            P("dp", "seq", None),
            P("dp", None),
            P(),
            P("dp", None),
            P("dp", None),
            P("dp", None),
            P("dp", None),
            P(),
            P(),
            P(),
            P(),
        ),
        check_vma=False,
    )
```

```python
import functools

import jax
import jax.numpy as jnp
from jax import lax
from jax.experimental import pallas as pl
from jax.experimental.pallas import tpu as pltpu
from jax.sharding import PartitionSpec as P

HEADS = 12
HEAD_DIM = 64
FEEDFWD_UNITS = 3072
STEP = 10


NORM_EPS = 1e-06
MASK_FILL = -1e30
MAX_NORM = 1.0
ADAM_ONE = 0.9
ADAM_TWO = 0.999
ADAM_EPS = 1e-08
WEIGHT_DECAY = 0.01
RATE_MATRIX = 0.04
RATE_VECTOR = 0.5

FWD_PAIRS = 3
BACK_PAIRS = 1
TILE = 384
VMEM_LIMIT = 60 * 1024 * 1024
MESH_ID = pl.DeviceIdType.MESH
LOW = jnp.bfloat16
WIDE = jnp.float32


def adam_step(master, moment_one, moment_two, gradient, learn_rate, decay_rate):
    moment_one = ADAM_ONE * moment_one + (1.0 - ADAM_ONE) * gradient
    moment_two = ADAM_TWO * moment_two + (1.0 - ADAM_TWO) * gradient * gradient
    scaled_one = moment_one / (1.0 - ADAM_ONE**STEP)
    scaled_two = moment_two / (1.0 - ADAM_TWO**STEP)
    master = master - learn_rate * (
        scaled_one / (jnp.sqrt(scaled_two) + ADAM_EPS) + decay_rate * master
    )
    return (moment_one, moment_two, master)


def dot_nn(left, right):
    return jnp.dot(left, right, preferred_element_type=WIDE)


def dot_nt(left, right):
    return lax.dot_general(
        left, right, (((1,), (1,)), ((), ())), preferred_element_type=WIDE
    )


def dot_tn(left, right):
    return lax.dot_general(
        left, right, (((0,), (0,)), ((), ())), preferred_element_type=WIDE
    )


def tile_at(owners, tile):
    return 3 * owners[tile // 3] + tile % 3


def params(**kwargs):
    return pltpu.CompilerParams(vmem_limit_bytes=VMEM_LIMIT, **kwargs)


def gather_body(w_ref, x_ref, out_ref, xo_ref, send_sem, recv_sem, tok_recv, local_sem):
    dp, sq = lax.axis_index("dp"), lax.axis_index("seq")
    z, x = dp // 2, dp % 2
    y, c = sq // 2, sq % 2
    q, qc, qy, qyc = sq, sq ^ 1, sq ^ 2, sq ^ 3
    dev_c, dev_y, dev_yc, dev_x = (dp, sq ^ 1), (dp, sq ^ 2), (dp, sq ^ 3), (dp ^ 1, sq)
    has_up, has_down, inner = z < 3, z > 0, (z > 0) & (z < 3)
    dev_up = (jnp.minimum(dp + 2, dp % 2 + 6), sq)
    dev_down = (jnp.maximum(dp - 2, dp % 2), sq)
    first = jnp.where(z > 0, z - 1, 1)
    second = jnp.where(z < 2, 2, jnp.where(z == 2, 3, 1))
    third = jnp.where(z < 2, 3, 0)

    barrier = pltpu.get_barrier_semaphore()

    def greet(device):
        pl.semaphore_signal(barrier, inc=1, device_id=device, device_id_type=MESH_ID)

    for device in (dev_c, dev_y, dev_yc, dev_x):
        greet(device)
    pl.when(has_up)(lambda: greet(dev_up))
    pl.when(has_down)(lambda: greet(dev_down))
    pl.semaphore_wait(barrier, 4 + jnp.where(inner, 2, 1))

    count = [0]
    started = []

    def remote(src, dst, recv, device):
        copy = pltpu.make_async_remote_copy(
            src_ref=src,
            dst_ref=dst,
            send_sem=send_sem.at[count[0]],
            recv_sem=recv,
            device_id=device,
            device_id_type=MESH_ID,
        )
        count[0] += 1
        return copy

    def send(src, dst, recv, device):
        copy = remote(src, dst, recv, device)
        copy.start()
        started.append((copy, None))

    def send_if(pred, src, dst, recv, device):
        copy = remote(src, dst, recv, device)
        pl.when(pred)(lambda: copy.start())
        started.append((copy, pred))

    def piece(slot, quarter, device, src=None):
        at = out_ref.at[slot, quarter]
        send(at if src is None else src, at, recv_sem.at[slot, quarter], device)

    def arrived(slot, quarter):
        at = out_ref.at[slot, quarter]
        pltpu.make_async_copy(at, at, recv_sem.at[slot, quarter]).wait()

    locals_ = [pltpu.make_async_copy(w_ref, out_ref.at[dp], local_sem.at[0])]
    oy = 1 - y
    full_own, full_sib = 3 * y + 2 * c, 3 * y + 2 * (1 - c)
    full_far, full_cross = 3 * oy + 2 * c, 3 * oy + 2 * (1 - c)

    def full_rows(j):
        return xo_ref.at[pl.ds(128 * j, 128)]

    def half_rows(part, j, core):
        return xo_ref.at[pl.ds(512 + 256 * (part ^ core) + 64 * j, 64)]

    locals_.append(pltpu.make_async_copy(x_ref.at[full_own], full_rows(sq), local_sem.at[1]))
    for part in range(2):
        locals_.append(
            pltpu.make_async_copy(
                x_ref.at[3 * y + 1, pl.ds(64 * part, 64)],
                half_rows(part, sq, c),
                local_sem.at[2 + part],
            )
        )
    send(x_ref.at[full_far], full_rows(sq), tok_recv.at[sq, 0], dev_y)
    for part in range(2):
        send(
            x_ref.at[3 * oy + 1, pl.ds(64 * part, 64)],
            half_rows(part, sq, c),
            tok_recv.at[sq, 1 + part],
            dev_y,
        )
    send(x_ref.at[full_cross], full_rows(sq), tok_recv.at[sq, 0], dev_yc)
    own = w_ref.at[q]
    piece(dp, q, dev_x, own)
    at = out_ref.at[dp, q]
    send_if(has_up, own, at, recv_sem.at[dp, q], dev_up)
    send_if(has_down, own, at, recv_sem.at[dp, q], dev_down)
    send(x_ref.at[full_sib], full_rows(sq), tok_recv.at[sq, 0], dev_c)
    for part in range(2):
        send(
            x_ref.at[3 * y + 1, pl.ds(64 * part, 64)],
            half_rows(part, sq, 1 - c),
            tok_recv.at[sq, 1 + part],
            dev_c,
        )
    for copy in locals_:
        copy.start()

    def line_step(source):
        slot = 2 * source + x
        arrived(slot, q)
        at = out_ref.at[slot, q]
        onward = (jnp.where(source < z, dev_up[0], dev_down[0]), sq)
        send_if(inner, at, at, recv_sem.at[slot, q], onward)
        piece(slot, q, dev_x)
        piece(slot, q, dev_y)
        piece(slot, q, dev_c)

    far = lambda source: 2 * source + (1 - x)
    line_step(first)
    arrived(dp ^ 1, q)
    piece(dp ^ 1, q, dev_c)
    line_step(second)
    arrived(far(first), q)
    piece(far(first), q, dev_c)
    for part in range(2):
        at = half_rows(part, sq ^ 2, c)
        pltpu.make_async_copy(at, at, tok_recv.at[sq ^ 2, 1 + part]).wait()
        send(at, half_rows(part, sq ^ 2, 1 - c), tok_recv.at[sq ^ 2, 1 + part], dev_c)
    line_step(third)
    arrived(far(second), q)
    piece(far(second), q, dev_y)
    piece(far(second), q, dev_c)
    arrived(2 * first + x, qy)
    piece(2 * first + x, qy, dev_x)
    piece(2 * first + x, qy, dev_c)
    piece(dp, qy, dev_x, w_ref.at[qy])
    arrived(2 * second + x, qy)
    piece(2 * second + x, qy, dev_c)
    arrived(far(third), q)
    piece(far(third), q, dev_y)
    piece(far(third), q, dev_c)
    for slot in (2 * third + x, far(second), far(first), dp ^ 1, far(third)):
        arrived(slot, qy)
        piece(slot, qy, dev_c)
    for step in range(1, 8):
        slot = (dp + step) % 8
        arrived(slot, qc)
        arrived(slot, qyc)
    for other in (sq ^ 1, sq ^ 2, sq ^ 3):
        at = full_rows(other)
        pltpu.make_async_copy(at, at, tok_recv.at[other, 0]).wait()
    for other in (sq ^ 1, sq ^ 3):
        for part in range(2):
            at = half_rows(part, other, c)
            pltpu.make_async_copy(at, at, tok_recv.at[other, 1 + part]).wait()
    for copy in locals_:
        copy.wait()
    for copy, pred in started:
        if pred is None:
            copy.wait_send()
        else:
            pl.when(pred)(lambda copy=copy: copy.wait_send())


def gather_all(block_low, tokens):
    block_rows, width = block_low.shape
    quarter = block_rows // 4
    out, spread = pl.pallas_call(
        gather_body,
        out_shape=(
            jax.ShapeDtypeStruct((8, 4, quarter, width), LOW),
            jax.ShapeDtypeStruct((1024, width), LOW),
        ),
        in_specs=[pl.BlockSpec(memory_space=pl.ANY)] * 2,
        out_specs=(pl.BlockSpec(memory_space=pl.ANY),) * 2,
        scratch_shapes=[
            pltpu.SemaphoreType.DMA((64,)),
            pltpu.SemaphoreType.DMA((8, 4)),
            pltpu.SemaphoreType.DMA((4, 3)),
            pltpu.SemaphoreType.DMA((4,)),
        ],
        compiler_params=params(collective_id=1, has_side_effects=True),
        name="gather_weights",
    )(block_low.reshape(4, quarter, width), tokens)
    return out.reshape(8 * block_rows // TILE, TILE, width), spread


def qkv_body(map_ref, x_ref, top_ref, low_ref, vec_ref, out_ref):
    part = pl.program_id(0)
    scale = jnp.where(part == 0, HEAD_DIM ** (-0.5), 1.0)
    value = dot_nn(x_ref[:, :TILE], top_ref[0]) + dot_nn(x_ref[:, TILE:], low_ref[0])
    bias = jnp.where(part == 0, vec_ref[0:1], jnp.where(part == 2, vec_ref[1:2], 0.0))
    out_ref[0] = ((value + bias) * scale).astype(LOW)


def qkv_project(owners, rows, weights, vectors):
    count, width = rows.shape
    return pl.pallas_call(
        qkv_body,
        grid_spec=pltpu.PrefetchScalarGridSpec(
            num_scalar_prefetch=1,
            grid=(3,),
            in_specs=[
                pl.BlockSpec((count, width), lambda i, m: (0, 0)),
                pl.BlockSpec((1, TILE, width), lambda i, m: (tile_at(m, 2 * i), 0, 0)),
                pl.BlockSpec((1, TILE, width), lambda i, m: (tile_at(m, 2 * i + 1), 0, 0)),
                pl.BlockSpec(vectors.shape, lambda i, m: (0, 0)),
            ],
            out_specs=pl.BlockSpec((1, count, width), lambda i, m: (i, 0, 0)),
        ),
        out_shape=jax.ShapeDtypeStruct((3, count, width), LOW),
        compiler_params=params(),
        name="qkv",
    )(owners, rows, weights, weights, vectors)


def group_barrier(dp, sq):
    barrier = pltpu.get_barrier_semaphore()
    for step in range(1, 4):
        pl.semaphore_signal(
            barrier, inc=1, device_id=(dp, sq ^ step), device_id_type=MESH_ID
        )
    pl.semaphore_wait(barrier, 3)


class Exchange:
    def __init__(self, pieces, send_sem, recv_sem, local_sem):
        self.dp, self.sq = lax.axis_index("dp"), lax.axis_index("seq")
        self.pieces = pieces
        self.sems = (send_sem, recv_sem, local_sem)

    def copies(self):
        send_sem, recv_sem, local_sem = self.sems
        out = []
        for step in (2, 3, 1):
            target = self.sq ^ step
            for kind, (src, dst) in enumerate(self.pieces(self.sq, target)):
                out.append(
                    pltpu.make_async_remote_copy(
                        src_ref=src,
                        dst_ref=dst,
                        send_sem=send_sem.at[step - 1, kind],
                        recv_sem=recv_sem.at[self.sq, kind],
                        device_id=(self.dp, target),
                        device_id_type=MESH_ID,
                    )
                )
        for kind, (src, dst) in enumerate(self.pieces(self.sq, self.sq)):
            out.append(pltpu.make_async_copy(src, dst, local_sem.at[kind]))
        return out

    def start(self):
        for copy in self.copies():
            copy.start()

    def finish(self):
        copies = self.copies()
        for copy in copies[:6]:
            copy.wait_send()
        for copy in copies[6:]:
            copy.wait()
        for step in range(1, 4):
            source = self.sq ^ step
            for kind, (_, dst) in enumerate(self.pieces(source, self.sq)):
                pltpu.make_async_copy(dst, dst, self.sems[1].at[source, kind]).wait()


EXCHANGE_SEMS = [
    pltpu.SemaphoreType.DMA((3, 2)),
    pltpu.SemaphoreType.DMA((4, 2)),
    pltpu.SemaphoreType.DMA((2,)),
]


def by_sentence(src, dst):
    def pieces(source, target):
        y, c = target // 2, target % 2
        return (
            (src.at[3 * y + 2 * c], dst.at[pl.ds(128 * source, 128)]),
            (src.at[3 * y + 1, pl.ds(64 * c, 64)], dst.at[pl.ds(512 + 64 * source, 64)]),
        )

    return pieces


def by_position(src, dst):
    def pieces(source, target):
        y, c = source // 2, source % 2
        return (
            (src.at[pl.ds(128 * target, 128)], dst.at[3 * y + 2 * c]),
            (src.at[pl.ds(512 + 64 * target, 64)], dst.at[3 * y + 1, pl.ds(64 * c, 64)]),
        )

    return pieces


def sentence_length(lengths_ref, shared):
    sq = lax.axis_index("seq")
    group, core = sq // 2, sq % 2
    return jnp.where(shared, lengths_ref[3 * group + 1], lengths_ref[3 * group + 2 * core])


def positions(shape, shared):
    row = lax.broadcasted_iota(jnp.int32, shape, 0)
    own = lax.axis_index("seq") % 2
    half = row // 256
    part = row - 256 * half
    core = own + half - 2 * own * half
    mixed = (part // 64) * 128 + part % 64 + 64 * core
    return jnp.where(shared, mixed, row)


def key_bias(lengths_ref, shared):
    inside = positions((512, 128), shared) < sentence_length(lengths_ref, shared)
    bias = jnp.where(inside, 0.0, MASK_FILL)
    return jnp.concatenate([bias, bias], axis=1)


def head_masks(shape):
    lane = lax.broadcasted_iota(jnp.int32, shape, 1)
    return (lane < HEAD_DIM, lane >= HEAD_DIM)


def attend_body(
    len_ref, q_ref, k_ref, v_ref, g_ref, o_ref, lse_ref, gy_ref, send_sem, recv_sem, local_sem
):
    block, group = pl.program_id(0), pl.program_id(1)
    exchange = Exchange(by_sentence(g_ref, gy_ref), send_sem, recv_sem, local_sem)

    @pl.when((block == 0) & (group == 0))
    def _():
        group_barrier(exchange.dp, exchange.sq)
        exchange.start()

    bias = key_bias(len_ref, block == 2)
    for pair in range(q_ref.shape[-1] // 128):
        lanes = slice(128 * pair, 128 * (pair + 1))
        queries, keys = q_ref[0, :, lanes], k_ref[0, :, lanes]
        value_t = v_ref[0, :, lanes].T
        outs = []
        for head, mask in enumerate(head_masks(queries.shape)):
            scores = dot_nt(keys, jnp.where(mask, queries, jnp.zeros_like(queries))) + bias
            top = jnp.max(scores, axis=0, keepdims=True)
            shifted = jnp.exp(scores - top)
            total = jnp.sum(shifted, axis=0, keepdims=True)
            part = value_t[HEAD_DIM * head : HEAD_DIM * (head + 1)]
            outs.append(dot_nn(part, shifted.astype(LOW)) * (1.0 / total))
            lse_ref[0, 2 * pair + head : 2 * pair + head + 1, :] = top + jnp.log(total)
        o_ref[:, lanes] = jnp.concatenate(outs, axis=0).T.astype(LOW)

    @pl.when((block == 2) & (group == pl.num_programs(1) - 1))
    def _():
        exchange.finish()


def attend(lengths, qkv, grad_out):
    width = qkv.shape[-1]
    groups = width // 128 // FWD_PAIRS
    lanes = 128 * FWD_PAIRS
    hbm = pl.BlockSpec(memory_space=pl.ANY)
    return pl.pallas_call(
        attend_body,
        grid=(3, groups),
        in_specs=[
            pl.BlockSpec(memory_space=pltpu.SMEM),
            pl.BlockSpec((1, 256, lanes), lambda i, h: (0, i, h)),
            pl.BlockSpec((1, 512, lanes), lambda i, h: (1, i // 2, h)),
            pl.BlockSpec((1, 512, lanes), lambda i, h: (2, i // 2, h)),
            hbm,
        ],
        out_specs=(
            pl.BlockSpec((256, lanes), lambda i, h: (i, h)),
            pl.BlockSpec((1, 2 * FWD_PAIRS, 256), lambda i, h: (h, 0, i)),
            hbm,
        ),
        out_shape=(
            jax.ShapeDtypeStruct((768, width), LOW),
            jax.ShapeDtypeStruct((groups, 2 * FWD_PAIRS, 768), WIDE),
            jax.ShapeDtypeStruct((768, width), LOW),
        ),
        scratch_shapes=EXCHANGE_SEMS,
        compiler_params=params(collective_id=3, has_side_effects=True),
        name="attend",
    )(lengths, qkv, qkv, qkv, grad_out)


def attend_back_body(
    len_ref, q_ref, k_ref, v_ref, lse_ref, do_ref, o_ref, y_ref,
    dq_ref, dk_ref, dv_ref, out_ref,
    acc, keep, give, take, send_sem, recv_sem, local_sem, give_sem, take_sem,
):
    group, block = pl.program_id(0), pl.program_id(1)
    exchange = Exchange(by_position(y_ref, out_ref), send_sem, recv_sem, local_sem)
    dp, sq = exchange.dp, exchange.sq

    @pl.when((block == 0) & (group == 0))
    def _():
        group_barrier(dp, sq)
        exchange.start()

    bias = key_bias(len_ref, block == 0)
    d_keys, d_values = [], []
    for pair in range(q_ref.shape[-1] // 128):
        lanes = slice(128 * pair, 128 * (pair + 1))
        queries, keys, values = q_ref[0, :, lanes], k_ref[0, :, lanes], v_ref[0, :, lanes]
        grads = do_ref[:, lanes]
        keys_t = keys.T
        inner = (grads.astype(WIDE) * o_ref[:, lanes].astype(WIDE)).T
        d_query = []
        d_key = d_value = 0.0
        for head, mask in enumerate(head_masks(queries.shape)):
            query = jnp.where(mask, queries, jnp.zeros_like(queries))
            grad = jnp.where(mask, grads, jnp.zeros_like(grads))
            rows = slice(HEAD_DIM * head, HEAD_DIM * (head + 1))
            inner_sum = jnp.sum(inner[rows], axis=0, keepdims=True)
            scores = dot_nt(keys, query) + bias
            probs = jnp.exp(scores - lse_ref[0, 2 * pair + head : 2 * pair + head + 1, :])
            d_probs = dot_nt(values, grad)
            d_scores = (probs * (d_probs - inner_sum)).astype(LOW)
            d_value = d_value + dot_nn(probs.astype(LOW), grad)
            d_key = d_key + dot_nn(d_scores, query)
            d_query.append(dot_nn(keys_t[rows], d_scores))
        d_query = jnp.concatenate(d_query, axis=0) * HEAD_DIM ** (-0.5)
        dq_ref[:, lanes] = d_query.T.astype(LOW)
        d_keys.append((lanes, d_key))
        d_values.append((lanes, d_value))
    pairs = ((0, d_keys), (1, d_values))

    def swap(kind):
        return pltpu.make_async_remote_copy(
            src_ref=give.at[group, kind],
            dst_ref=take.at[group, kind],
            send_sem=give_sem.at[group, kind],
            recv_sem=take_sem.at[group, kind],
            device_id=(dp, sq ^ 1),
            device_id_type=MESH_ID,
        )

    @pl.when(block == 0)
    def _():
        for kind, parts in pairs:
            for lanes, part in parts:
                keep[kind, :, lanes] = part[:256]
                give[group, kind, :, lanes] = part[256:].astype(LOW)
            swap(kind).start()

    @pl.when(block == 1)
    def _():
        for kind, parts in pairs:
            for lanes, part in parts:
                acc[kind, :, lanes] = part

    @pl.when(block == 2)
    def _():
        for (kind, parts), ref in zip(pairs, (dk_ref, dv_ref)):
            swap(kind).wait()
            for lanes, part in parts:
                ref[:512, lanes] = (acc[kind, :, lanes] + part).astype(LOW)
                other = take[group, kind, :, lanes].astype(WIDE)
                ref[512:, lanes] = (keep[kind, :, lanes] + other).astype(LOW)

    @pl.when((block == 2) & (group == pl.num_programs(0) - 1))
    def _():
        exchange.finish()


def attend_back(lengths, qkv, lse, d_out, out, result, sent_dev):
    width = qkv.shape[-1]
    groups = width // 128 // BACK_PAIRS
    lanes = 128 * BACK_PAIRS
    hbm = pl.BlockSpec(memory_space=pl.ANY)
    query = pl.BlockSpec((256, lanes), lambda h, i: ((i + 2) % 3, h))
    keys = pl.BlockSpec((768, lanes), lambda h, i: (0, h))
    flat = jax.ShapeDtypeStruct((768, width), LOW)
    shared = lambda i: jnp.where(i == 0, 1, 0)
    return pl.pallas_call(
        attend_back_body,
        grid=(groups, 3),
        in_specs=[
            pl.BlockSpec(memory_space=pltpu.SMEM),
            pl.BlockSpec((1, 256, lanes), lambda h, i: (0, (i + 2) % 3, h)),
            pl.BlockSpec((1, 512, lanes), lambda h, i: (1, shared(i), h)),
            pl.BlockSpec((1, 512, lanes), lambda h, i: (2, shared(i), h)),
            pl.BlockSpec((1, 2 * BACK_PAIRS, 256), lambda h, i: (h, 0, (i + 2) % 3)),
            query,
            query,
            hbm,
        ],
        out_specs=(query, keys, keys, hbm),
        out_shape=(flat, flat, flat, jax.ShapeDtypeStruct((sent_dev, 128, width), LOW)),
        scratch_shapes=[
            pltpu.VMEM((2, 512, lanes), WIDE),
            pltpu.VMEM((2, 256, lanes), WIDE),
            pltpu.VMEM((groups, 2, 256, lanes), LOW),
            pltpu.VMEM((groups, 2, 256, lanes), LOW),
        ]
        + EXCHANGE_SEMS
        + [pltpu.SemaphoreType.DMA((groups, 2)), pltpu.SemaphoreType.DMA((groups, 2))],
        compiler_params=params(collective_id=4, has_side_effects=True),
        name="attend_back",
    )(lengths, qkv, qkv, qkv, lse.reshape(groups, 2 * BACK_PAIRS, 768), d_out, out, result)


def row_mean(value):
    return jnp.mean(value, axis=-1, keepdims=True)


def col_sum(value):
    return jnp.sum(value, axis=0, keepdims=True)


def middle_body(
    map_ref, len_ref, o_ref, x_ref, gy_ref, w_ref, vec_ref,
    y_ref, left_ref, right_ref, do_ref, da_ref, dh_ref, sums_ref,
    w_buf, slope, total, hat_one, rstd_one, sem,
):
    step = pl.program_id(0)
    tiles = w_buf.shape[0]
    chunks = FEEDFWD_UNITS // 768

    def fetch(t):
        return pltpu.make_async_copy(w_ref.at[tile_at(map_ref, 6 + t)], w_buf.at[t], sem.at[t])

    def ready(first, count):
        @pl.when(step == 0)
        def _():
            for t in range(first, first + count):
                fetch(t).wait()

    @pl.when(step == 0)
    def _():
        for t in range(tiles):
            fetch(t).start()
        sums_ref[...] = jnp.zeros_like(sums_ref)

    def add_row(row, value):
        sums_ref[row : row + 1, :] += value

    def vec(row):
        return vec_ref[row : row + 1, :]

    ready(0, 2)
    branch = dot_nn(o_ref[:, :TILE], w_buf[0]) + dot_nn(o_ref[:, TILE:], w_buf[1]) + vec(2)
    resid = x_ref[...].astype(WIDE) + branch
    centered = resid - row_mean(resid)
    rstd = lax.rsqrt(row_mean(centered * centered) + NORM_EPS)
    rstd_one[...] = rstd
    hat = centered * rstd
    hat_one[...] = hat
    first = hat * vec(4) + vec(5)
    total[...] = first + vec(3)
    first_low = first.astype(LOW)
    right_ref[0] = first_low

    for c in range(chunks):
        ready(2 + 2 * c, 2)
        ready(10 + 2 * c, 2)
        for u in range(2):
            t = 2 * c + u
            cols = slice(TILE * t, TILE * (t + 1))
            act = dot_nt(first_low, w_buf[2 + t]) + vec_ref[
                8 + c : 9 + c, TILE * u : TILE * (u + 1)
            ]
            cdf = 0.5 + 0.5 * lax.erf(act * (0.5**0.5))
            pdf = jnp.exp(-0.5 * act * act) * 0.3989422804014327
            slope[:, cols] = cdf + act * pdf
            active = (act * cdf).astype(LOW)
            left_ref[8 + t] = active
            total[...] += dot_nn(active, w_buf[10 + t])

    resid = total[...]
    centered = resid - row_mean(resid)
    rstd = lax.rsqrt(row_mean(centered * centered) + NORM_EPS)
    hat = centered * rstd
    result = hat * vec(6) + vec(7)
    y_ref[...] = result.astype(LOW)
    shared = step == 2
    row = positions((256, 128), shared) + jnp.where(shared, 0, 256 * step)
    valid = jnp.where(row < sentence_length(len_ref, shared), 1.0, 0.0)
    valid = jnp.concatenate([valid] * (result.shape[1] // 128), axis=1)
    pooled = col_sum(result * valid)
    sums_ref[pl.ds(10 + step // 2, 1), :] += pooled
    grad = gy_ref[...].astype(WIDE)
    add_row(4, col_sum(grad * hat))
    add_row(5, col_sum(grad))
    grad = grad * vec(6)
    d_resid = rstd * (grad - row_mean(grad) - hat * row_mean(grad * hat))
    total[...] = d_resid
    grad_low = d_resid.astype(LOW)
    right_ref[1] = grad_low
    add_row(1, col_sum(grad_low.astype(WIDE)))

    for c in range(chunks):
        for u in range(2):
            t = 2 * c + u
            cols = slice(TILE * t, TILE * (t + 1))
            d_active = dot_nt(grad_low, w_buf[10 + t])
            d_act = (d_active * slope[:, cols]).astype(LOW)
            left_ref[t] = d_act
            sums_ref[6 + c : 7 + c, TILE * u : TILE * (u + 1)] += col_sum(d_act.astype(WIDE))
            total[...] += dot_nn(d_act, w_buf[2 + t])

    grad = total[...]
    hat = hat_one[...]
    add_row(2, col_sum(grad * hat))
    add_row(3, col_sum(grad))
    grad = grad * vec(4)
    d_resid = rstd_one[...] * (grad - row_mean(grad) - hat * row_mean(grad * hat))
    dh_ref[...] = d_resid
    grad_low = d_resid.astype(LOW)
    da_ref[...] = grad_low
    add_row(0, col_sum(grad_low.astype(WIDE)))
    do_ref[:, :TILE] = dot_nt(grad_low, w_buf[0]).astype(LOW)
    do_ref[:, TILE:] = dot_nt(grad_low, w_buf[1]).astype(LOW)


def middle(owners, lengths, attended, rows, out_grad, weights, vectors):
    width = attended.shape[1]
    tiles = 2 + 2 * FEEDFWD_UNITS // TILE
    block = pl.BlockSpec((256, width), lambda i, m: (i, 0))
    flat = jax.ShapeDtypeStruct((768, width), LOW)
    return pl.pallas_call(
        middle_body,
        grid_spec=pltpu.PrefetchScalarGridSpec(
            num_scalar_prefetch=1,
            grid=(3,),
            in_specs=[
                pl.BlockSpec(memory_space=pltpu.SMEM),
                block,
                block,
                block,
                pl.BlockSpec(memory_space=pl.ANY),
                pl.BlockSpec(vectors.shape, lambda i, m: (0, 0)),
            ],
            out_specs=(
                block,
                pl.BlockSpec((tiles - 2, 256, TILE), lambda i, m: (0, i, 0)),
                pl.BlockSpec((2, 256, width), lambda i, m: (0, i, 0)),
                block,
                block,
                block,
                pl.BlockSpec((16, width), lambda i, m: (0, 0)),
            ),
            scratch_shapes=[
                pltpu.VMEM((tiles, TILE, width), LOW),
                pltpu.VMEM((256, FEEDFWD_UNITS), WIDE),
                pltpu.VMEM((256, width), WIDE),
                pltpu.VMEM((256, width), WIDE),
                pltpu.VMEM((256, 1), WIDE),
                pltpu.SemaphoreType.DMA((tiles,)),
            ],
        ),
        out_shape=(
            flat,
            jax.ShapeDtypeStruct((tiles - 2, 768, TILE), LOW),
            jax.ShapeDtypeStruct((2, 768, width), LOW),
            flat,
            flat,
            jax.ShapeDtypeStruct((768, width), WIDE),
            jax.ShapeDtypeStruct((16, width), WIDE),
        ),
        compiler_params=params(),
        name="feed_forward",
    )(owners, lengths, attended, rows, out_grad, weights, vectors)


def grad_ff_body(map_ref, left_ref, right_ref, out_ref):
    out_ref[0] = dot_tn(left_ref[0], right_ref[0]).astype(LOW)


def grad_ff(owners, left, right):
    per = FEEDFWD_UNITS // TILE
    count, width = right.shape[1:]
    return pl.pallas_call(
        grad_ff_body,
        grid_spec=pltpu.PrefetchScalarGridSpec(
            num_scalar_prefetch=1,
            grid=(2 * per,),
            in_specs=[
                pl.BlockSpec((1, count, TILE), lambda i, m: (i, 0, 0)),
                pl.BlockSpec((1, count, width), lambda i, m: (i // per, 0, 0)),
            ],
            out_specs=pl.BlockSpec((1, TILE, width), lambda i, m: (tile_at(m, 8 + i), 0, 0)),
        ),
        out_shape=jax.ShapeDtypeStruct((8 + 2 * per, TILE, width), LOW),
        compiler_params=params(),
        name="grad_ff",
    )(owners, left, right)


def grad_attn_body(
    map_ref, x_ref, dq_ref, dk_ref, dv_ref, o_ref, da_ref, into_ref, out_ref, sums_ref
):
    step = pl.program_id(0)
    for part, grad_ref in enumerate((dq_ref, dk_ref, dv_ref)):

        @pl.when(step // 2 == part)
        def _(grad_ref=grad_ref):
            out_ref[0] = dot_tn(x_ref[...], grad_ref[...]).astype(LOW)

    @pl.when(step // 2 == 3)
    def _():
        out_ref[0] = dot_tn(o_ref[...], da_ref[...]).astype(LOW)

    @pl.when(step == 0)
    def _():
        sums_ref[...] = jnp.zeros_like(sums_ref)
        sums_ref[0:1, :] = col_sum(dq_ref[...].astype(WIDE))
        sums_ref[1:2, :] = col_sum(dv_ref[...].astype(WIDE))


def grad_attn(owners, rows, dq, dk, dv, attended, da, into):
    count, width = dq.shape
    whole = pl.BlockSpec((count, width), lambda i, m: (0, 0))
    return pl.pallas_call(
        grad_attn_body,
        grid_spec=pltpu.PrefetchScalarGridSpec(
            num_scalar_prefetch=1,
            grid=(8,),
            in_specs=[
                pl.BlockSpec((count, TILE), lambda i, m: (0, i % 2)),
                whole,
                whole,
                whole,
                pl.BlockSpec((768, TILE), lambda i, m: (0, i % 2)),
                pl.BlockSpec((768, width), lambda i, m: (0, 0)),
                pl.BlockSpec(memory_space=pl.ANY),
            ],
            out_specs=(
                pl.BlockSpec((1, TILE, width), lambda i, m: (tile_at(m, i), 0, 0)),
                pl.BlockSpec((8, width), lambda i, m: (0, 0)),
            ),
        ),
        out_shape=(
            jax.ShapeDtypeStruct(into.shape, LOW),
            jax.ShapeDtypeStruct((8, width), WIDE),
        ),
        input_output_aliases={7: 0},
        compiler_params=params(),
        name="grad_attn",
    )(owners, rows, dq, dk, dv, attended, da, into)


def grad_in_body(map_ref, dq_ref, dk_ref, dv_ref, dh_ref, *refs):
    w_refs, out_ref = refs[:6], refs[6]
    for half in range(2):
        cols = slice(TILE * half, TILE * (half + 1))
        value = dh_ref[:, cols]
        for part, grad_ref in enumerate((dq_ref, dk_ref, dv_ref)):
            value = value + dot_nt(grad_ref[...], w_refs[2 * part + half][0])
        out_ref[:, cols] = value.astype(LOW)


def grad_in(owners, dq, dk, dv, dh, weights):
    count, width = dq.shape
    block = pl.BlockSpec((256, width), lambda i, m: (i, 0))
    return pl.pallas_call(
        grad_in_body,
        grid_spec=pltpu.PrefetchScalarGridSpec(
            num_scalar_prefetch=1,
            grid=(count // 256,),
            in_specs=[block] * 4
            + [
                pl.BlockSpec((1, TILE, width), lambda i, m, t=t: (tile_at(m, t), 0, 0)) for t in range(6)
            ],
            out_specs=block,
        ),
        out_shape=jax.ShapeDtypeStruct((count, width), LOW),
        compiler_params=params(),
        name="grad_in",
    )(owners, dq, dk, dv, dh, *([weights] * 6))


REDUCE_ORDER = (
    ("fp", 3, 2), ("lp", 0, 0), ("in",), ("fp", 2, 1), ("fc", 3, 2), ("lc", 0, 0), ("lp", 0, 1),
    ("lp", 2, 1), ("fc", 2, 1), ("fp", 0, 1), ("fp", 2, 2), ("lp", 1, 1), ("lc", 0, 1),
    ("fp", 1, 1), ("lc", 1, 1), ("lm", 0, 0), ("lp", 2, 0), ("fc", 2, 2), ("fp", 3, 1),
    ("fc", 0, 1), ("fc", 1, 1), ("fp", 0, 2), ("np", 1, 1), ("np", 1, 2), ("np", 3, 1),
    ("lm", 0, 1), ("fc", 0, 2), ("fc", 3, 1), ("nc", 1, 1), ("fp", 1, 2), ("nc", 3, 1),
    ("np", 2, 1), ("lc", 2, 1), ("vs", 0), ("lp", 1, 0), ("fc", 1, 2), ("lm", 2, 1), ("lp", 3, 0),
    ("nc", 1, 2), ("lp", 3, 1), ("np", 0, 2), ("nc", 2, 1), ("lm", 1, 1), ("np", 0, 1),
    ("np", 3, 2), ("np", 2, 2), ("va", 0), ("vs", 1), ("lc", 1, 0), ("nc", 0, 1), ("nc", 0, 2),
    ("turn", 2, 1), ("lm", 1, 0), ("nc", 3, 2), ("nc", 2, 2), ("lc", 2, 0), ("lc", 3, 0),
    ("turn", 1, 1), ("lc", 3, 1), ("turn", 3, 2), ("turn", 0, 1), ("turn", 1, 2), ("le", 1),
    ("turn", 0, 2), ("lm", 2, 0), ("on", 0, 1), ("le", 0), ("lo",), ("turn", 3, 1), ("turn", 2, 2),
    ("on", 0, 2), ("on", 1, 1), ("va", 1), ("vs", 2), ("on", 2, 1), ("on", 1, 2), ("turn", 3, 0),
    ("va", 2), ("vs", 3), ("end", 1), ("on", 2, 2), ("va", 3), ("vs", 4), ("end", 0), ("end", 2),
    ("va", 4),
)


def reduce_body(
    own_of_ref, x_ref, o_ref, left_ref, dq_ref, dk_ref, dv_ref, da_ref, right_ref,
    sums_ref, g_ref, own_ref, vt_ref, sq_ref, gi_ref,
    lbuf, rbuf, pbuf, core_in, x_in, y_in, y_pair, z_in, zf_in, ebuf, tbuf, tlow,
    vbuf, v_in, s_own, s_seq, s_dp,
    send_sem, local_sem, core_sem, x_sem, y_sem, ypair_sem, z_sem, zf_sem, v_sem, out_sem,
    seq_sem, dp_sem, in_sem,
):
    dp, sq = lax.axis_index("dp"), lax.axis_index("seq")
    z, x = dp // 2, dp % 2
    y, c = sq // 2, sq % 2
    dev_c, dev_y, dev_yc, dev_x = (dp, sq ^ 1), (dp, sq ^ 2), (dp, sq ^ 3), (dp ^ 1, sq)
    has_up, has_down, inner = z < 3, z > 0, (z > 0) & (z < 3)
    order = (
        jnp.where(z < 2, 3, 0),
        jnp.where(z == 0, 2, jnp.where(z == 1, 0, jnp.where(z == 2, 3, 1))),
        jnp.where(z == 0, 1, jnp.where(z == 1, 2, jnp.where(z == 2, 1, 2))),
        z,
    )

    used = [0, 0]
    remotes, own_moves = [], []

    def move(src, dst):
        copy = pltpu.make_async_copy(src, dst, local_sem.at[used[1]])
        used[1] += 1
        copy.start()
        return copy

    loads = [move(left_ref, lbuf.at[pl.ds(4, 16)]), move(right_ref, rbuf.at[pl.ds(4, 2)])]
    for index, ref in enumerate((dq_ref, dk_ref, dv_ref, da_ref)):
        loads.append(move(ref, rbuf.at[index]))
    for half in range(2):
        cols = pl.ds(TILE * half, TILE)
        loads.append(move(x_ref.at[pl.ds(0, 768), cols], lbuf.at[half]))
        loads.append(move(o_ref.at[:, cols], lbuf.at[2 + half]))

    barrier = pltpu.get_barrier_semaphore()
    for step in range(1, 4):
        pl.semaphore_signal(
            barrier, inc=1, device_id=(dp, sq ^ step), device_id_type=MESH_ID
        )
    for step in range(1, 8):
        pl.semaphore_signal(
            barrier, inc=1, device_id=(dp ^ step, sq), device_id_type=MESH_ID
        )
    pl.semaphore_wait(barrier, 10)

    def send(src, dst, recv, device, pred=None):
        copy = pltpu.make_async_remote_copy(
            src_ref=src,
            dst_ref=dst,
            send_sem=send_sem.at[used[0]],
            recv_sem=recv,
            device_id=device,
            device_id_type=MESH_ID,
        )
        used[0] += 1
        if pred is None:
            copy.start()
        else:
            pl.when(pred)(lambda: copy.start())
        remotes.append((copy, pred))

    def arrived(at, sem):
        pltpu.make_async_copy(at, at, sem).wait()

    def wide(ref, *at):
        return ref[at].astype(WIDE)

    partners = (dev_c, dev_y, dev_x, (dp ^ 2, sq), (dp ^ 4, sq))

    def vec_send(step):
        send(vbuf.at[step], v_in.at[step], v_sem.at[step], partners[step])

    def vec_add(step):
        arrived(v_in.at[step], v_sem.at[step])
        vbuf[step + 1] = vbuf[step] + v_in[step]

    def in_full(j):
        return g_ref.at[pl.ds(128 * j, 128)], gi_ref.at[3 * y + 2 * c]

    def in_half(j):
        return g_ref.at[pl.ds(512 + 64 * j, 64)], gi_ref.at[3 * y + 1, pl.ds(64 * c, 64)]

    def input_send():
        for device in (dev_y, dev_yc, dev_c):
            for kind, pair in enumerate((in_full(device[1]), in_half(device[1]))):
                send(pair[0], pair[1], in_sem.at[sq, kind], device)
        own_moves.append(move(*in_full(sq)))
        own_moves.append(move(*in_half(sq)))

    for copy in loads:
        copy.wait()

    def standard_of(slot):
        found = jnp.int32(0)
        for block in range(8):
            found = jnp.maximum(found, jnp.where(own_of_ref[block] == slot, block, 0))
        return found

    def partial(slot, t):
        tile = 3 * standard_of(slot) + t
        left = jnp.where(tile < 6, tile % 2, tile - 4)
        right = jnp.where(tile < 8, tile // 2, 4 + (tile - 8) // 8)
        value = dot_tn(lbuf[left], rbuf[right]).astype(LOW)
        for quarter in range(4):
            rows = slice(96 * quarter, 96 * (quarter + 1))
            pbuf[quarter % 2, t, slot, quarter // 2] = value[rows]
        send(pbuf.at[1 - c, t, slot], core_in.at[t, slot], core_sem.at[t, slot], dev_c)

    def combine(slot, t):
        arrived(core_in.at[t, slot], core_sem.at[t, slot])
        pbuf[c, t, slot] = (wide(pbuf, c, t, slot) + wide(core_in, t, slot)).astype(LOW)

    def cbuf(*at):
        return pbuf.at[(c, *at)]

    def line_send(k, sub, pred):
        d = order[k]
        up = d > z
        step = jnp.where(up, 1, -1)
        index = jnp.where(z + step == d, jnp.where(up, 4, 5), d)
        send(
            cbuf(0, 2 * d + sub), zf_in.at[index, sub], zf_sem.at[index, sub],
            (dp + 2 * step, sq), pred,
        )

    def line_partial(k, sub):
        partial(2 * order[k] + sub, 0)

    def line_combine(k, sub):
        combine(2 * order[k] + sub, 0)
        if k < 3:
            line_send(k, sub, jnp.logical_not(inner))

    def line_add(slot, index, sub):
        arrived(zf_in.at[index, sub], zf_sem.at[index, sub])
        pbuf[c, 0, slot] = (wide(pbuf, c, 0, slot) + wide(zf_in, index, sub)).astype(LOW)

    def line_middle(k, sub):
        d = order[k]
        pl.when(inner)(lambda: line_add(2 * d + sub, d, sub))
        line_send(k, sub, inner)

    def line_end(sub):
        pl.when(has_down)(lambda: line_add(2 * z + sub, 4, sub))
        pl.when(has_up)(lambda: line_add(2 * z + sub, 5, sub))

    def line_out():
        send(cbuf(0, 2 * z + 1 - x), x_in.at[z, 0], x_sem.at[z, 0], dev_x)

    def far_partial(k, t):
        partial(2 * order[k] + 1 - x, t)

    def near_partial(k, t):
        partial(2 * order[k] + x, t)

    def far_combine(k, t):
        d = order[k]
        slot = 2 * d + 1 - x
        combine(slot, t)
        if k == 1:
            send(cbuf(t, slot, 1 - y), y_pair.at[t, 1], ypair_sem.at[t, 1], dev_y)
        else:
            send(cbuf(t, slot), x_in.at[d, t], x_sem.at[d, t], dev_x)

    def near_combine(k, t):
        slot = 2 * order[k] + x
        combine(slot, t)
        if k == 1:
            send(cbuf(t, slot, 1 - y), y_pair.at[t, 0], ypair_sem.at[t, 0], dev_y)

    def turn(k, t):
        d = order[k]
        near, far = 2 * d + x, 2 * d + 1 - x
        if k == 1:
            for half in range(2):
                arrived(y_pair.at[t, half], ypair_sem.at[t, half])
            pbuf[c, t, far, y] = (
                wide(pbuf, c, t, far, y) + wide(y_pair, t, 1)
            ).astype(LOW)
            send(cbuf(t, far, y), x_in.at[d, t, 0], x_sem.at[d, t], dev_x)
        else:
            arrived(x_in.at[d, t], x_sem.at[d, t])
            pbuf[c, t, near] = (wide(pbuf, c, t, near) + wide(x_in, d, t)).astype(LOW)
            send(cbuf(t, near, 1 - y), y_in.at[d, t], y_sem.at[d, t], dev_y)

    def plane_sum(k, t):
        d = order[k]
        near = 2 * d + x
        mine = wide(pbuf, c, t, near, y)
        if k == 1:
            arrived(x_in.at[d, t, 0], x_sem.at[d, t])
            return mine + wide(y_pair, t, 0) + wide(x_in, d, t, 0)
        arrived(y_in.at[d, t], y_sem.at[d, t])
        return mine + wide(y_in, d, t)

    def onward(k, t):
        d = order[k]
        tbuf[...] = plane_sum(k, t)

        @pl.when(inner)
        def _():
            arrived(z_in.at[d, t], z_sem.at[d, t])
            tbuf[...] += wide(z_in, d, t)

        ebuf[k, t] = tbuf[...].astype(LOW)
        up = d > z
        step = jnp.where(up, 1, -1)
        index = jnp.where(z + step == d, jnp.where(up, 4, 5), d)
        send(ebuf.at[k, t], z_in.at[index, t], z_sem.at[index, t], (dp + 2 * step, sq))

    squares = []

    def finish(t):
        tbuf[...] = plane_sum(3, t)
        if t > 0:
            for index, there in ((4, has_down), (5, has_up)):

                @pl.when(there)
                def _(index=index):
                    arrived(z_in.at[index, t], z_sem.at[index, t])
                    tbuf[...] += wide(z_in, index, t)

        total = tbuf[...].astype(LOW)
        tlow[t] = total
        wide_total = total.astype(WIDE)
        rows = (wide_total * wide_total).reshape(-1, 8, wide_total.shape[-1])
        squares.append(jnp.sum(rows, axis=0))
        at = own_ref.at[t, sq]
        for device in (dev_y, dev_c):
            send(tlow.at[t], at, out_sem.at[t, sq], device)
        own_moves.append(move(tlow.at[t], at))

    vbuf[0] = jnp.zeros(vbuf.shape[1:], WIDE)
    vbuf[0, 0:1] = col_sum(wide(rbuf, 0))
    vbuf[0, 1:2] = col_sum(wide(rbuf, 2))
    vbuf[0, 2:12] = sums_ref[0:10]
    vbuf[0, pl.ds(16 + 3 * y + 2 * c, 1)] = sums_ref[10:11]
    vbuf[0, pl.ds(16 + 3 * y + 1, 1)] = sums_ref[11:12]
    steps = {
        "lp": line_partial,
        "lc": line_combine,
        "lm": line_middle,
        "le": line_end,
        "lo": line_out,
        "fp": far_partial,
        "np": near_partial,
        "fc": far_combine,
        "nc": near_combine,
        "turn": turn,
        "on": onward,
        "end": finish,
        "vs": vec_send,
        "va": vec_add,
        "in": input_send,
    }
    for name, *at in REDUCE_ORDER:
        steps[name](*at)

    squares = squares[0] + squares[1] + squares[2]
    folded = squares[:, :128]
    for lane in range(1, squares.shape[-1] // 128):
        folded = folded + squares[:, 128 * lane : 128 * (lane + 1)]
    s_own[...] = folded
    for step in range(1, 4):
        send(s_own, s_seq.at[sq], seq_sem.at[sq], (dp, sq ^ step))
    s_seq[sq] = folded
    for t in (1, 0, 2):
        arrived(own_ref.at[t, sq ^ 2], out_sem.at[t, sq ^ 2])
        send(own_ref.at[t, sq ^ 2], own_ref.at[t, sq ^ 2], out_sem.at[t, sq ^ 2], dev_c)
    for step in range(1, 4):
        arrived(s_seq.at[sq ^ step], seq_sem.at[sq ^ step])
    group = s_seq[0] + s_seq[1] + s_seq[2] + s_seq[3]
    s_dp[dp] = group
    for step in range(1, 8):
        send(s_dp.at[dp], s_dp.at[dp], dp_sem.at[dp], (dp ^ step, sq))
    for step in range(1, 8):
        arrived(s_dp.at[dp ^ step], dp_sem.at[dp ^ step])
    everyone = s_dp[0]
    for index in range(1, 8):
        everyone = everyone + s_dp[index]
    sq_ref[...] = everyone
    vt_ref[0:16] = vbuf[5][0:16]
    vt_ref[16:24] = vbuf[2][16:24]

    for t in range(3):
        arrived(own_ref.at[t, sq ^ 1], out_sem.at[t, sq ^ 1])
        arrived(own_ref.at[t, sq ^ 3], out_sem.at[t, sq ^ 3])
    for step in range(1, 4):
        other = sq ^ step
        there, member = other // 2, other % 2
        arrived(gi_ref.at[3 * there + 2 * member], in_sem.at[other, 0])
        arrived(gi_ref.at[3 * there + 1, pl.ds(64 * member, 64)], in_sem.at[other, 1])
    for copy in own_moves:
        copy.wait()
    for copy, pred in remotes:
        if pred is None:
            copy.wait_send()
        else:
            pl.when(pred)(lambda copy=copy: copy.wait_send())


def reduce_all(owners, rows, out, left, grads, right, sums, grad_rows, sent_dev):
    width = rows.shape[-1]
    part = TILE // 4
    hbm = pl.BlockSpec(memory_space=pl.ANY)
    vmem = pl.BlockSpec(memory_space=pltpu.VMEM)
    smem = pl.BlockSpec(memory_space=pltpu.SMEM)
    dma = pltpu.SemaphoreType.DMA
    owned, totals, squares, input_grad = pl.pallas_call(
        reduce_body,
        out_shape=(
            jax.ShapeDtypeStruct((3, 4, part, width), LOW),
            jax.ShapeDtypeStruct((24, width), WIDE),
            jax.ShapeDtypeStruct((8, 128), WIDE),
            jax.ShapeDtypeStruct((sent_dev, 128, width), LOW),
        ),
        in_specs=[smem] + [hbm] * 8 + [vmem, hbm],
        out_specs=(hbm, vmem, vmem, hbm),
        scratch_shapes=[
            pltpu.VMEM((20, 768, TILE), LOW),
            pltpu.VMEM((6, 768, width), LOW),
            pltpu.VMEM((2, 3, 8, 2, part, width), LOW),
            pltpu.VMEM((3, 8, 2, part, width), LOW),
            pltpu.VMEM((4, 3, 2, part, width), LOW),
            pltpu.VMEM((4, 3, part, width), LOW),
            pltpu.VMEM((3, 2, part, width), LOW),
            pltpu.VMEM((6, 3, part, width), LOW),
            pltpu.VMEM((6, 2, 2, part, width), LOW),
            pltpu.VMEM((3, 3, part, width), LOW),
            pltpu.VMEM((part, width), WIDE),
            pltpu.VMEM((3, part, width), LOW),
            pltpu.VMEM((6, 24, width), WIDE),
            pltpu.VMEM((5, 24, width), WIDE),
            pltpu.VMEM((8, 128), WIDE),
            pltpu.VMEM((4, 8, 128), WIDE),
            pltpu.VMEM((8, 8, 128), WIDE),
            dma((96,)),
            dma((32,)),
            dma((3, 8)),
            dma((4, 3)),
            dma((4, 3)),
            dma((3, 2)),
            dma((6, 3)),
            dma((6, 2)),
            dma((5,)),
            dma((3, 4)),
            dma((4,)),
            dma((8,)),
            dma((4, 2)),
        ],
        compiler_params=params(collective_id=2, has_side_effects=True),
        name="reduce_gradients",
    )(owners, rows, out, left, *grads, right, sums, grad_rows)
    return owned.reshape(3 * TILE, width), totals, squares, input_grad


def optimizer_body(
    len_ref, mem_ref, g_ref, sq_ref, tot_ref, w_ref, one_ref, two_ref, vw_ref, vone_ref, vtwo_ref,
    norm_ref, emb_ref, *outs,
):
    count = vw_ref.shape[0]
    gradient = tot_ref[:count]
    norm = jnp.sqrt(jnp.sum(sq_ref[...]) + jnp.sum(gradient * gradient))
    clip = MAX_NORM / jnp.maximum(norm, MAX_NORM)

    def update(refs, outs, gradient, rate, decay):
        new = adam_step(refs[2][...], refs[0][...], refs[1][...], gradient, rate, decay)
        for ref, value in zip(outs, new + (new[2].astype(LOW),)):
            ref[...] = value

    update(
        (one_ref, two_ref, w_ref), outs[:4], g_ref[...].astype(WIDE) * clip,
        RATE_MATRIX, WEIGHT_DECAY,
    )

    @pl.when(pl.program_id(0) == 0)
    def _():
        norm_ref[0, 0] = norm
        update((vone_ref, vtwo_ref, vw_ref), outs[4:], gradient * clip, RATE_VECTOR, 0.0)
        groups, most = mem_ref.shape
        sentences = len_ref.shape[0]
        first = lax.axis_index("dp") * sentences
        pooled = [
            tot_ref[16 + s : 17 + s] / len_ref[s].astype(WIDE) for s in range(sentences)
        ]
        for g in range(groups):
            listed = jnp.int32(0)
            total = jnp.zeros_like(pooled[0])
            for m in range(most):
                listed += jnp.where(mem_ref[g, m] >= 0, 1, 0)
            for s in range(sentences):
                times = jnp.int32(0)
                for m in range(most):
                    times += jnp.where(mem_ref[g, m] == first + s, 1, 0)
                total = total + pooled[s] * times.astype(WIDE)
            emb_ref[g : g + 1] = total / listed.astype(WIDE)


def optimizer(lengths, members, owned, squares, totals, matrices, vectors):
    block_rows, width = owned.shape
    steps = 6 if block_rows % 96 == 0 else 3
    smem = pl.BlockSpec(memory_space=pltpu.SMEM)
    mat = pl.BlockSpec((block_rows // steps, width), lambda i: (i, 0))

    def whole(shape):
        return pl.BlockSpec(shape, lambda i: (0, 0))

    vec = whole(vectors[0].shape)
    embeddings = (members.shape[0], width)
    return pl.pallas_call(
        optimizer_body,
        grid=(steps,),
        in_specs=[smem, smem, mat, whole(squares.shape), whole(totals.shape)]
        + [mat] * 3
        + [vec] * 3,
        out_specs=(smem, whole(embeddings)) + (mat,) * 4 + (vec,) * 4,
        out_shape=(
            jax.ShapeDtypeStruct((1, 1), WIDE),
            jax.ShapeDtypeStruct(embeddings, WIDE),
        )
        + tuple(
            jax.ShapeDtypeStruct(like.shape, dtype)
            for like in (owned, vectors[0])
            for dtype in (WIDE, WIDE, WIDE, LOW)
        ),
        compiler_params=params(),
        name="optimizer",
    )(lengths, members, owned, squares, totals, *matrices, *vectors)


def to_positions(value):
    width = value.shape[1]
    moved = jnp.concatenate(
        [value[:512].reshape(4, 128, width), value[512:].reshape(4, 64, width)], axis=1
    )
    moved = lax.all_to_all(moved, "seq", split_axis=0, concat_axis=0, tiled=True)
    rows = []
    for y in range(2):
        rows.append(moved[2 * y, :128])
        rows.append(jnp.concatenate([moved[2 * y, 128:], moved[2 * y + 1, 128:]], axis=0))
        rows.append(moved[2 * y + 1, :128])
    return jnp.stack(rows)


def to_rows(tokens):
    width = tokens.shape[-1]
    core = lax.axis_index("seq") % 2
    pieces = []
    for j in range(4):
        y, c = j // 2, j % 2
        pieces += [tokens[3 * y + 2 * c], tokens[3 * y + 1]]
    moved = jnp.concatenate(pieces, axis=0).reshape(4, 256, width)
    moved = lax.all_to_all(moved, "seq", split_axis=0, concat_axis=0, tiled=True)
    shared = moved[:, 128:].reshape(4, 2, 64, width)
    own = lax.dynamic_index_in_dim(shared, core, 1, keepdims=False)
    other = lax.dynamic_index_in_dim(shared, 1 - core, 1, keepdims=False)
    return jnp.concatenate(
        [moved[:, :128].reshape(512, width), own.reshape(256, width), other.reshape(256, width)],
        axis=0,
    )


def local(
    tokens,
    grad_out,
    lengths,
    members,
    owners,
    mat_master,
    mat_moment1,
    mat_moment2,
    vec_master,
    vec_moment1,
    vec_moment2,
):
    sent_dev, local_len, model_width = tokens.shape
    dp_count = lax.axis_size("dp")
    block_rows = mat_master.shape[0]
    direct = dp_count == 8 and block_rows == 3 * TILE

    block_low = mat_master.astype(LOW)
    if direct:
        weights, rows = gather_all(block_low, tokens)
        blocks = owners
    else:
        gathered = lax.all_gather(block_low, "dp", axis=0, tiled=True)
        weights = gathered.reshape(dp_count, block_rows, model_width)[owners]
        weights = weights.reshape(-1, TILE, model_width)
        rows = to_rows(tokens)
        blocks = jnp.arange(weights.shape[0] // 3, dtype=jnp.int32)

    qkv = qkv_project(blocks, rows, weights, vec_master)
    attended, lse, out_grad = attend(lengths, qkv, grad_out)
    result, left, right, d_attended, d_branch, d_resid, sums = middle(
        blocks, lengths, attended, rows, out_grad, weights, vec_master
    )
    dq, dk, dv, output = attend_back(
        lengths, qkv, lse, d_attended, attended, result, sent_dev
    )
    grad_rows = grad_in(blocks, dq, dk, dv, d_resid, weights)

    if direct:
        owned, totals, squares, input_grad = reduce_all(
            owners, rows, attended, left, (dq, dk, dv, d_branch), right, sums, grad_rows, sent_dev
        )
    else:
        grads = grad_ff(blocks, left, right)
        grads, sums_qv = grad_attn(blocks, rows, dq, dk, dv, attended, d_branch, grads)
        input_grad = to_positions(grad_rows)
        inverse = jnp.argsort(owners)
        grads = grads.reshape(dp_count, block_rows, model_width)[inverse]
        grads = grads.reshape(dp_count * block_rows, model_width)
        quarter = lax.psum_scatter(grads, ("dp", "seq"), scatter_dimension=0, tiled=True)
        owned = lax.all_gather(quarter, "seq", axis=0, tiled=True)
        quarter = quarter.astype(WIDE)
        group = lax.axis_index("seq") // 2
        core = lax.axis_index("seq") % 2
        place = jnp.arange(8)[:, None]
        pooled = jnp.where(place == 3 * group + 2 * core, sums[10:11], 0.0) + jnp.where(
            place == 3 * group + 1, sums[11:12], 0.0
        )
        pooled = lax.psum(pooled, "seq")
        local_vec = jnp.concatenate([sums_qv[0:2], sums[0:14]], axis=0)
        squares, vec_total = lax.psum(
            (jnp.sum(quarter * quarter), local_vec), ("dp", "seq")
        )
        squares = jnp.full((8, 128), squares / 1024.0)
        totals = jnp.concatenate([vec_total, pooled], axis=0)

    norm, embeddings, *new = optimizer(
        lengths,
        members,
        owned,
        squares,
        totals,
        (mat_master, mat_moment1, mat_moment2),
        (vec_master, vec_moment1, vec_moment2),
    )
    return (output, input_grad, embeddings, norm.reshape(()), *new)


def solution(mesh):
    placed = (
        P("dp", "seq", None),
        P("dp", "seq", None),
        P("dp"),
        P("dp", None),
        P(),
        P("dp", None),
        P("dp", None),
        P("dp", None),
        P(),
        P(),
        P(),
    )
    return jax.shard_map(
        local,
        mesh=mesh,
        in_specs=placed,
        out_specs=(
            P("dp", "seq", None),
            P("dp", "seq", None),
            P("dp", None),
            P(),
            P("dp", None),
            P("dp", None),
            P("dp", None),
            P("dp", None),
            P(),
            P(),
            P(),
            P(),
        ),
        check_vma=False,
    )
```

```python
import functools

import jax
import jax.numpy as jnp
from jax import lax
from jax.experimental import pallas as pl
from jax.experimental.pallas import tpu as pltpu
from jax.sharding import PartitionSpec as P

HEADS = 12
HEAD_DIM = 64
FEEDFWD_UNITS = 3072
STEP = 10


NORM_EPS = 1e-06
MASK_FILL = -1e30
MAX_NORM = 1.0
ADAM_ONE = 0.9
ADAM_TWO = 0.999
ADAM_EPS = 1e-08
WEIGHT_DECAY = 0.01
RATE_MATRIX = 0.04
RATE_VECTOR = 0.5

FWD_PAIRS = 6
BACK_PAIRS = 6
NORM_ROWS = 128
TILE = 384
VMEM_LIMIT = 60 * 1024 * 1024
MESH_ID = pl.DeviceIdType.MESH
LOW = jnp.bfloat16
WIDE = jnp.float32


def adam_step(master, moment_one, moment_two, gradient, learn_rate, decay_rate):
    moment_one = ADAM_ONE * moment_one + (1.0 - ADAM_ONE) * gradient
    moment_two = ADAM_TWO * moment_two + (1.0 - ADAM_TWO) * gradient * gradient
    scaled_one = moment_one / (1.0 - ADAM_ONE**STEP)
    scaled_two = moment_two / (1.0 - ADAM_TWO**STEP)
    master = master - learn_rate * (
        scaled_one / (jnp.sqrt(scaled_two) + ADAM_EPS) + decay_rate * master
    )
    return (moment_one, moment_two, master)


def dot_nn(left, right):
    return jnp.dot(left, right, preferred_element_type=WIDE)


def dot_nt(left, right):
    return lax.dot_general(
        left, right, (((1,), (1,)), ((), ())), preferred_element_type=WIDE
    )


def dot_tn(left, right):
    return lax.dot_general(
        left, right, (((0,), (0,)), ((), ())), preferred_element_type=WIDE
    )


def tile_at(owners, tile):
    return 3 * owners[tile // 3] + tile % 3


def params(**kwargs):
    return pltpu.CompilerParams(vmem_limit_bytes=VMEM_LIMIT, **kwargs)


GATHER_HEAD = 10
GATHER_ORDER = (
    ("tk",), ("xb", 1), ("xs", 0), ("zs", 0), ("zs", 2), ("xb", 0), ("r", 1, 0), ("r", 0, 0),
    ("xs", 1), ("r", 1, 2), ("zs", 1), ("xr", 1, 0), ("r", 0, 2), ("xb", 2), ("r", 1, 1),
    ("r", 2, 0), ("r", 2, 2), ("r", 0, 1), ("xs", 2), ("xob", 2), ("r", 2, 1), ("zx", 0),
    ("xo", 0), ("zx", 1), ("yr", 1, 2), ("xr", 1, 1), ("tf",), ("zx", 2), ("xr", 2, 0), ("xo", 2),
    ("yr", 2, 1), ("e1", 0), ("xob", 1), ("xr", 2, 2), ("yx", 1, 1), ("xo", 1), ("xr", 1, 2),
    ("xr", 2, 1), ("e1", 1), ("xsr", 0), ("yx", 1, 0), ("e1", 2), ("yx", 1, 2), ("yx", 2, 2),
    ("yr", 2, 0), ("yr", 1, 0), ("e2", 2), ("yr", 1, 1), ("xsr", 1), ("xob", 0), ("e2", 1),
    ("yx", 2, 0), ("xsr", 2), ("yr", 2, 2), ("e2", 0), ("yx", 2, 1),
)


def gather_body(
    w_ref, x_ref, out_ref, xo_ref, wide_buf, own_buf, send_sem, recv_sem, tok_recv, local_sem
):
    dp, sq = lax.axis_index("dp"), lax.axis_index("seq")
    z, x = dp // 2, dp % 2
    y, c = sq // 2, sq % 2
    q, qc, qy, qyc = sq, sq ^ 1, sq ^ 2, sq ^ 3
    dev_c, dev_y, dev_yc, dev_x = (dp, sq ^ 1), (dp, sq ^ 2), (dp, sq ^ 3), (dp ^ 1, sq)
    dev_near = (dp ^ 2, sq)
    has_up, has_down, inner = z < 3, z > 0, (z > 0) & (z < 3)
    dev_up = (jnp.minimum(dp + 2, dp % 2 + 6), sq)
    dev_down = (jnp.maximum(dp - 2, dp % 2), sq)
    sources = (z ^ 1, jnp.where(z < 2, 2, 1), jnp.where(z < 2, 3, 0))
    used = [0, 0]
    started, locals_ = [], []

    def move(src, dst):
        copy = pltpu.make_async_copy(src, dst, local_sem.at[used[1]])
        used[1] += 1
        copy.start()
        return copy

    loads = [move(w_ref.at[at], wide_buf.at[at]) for at in (q, qy, qc, qyc)]

    barrier = pltpu.get_barrier_semaphore()

    def greet(device):
        pl.semaphore_signal(barrier, inc=1, device_id=device, device_id_type=MESH_ID)

    for device in (dev_c, dev_y, dev_yc, dev_x):
        greet(device)
    pl.when(has_up)(lambda: greet(dev_up))
    pl.when(has_down)(lambda: greet(dev_down))
    pl.semaphore_wait(barrier, 4 + jnp.where(inner, 2, 1))

    def send(src, dst, recv, device, pred=None):
        copy = pltpu.make_async_remote_copy(
            src_ref=src,
            dst_ref=dst,
            send_sem=send_sem.at[used[0]],
            recv_sem=recv,
            device_id=device,
            device_id_type=MESH_ID,
        )
        used[0] += 1
        if pred is None:
            copy.start()
        else:
            pl.when(pred)(lambda: copy.start())
        started.append((copy, pred))

    def piece(slot, quarter, h, device, pred=None, own=False):
        at = out_ref.at[slot, quarter, h]
        src = own_buf.at[quarter, h] if own else at
        send(src, at, recv_sem.at[slot, quarter, h], device, pred)

    def arrived(slot, quarter, h):
        at = out_ref.at[slot, quarter, h]
        pltpu.make_async_copy(at, at, recv_sem.at[slot, quarter, h]).wait()

    def taken(slot, quarter, h):
        arrived(slot, quarter, h)
        piece(slot, quarter, h, dev_c)

    def near(k):
        return 2 * sources[k] + x

    def far(k):
        return 2 * sources[k] + 1 - x

    oy = 1 - y
    full_own, full_sib = 3 * y + 2 * c, 3 * y + 2 * (1 - c)
    full_far, full_cross = 3 * oy + 2 * c, 3 * oy + 2 * (1 - c)

    def full_rows(j):
        return xo_ref.at[pl.ds(128 * j, 128)]

    def half_rows(part, j, core):
        return xo_ref.at[pl.ds(512 + 256 * (part ^ core) + 64 * j, 64)]

    def token_send():
        send(x_ref.at[full_far], full_rows(sq), tok_recv.at[sq, 0], dev_y)
        for part in range(2):
            src = x_ref.at[3 * oy + 1, pl.ds(64 * part, 64)]
            send(src, half_rows(part, sq, c), tok_recv.at[sq, 1 + part], dev_y)
        send(x_ref.at[full_cross], full_rows(sq), tok_recv.at[sq, 0], dev_yc)
        send(x_ref.at[full_sib], full_rows(sq), tok_recv.at[sq, 0], dev_c)
        locals_.append(move(x_ref.at[full_own], full_rows(sq)))
        for part in range(2):
            src = x_ref.at[3 * y + 1, pl.ds(64 * part, 64)]
            send(src, half_rows(part, sq, 1 - c), tok_recv.at[sq, 1 + part], dev_c)
            locals_.append(move(src, half_rows(part, sq, c)))

    def token_forward():
        for part in range(2):
            at = half_rows(part, sq ^ 2, c)
            pltpu.make_async_copy(at, at, tok_recv.at[sq ^ 2, 1 + part]).wait()
            send(at, half_rows(part, sq ^ 2, 1 - c), tok_recv.at[sq ^ 2, 1 + part], dev_c)

    def own_line(h):
        piece(dp, q, h, dev_up, has_up, own=True)
        piece(dp, q, h, dev_down, has_down, own=True)

    def line(k, h):
        arrived(near(k), q, h)
        onward = (jnp.where(sources[k] < z, dev_up[0], dev_down[0]), sq)
        piece(near(k), q, h, onward, inner)
        if k > 0:
            piece(near(k), q, h, dev_x)
            piece(near(k), q, h, dev_y)
        piece(near(k), q, h, dev_c)

    def from_x_own(h):
        arrived(dp ^ 1, q, h)
        piece(dp ^ 1, q, h, dev_near)
        piece(dp ^ 1, q, h, dev_c)

    def near_other_half(h):
        arrived(near(0), qy, h)
        piece(near(0), qy, h, dev_x)
        piece(near(0), qy, h, dev_c)

    def from_x(k, h):
        arrived(far(k), q, h)
        piece(far(k), q, h, dev_y)
        piece(far(k), q, h, dev_c)

    steps = {
        "tk": token_send,
        "tf": token_forward,
        "zs": own_line,
        "zx": lambda h: piece(dp, qy, h, dev_near, own=True),
        "xs": lambda h: piece(dp, q, h, dev_x, own=True),
        "xb": lambda h: piece(dp, qy, h, dev_x, own=True),
        "r": line,
        "xo": from_x_own,
        "xob": lambda h: taken(dp ^ 1, qy, h),
        "e1": near_other_half,
        "e2": lambda h: taken(far(0), q, h),
        "yr": lambda k, h: taken(near(k), qy, h),
        "xr": from_x,
        "xsr": lambda h: taken(far(0), qy, h),
        "yx": lambda k, h: taken(far(k), qy, h),
    }

    def round_own(index, quarter):
        loads[index].wait()
        own_buf[quarter] = wide_buf[quarter].astype(LOW)

    round_own(0, q)
    round_own(1, qy)
    for name, *at in GATHER_ORDER[:GATHER_HEAD]:
        steps[name](*at)
    round_own(2, qc)
    round_own(3, qyc)
    locals_.append(move(own_buf, out_ref.at[dp]))
    for name, *at in GATHER_ORDER[GATHER_HEAD:]:
        steps[name](*at)
    for step in range(1, 8):
        for h in range(3):
            arrived(dp ^ step, qc, h)
            arrived(dp ^ step, qyc, h)
    for other in (sq ^ 1, sq ^ 2, sq ^ 3):
        at = full_rows(other)
        pltpu.make_async_copy(at, at, tok_recv.at[other, 0]).wait()
    for other in (sq ^ 1, sq ^ 3):
        for part in range(2):
            at = half_rows(part, other, c)
            pltpu.make_async_copy(at, at, tok_recv.at[other, 1 + part]).wait()
    for copy in locals_:
        copy.wait()
    for copy, pred in started:
        if pred is None:
            copy.wait_send()
        else:
            pl.when(pred)(lambda copy=copy: copy.wait_send())


def gather_all(block, tokens):
    block_rows, width = block.shape
    part = block_rows // 12
    hbm = pl.BlockSpec(memory_space=pl.ANY)
    dma = pltpu.SemaphoreType.DMA
    out, spread = pl.pallas_call(
        gather_body,
        out_shape=(
            jax.ShapeDtypeStruct((8, 4, 3, part, width), LOW),
            jax.ShapeDtypeStruct((1024, width), LOW),
        ),
        in_specs=[hbm] * 2,
        out_specs=(hbm,) * 2,
        scratch_shapes=[
            pltpu.VMEM((4, 3, part, width), WIDE),
            pltpu.VMEM((4, 3, part, width), LOW),
            dma((160,)),
            dma((8, 4, 3)),
            dma((4, 3)),
            dma((8,)),
        ],
        compiler_params=params(collective_id=1, has_side_effects=True),
        name="gather_weights",
    )(block.reshape(4, 3, part, width), tokens)
    return out.reshape(8 * block_rows // TILE, TILE, width), spread


def qkv_body(map_ref, x_ref, top_ref, low_ref, vec_ref, out_ref):
    part = pl.program_id(0)
    scale = jnp.where(part == 0, HEAD_DIM ** (-0.5), 1.0)
    value = dot_nn(x_ref[:, :TILE], top_ref[0]) + dot_nn(x_ref[:, TILE:], low_ref[0])
    bias = jnp.where(part == 0, vec_ref[0:1], jnp.where(part == 2, vec_ref[1:2], 0.0))
    out_ref[0] = ((value + bias) * scale).astype(LOW)


def qkv_project(owners, rows, weights, vectors):
    count, width = rows.shape
    return pl.pallas_call(
        qkv_body,
        grid_spec=pltpu.PrefetchScalarGridSpec(
            num_scalar_prefetch=1,
            grid=(3,),
            in_specs=[
                pl.BlockSpec((count, width), lambda i, m: (0, 0)),
                pl.BlockSpec((1, TILE, width), lambda i, m: (tile_at(m, 2 * i), 0, 0)),
                pl.BlockSpec((1, TILE, width), lambda i, m: (tile_at(m, 2 * i + 1), 0, 0)),
                pl.BlockSpec(vectors.shape, lambda i, m: (0, 0)),
            ],
            out_specs=pl.BlockSpec((1, count, width), lambda i, m: (i, 0, 0)),
        ),
        out_shape=jax.ShapeDtypeStruct((3, count, width), LOW),
        compiler_params=params(),
        name="qkv",
    )(owners, rows, weights, weights, vectors)


def group_barrier(dp, sq):
    barrier = pltpu.get_barrier_semaphore()
    for step in range(1, 4):
        pl.semaphore_signal(
            barrier, inc=1, device_id=(dp, sq ^ step), device_id_type=MESH_ID
        )
    pl.semaphore_wait(barrier, 3)


class Exchange:
    def __init__(self, pieces, send_sem, recv_sem, local_sem):
        self.dp, self.sq = lax.axis_index("dp"), lax.axis_index("seq")
        self.pieces = pieces
        self.sems = (send_sem, recv_sem, local_sem)

    def copies(self):
        send_sem, recv_sem, local_sem = self.sems
        out = []
        for step in (2, 3, 1):
            target = self.sq ^ step
            for kind, (src, dst) in enumerate(self.pieces(self.sq, target)):
                out.append(
                    pltpu.make_async_remote_copy(
                        src_ref=src,
                        dst_ref=dst,
                        send_sem=send_sem.at[step - 1, kind],
                        recv_sem=recv_sem.at[self.sq, kind],
                        device_id=(self.dp, target),
                        device_id_type=MESH_ID,
                    )
                )
        for kind, (src, dst) in enumerate(self.pieces(self.sq, self.sq)):
            out.append(pltpu.make_async_copy(src, dst, local_sem.at[kind]))
        return out

    def start(self):
        for copy in self.copies():
            copy.start()

    def finish(self):
        copies = self.copies()
        for copy in copies[:6]:
            copy.wait_send()
        for copy in copies[6:]:
            copy.wait()
        for step in range(1, 4):
            source = self.sq ^ step
            for kind, (_, dst) in enumerate(self.pieces(source, self.sq)):
                pltpu.make_async_copy(dst, dst, self.sems[1].at[source, kind]).wait()


EXCHANGE_SEMS = [
    pltpu.SemaphoreType.DMA((3, 2)),
    pltpu.SemaphoreType.DMA((4, 2)),
    pltpu.SemaphoreType.DMA((2,)),
]


def by_sentence(src, dst):
    def pieces(source, target):
        y, c = target // 2, target % 2
        return (
            (src.at[3 * y + 2 * c], dst.at[pl.ds(128 * source, 128)]),
            (src.at[3 * y + 1, pl.ds(64 * c, 64)], dst.at[pl.ds(512 + 64 * source, 64)]),
        )

    return pieces


def by_position(src, dst):
    def pieces(source, target):
        y, c = source // 2, source % 2
        return (
            (src.at[pl.ds(128 * target, 128)], dst.at[3 * y + 2 * c]),
            (src.at[pl.ds(512 + 64 * target, 64)], dst.at[3 * y + 1, pl.ds(64 * c, 64)]),
        )

    return pieces


def sentence_length(lengths_ref, shared):
    sq = lax.axis_index("seq")
    group, core = sq // 2, sq % 2
    return jnp.where(shared, lengths_ref[3 * group + 1], lengths_ref[3 * group + 2 * core])


def positions(shape, shared, first=0):
    row = first + lax.broadcasted_iota(jnp.int32, shape, 0)
    own = lax.axis_index("seq") % 2
    half = row // 256
    part = row - 256 * half
    core = own + half - 2 * own * half
    mixed = (part // 64) * 128 + part % 64 + 64 * core
    return jnp.where(shared, mixed, row)


def key_bias(lengths_ref, shared):
    inside = positions((512, 128), shared) < sentence_length(lengths_ref, shared)
    bias = jnp.where(inside, 0.0, MASK_FILL)
    return jnp.concatenate([bias, bias], axis=1)


def head_masks(shape):
    lane = lax.broadcasted_iota(jnp.int32, shape, 1)
    return (lane < HEAD_DIM, lane >= HEAD_DIM)


def attend_body(
    len_ref, q_ref, k_ref, v_ref, g_ref, o_ref, lse_ref, gy_ref, send_sem, recv_sem, local_sem
):
    block, group = pl.program_id(0), pl.program_id(1)
    exchange = Exchange(by_sentence(g_ref, gy_ref), send_sem, recv_sem, local_sem)

    @pl.when((block == 0) & (group == 0))
    def _():
        group_barrier(exchange.dp, exchange.sq)
        exchange.start()

    bias = key_bias(len_ref, block == 2)
    for pair in range(q_ref.shape[-1] // 128):
        lanes = slice(128 * pair, 128 * (pair + 1))
        queries, keys = q_ref[0, :, lanes], k_ref[0, :, lanes]
        value_t = v_ref[0, :, lanes].T
        outs = []
        for head, mask in enumerate(head_masks(queries.shape)):
            scores = dot_nt(keys, jnp.where(mask, queries, jnp.zeros_like(queries))) + bias
            top = jnp.max(scores, axis=0, keepdims=True)
            shifted = jnp.exp(scores - top)
            total = jnp.sum(shifted, axis=0, keepdims=True)
            part = value_t[HEAD_DIM * head : HEAD_DIM * (head + 1)]
            outs.append(dot_nn(part, shifted.astype(LOW)) * (1.0 / total))
            lse_ref[0, 2 * pair + head : 2 * pair + head + 1, :] = top + jnp.log(total)
        o_ref[:, lanes] = jnp.concatenate(outs, axis=0).T.astype(LOW)

    @pl.when((block == 2) & (group == pl.num_programs(1) - 1))
    def _():
        exchange.finish()


def attend(lengths, qkv, grad_out):
    width = qkv.shape[-1]
    groups = width // 128 // FWD_PAIRS
    lanes = 128 * FWD_PAIRS
    hbm = pl.BlockSpec(memory_space=pl.ANY)
    return pl.pallas_call(
        attend_body,
        grid=(3, groups),
        in_specs=[
            pl.BlockSpec(memory_space=pltpu.SMEM),
            pl.BlockSpec((1, 256, lanes), lambda i, h: (0, i, h)),
            pl.BlockSpec((1, 512, lanes), lambda i, h: (1, i // 2, h)),
            pl.BlockSpec((1, 512, lanes), lambda i, h: (2, i // 2, h)),
            hbm,
        ],
        out_specs=(
            pl.BlockSpec((256, lanes), lambda i, h: (i, h)),
            pl.BlockSpec((1, 2 * FWD_PAIRS, 256), lambda i, h: (h, 0, i)),
            hbm,
        ),
        out_shape=(
            jax.ShapeDtypeStruct((768, width), LOW),
            jax.ShapeDtypeStruct((groups, 2 * FWD_PAIRS, 768), WIDE),
            jax.ShapeDtypeStruct((768, width), LOW),
        ),
        scratch_shapes=EXCHANGE_SEMS,
        compiler_params=params(collective_id=3, has_side_effects=True),
        name="attend",
    )(lengths, qkv, qkv, qkv, grad_out)


def attend_back_body(
    len_ref, q_ref, k_ref, v_ref, lse_ref, do_ref, o_ref, y_ref,
    dq_ref, dk_ref, dv_ref, out_ref,
    acc, keep, give, take, send_sem, recv_sem, local_sem, give_sem, take_sem,
):
    group, block = pl.program_id(0), pl.program_id(1)
    exchange = Exchange(by_position(y_ref, out_ref), send_sem, recv_sem, local_sem)
    dp, sq = exchange.dp, exchange.sq

    @pl.when((block == 0) & (group == 0))
    def _():
        group_barrier(dp, sq)
        exchange.start()

    bias = key_bias(len_ref, block == 0)
    d_keys, d_values = [], []
    for pair in range(q_ref.shape[-1] // 128):
        lanes = slice(128 * pair, 128 * (pair + 1))
        queries, keys, values = q_ref[0, :, lanes], k_ref[0, :, lanes], v_ref[0, :, lanes]
        grads = do_ref[:, lanes]
        keys_t = keys.T
        inner = (grads.astype(WIDE) * o_ref[:, lanes].astype(WIDE)).T
        d_query = []
        d_key = d_value = 0.0
        for head, mask in enumerate(head_masks(queries.shape)):
            query = jnp.where(mask, queries, jnp.zeros_like(queries))
            grad = jnp.where(mask, grads, jnp.zeros_like(grads))
            rows = slice(HEAD_DIM * head, HEAD_DIM * (head + 1))
            inner_sum = jnp.sum(inner[rows], axis=0, keepdims=True)
            scores = dot_nt(keys, query) + bias
            probs = jnp.exp(scores - lse_ref[0, 2 * pair + head : 2 * pair + head + 1, :])
            d_probs = dot_nt(values, grad)
            d_scores = (probs * (d_probs - inner_sum)).astype(LOW)
            d_value = d_value + dot_nn(probs.astype(LOW), grad)
            d_key = d_key + dot_nn(d_scores, query)
            d_query.append(dot_nn(keys_t[rows], d_scores))
        d_query = jnp.concatenate(d_query, axis=0) * HEAD_DIM ** (-0.5)
        dq_ref[:, lanes] = d_query.T.astype(LOW)
        d_keys.append((lanes, d_key))
        d_values.append((lanes, d_value))
    pairs = ((0, d_keys), (1, d_values))

    def swap(kind):
        return pltpu.make_async_remote_copy(
            src_ref=give.at[group, kind],
            dst_ref=take.at[group, kind],
            send_sem=give_sem.at[group, kind],
            recv_sem=take_sem.at[group, kind],
            device_id=(dp, sq ^ 1),
            device_id_type=MESH_ID,
        )

    @pl.when(block == 0)
    def _():
        for kind, parts in pairs:
            for lanes, part in parts:
                keep[kind, :, lanes] = part[:256]
                give[group, kind, :, lanes] = part[256:].astype(LOW)
            swap(kind).start()

    @pl.when(block == 1)
    def _():
        for kind, parts in pairs:
            for lanes, part in parts:
                acc[kind, :, lanes] = part

    @pl.when(block == 2)
    def _():
        for (kind, parts), ref in zip(pairs, (dk_ref, dv_ref)):
            swap(kind).wait()
            for lanes, part in parts:
                ref[:512, lanes] = (acc[kind, :, lanes] + part).astype(LOW)
                other = take[group, kind, :, lanes].astype(WIDE)
                ref[512:, lanes] = (keep[kind, :, lanes] + other).astype(LOW)

    @pl.when((block == 2) & (group == pl.num_programs(0) - 1))
    def _():
        exchange.finish()


def attend_back(lengths, qkv, lse, d_out, out, result, sent_dev):
    width = qkv.shape[-1]
    groups = width // 128 // BACK_PAIRS
    lanes = 128 * BACK_PAIRS
    hbm = pl.BlockSpec(memory_space=pl.ANY)
    query = pl.BlockSpec((256, lanes), lambda h, i: ((i + 2) % 3, h))
    keys = pl.BlockSpec((768, lanes), lambda h, i: (0, h))
    flat = jax.ShapeDtypeStruct((768, width), LOW)
    shared = lambda i: jnp.where(i == 0, 1, 0)
    return pl.pallas_call(
        attend_back_body,
        grid=(groups, 3),
        in_specs=[
            pl.BlockSpec(memory_space=pltpu.SMEM),
            pl.BlockSpec((1, 256, lanes), lambda h, i: (0, (i + 2) % 3, h)),
            pl.BlockSpec((1, 512, lanes), lambda h, i: (1, shared(i), h)),
            pl.BlockSpec((1, 512, lanes), lambda h, i: (2, shared(i), h)),
            pl.BlockSpec((1, 2 * BACK_PAIRS, 256), lambda h, i: (h, 0, (i + 2) % 3)),
            query,
            query,
            hbm,
        ],
        out_specs=(query, keys, keys, hbm),
        out_shape=(flat, flat, flat, jax.ShapeDtypeStruct((sent_dev, 128, width), LOW)),
        scratch_shapes=[
            pltpu.VMEM((2, 512, lanes), WIDE),
            pltpu.VMEM((2, 256, lanes), WIDE),
            pltpu.VMEM((groups, 2, 256, lanes), LOW),
            pltpu.VMEM((groups, 2, 256, lanes), LOW),
        ]
        + EXCHANGE_SEMS
        + [pltpu.SemaphoreType.DMA((groups, 2)), pltpu.SemaphoreType.DMA((groups, 2))],
        compiler_params=params(collective_id=4, has_side_effects=True),
        name="attend_back",
    )(lengths, qkv, qkv, qkv, lse.reshape(groups, 2 * BACK_PAIRS, 768), d_out, out, result)


def row_mean(value):
    return jnp.mean(value, axis=-1, keepdims=True)


def col_sum(value):
    return jnp.sum(value, axis=0, keepdims=True)


def middle_body(
    map_ref, len_ref, o_hbm, x_hbm, gy_hbm, w_ref, vec_ref,
    y_hbm, left_hbm, right_hbm, do_hbm, da_hbm, dh_hbm, sums_ref,
    w_buf, o_buf, x_buf, gy_buf, left, right, slope, total, hat_one, rstd_one, low_buf,
    sem, in_sem, out_sem,
):
    count, width = o_buf.shape
    tiles = w_buf.shape[0]
    chunks = FEEDFWD_UNITS // width

    def fetch(t):
        return pltpu.make_async_copy(w_ref.at[tile_at(map_ref, 6 + t)], w_buf.at[t], sem.at[t])

    inputs = [
        pltpu.make_async_copy(src, dst, in_sem.at[i])
        for i, (src, dst) in enumerate(
            (
                (o_hbm, o_buf),
                (x_hbm.at[pl.ds(0, count)], x_buf),
                (gy_hbm, gy_buf),
            )
        )
    ]
    inputs[0].start()
    for t in range(2):
        fetch(t).start()
    inputs[1].start()
    for c in range(chunks):
        for t in (2 + 2 * c, 3 + 2 * c, 10 + 2 * c, 11 + 2 * c):
            fetch(t).start()
    inputs[2].start()
    outputs = []

    def put(src, dst):
        copy = pltpu.make_async_copy(src, dst, out_sem.at[len(outputs)])
        copy.start()
        outputs.append(copy)

    def put_left(t, value):
        for u in range(2):
            left[t + u] = value[:, TILE * u : TILE * (u + 1)]
            put(left.at[t + u], left_hbm.at[t + u])

    def ready(*which):
        for t in which:
            fetch(t).wait()

    def pair(t):
        return w_buf[t : t + 2].reshape(2 * TILE, width)

    def vec(row):
        return vec_ref[row : row + 1, :]

    def fold(value):
        return jnp.sum(value.reshape(-1, 8, width), axis=0)

    def over_rows(body, carried):
        zero = (jnp.zeros((8, width), WIDE),) * carried

        def step(i, carry):
            return body(pl.ds(pl.multiple_of(i * NORM_ROWS, NORM_ROWS), NORM_ROWS), i, carry)

        return lax.fori_loop(0, count // NORM_ROWS, step, zero)

    inputs[0].wait()
    ready(0, 1)
    total[...] = dot_nn(o_buf[...], pair(0))
    inputs[1].wait()

    def norm_one(at, i, carry):
        resid = x_buf[at].astype(WIDE) + (total[at] + vec(2))
        centered = resid - row_mean(resid)
        rstd = lax.rsqrt(row_mean(centered * centered) + NORM_EPS)
        rstd_one[at] = rstd
        hat = centered * rstd
        hat_one[at] = hat
        first = hat * vec(4) + vec(5)
        total[at] = first + vec(3)
        right[0, at] = first.astype(LOW)
        return carry

    over_rows(norm_one, 0)
    put(right.at[0], right_hbm.at[0])

    first_low = right[0]
    for c in range(chunks):
        ready(2 + 2 * c, 3 + 2 * c, 10 + 2 * c, 11 + 2 * c)
        act = dot_nt(first_low, pair(2 + 2 * c)) + vec(8 + c)
        cdf = 0.5 + 0.5 * lax.erf(act * (0.5**0.5))
        pdf = jnp.exp(-0.5 * act * act) * 0.3989422804014327
        slope[c] = cdf + act * pdf
        active = (act * cdf).astype(LOW)
        put_left(8 + 2 * c, active)
        total[...] += dot_nn(active, pair(10 + 2 * c))
    inputs[2].wait()

    def norm_two(at, i, carry):
        d_gain, d_shift, d_bias, pool_full, pool_half = carry
        resid = total[at]
        centered = resid - row_mean(resid)
        rstd = lax.rsqrt(row_mean(centered * centered) + NORM_EPS)
        hat = centered * rstd
        result = hat * vec(6) + vec(7)
        low_buf[0, at] = result.astype(LOW)
        shared = i * NORM_ROWS >= 512
        row = positions((NORM_ROWS, 128), shared, i * NORM_ROWS - jnp.where(shared, 512, 0))
        valid = jnp.where(row < sentence_length(len_ref, shared), 1.0, 0.0)
        pooled = fold(result * jnp.concatenate([valid] * (width // 128), axis=1))
        part = shared.astype(WIDE)
        grad = gy_buf[at].astype(WIDE)
        d_gain = d_gain + fold(grad * hat)
        d_shift = d_shift + fold(grad)
        grad = grad * vec(6)
        d_resid = rstd * (grad - row_mean(grad) - hat * row_mean(grad * hat))
        total[at] = d_resid
        grad_low = d_resid.astype(LOW)
        right[1, at] = grad_low
        return (
            d_gain,
            d_shift,
            d_bias + fold(grad_low.astype(WIDE)),
            pool_full + pooled * (1.0 - part),
            pool_half + pooled * part,
        )

    sums_ref[...] = jnp.zeros_like(sums_ref)
    found = over_rows(norm_two, 5)
    for row, value in zip((4, 5, 1, 10, 11), found):
        sums_ref[row : row + 1, :] = col_sum(value)
    put(low_buf.at[0], y_hbm)
    put(right.at[1], right_hbm.at[1])

    grad_low = right[1]
    for c in range(chunks):
        d_active = dot_nt(grad_low, pair(10 + 2 * c))
        d_act = (d_active * slope[c]).astype(LOW)
        put_left(2 * c, d_act)
        sums_ref[6 + c : 7 + c, :] = col_sum(d_act.astype(WIDE))
        total[...] += dot_nn(d_act, pair(2 + 2 * c))

    def norm_back(at, i, carry):
        d_gain, d_shift, d_bias = carry
        grad = total[at]
        hat = hat_one[at]
        d_gain = d_gain + fold(grad * hat)
        d_shift = d_shift + fold(grad)
        grad = grad * vec(4)
        d_resid = rstd_one[at] * (grad - row_mean(grad) - hat * row_mean(grad * hat))
        total[at] = d_resid
        grad_low = d_resid.astype(LOW)
        low_buf[1, at] = grad_low
        return (d_gain, d_shift, d_bias + fold(grad_low.astype(WIDE)))

    found = over_rows(norm_back, 3)
    for row, value in zip((2, 3, 0), found):
        sums_ref[row : row + 1, :] = col_sum(value)
    put(total, dh_hbm)
    put(low_buf.at[1], da_hbm)
    low_buf[2] = dot_nt(low_buf[1], pair(0)).astype(LOW)
    put(low_buf.at[2], do_hbm)
    for copy in outputs:
        copy.wait()


def middle(owners, lengths, attended, rows, out_grad, weights, vectors):
    count, width = attended.shape
    half = FEEDFWD_UNITS // TILE
    tiles = 2 + 2 * half
    hbm = pl.BlockSpec(memory_space=pl.ANY)
    smem = pl.BlockSpec(memory_space=pltpu.SMEM)
    vmem = pl.BlockSpec(memory_space=pltpu.VMEM)
    flat = jax.ShapeDtypeStruct((count, width), LOW)
    return pl.pallas_call(
        middle_body,
        in_specs=[smem, smem] + [hbm] * 4 + [vmem],
        out_specs=(hbm,) * 6 + (vmem,),
        out_shape=(
            flat,
            jax.ShapeDtypeStruct((2 * half, count, TILE), LOW),
            jax.ShapeDtypeStruct((2, count, width), LOW),
            flat,
            flat,
            jax.ShapeDtypeStruct((count, width), WIDE),
            jax.ShapeDtypeStruct((16, width), WIDE),
        ),
        scratch_shapes=[
            pltpu.VMEM((tiles, TILE, width), LOW),
            pltpu.VMEM((count, width), LOW),
            pltpu.VMEM((count, width), LOW),
            pltpu.VMEM((count, width), LOW),
            pltpu.VMEM((2 * half, count, TILE), LOW),
            pltpu.VMEM((2, count, width), LOW),
            pltpu.VMEM((half // 2, count, width), WIDE),
            pltpu.VMEM((count, width), WIDE),
            pltpu.VMEM((count, width), WIDE),
            pltpu.VMEM((count, 1), WIDE),
            pltpu.VMEM((3, count, width), LOW),
            pltpu.SemaphoreType.DMA((tiles,)),
            pltpu.SemaphoreType.DMA((3,)),
            pltpu.SemaphoreType.DMA((2 * half + 6,)),
        ],
        compiler_params=params(),
        name="feed_forward",
    )(owners, lengths, attended, rows, out_grad, weights, vectors)


def grad_ff_body(map_ref, left_ref, right_ref, out_ref):
    out_ref[0] = dot_tn(left_ref[0], right_ref[0]).astype(LOW)


def grad_ff(owners, left, right):
    per = FEEDFWD_UNITS // TILE
    count, width = right.shape[1:]
    return pl.pallas_call(
        grad_ff_body,
        grid_spec=pltpu.PrefetchScalarGridSpec(
            num_scalar_prefetch=1,
            grid=(2 * per,),
            in_specs=[
                pl.BlockSpec((1, count, TILE), lambda i, m: (i, 0, 0)),
                pl.BlockSpec((1, count, width), lambda i, m: (i // per, 0, 0)),
            ],
            out_specs=pl.BlockSpec((1, TILE, width), lambda i, m: (tile_at(m, 8 + i), 0, 0)),
        ),
        out_shape=jax.ShapeDtypeStruct((8 + 2 * per, TILE, width), LOW),
        compiler_params=params(),
        name="grad_ff",
    )(owners, left, right)


def grad_attn_body(
    map_ref, x_ref, dq_ref, dk_ref, dv_ref, o_ref, da_ref, into_ref, out_ref, sums_ref
):
    step = pl.program_id(0)
    for part, grad_ref in enumerate((dq_ref, dk_ref, dv_ref)):

        @pl.when(step // 2 == part)
        def _(grad_ref=grad_ref):
            out_ref[0] = dot_tn(x_ref[...], grad_ref[...]).astype(LOW)

    @pl.when(step // 2 == 3)
    def _():
        out_ref[0] = dot_tn(o_ref[...], da_ref[...]).astype(LOW)

    @pl.when(step == 0)
    def _():
        sums_ref[...] = jnp.zeros_like(sums_ref)
        sums_ref[0:1, :] = col_sum(dq_ref[...].astype(WIDE))
        sums_ref[1:2, :] = col_sum(dv_ref[...].astype(WIDE))


def grad_attn(owners, rows, dq, dk, dv, attended, da, into):
    count, width = dq.shape
    whole = pl.BlockSpec((count, width), lambda i, m: (0, 0))
    return pl.pallas_call(
        grad_attn_body,
        grid_spec=pltpu.PrefetchScalarGridSpec(
            num_scalar_prefetch=1,
            grid=(8,),
            in_specs=[
                pl.BlockSpec((count, TILE), lambda i, m: (0, i % 2)),
                whole,
                whole,
                whole,
                pl.BlockSpec((768, TILE), lambda i, m: (0, i % 2)),
                pl.BlockSpec((768, width), lambda i, m: (0, 0)),
                pl.BlockSpec(memory_space=pl.ANY),
            ],
            out_specs=(
                pl.BlockSpec((1, TILE, width), lambda i, m: (tile_at(m, i), 0, 0)),
                pl.BlockSpec((8, width), lambda i, m: (0, 0)),
            ),
        ),
        out_shape=(
            jax.ShapeDtypeStruct(into.shape, LOW),
            jax.ShapeDtypeStruct((8, width), WIDE),
        ),
        input_output_aliases={7: 0},
        compiler_params=params(),
        name="grad_attn",
    )(owners, rows, dq, dk, dv, attended, da, into)


def grad_in_body(map_ref, dq_ref, dk_ref, dv_ref, dh_ref, *refs):
    w_refs, out_ref = refs[:6], refs[6]
    for half in range(2):
        cols = slice(TILE * half, TILE * (half + 1))
        value = dh_ref[:, cols]
        for part, grad_ref in enumerate((dq_ref, dk_ref, dv_ref)):
            value = value + dot_nt(grad_ref[...], w_refs[2 * part + half][0])
        out_ref[:, cols] = value.astype(LOW)


def grad_in(owners, dq, dk, dv, dh, weights):
    count, width = dq.shape
    block = pl.BlockSpec((256, width), lambda i, m: (i, 0))
    return pl.pallas_call(
        grad_in_body,
        grid_spec=pltpu.PrefetchScalarGridSpec(
            num_scalar_prefetch=1,
            grid=(count // 256,),
            in_specs=[block] * 4
            + [
                pl.BlockSpec((1, TILE, width), lambda i, m, t=t: (tile_at(m, t), 0, 0)) for t in range(6)
            ],
            out_specs=block,
        ),
        out_shape=jax.ShapeDtypeStruct((count, width), LOW),
        compiler_params=params(),
        name="grad_in",
    )(owners, dq, dk, dv, dh, *([weights] * 6))


REDUCE_ORDER = (
    ("fp", 3, 2), ("lp", 0, 0), ("in",), ("fp", 2, 1), ("fc", 3, 2), ("lc", 0, 0), ("lp", 0, 1),
    ("lp", 2, 1), ("fc", 2, 1), ("fp", 0, 1), ("fp", 2, 2), ("lp", 1, 1), ("lc", 0, 1),
    ("fp", 1, 1), ("lc", 1, 1), ("lm", 0, 0), ("lp", 2, 0), ("fc", 2, 2), ("fp", 3, 1),
    ("fc", 0, 1), ("fc", 1, 1), ("fp", 0, 2), ("np", 1, 1), ("np", 1, 2), ("np", 3, 1),
    ("lm", 0, 1), ("fc", 0, 2), ("fc", 3, 1), ("nc", 1, 1), ("fp", 1, 2), ("nc", 3, 1),
    ("np", 2, 1), ("lc", 2, 1), ("vs", 0), ("lp", 1, 0), ("fc", 1, 2), ("lm", 2, 1), ("lp", 3, 0),
    ("nc", 1, 2), ("lp", 3, 1), ("np", 0, 2), ("nc", 2, 1), ("lm", 1, 1), ("np", 0, 1),
    ("np", 3, 2), ("np", 2, 2), ("va", 0), ("vs", 1), ("lc", 1, 0), ("nc", 0, 1), ("nc", 0, 2),
    ("turn", 2, 1), ("lm", 1, 0), ("nc", 3, 2), ("nc", 2, 2), ("lc", 2, 0), ("lc", 3, 0),
    ("turn", 1, 1), ("lc", 3, 1), ("turn", 3, 2), ("turn", 0, 1), ("turn", 1, 2), ("le", 1),
    ("turn", 0, 2), ("lm", 2, 0), ("on", 0, 1), ("le", 0), ("lo",), ("turn", 3, 1), ("turn", 2, 2),
    ("on", 0, 2), ("on", 1, 1), ("va", 1), ("vs", 2), ("on", 2, 1), ("on", 1, 2), ("turn", 3, 0),
    ("va", 2), ("vs", 3), ("end", 1), ("on", 2, 2), ("va", 3), ("vs", 4), ("end", 0), ("end", 2),
    ("va", 4),
)


def reduce_body(
    own_of_ref, x_ref, o_ref, left_ref, dq_ref, dk_ref, dv_ref, da_ref, right_ref,
    sums_ref, g_ref, own_ref, vt_ref, sq_ref, gi_ref,
    lbuf, rbuf, pbuf, core_in, x_in, y_in, y_pair, z_in, zf_in, ebuf, tbuf, tlow,
    vbuf, v_in, s_own, s_seq, s_dp,
    send_sem, local_sem, core_sem, x_sem, y_sem, ypair_sem, z_sem, zf_sem, v_sem, out_sem,
    seq_sem, dp_sem, in_sem,
):
    dp, sq = lax.axis_index("dp"), lax.axis_index("seq")
    z, x = dp // 2, dp % 2
    y, c = sq // 2, sq % 2
    dev_c, dev_y, dev_yc, dev_x = (dp, sq ^ 1), (dp, sq ^ 2), (dp, sq ^ 3), (dp ^ 1, sq)
    has_up, has_down, inner = z < 3, z > 0, (z > 0) & (z < 3)
    order = (
        jnp.where(z < 2, 3, 0),
        jnp.where(z == 0, 2, jnp.where(z == 1, 0, jnp.where(z == 2, 3, 1))),
        jnp.where(z == 0, 1, jnp.where(z == 1, 2, jnp.where(z == 2, 1, 2))),
        z,
    )

    used = [0, 0]
    remotes, own_moves = [], []

    def move(src, dst):
        copy = pltpu.make_async_copy(src, dst, local_sem.at[used[1]])
        used[1] += 1
        copy.start()
        return copy

    loads = [move(left_ref, lbuf.at[pl.ds(4, 16)]), move(right_ref, rbuf.at[pl.ds(4, 2)])]
    for index, ref in enumerate((dq_ref, dk_ref, dv_ref, da_ref)):
        loads.append(move(ref, rbuf.at[index]))
    for half in range(2):
        cols = pl.ds(TILE * half, TILE)
        loads.append(move(x_ref.at[pl.ds(0, 768), cols], lbuf.at[half]))
        loads.append(move(o_ref.at[:, cols], lbuf.at[2 + half]))

    barrier = pltpu.get_barrier_semaphore()
    for step in range(1, 4):
        pl.semaphore_signal(
            barrier, inc=1, device_id=(dp, sq ^ step), device_id_type=MESH_ID
        )
    for step in range(1, 8):
        pl.semaphore_signal(
            barrier, inc=1, device_id=(dp ^ step, sq), device_id_type=MESH_ID
        )
    pl.semaphore_wait(barrier, 10)

    def send(src, dst, recv, device, pred=None):
        copy = pltpu.make_async_remote_copy(
            src_ref=src,
            dst_ref=dst,
            send_sem=send_sem.at[used[0]],
            recv_sem=recv,
            device_id=device,
            device_id_type=MESH_ID,
        )
        used[0] += 1
        if pred is None:
            copy.start()
        else:
            pl.when(pred)(lambda: copy.start())
        remotes.append((copy, pred))

    def arrived(at, sem):
        pltpu.make_async_copy(at, at, sem).wait()

    def wide(ref, *at):
        return ref[at].astype(WIDE)

    partners = (dev_c, dev_y, dev_x, (dp ^ 2, sq), (dp ^ 4, sq))

    def vec_send(step):
        send(vbuf.at[step], v_in.at[step], v_sem.at[step], partners[step])

    def vec_add(step):
        arrived(v_in.at[step], v_sem.at[step])
        vbuf[step + 1] = vbuf[step] + v_in[step]

    def in_full(j):
        return g_ref.at[pl.ds(128 * j, 128)], gi_ref.at[3 * y + 2 * c]

    def in_half(j):
        return g_ref.at[pl.ds(512 + 64 * j, 64)], gi_ref.at[3 * y + 1, pl.ds(64 * c, 64)]

    def input_send():
        for device in (dev_y, dev_yc, dev_c):
            for kind, pair in enumerate((in_full(device[1]), in_half(device[1]))):
                send(pair[0], pair[1], in_sem.at[sq, kind], device)
        own_moves.append(move(*in_full(sq)))
        own_moves.append(move(*in_half(sq)))

    for copy in loads:
        copy.wait()

    def standard_of(slot):
        found = jnp.int32(0)
        for block in range(8):
            found = jnp.maximum(found, jnp.where(own_of_ref[block] == slot, block, 0))
        return found

    def partial(slot, t):
        tile = 3 * standard_of(slot) + t
        left = jnp.where(tile < 6, tile % 2, tile - 4)
        right = jnp.where(tile < 8, tile // 2, 4 + (tile - 8) // 8)
        value = dot_tn(lbuf[left], rbuf[right]).astype(LOW)
        for quarter in range(4):
            rows = slice(96 * quarter, 96 * (quarter + 1))
            pbuf[quarter % 2, t, slot, quarter // 2] = value[rows]
        send(pbuf.at[1 - c, t, slot], core_in.at[t, slot], core_sem.at[t, slot], dev_c)

    def combine(slot, t):
        arrived(core_in.at[t, slot], core_sem.at[t, slot])
        pbuf[c, t, slot] = (wide(pbuf, c, t, slot) + wide(core_in, t, slot)).astype(LOW)

    def cbuf(*at):
        return pbuf.at[(c, *at)]

    def line_send(k, sub, pred):
        d = order[k]
        up = d > z
        step = jnp.where(up, 1, -1)
        index = jnp.where(z + step == d, jnp.where(up, 4, 5), d)
        send(
            cbuf(0, 2 * d + sub), zf_in.at[index, sub], zf_sem.at[index, sub],
            (dp + 2 * step, sq), pred,
        )

    def line_partial(k, sub):
        partial(2 * order[k] + sub, 0)

    def line_combine(k, sub):
        combine(2 * order[k] + sub, 0)
        if k < 3:
            line_send(k, sub, jnp.logical_not(inner))

    def line_add(slot, index, sub):
        arrived(zf_in.at[index, sub], zf_sem.at[index, sub])
        pbuf[c, 0, slot] = (wide(pbuf, c, 0, slot) + wide(zf_in, index, sub)).astype(LOW)

    def line_middle(k, sub):
        d = order[k]
        pl.when(inner)(lambda: line_add(2 * d + sub, d, sub))
        line_send(k, sub, inner)

    def line_end(sub):
        pl.when(has_down)(lambda: line_add(2 * z + sub, 4, sub))
        pl.when(has_up)(lambda: line_add(2 * z + sub, 5, sub))

    def line_out():
        send(cbuf(0, 2 * z + 1 - x), x_in.at[z, 0], x_sem.at[z, 0], dev_x)

    def far_partial(k, t):
        partial(2 * order[k] + 1 - x, t)

    def near_partial(k, t):
        partial(2 * order[k] + x, t)

    def far_combine(k, t):
        d = order[k]
        slot = 2 * d + 1 - x
        combine(slot, t)
        if k == 1:
            send(cbuf(t, slot, 1 - y), y_pair.at[t, 1], ypair_sem.at[t, 1], dev_y)
        else:
            send(cbuf(t, slot), x_in.at[d, t], x_sem.at[d, t], dev_x)

    def near_combine(k, t):
        slot = 2 * order[k] + x
        combine(slot, t)
        if k == 1:
            send(cbuf(t, slot, 1 - y), y_pair.at[t, 0], ypair_sem.at[t, 0], dev_y)

    def turn(k, t):
        d = order[k]
        near, far = 2 * d + x, 2 * d + 1 - x
        if k == 1:
            for half in range(2):
                arrived(y_pair.at[t, half], ypair_sem.at[t, half])
            pbuf[c, t, far, y] = (
                wide(pbuf, c, t, far, y) + wide(y_pair, t, 1)
            ).astype(LOW)
            send(cbuf(t, far, y), x_in.at[d, t, 0], x_sem.at[d, t], dev_x)
        else:
            arrived(x_in.at[d, t], x_sem.at[d, t])
            pbuf[c, t, near] = (wide(pbuf, c, t, near) + wide(x_in, d, t)).astype(LOW)
            send(cbuf(t, near, 1 - y), y_in.at[d, t], y_sem.at[d, t], dev_y)

    def plane_sum(k, t):
        d = order[k]
        near = 2 * d + x
        mine = wide(pbuf, c, t, near, y)
        if k == 1:
            arrived(x_in.at[d, t, 0], x_sem.at[d, t])
            return mine + wide(y_pair, t, 0) + wide(x_in, d, t, 0)
        arrived(y_in.at[d, t], y_sem.at[d, t])
        return mine + wide(y_in, d, t)

    def onward(k, t):
        d = order[k]
        tbuf[...] = plane_sum(k, t)

        @pl.when(inner)
        def _():
            arrived(z_in.at[d, t], z_sem.at[d, t])
            tbuf[...] += wide(z_in, d, t)

        ebuf[k, t] = tbuf[...].astype(LOW)
        up = d > z
        step = jnp.where(up, 1, -1)
        index = jnp.where(z + step == d, jnp.where(up, 4, 5), d)
        send(ebuf.at[k, t], z_in.at[index, t], z_sem.at[index, t], (dp + 2 * step, sq))

    squares = []

    def finish(t):
        tbuf[...] = plane_sum(3, t)
        if t > 0:
            for index, there in ((4, has_down), (5, has_up)):

                @pl.when(there)
                def _(index=index):
                    arrived(z_in.at[index, t], z_sem.at[index, t])
                    tbuf[...] += wide(z_in, index, t)

        total = tbuf[...].astype(LOW)
        tlow[t] = total
        wide_total = total.astype(WIDE)
        rows = (wide_total * wide_total).reshape(-1, 8, wide_total.shape[-1])
        squares.append(jnp.sum(rows, axis=0))
        at = own_ref.at[t, sq]
        for device in (dev_y, dev_c):
            send(tlow.at[t], at, out_sem.at[t, sq], device)
        own_moves.append(move(tlow.at[t], at))

    vbuf[0] = jnp.zeros(vbuf.shape[1:], WIDE)
    vbuf[0, 0:1] = col_sum(wide(rbuf, 0))
    vbuf[0, 1:2] = col_sum(wide(rbuf, 2))
    vbuf[0, 2:12] = sums_ref[0:10]
    vbuf[0, pl.ds(16 + 3 * y + 2 * c, 1)] = sums_ref[10:11]
    vbuf[0, pl.ds(16 + 3 * y + 1, 1)] = sums_ref[11:12]
    steps = {
        "lp": line_partial,
        "lc": line_combine,
        "lm": line_middle,
        "le": line_end,
        "lo": line_out,
        "fp": far_partial,
        "np": near_partial,
        "fc": far_combine,
        "nc": near_combine,
        "turn": turn,
        "on": onward,
        "end": finish,
        "vs": vec_send,
        "va": vec_add,
        "in": input_send,
    }
    for name, *at in REDUCE_ORDER:
        steps[name](*at)

    squares = squares[0] + squares[1] + squares[2]
    folded = squares[:, :128]
    for lane in range(1, squares.shape[-1] // 128):
        folded = folded + squares[:, 128 * lane : 128 * (lane + 1)]
    s_own[...] = folded
    for step in range(1, 4):
        send(s_own, s_seq.at[sq], seq_sem.at[sq], (dp, sq ^ step))
    s_seq[sq] = folded
    for t in (1, 0, 2):
        arrived(own_ref.at[t, sq ^ 2], out_sem.at[t, sq ^ 2])
        send(own_ref.at[t, sq ^ 2], own_ref.at[t, sq ^ 2], out_sem.at[t, sq ^ 2], dev_c)
    for step in range(1, 4):
        arrived(s_seq.at[sq ^ step], seq_sem.at[sq ^ step])
    group = s_seq[0] + s_seq[1] + s_seq[2] + s_seq[3]
    s_dp[dp] = group
    for step in range(1, 8):
        send(s_dp.at[dp], s_dp.at[dp], dp_sem.at[dp], (dp ^ step, sq))
    for step in range(1, 8):
        arrived(s_dp.at[dp ^ step], dp_sem.at[dp ^ step])
    everyone = s_dp[0]
    for index in range(1, 8):
        everyone = everyone + s_dp[index]
    sq_ref[...] = everyone
    vt_ref[0:16] = vbuf[5][0:16]
    vt_ref[16:24] = vbuf[2][16:24]

    for t in range(3):
        arrived(own_ref.at[t, sq ^ 1], out_sem.at[t, sq ^ 1])
        arrived(own_ref.at[t, sq ^ 3], out_sem.at[t, sq ^ 3])
    for step in range(1, 4):
        other = sq ^ step
        there, member = other // 2, other % 2
        arrived(gi_ref.at[3 * there + 2 * member], in_sem.at[other, 0])
        arrived(gi_ref.at[3 * there + 1, pl.ds(64 * member, 64)], in_sem.at[other, 1])
    for copy in own_moves:
        copy.wait()
    for copy, pred in remotes:
        if pred is None:
            copy.wait_send()
        else:
            pl.when(pred)(lambda copy=copy: copy.wait_send())


def reduce_all(owners, rows, out, left, grads, right, sums, grad_rows, sent_dev):
    width = rows.shape[-1]
    part = TILE // 4
    hbm = pl.BlockSpec(memory_space=pl.ANY)
    vmem = pl.BlockSpec(memory_space=pltpu.VMEM)
    smem = pl.BlockSpec(memory_space=pltpu.SMEM)
    dma = pltpu.SemaphoreType.DMA
    owned, totals, squares, input_grad = pl.pallas_call(
        reduce_body,
        out_shape=(
            jax.ShapeDtypeStruct((3, 4, part, width), LOW),
            jax.ShapeDtypeStruct((24, width), WIDE),
            jax.ShapeDtypeStruct((8, 128), WIDE),
            jax.ShapeDtypeStruct((sent_dev, 128, width), LOW),
        ),
        in_specs=[smem] + [hbm] * 8 + [vmem, hbm],
        out_specs=(hbm, vmem, vmem, hbm),
        scratch_shapes=[
            pltpu.VMEM((20, 768, TILE), LOW),
            pltpu.VMEM((6, 768, width), LOW),
            pltpu.VMEM((2, 3, 8, 2, part, width), LOW),
            pltpu.VMEM((3, 8, 2, part, width), LOW),
            pltpu.VMEM((4, 3, 2, part, width), LOW),
            pltpu.VMEM((4, 3, part, width), LOW),
            pltpu.VMEM((3, 2, part, width), LOW),
            pltpu.VMEM((6, 3, part, width), LOW),
            pltpu.VMEM((6, 2, 2, part, width), LOW),
            pltpu.VMEM((3, 3, part, width), LOW),
            pltpu.VMEM((part, width), WIDE),
            pltpu.VMEM((3, part, width), LOW),
            pltpu.VMEM((6, 24, width), WIDE),
            pltpu.VMEM((5, 24, width), WIDE),
            pltpu.VMEM((8, 128), WIDE),
            pltpu.VMEM((4, 8, 128), WIDE),
            pltpu.VMEM((8, 8, 128), WIDE),
            dma((96,)),
            dma((32,)),
            dma((3, 8)),
            dma((4, 3)),
            dma((4, 3)),
            dma((3, 2)),
            dma((6, 3)),
            dma((6, 2)),
            dma((5,)),
            dma((3, 4)),
            dma((4,)),
            dma((8,)),
            dma((4, 2)),
        ],
        compiler_params=params(collective_id=2, has_side_effects=True),
        name="reduce_gradients",
    )(owners, rows, out, left, *grads, right, sums, grad_rows)
    return owned.reshape(3 * TILE, width), totals, squares, input_grad


def optimizer_body(
    len_ref, mem_ref, g_ref, sq_ref, tot_ref, w_ref, one_ref, two_ref, vw_ref, vone_ref, vtwo_ref,
    norm_ref, emb_ref, *rest,
):
    outs, clip_ref = rest[:-1], rest[-1]
    count = vw_ref.shape[0]

    @pl.when(pl.program_id(0) == 0)
    def _():
        gradient = tot_ref[:count]
        total = jnp.sum(sq_ref[...], keepdims=True) + jnp.sum(gradient * gradient, keepdims=True)
        norm = jnp.sqrt(total)
        norm_ref[...] = norm
        clip_ref[...] = jnp.broadcast_to(MAX_NORM / jnp.maximum(norm, MAX_NORM), clip_ref.shape)

    clip = clip_ref[...]

    def update(refs, outs, gradient, rate, decay):
        new = adam_step(refs[2][...], refs[0][...], refs[1][...], gradient, rate, decay)
        for ref, value in zip(outs, new + (new[2].astype(LOW),)):
            ref[...] = value

    update(
        (one_ref, two_ref, w_ref), outs[:4], g_ref[...].astype(WIDE) * clip,
        RATE_MATRIX, WEIGHT_DECAY,
    )

    @pl.when(pl.program_id(0) == 0)
    def _():
        update((vone_ref, vtwo_ref, vw_ref), outs[4:], tot_ref[:count] * clip, RATE_VECTOR, 0.0)
        groups, most = mem_ref.shape
        sentences = len_ref.shape[0]
        first = lax.axis_index("dp") * sentences
        pooled = [
            tot_ref[16 + s : 17 + s] / len_ref[s].astype(WIDE) for s in range(sentences)
        ]
        for g in range(groups):
            listed = jnp.int32(0)
            total = jnp.zeros_like(pooled[0])
            for m in range(most):
                listed += jnp.where(mem_ref[g, m] >= 0, 1, 0)
            for s in range(sentences):
                times = jnp.int32(0)
                for m in range(most):
                    times += jnp.where(mem_ref[g, m] == first + s, 1, 0)
                total = total + pooled[s] * times.astype(WIDE)
            emb_ref[g : g + 1] = total / listed.astype(WIDE)


def optimizer(lengths, members, owned, squares, totals, matrices, vectors):
    block_rows, width = owned.shape
    steps = 4 if block_rows % 64 == 0 else 3
    smem = pl.BlockSpec(memory_space=pltpu.SMEM)
    mat = pl.BlockSpec((block_rows // steps, width), lambda i: (i, 0))

    def whole(shape):
        return pl.BlockSpec(shape, lambda i: (0, 0))

    vec = whole(vectors[0].shape)
    embeddings = (members.shape[0], width)
    return pl.pallas_call(
        optimizer_body,
        grid=(steps,),
        in_specs=[smem, smem, mat, whole(squares.shape), whole(totals.shape)]
        + [mat] * 3
        + [vec] * 3,
        out_specs=(whole((1, 1)), whole(embeddings)) + (mat,) * 4 + (vec,) * 4,
        out_shape=(
            jax.ShapeDtypeStruct((1, 1), WIDE),
            jax.ShapeDtypeStruct(embeddings, WIDE),
        )
        + tuple(
            jax.ShapeDtypeStruct(like.shape, dtype)
            for like in (owned, vectors[0])
            for dtype in (WIDE, WIDE, WIDE, LOW)
        ),
        scratch_shapes=[pltpu.VMEM((1, width), WIDE)],
        compiler_params=params(),
        name="optimizer",
    )(lengths, members, owned, squares, totals, *matrices, *vectors)


def to_positions(value):
    width = value.shape[1]
    moved = jnp.concatenate(
        [value[:512].reshape(4, 128, width), value[512:].reshape(4, 64, width)], axis=1
    )
    moved = lax.all_to_all(moved, "seq", split_axis=0, concat_axis=0, tiled=True)
    rows = []
    for y in range(2):
        rows.append(moved[2 * y, :128])
        rows.append(jnp.concatenate([moved[2 * y, 128:], moved[2 * y + 1, 128:]], axis=0))
        rows.append(moved[2 * y + 1, :128])
    return jnp.stack(rows)


def to_rows(tokens):
    width = tokens.shape[-1]
    core = lax.axis_index("seq") % 2
    pieces = []
    for j in range(4):
        y, c = j // 2, j % 2
        pieces += [tokens[3 * y + 2 * c], tokens[3 * y + 1]]
    moved = jnp.concatenate(pieces, axis=0).reshape(4, 256, width)
    moved = lax.all_to_all(moved, "seq", split_axis=0, concat_axis=0, tiled=True)
    shared = moved[:, 128:].reshape(4, 2, 64, width)
    own = lax.dynamic_index_in_dim(shared, core, 1, keepdims=False)
    other = lax.dynamic_index_in_dim(shared, 1 - core, 1, keepdims=False)
    return jnp.concatenate(
        [moved[:, :128].reshape(512, width), own.reshape(256, width), other.reshape(256, width)],
        axis=0,
    )


def local(
    tokens,
    grad_out,
    lengths,
    members,
    owners,
    mat_master,
    mat_moment1,
    mat_moment2,
    vec_master,
    vec_moment1,
    vec_moment2,
):
    sent_dev, local_len, model_width = tokens.shape
    dp_count = lax.axis_size("dp")
    block_rows = mat_master.shape[0]
    direct = dp_count == 8 and block_rows == 3 * TILE

    if direct:
        weights, rows = gather_all(mat_master, tokens)
        blocks = owners
    else:
        gathered = lax.all_gather(mat_master.astype(LOW), "dp", axis=0, tiled=True)
        weights = gathered.reshape(dp_count, block_rows, model_width)[owners]
        weights = weights.reshape(-1, TILE, model_width)
        rows = to_rows(tokens)
        blocks = jnp.arange(weights.shape[0] // 3, dtype=jnp.int32)

    qkv = qkv_project(blocks, rows, weights, vec_master)
    attended, lse, out_grad = attend(lengths, qkv, grad_out)
    result, left, right, d_attended, d_branch, d_resid, sums = middle(
        blocks, lengths, attended, rows, out_grad, weights, vec_master
    )
    dq, dk, dv, output = attend_back(
        lengths, qkv, lse, d_attended, attended, result, sent_dev
    )
    grad_rows = grad_in(blocks, dq, dk, dv, d_resid, weights)

    if direct:
        owned, totals, squares, input_grad = reduce_all(
            owners, rows, attended, left, (dq, dk, dv, d_branch), right, sums, grad_rows, sent_dev
        )
    else:
        grads = grad_ff(blocks, left, right)
        grads, sums_qv = grad_attn(blocks, rows, dq, dk, dv, attended, d_branch, grads)
        input_grad = to_positions(grad_rows)
        inverse = jnp.argsort(owners)
        grads = grads.reshape(dp_count, block_rows, model_width)[inverse]
        grads = grads.reshape(dp_count * block_rows, model_width)
        quarter = lax.psum_scatter(grads, ("dp", "seq"), scatter_dimension=0, tiled=True)
        owned = lax.all_gather(quarter, "seq", axis=0, tiled=True)
        quarter = quarter.astype(WIDE)
        group = lax.axis_index("seq") // 2
        core = lax.axis_index("seq") % 2
        place = jnp.arange(8)[:, None]
        pooled = jnp.where(place == 3 * group + 2 * core, sums[10:11], 0.0) + jnp.where(
            place == 3 * group + 1, sums[11:12], 0.0
        )
        pooled = lax.psum(pooled, "seq")
        local_vec = jnp.concatenate([sums_qv[0:2], sums[0:14]], axis=0)
        squares, vec_total = lax.psum(
            (jnp.sum(quarter * quarter), local_vec), ("dp", "seq")
        )
        squares = jnp.full((8, 128), squares / 1024.0)
        totals = jnp.concatenate([vec_total, pooled], axis=0)

    norm, embeddings, *new = optimizer(
        lengths,
        members,
        owned,
        squares,
        totals,
        (mat_master, mat_moment1, mat_moment2),
        (vec_master, vec_moment1, vec_moment2),
    )
    return (output, input_grad, embeddings, norm.reshape(()), *new)


def solution(mesh):
    placed = (
        P("dp", "seq", None),
        P("dp", "seq", None),
        P("dp"),
        P("dp", None),
        P(),
        P("dp", None),
        P("dp", None),
        P("dp", None),
        P(),
        P(),
        P(),
    )
    return jax.shard_map(
        local,
        mesh=mesh,
        in_specs=placed,
        out_specs=(
            P("dp", "seq", None),
            P("dp", "seq", None),
            P("dp", None),
            P(),
            P("dp", None),
            P("dp", None),
            P("dp", None),
            P("dp", None),
            P(),
            P(),
            P(),
            P(),
        ),
        check_vma=False,
    )
```

```python
import functools

import jax
import jax.numpy as jnp
from jax import lax
from jax.experimental import pallas as pl
from jax.experimental.pallas import tpu as pltpu
from jax.sharding import PartitionSpec as P

HEADS = 12
HEAD_DIM = 64
FEEDFWD_UNITS = 3072
STEP = 10


NORM_EPS = 1e-06
MASK_FILL = -1e30
MAX_NORM = 1.0
ADAM_ONE = 0.9
ADAM_TWO = 0.999
ADAM_EPS = 1e-08
WEIGHT_DECAY = 0.01
RATE_MATRIX = 0.04
RATE_VECTOR = 0.5

FWD_PAIRS = 6
BACK_PAIRS = 6
NORM_ROWS = 128
TILE = 384
VMEM_LIMIT = 60 * 1024 * 1024
MESH_ID = pl.DeviceIdType.MESH
LOW = jnp.bfloat16
WIDE = jnp.float32


def adam_step(master, moment_one, moment_two, gradient, learn_rate, decay_rate):
    moment_one = ADAM_ONE * moment_one + (1.0 - ADAM_ONE) * gradient
    moment_two = ADAM_TWO * moment_two + (1.0 - ADAM_TWO) * gradient * gradient
    scaled_one = moment_one / (1.0 - ADAM_ONE**STEP)
    scaled_two = moment_two / (1.0 - ADAM_TWO**STEP)
    master = master - learn_rate * (
        scaled_one / (jnp.sqrt(scaled_two) + ADAM_EPS) + decay_rate * master
    )
    return (moment_one, moment_two, master)


def dot_nn(left, right):
    return jnp.dot(left, right, preferred_element_type=WIDE)


def dot_nt(left, right):
    return lax.dot_general(
        left, right, (((1,), (1,)), ((), ())), preferred_element_type=WIDE
    )


def dot_tn(left, right):
    return lax.dot_general(
        left, right, (((0,), (0,)), ((), ())), preferred_element_type=WIDE
    )


def tile_at(owners, tile):
    return 3 * owners[tile // 3] + tile % 3


def params(**kwargs):
    return pltpu.CompilerParams(vmem_limit_bytes=VMEM_LIMIT, **kwargs)


GATHER_HEAD = 10
GATHER_ORDER = (
    ("tk",), ("xb", 1), ("xs", 0), ("zs", 0), ("zs", 2), ("xb", 0), ("r", 1, 0), ("r", 0, 0),
    ("xs", 1), ("r", 1, 2), ("zs", 1), ("xr", 1, 0), ("r", 0, 2), ("xb", 2), ("r", 1, 1),
    ("r", 2, 0), ("r", 2, 2), ("r", 0, 1), ("xs", 2), ("xob", 2), ("r", 2, 1), ("zx", 0),
    ("xo", 0), ("zx", 1), ("yr", 1, 2), ("xr", 1, 1), ("tf",), ("zx", 2), ("xr", 2, 0), ("xo", 2),
    ("yr", 2, 1), ("e1", 0), ("xob", 1), ("xr", 2, 2), ("yx", 1, 1), ("xo", 1), ("xr", 1, 2),
    ("xr", 2, 1), ("e1", 1), ("xsr", 0), ("yx", 1, 0), ("e1", 2), ("yx", 1, 2), ("yx", 2, 2),
    ("yr", 2, 0), ("yr", 1, 0), ("e2", 2), ("yr", 1, 1), ("xsr", 1), ("xob", 0), ("e2", 1),
    ("yx", 2, 0), ("xsr", 2), ("yr", 2, 2), ("e2", 0), ("yx", 2, 1),
)


def front_body(
    own_of_ref, len_ref, w_ref, x_ref, g_ref, vec_ref,
    weights_ref, rows_ref, qkv_ref, o_ref, gy_ref, lse_ref,
    wide_buf, own_buf, out_ref, xo_ref, qkv_buf, o_buf,
    send_sem, recv_sem, tok_recv, local_sem, ex_send, ex_recv, ex_local,
):
    dp, sq = lax.axis_index("dp"), lax.axis_index("seq")
    z, x = dp // 2, dp % 2
    y, c = sq // 2, sq % 2
    q, qc, qy, qyc = sq, sq ^ 1, sq ^ 2, sq ^ 3
    dev_c, dev_y, dev_yc, dev_x = (dp, sq ^ 1), (dp, sq ^ 2), (dp, sq ^ 3), (dp ^ 1, sq)
    dev_near = (dp ^ 2, sq)
    has_up, has_down, inner = z < 3, z > 0, (z > 0) & (z < 3)
    dev_up = (jnp.minimum(dp + 2, dp % 2 + 6), sq)
    dev_down = (jnp.maximum(dp - 2, dp % 2), sq)
    sources = (z ^ 1, jnp.where(z < 2, 2, 1), jnp.where(z < 2, 3, 0))
    used = [0, 0]
    started, locals_ = [], []

    def move(src, dst):
        copy = pltpu.make_async_copy(src, dst, local_sem.at[used[1]])
        used[1] += 1
        copy.start()
        return copy

    loads = []
    for at in (q, qy, qc, qyc):
        thirds = pl.ds(3 * at, 3)
        loads.append(move(w_ref.at[thirds], wide_buf.at[thirds]))

    barrier = pltpu.get_barrier_semaphore()

    def greet(device):
        pl.semaphore_signal(barrier, inc=1, device_id=device, device_id_type=MESH_ID)

    for device in (dev_c, dev_y, dev_yc, dev_x):
        greet(device)
    pl.when(has_up)(lambda: greet(dev_up))
    pl.when(has_down)(lambda: greet(dev_down))
    pl.semaphore_wait(barrier, 4 + jnp.where(inner, 2, 1))

    def send(src, dst, recv, device, pred=None):
        copy = pltpu.make_async_remote_copy(
            src_ref=src,
            dst_ref=dst,
            send_sem=send_sem.at[used[0]],
            recv_sem=recv,
            device_id=device,
            device_id_type=MESH_ID,
        )
        used[0] += 1
        if pred is None:
            copy.start()
        else:
            pl.when(pred)(lambda: copy.start())
        started.append((copy, pred))

    def piece(slot, quarter, h, device, pred=None, own=False):
        at = out_ref.at[slot, 3 * quarter + h]
        src = own_buf.at[3 * quarter + h] if own else at
        send(src, at, recv_sem.at[slot, quarter, h], device, pred)

    def arrived(slot, quarter, h):
        at = out_ref.at[slot, 3 * quarter + h]
        pltpu.make_async_copy(at, at, recv_sem.at[slot, quarter, h]).wait()

    def taken(slot, quarter, h):
        arrived(slot, quarter, h)
        piece(slot, quarter, h, dev_c)

    def near(k):
        return 2 * sources[k] + x

    def far(k):
        return 2 * sources[k] + 1 - x

    oy = 1 - y
    full_own, full_sib = 3 * y + 2 * c, 3 * y + 2 * (1 - c)
    full_far, full_cross = 3 * oy + 2 * c, 3 * oy + 2 * (1 - c)

    def full_rows(j):
        return xo_ref.at[pl.ds(128 * j, 128)]

    def half_rows(part, j, core):
        return xo_ref.at[pl.ds(512 + 256 * (part ^ core) + 64 * j, 64)]

    def token_send():
        send(x_ref.at[full_far], full_rows(sq), tok_recv.at[sq, 0], dev_y)
        for part in range(2):
            src = x_ref.at[3 * oy + 1, pl.ds(64 * part, 64)]
            send(src, half_rows(part, sq, c), tok_recv.at[sq, 1 + part], dev_y)
        send(x_ref.at[full_cross], full_rows(sq), tok_recv.at[sq, 0], dev_yc)
        send(x_ref.at[full_sib], full_rows(sq), tok_recv.at[sq, 0], dev_c)
        locals_.append(move(x_ref.at[full_own], full_rows(sq)))
        for part in range(2):
            src = x_ref.at[3 * y + 1, pl.ds(64 * part, 64)]
            send(src, half_rows(part, sq, 1 - c), tok_recv.at[sq, 1 + part], dev_c)
            locals_.append(move(src, half_rows(part, sq, c)))

    def token_forward():
        for part in range(2):
            at = half_rows(part, sq ^ 2, c)
            pltpu.make_async_copy(at, at, tok_recv.at[sq ^ 2, 1 + part]).wait()
            send(at, half_rows(part, sq ^ 2, 1 - c), tok_recv.at[sq ^ 2, 1 + part], dev_c)

    def own_line(h):
        piece(dp, q, h, dev_up, has_up, own=True)
        piece(dp, q, h, dev_down, has_down, own=True)

    def line(k, h):
        arrived(near(k), q, h)
        onward = (jnp.where(sources[k] < z, dev_up[0], dev_down[0]), sq)
        piece(near(k), q, h, onward, inner)
        if k > 0:
            piece(near(k), q, h, dev_x)
            piece(near(k), q, h, dev_y)
        piece(near(k), q, h, dev_c)

    def from_x_own(h):
        arrived(dp ^ 1, q, h)
        piece(dp ^ 1, q, h, dev_near)
        piece(dp ^ 1, q, h, dev_c)

    def near_other_half(h):
        arrived(near(0), qy, h)
        piece(near(0), qy, h, dev_x)
        piece(near(0), qy, h, dev_c)

    def from_x(k, h):
        arrived(far(k), q, h)
        piece(far(k), q, h, dev_y)
        piece(far(k), q, h, dev_c)

    steps = {
        "tk": token_send,
        "tf": token_forward,
        "zs": own_line,
        "zx": lambda h: piece(dp, qy, h, dev_near, own=True),
        "xs": lambda h: piece(dp, q, h, dev_x, own=True),
        "xb": lambda h: piece(dp, qy, h, dev_x, own=True),
        "r": line,
        "xo": from_x_own,
        "xob": lambda h: taken(dp ^ 1, qy, h),
        "e1": near_other_half,
        "e2": lambda h: taken(far(0), q, h),
        "yr": lambda k, h: taken(near(k), qy, h),
        "xr": from_x,
        "xsr": lambda h: taken(far(0), qy, h),
        "yx": lambda k, h: taken(far(k), qy, h),
    }

    def round_own(index, quarter):
        loads[index].wait()
        thirds = pl.ds(3 * quarter, 3)
        own_buf[thirds] = wide_buf[thirds].astype(LOW)

    round_own(0, q)
    round_own(1, qy)
    for name, *at in GATHER_ORDER[:GATHER_HEAD]:
        steps[name](*at)
    round_own(2, qc)
    round_own(3, qyc)
    locals_.append(move(own_buf, out_ref.at[dp]))
    for name, *at in GATHER_ORDER[GATHER_HEAD:]:
        steps[name](*at)
    exchange = Exchange(by_sentence(g_ref, gy_ref), ex_send, ex_recv, ex_local)
    exchange.start()
    for step in range(1, 8):
        for h in range(3):
            arrived(dp ^ step, qc, h)
            arrived(dp ^ step, qyc, h)
    for other in (sq ^ 1, sq ^ 2, sq ^ 3):
        at = full_rows(other)
        pltpu.make_async_copy(at, at, tok_recv.at[other, 0]).wait()
    for other in (sq ^ 1, sq ^ 3):
        for part in range(2):
            at = half_rows(part, other, c)
            pltpu.make_async_copy(at, at, tok_recv.at[other, 1 + part]).wait()
    for copy in locals_:
        copy.wait()
    stores = [move(out_ref.at[slot], weights_ref.at[slot]) for slot in range(8)]
    stores.append(move(xo_ref, rows_ref))

    for part in range(3):
        tiles = []
        for tile in (2 * part, 2 * part + 1):
            held = out_ref[own_of_ref[tile // 3], 4 * (tile % 3) : 4 * (tile % 3) + 4]
            tiles.append(held.reshape(TILE, held.shape[-1]))
        value = dot_nn(xo_ref[...], jnp.concatenate(tiles, axis=0))
        if part == 0:
            value = (value + vec_ref[0:1]) * HEAD_DIM ** (-0.5)
        elif part == 2:
            value = value + vec_ref[1:2]
        qkv_buf[part] = value.astype(LOW)
        stores.append(move(qkv_buf.at[part], qkv_ref.at[part]))

    def attend_block(block, carry):
        bias = key_bias(len_ref, block == 2)
        at = pl.ds(pl.multiple_of(256 * block, 256), 256)
        keys = pl.ds(pl.multiple_of(512 * (block // 2), 512), 512)
        for pair in range(qkv_buf.shape[-1] // 128):
            lanes = slice(128 * pair, 128 * (pair + 1))
            out, logs = attend_pair(
                qkv_buf[0, at, lanes], qkv_buf[1, keys, lanes], qkv_buf[2, keys, lanes], bias
            )
            o_buf[at, lanes] = out
            for head in range(2):
                lse_ref[2 * pair + head : 2 * pair + head + 1, at] = logs[head]
        return carry

    lax.fori_loop(0, 3, attend_block, 0)
    stores.append(move(o_buf, o_ref))
    exchange.finish()
    for copy in stores:
        copy.wait()
    for copy, pred in started:
        if pred is None:
            copy.wait_send()
        else:
            pl.when(pred)(lambda copy=copy: copy.wait_send())


def front(owners, lengths, block, tokens, grad_out, vectors):
    block_rows, width = block.shape
    part = block_rows // 12
    hbm = pl.BlockSpec(memory_space=pl.ANY)
    smem = pl.BlockSpec(memory_space=pltpu.SMEM)
    vmem = pl.BlockSpec(memory_space=pltpu.VMEM)
    dma = pltpu.SemaphoreType.DMA
    flat = jax.ShapeDtypeStruct((768, width), LOW)
    weights, *rest = pl.pallas_call(
        front_body,
        out_shape=(
            jax.ShapeDtypeStruct((8, 12, part, width), LOW),
            jax.ShapeDtypeStruct((1024, width), LOW),
            jax.ShapeDtypeStruct((3, 1024, width), LOW),
            flat,
            flat,
            jax.ShapeDtypeStruct((HEADS, 768), WIDE),
        ),
        in_specs=[smem] * 2 + [hbm] * 3 + [vmem],
        out_specs=(hbm,) * 5 + (vmem,),
        scratch_shapes=[
            pltpu.VMEM((12, part, width), WIDE),
            pltpu.VMEM((12, part, width), LOW),
            pltpu.VMEM((8, 12, part, width), LOW),
            pltpu.VMEM((1024, width), LOW),
            pltpu.VMEM((3, 1024, width), LOW),
            pltpu.VMEM((768, width), LOW),
            dma((160,)),
            dma((8, 4, 3)),
            dma((4, 3)),
            dma((24,)),
        ]
        + EXCHANGE_SEMS,
        compiler_params=params(collective_id=1, has_side_effects=True),
        name="gather_attend",
    )(owners, lengths, block.reshape(12, part, width), tokens, grad_out, vectors)
    return weights.reshape(8 * block_rows // TILE, TILE, width), *rest


def qkv_body(map_ref, x_ref, top_ref, low_ref, vec_ref, out_ref):
    part = pl.program_id(0)
    scale = jnp.where(part == 0, HEAD_DIM ** (-0.5), 1.0)
    value = dot_nn(x_ref[:, :TILE], top_ref[0]) + dot_nn(x_ref[:, TILE:], low_ref[0])
    bias = jnp.where(part == 0, vec_ref[0:1], jnp.where(part == 2, vec_ref[1:2], 0.0))
    out_ref[0] = ((value + bias) * scale).astype(LOW)


def qkv_project(owners, rows, weights, vectors):
    count, width = rows.shape
    return pl.pallas_call(
        qkv_body,
        grid_spec=pltpu.PrefetchScalarGridSpec(
            num_scalar_prefetch=1,
            grid=(3,),
            in_specs=[
                pl.BlockSpec((count, width), lambda i, m: (0, 0)),
                pl.BlockSpec((1, TILE, width), lambda i, m: (tile_at(m, 2 * i), 0, 0)),
                pl.BlockSpec((1, TILE, width), lambda i, m: (tile_at(m, 2 * i + 1), 0, 0)),
                pl.BlockSpec(vectors.shape, lambda i, m: (0, 0)),
            ],
            out_specs=pl.BlockSpec((1, count, width), lambda i, m: (i, 0, 0)),
        ),
        out_shape=jax.ShapeDtypeStruct((3, count, width), LOW),
        compiler_params=params(),
        name="qkv",
    )(owners, rows, weights, weights, vectors)


def group_barrier(dp, sq):
    barrier = pltpu.get_barrier_semaphore()
    for step in range(1, 4):
        pl.semaphore_signal(
            barrier, inc=1, device_id=(dp, sq ^ step), device_id_type=MESH_ID
        )
    pl.semaphore_wait(barrier, 3)


class Exchange:
    def __init__(self, pieces, send_sem, recv_sem, local_sem):
        self.dp, self.sq = lax.axis_index("dp"), lax.axis_index("seq")
        self.pieces = pieces
        self.sems = (send_sem, recv_sem, local_sem)

    def copies(self):
        send_sem, recv_sem, local_sem = self.sems
        out = []
        for step in (2, 3, 1):
            target = self.sq ^ step
            for kind, (src, dst) in enumerate(self.pieces(self.sq, target)):
                out.append(
                    pltpu.make_async_remote_copy(
                        src_ref=src,
                        dst_ref=dst,
                        send_sem=send_sem.at[step - 1, kind],
                        recv_sem=recv_sem.at[self.sq, kind],
                        device_id=(self.dp, target),
                        device_id_type=MESH_ID,
                    )
                )
        for kind, (src, dst) in enumerate(self.pieces(self.sq, self.sq)):
            out.append(pltpu.make_async_copy(src, dst, local_sem.at[kind]))
        return out

    def start(self):
        for copy in self.copies():
            copy.start()

    def finish(self):
        copies = self.copies()
        for copy in copies[:6]:
            copy.wait_send()
        for copy in copies[6:]:
            copy.wait()
        for step in range(1, 4):
            source = self.sq ^ step
            for kind, (_, dst) in enumerate(self.pieces(source, self.sq)):
                pltpu.make_async_copy(dst, dst, self.sems[1].at[source, kind]).wait()


EXCHANGE_SEMS = [
    pltpu.SemaphoreType.DMA((3, 2)),
    pltpu.SemaphoreType.DMA((4, 2)),
    pltpu.SemaphoreType.DMA((2,)),
]


def by_sentence(src, dst):
    def pieces(source, target):
        y, c = target // 2, target % 2
        return (
            (src.at[3 * y + 2 * c], dst.at[pl.ds(128 * source, 128)]),
            (src.at[3 * y + 1, pl.ds(64 * c, 64)], dst.at[pl.ds(512 + 64 * source, 64)]),
        )

    return pieces


def by_position(src, dst):
    def pieces(source, target):
        y, c = source // 2, source % 2
        return (
            (src.at[pl.ds(128 * target, 128)], dst.at[3 * y + 2 * c]),
            (src.at[pl.ds(512 + 64 * target, 64)], dst.at[3 * y + 1, pl.ds(64 * c, 64)]),
        )

    return pieces


def sentence_length(lengths_ref, shared):
    sq = lax.axis_index("seq")
    group, core = sq // 2, sq % 2
    return jnp.where(shared, lengths_ref[3 * group + 1], lengths_ref[3 * group + 2 * core])


def positions(shape, shared, first=0):
    row = first + lax.broadcasted_iota(jnp.int32, shape, 0)
    own = lax.axis_index("seq") % 2
    half = row // 256
    part = row - 256 * half
    core = own + half - 2 * own * half
    mixed = (part // 64) * 128 + part % 64 + 64 * core
    return jnp.where(shared, mixed, row)


def key_bias(lengths_ref, shared):
    inside = positions((512, 128), shared) < sentence_length(lengths_ref, shared)
    bias = jnp.where(inside, 0.0, MASK_FILL)
    return jnp.concatenate([bias, bias], axis=1)


def head_masks(shape):
    lane = lax.broadcasted_iota(jnp.int32, shape, 1)
    return (lane < HEAD_DIM, lane >= HEAD_DIM)


def attend_pair(queries, keys, values, bias):
    value_t = values.T
    outs, logs = [], []
    for head, mask in enumerate(head_masks(queries.shape)):
        scores = dot_nt(keys, jnp.where(mask, queries, jnp.zeros_like(queries))) + bias
        top = jnp.max(scores, axis=0, keepdims=True)
        shifted = jnp.exp(scores - top)
        total = jnp.sum(shifted, axis=0, keepdims=True)
        part = value_t[HEAD_DIM * head : HEAD_DIM * (head + 1)]
        outs.append(dot_nn(part, shifted.astype(LOW)) * (1.0 / total))
        logs.append(top + jnp.log(total))
    return jnp.concatenate(outs, axis=0).T.astype(LOW), logs


def attend_body(
    len_ref, q_ref, k_ref, v_ref, g_ref, o_ref, lse_ref, gy_ref, send_sem, recv_sem, local_sem
):
    block, group = pl.program_id(0), pl.program_id(1)
    exchange = Exchange(by_sentence(g_ref, gy_ref), send_sem, recv_sem, local_sem)

    @pl.when((block == 0) & (group == 0))
    def _():
        group_barrier(exchange.dp, exchange.sq)
        exchange.start()

    bias = key_bias(len_ref, block == 2)
    for pair in range(q_ref.shape[-1] // 128):
        lanes = slice(128 * pair, 128 * (pair + 1))
        out, logs = attend_pair(q_ref[0, :, lanes], k_ref[0, :, lanes], v_ref[0, :, lanes], bias)
        o_ref[:, lanes] = out
        for head in range(2):
            lse_ref[0, 2 * pair + head : 2 * pair + head + 1, :] = logs[head]

    @pl.when((block == 2) & (group == pl.num_programs(1) - 1))
    def _():
        exchange.finish()


def attend(lengths, qkv, grad_out):
    width = qkv.shape[-1]
    groups = width // 128 // FWD_PAIRS
    lanes = 128 * FWD_PAIRS
    hbm = pl.BlockSpec(memory_space=pl.ANY)
    return pl.pallas_call(
        attend_body,
        grid=(3, groups),
        in_specs=[
            pl.BlockSpec(memory_space=pltpu.SMEM),
            pl.BlockSpec((1, 256, lanes), lambda i, h: (0, i, h)),
            pl.BlockSpec((1, 512, lanes), lambda i, h: (1, i // 2, h)),
            pl.BlockSpec((1, 512, lanes), lambda i, h: (2, i // 2, h)),
            hbm,
        ],
        out_specs=(
            pl.BlockSpec((256, lanes), lambda i, h: (i, h)),
            pl.BlockSpec((1, 2 * FWD_PAIRS, 256), lambda i, h: (h, 0, i)),
            hbm,
        ),
        out_shape=(
            jax.ShapeDtypeStruct((768, width), LOW),
            jax.ShapeDtypeStruct((groups, 2 * FWD_PAIRS, 768), WIDE),
            jax.ShapeDtypeStruct((768, width), LOW),
        ),
        scratch_shapes=EXCHANGE_SEMS,
        compiler_params=params(collective_id=3, has_side_effects=True),
        name="attend",
    )(lengths, qkv, qkv, qkv, grad_out)


def attend_back_body(
    len_ref, q_ref, k_ref, v_ref, lse_ref, do_ref, o_ref, y_ref,
    dq_ref, dk_ref, dv_ref, out_ref,
    acc, keep, give, take, send_sem, recv_sem, local_sem, give_sem, take_sem,
):
    group, block = pl.program_id(0), pl.program_id(1)
    exchange = Exchange(by_position(y_ref, out_ref), send_sem, recv_sem, local_sem)
    dp, sq = exchange.dp, exchange.sq

    @pl.when((block == 0) & (group == 0))
    def _():
        group_barrier(dp, sq)
        exchange.start()

    bias = key_bias(len_ref, block == 0)
    d_keys, d_values = [], []
    for pair in range(q_ref.shape[-1] // 128):
        lanes = slice(128 * pair, 128 * (pair + 1))
        queries, keys, values = q_ref[0, :, lanes], k_ref[0, :, lanes], v_ref[0, :, lanes]
        grads = do_ref[:, lanes]
        keys_t = keys.T
        inner = (grads.astype(WIDE) * o_ref[:, lanes].astype(WIDE)).T
        d_query = []
        d_key = d_value = 0.0
        for head, mask in enumerate(head_masks(queries.shape)):
            query = jnp.where(mask, queries, jnp.zeros_like(queries))
            grad = jnp.where(mask, grads, jnp.zeros_like(grads))
            rows = slice(HEAD_DIM * head, HEAD_DIM * (head + 1))
            inner_sum = jnp.sum(inner[rows], axis=0, keepdims=True)
            scores = dot_nt(keys, query) + bias
            probs = jnp.exp(scores - lse_ref[0, 2 * pair + head : 2 * pair + head + 1, :])
            d_probs = dot_nt(values, grad)
            d_scores = (probs * (d_probs - inner_sum)).astype(LOW)
            d_value = d_value + dot_nn(probs.astype(LOW), grad)
            d_key = d_key + dot_nn(d_scores, query)
            d_query.append(dot_nn(keys_t[rows], d_scores))
        d_query = jnp.concatenate(d_query, axis=0) * HEAD_DIM ** (-0.5)
        dq_ref[:, lanes] = d_query.T.astype(LOW)
        d_keys.append((lanes, d_key))
        d_values.append((lanes, d_value))
    pairs = ((0, d_keys), (1, d_values))

    def swap(kind):
        return pltpu.make_async_remote_copy(
            src_ref=give.at[group, kind],
            dst_ref=take.at[group, kind],
            send_sem=give_sem.at[group, kind],
            recv_sem=take_sem.at[group, kind],
            device_id=(dp, sq ^ 1),
            device_id_type=MESH_ID,
        )

    @pl.when(block == 0)
    def _():
        for kind, parts in pairs:
            for lanes, part in parts:
                keep[kind, :, lanes] = part[:256]
                give[group, kind, :, lanes] = part[256:].astype(LOW)
            swap(kind).start()

    @pl.when(block == 1)
    def _():
        for kind, parts in pairs:
            for lanes, part in parts:
                acc[kind, :, lanes] = part

    @pl.when(block == 2)
    def _():
        for (kind, parts), ref in zip(pairs, (dk_ref, dv_ref)):
            swap(kind).wait()
            for lanes, part in parts:
                ref[:512, lanes] = (acc[kind, :, lanes] + part).astype(LOW)
                other = take[group, kind, :, lanes].astype(WIDE)
                ref[512:, lanes] = (keep[kind, :, lanes] + other).astype(LOW)

    @pl.when((block == 2) & (group == pl.num_programs(0) - 1))
    def _():
        exchange.finish()


def attend_back(lengths, qkv, lse, d_out, out, result, sent_dev):
    width = qkv.shape[-1]
    groups = width // 128 // BACK_PAIRS
    lanes = 128 * BACK_PAIRS
    hbm = pl.BlockSpec(memory_space=pl.ANY)
    query = pl.BlockSpec((256, lanes), lambda h, i: ((i + 2) % 3, h))
    keys = pl.BlockSpec((768, lanes), lambda h, i: (0, h))
    flat = jax.ShapeDtypeStruct((768, width), LOW)
    shared = lambda i: jnp.where(i == 0, 1, 0)
    return pl.pallas_call(
        attend_back_body,
        grid=(groups, 3),
        in_specs=[
            pl.BlockSpec(memory_space=pltpu.SMEM),
            pl.BlockSpec((1, 256, lanes), lambda h, i: (0, (i + 2) % 3, h)),
            pl.BlockSpec((1, 512, lanes), lambda h, i: (1, shared(i), h)),
            pl.BlockSpec((1, 512, lanes), lambda h, i: (2, shared(i), h)),
            pl.BlockSpec((1, 2 * BACK_PAIRS, 256), lambda h, i: (h, 0, (i + 2) % 3)),
            query,
            query,
            hbm,
        ],
        out_specs=(query, keys, keys, hbm),
        out_shape=(flat, flat, flat, jax.ShapeDtypeStruct((sent_dev, 128, width), LOW)),
        scratch_shapes=[
            pltpu.VMEM((2, 512, lanes), WIDE),
            pltpu.VMEM((2, 256, lanes), WIDE),
            pltpu.VMEM((groups, 2, 256, lanes), LOW),
            pltpu.VMEM((groups, 2, 256, lanes), LOW),
        ]
        + EXCHANGE_SEMS
        + [pltpu.SemaphoreType.DMA((groups, 2)), pltpu.SemaphoreType.DMA((groups, 2))],
        compiler_params=params(collective_id=4, has_side_effects=True),
        name="attend_back",
    )(lengths, qkv, qkv, qkv, lse.reshape(groups, 2 * BACK_PAIRS, 768), d_out, out, result)


def row_mean(value):
    return jnp.mean(value, axis=-1, keepdims=True)


def col_sum(value):
    return jnp.sum(value, axis=0, keepdims=True)


def middle_body(
    map_ref, len_ref, o_hbm, x_hbm, gy_hbm, w_ref, vec_ref,
    y_hbm, left_hbm, right_hbm, do_hbm, da_hbm, dh_hbm, sums_ref,
    w_buf, o_buf, x_buf, gy_buf, left, right, slope, total, hat_one, rstd_one, low_buf,
    sem, in_sem, out_sem,
):
    count, width = o_buf.shape
    tiles = w_buf.shape[0]
    chunks = FEEDFWD_UNITS // width

    def fetch(t):
        return pltpu.make_async_copy(w_ref.at[tile_at(map_ref, 6 + t)], w_buf.at[t], sem.at[t])

    inputs = [
        pltpu.make_async_copy(src, dst, in_sem.at[i])
        for i, (src, dst) in enumerate(
            (
                (o_hbm, o_buf),
                (x_hbm.at[pl.ds(0, count)], x_buf),
                (gy_hbm, gy_buf),
            )
        )
    ]
    inputs[0].start()
    for t in range(2):
        fetch(t).start()
    inputs[1].start()
    for c in range(chunks):
        for t in (2 + 2 * c, 3 + 2 * c, 10 + 2 * c, 11 + 2 * c):
            fetch(t).start()
    inputs[2].start()
    outputs = []

    def put(src, dst):
        copy = pltpu.make_async_copy(src, dst, out_sem.at[len(outputs)])
        copy.start()
        outputs.append(copy)

    def put_left(t, value):
        for u in range(2):
            left[t + u] = value[:, TILE * u : TILE * (u + 1)]
            put(left.at[t + u], left_hbm.at[t + u])

    def ready(*which):
        for t in which:
            fetch(t).wait()

    def pair(t):
        return w_buf[t : t + 2].reshape(2 * TILE, width)

    def vec(row):
        return vec_ref[row : row + 1, :]

    def fold(value):
        return jnp.sum(value.reshape(-1, 8, width), axis=0)

    def over_rows(body, carried):
        zero = (jnp.zeros((8, width), WIDE),) * carried

        def step(i, carry):
            return body(pl.ds(pl.multiple_of(i * NORM_ROWS, NORM_ROWS), NORM_ROWS), i, carry)

        return lax.fori_loop(0, count // NORM_ROWS, step, zero)

    inputs[0].wait()
    ready(0, 1)
    total[...] = dot_nn(o_buf[...], pair(0))
    inputs[1].wait()

    def norm_one(at, i, carry):
        resid = x_buf[at].astype(WIDE) + (total[at] + vec(2))
        centered = resid - row_mean(resid)
        rstd = lax.rsqrt(row_mean(centered * centered) + NORM_EPS)
        rstd_one[at] = rstd
        hat = centered * rstd
        hat_one[at] = hat
        first = hat * vec(4) + vec(5)
        total[at] = first + vec(3)
        right[0, at] = first.astype(LOW)
        return carry

    over_rows(norm_one, 0)
    put(right.at[0], right_hbm.at[0])

    first_low = right[0]
    for c in range(chunks):
        ready(2 + 2 * c, 3 + 2 * c, 10 + 2 * c, 11 + 2 * c)
        act = dot_nt(first_low, pair(2 + 2 * c)) + vec(8 + c)
        cdf = 0.5 + 0.5 * lax.erf(act * (0.5**0.5))
        pdf = jnp.exp(-0.5 * act * act) * 0.3989422804014327
        slope[c] = cdf + act * pdf
        active = (act * cdf).astype(LOW)
        put_left(8 + 2 * c, active)
        total[...] += dot_nn(active, pair(10 + 2 * c))
    inputs[2].wait()

    def norm_two(at, i, carry):
        d_gain, d_shift, d_bias, pool_full, pool_half = carry
        resid = total[at]
        centered = resid - row_mean(resid)
        rstd = lax.rsqrt(row_mean(centered * centered) + NORM_EPS)
        hat = centered * rstd
        result = hat * vec(6) + vec(7)
        low_buf[0, at] = result.astype(LOW)
        shared = i * NORM_ROWS >= 512
        row = positions((NORM_ROWS, 128), shared, i * NORM_ROWS - jnp.where(shared, 512, 0))
        valid = jnp.where(row < sentence_length(len_ref, shared), 1.0, 0.0)
        pooled = fold(result * jnp.concatenate([valid] * (width // 128), axis=1))
        part = shared.astype(WIDE)
        grad = gy_buf[at].astype(WIDE)
        d_gain = d_gain + fold(grad * hat)
        d_shift = d_shift + fold(grad)
        grad = grad * vec(6)
        d_resid = rstd * (grad - row_mean(grad) - hat * row_mean(grad * hat))
        total[at] = d_resid
        grad_low = d_resid.astype(LOW)
        right[1, at] = grad_low
        return (
            d_gain,
            d_shift,
            d_bias + fold(grad_low.astype(WIDE)),
            pool_full + pooled * (1.0 - part),
            pool_half + pooled * part,
        )

    sums_ref[...] = jnp.zeros_like(sums_ref)
    found = over_rows(norm_two, 5)
    for row, value in zip((4, 5, 1, 10, 11), found):
        sums_ref[row : row + 1, :] = col_sum(value)
    put(low_buf.at[0], y_hbm)
    put(right.at[1], right_hbm.at[1])

    grad_low = right[1]
    for c in range(chunks):
        d_active = dot_nt(grad_low, pair(10 + 2 * c))
        d_act = (d_active * slope[c]).astype(LOW)
        put_left(2 * c, d_act)
        sums_ref[6 + c : 7 + c, :] = col_sum(d_act.astype(WIDE))
        total[...] += dot_nn(d_act, pair(2 + 2 * c))

    def norm_back(at, i, carry):
        d_gain, d_shift, d_bias = carry
        grad = total[at]
        hat = hat_one[at]
        d_gain = d_gain + fold(grad * hat)
        d_shift = d_shift + fold(grad)
        grad = grad * vec(4)
        d_resid = rstd_one[at] * (grad - row_mean(grad) - hat * row_mean(grad * hat))
        total[at] = d_resid
        grad_low = d_resid.astype(LOW)
        low_buf[1, at] = grad_low
        return (d_gain, d_shift, d_bias + fold(grad_low.astype(WIDE)))

    found = over_rows(norm_back, 3)
    for row, value in zip((2, 3, 0), found):
        sums_ref[row : row + 1, :] = col_sum(value)
    put(total, dh_hbm)
    put(low_buf.at[1], da_hbm)
    low_buf[2] = dot_nt(low_buf[1], pair(0)).astype(LOW)
    put(low_buf.at[2], do_hbm)
    for copy in outputs:
        copy.wait()


def middle(owners, lengths, attended, rows, out_grad, weights, vectors):
    count, width = attended.shape
    half = FEEDFWD_UNITS // TILE
    tiles = 2 + 2 * half
    hbm = pl.BlockSpec(memory_space=pl.ANY)
    smem = pl.BlockSpec(memory_space=pltpu.SMEM)
    vmem = pl.BlockSpec(memory_space=pltpu.VMEM)
    flat = jax.ShapeDtypeStruct((count, width), LOW)
    return pl.pallas_call(
        middle_body,
        in_specs=[smem, smem] + [hbm] * 4 + [vmem],
        out_specs=(hbm,) * 6 + (vmem,),
        out_shape=(
            flat,
            jax.ShapeDtypeStruct((2 * half, count, TILE), LOW),
            jax.ShapeDtypeStruct((2, count, width), LOW),
            flat,
            flat,
            jax.ShapeDtypeStruct((count, width), WIDE),
            jax.ShapeDtypeStruct((16, width), WIDE),
        ),
        scratch_shapes=[
            pltpu.VMEM((tiles, TILE, width), LOW),
            pltpu.VMEM((count, width), LOW),
            pltpu.VMEM((count, width), LOW),
            pltpu.VMEM((count, width), LOW),
            pltpu.VMEM((2 * half, count, TILE), LOW),
            pltpu.VMEM((2, count, width), LOW),
            pltpu.VMEM((half // 2, count, width), WIDE),
            pltpu.VMEM((count, width), WIDE),
            pltpu.VMEM((count, width), WIDE),
            pltpu.VMEM((count, 1), WIDE),
            pltpu.VMEM((3, count, width), LOW),
            pltpu.SemaphoreType.DMA((tiles,)),
            pltpu.SemaphoreType.DMA((3,)),
            pltpu.SemaphoreType.DMA((2 * half + 6,)),
        ],
        compiler_params=params(),
        name="feed_forward",
    )(owners, lengths, attended, rows, out_grad, weights, vectors)


def grad_ff_body(map_ref, left_ref, right_ref, out_ref):
    out_ref[0] = dot_tn(left_ref[0], right_ref[0]).astype(LOW)


def grad_ff(owners, left, right):
    per = FEEDFWD_UNITS // TILE
    count, width = right.shape[1:]
    return pl.pallas_call(
        grad_ff_body,
        grid_spec=pltpu.PrefetchScalarGridSpec(
            num_scalar_prefetch=1,
            grid=(2 * per,),
            in_specs=[
                pl.BlockSpec((1, count, TILE), lambda i, m: (i, 0, 0)),
                pl.BlockSpec((1, count, width), lambda i, m: (i // per, 0, 0)),
            ],
            out_specs=pl.BlockSpec((1, TILE, width), lambda i, m: (tile_at(m, 8 + i), 0, 0)),
        ),
        out_shape=jax.ShapeDtypeStruct((8 + 2 * per, TILE, width), LOW),
        compiler_params=params(),
        name="grad_ff",
    )(owners, left, right)


def grad_attn_body(
    map_ref, x_ref, dq_ref, dk_ref, dv_ref, o_ref, da_ref, into_ref, out_ref, sums_ref
):
    step = pl.program_id(0)
    for part, grad_ref in enumerate((dq_ref, dk_ref, dv_ref)):

        @pl.when(step // 2 == part)
        def _(grad_ref=grad_ref):
            out_ref[0] = dot_tn(x_ref[...], grad_ref[...]).astype(LOW)

    @pl.when(step // 2 == 3)
    def _():
        out_ref[0] = dot_tn(o_ref[...], da_ref[...]).astype(LOW)

    @pl.when(step == 0)
    def _():
        sums_ref[...] = jnp.zeros_like(sums_ref)
        sums_ref[0:1, :] = col_sum(dq_ref[...].astype(WIDE))
        sums_ref[1:2, :] = col_sum(dv_ref[...].astype(WIDE))


def grad_attn(owners, rows, dq, dk, dv, attended, da, into):
    count, width = dq.shape
    whole = pl.BlockSpec((count, width), lambda i, m: (0, 0))
    return pl.pallas_call(
        grad_attn_body,
        grid_spec=pltpu.PrefetchScalarGridSpec(
            num_scalar_prefetch=1,
            grid=(8,),
            in_specs=[
                pl.BlockSpec((count, TILE), lambda i, m: (0, i % 2)),
                whole,
                whole,
                whole,
                pl.BlockSpec((768, TILE), lambda i, m: (0, i % 2)),
                pl.BlockSpec((768, width), lambda i, m: (0, 0)),
                pl.BlockSpec(memory_space=pl.ANY),
            ],
            out_specs=(
                pl.BlockSpec((1, TILE, width), lambda i, m: (tile_at(m, i), 0, 0)),
                pl.BlockSpec((8, width), lambda i, m: (0, 0)),
            ),
        ),
        out_shape=(
            jax.ShapeDtypeStruct(into.shape, LOW),
            jax.ShapeDtypeStruct((8, width), WIDE),
        ),
        input_output_aliases={7: 0},
        compiler_params=params(),
        name="grad_attn",
    )(owners, rows, dq, dk, dv, attended, da, into)


def grad_in_body(map_ref, dq_ref, dk_ref, dv_ref, dh_ref, *refs):
    w_refs, out_ref = refs[:6], refs[6]
    for half in range(2):
        cols = slice(TILE * half, TILE * (half + 1))
        value = dh_ref[:, cols]
        for part, grad_ref in enumerate((dq_ref, dk_ref, dv_ref)):
            value = value + dot_nt(grad_ref[...], w_refs[2 * part + half][0])
        out_ref[:, cols] = value.astype(LOW)


def grad_in(owners, dq, dk, dv, dh, weights):
    count, width = dq.shape
    block = pl.BlockSpec((256, width), lambda i, m: (i, 0))
    return pl.pallas_call(
        grad_in_body,
        grid_spec=pltpu.PrefetchScalarGridSpec(
            num_scalar_prefetch=1,
            grid=(count // 256,),
            in_specs=[block] * 4
            + [
                pl.BlockSpec((1, TILE, width), lambda i, m, t=t: (tile_at(m, t), 0, 0)) for t in range(6)
            ],
            out_specs=block,
        ),
        out_shape=jax.ShapeDtypeStruct((count, width), LOW),
        compiler_params=params(),
        name="grad_in",
    )(owners, dq, dk, dv, dh, *([weights] * 6))


REDUCE_ORDER = (
    ("fp", 3, 2), ("lp", 0, 0), ("in",), ("fp", 2, 1), ("fc", 3, 2), ("lc", 0, 0), ("lp", 0, 1),
    ("lp", 2, 1), ("fc", 2, 1), ("fp", 0, 1), ("fp", 2, 2), ("lp", 1, 1), ("lc", 0, 1),
    ("fp", 1, 1), ("lc", 1, 1), ("lm", 0, 0), ("lp", 2, 0), ("fc", 2, 2), ("fp", 3, 1),
    ("fc", 0, 1), ("fc", 1, 1), ("fp", 0, 2), ("np", 1, 1), ("np", 1, 2), ("np", 3, 1),
    ("lm", 0, 1), ("fc", 0, 2), ("fc", 3, 1), ("nc", 1, 1), ("fp", 1, 2), ("nc", 3, 1),
    ("np", 2, 1), ("lc", 2, 1), ("vs", 0), ("lp", 1, 0), ("fc", 1, 2), ("lm", 2, 1), ("lp", 3, 0),
    ("nc", 1, 2), ("lp", 3, 1), ("np", 0, 2), ("nc", 2, 1), ("lm", 1, 1), ("np", 0, 1),
    ("np", 3, 2), ("np", 2, 2), ("va", 0), ("vs", 1), ("lc", 1, 0), ("nc", 0, 1), ("nc", 0, 2),
    ("turn", 2, 1), ("lm", 1, 0), ("nc", 3, 2), ("nc", 2, 2), ("lc", 2, 0), ("lc", 3, 0),
    ("turn", 1, 1), ("lc", 3, 1), ("turn", 3, 2), ("turn", 0, 1), ("turn", 1, 2), ("le", 1),
    ("turn", 0, 2), ("lm", 2, 0), ("on", 0, 1), ("le", 0), ("lo",), ("turn", 3, 1), ("turn", 2, 2),
    ("on", 0, 2), ("on", 1, 1), ("va", 1), ("vs", 2), ("on", 2, 1), ("on", 1, 2), ("turn", 3, 0),
    ("va", 2), ("vs", 3), ("end", 1), ("on", 2, 2), ("va", 3), ("vs", 4), ("end", 0), ("end", 2),
    ("va", 4),
)


def reduce_body(
    own_of_ref, x_ref, o_ref, left_ref, dq_ref, dk_ref, dv_ref, da_ref, right_ref,
    sums_ref, g_ref, own_ref, vt_ref, sq_ref, gi_ref,
    lbuf, rbuf, pbuf, core_in, x_in, y_in, y_pair, z_in, zf_in, ebuf, tbuf, tlow,
    vbuf, v_in, s_own, s_seq, s_dp,
    send_sem, local_sem, core_sem, x_sem, y_sem, ypair_sem, z_sem, zf_sem, v_sem, out_sem,
    seq_sem, dp_sem, in_sem,
):
    dp, sq = lax.axis_index("dp"), lax.axis_index("seq")
    z, x = dp // 2, dp % 2
    y, c = sq // 2, sq % 2
    dev_c, dev_y, dev_yc, dev_x = (dp, sq ^ 1), (dp, sq ^ 2), (dp, sq ^ 3), (dp ^ 1, sq)
    has_up, has_down, inner = z < 3, z > 0, (z > 0) & (z < 3)
    order = (
        jnp.where(z < 2, 3, 0),
        jnp.where(z == 0, 2, jnp.where(z == 1, 0, jnp.where(z == 2, 3, 1))),
        jnp.where(z == 0, 1, jnp.where(z == 1, 2, jnp.where(z == 2, 1, 2))),
        z,
    )

    used = [0, 0]
    remotes, own_moves = [], []

    def move(src, dst):
        copy = pltpu.make_async_copy(src, dst, local_sem.at[used[1]])
        used[1] += 1
        copy.start()
        return copy

    loads = [move(left_ref, lbuf.at[pl.ds(4, 16)]), move(right_ref, rbuf.at[pl.ds(4, 2)])]
    for index, ref in enumerate((dq_ref, dk_ref, dv_ref, da_ref)):
        loads.append(move(ref, rbuf.at[index]))
    for half in range(2):
        cols = pl.ds(TILE * half, TILE)
        loads.append(move(x_ref.at[pl.ds(0, 768), cols], lbuf.at[half]))
        loads.append(move(o_ref.at[:, cols], lbuf.at[2 + half]))

    barrier = pltpu.get_barrier_semaphore()
    for step in range(1, 4):
        pl.semaphore_signal(
            barrier, inc=1, device_id=(dp, sq ^ step), device_id_type=MESH_ID
        )
    for step in range(1, 8):
        pl.semaphore_signal(
            barrier, inc=1, device_id=(dp ^ step, sq), device_id_type=MESH_ID
        )
    pl.semaphore_wait(barrier, 10)

    def send(src, dst, recv, device, pred=None):
        copy = pltpu.make_async_remote_copy(
            src_ref=src,
            dst_ref=dst,
            send_sem=send_sem.at[used[0]],
            recv_sem=recv,
            device_id=device,
            device_id_type=MESH_ID,
        )
        used[0] += 1
        if pred is None:
            copy.start()
        else:
            pl.when(pred)(lambda: copy.start())
        remotes.append((copy, pred))

    def arrived(at, sem):
        pltpu.make_async_copy(at, at, sem).wait()

    def wide(ref, *at):
        return ref[at].astype(WIDE)

    partners = (dev_c, dev_y, dev_x, (dp ^ 2, sq), (dp ^ 4, sq))

    def vec_send(step):
        send(vbuf.at[step], v_in.at[step], v_sem.at[step], partners[step])

    def vec_add(step):
        arrived(v_in.at[step], v_sem.at[step])
        vbuf[step + 1] = vbuf[step] + v_in[step]

    def in_full(j):
        return g_ref.at[pl.ds(128 * j, 128)], gi_ref.at[3 * y + 2 * c]

    def in_half(j):
        return g_ref.at[pl.ds(512 + 64 * j, 64)], gi_ref.at[3 * y + 1, pl.ds(64 * c, 64)]

    def input_send():
        for device in (dev_y, dev_yc, dev_c):
            for kind, pair in enumerate((in_full(device[1]), in_half(device[1]))):
                send(pair[0], pair[1], in_sem.at[sq, kind], device)
        own_moves.append(move(*in_full(sq)))
        own_moves.append(move(*in_half(sq)))

    for copy in loads:
        copy.wait()

    def standard_of(slot):
        found = jnp.int32(0)
        for block in range(8):
            found = jnp.maximum(found, jnp.where(own_of_ref[block] == slot, block, 0))
        return found

    def partial(slot, t):
        tile = 3 * standard_of(slot) + t
        left = jnp.where(tile < 6, tile % 2, tile - 4)
        right = jnp.where(tile < 8, tile // 2, 4 + (tile - 8) // 8)
        value = dot_tn(lbuf[left], rbuf[right]).astype(LOW)
        for quarter in range(4):
            rows = slice(96 * quarter, 96 * (quarter + 1))
            pbuf[quarter % 2, t, slot, quarter // 2] = value[rows]
        send(pbuf.at[1 - c, t, slot], core_in.at[t, slot], core_sem.at[t, slot], dev_c)

    def combine(slot, t):
        arrived(core_in.at[t, slot], core_sem.at[t, slot])
        pbuf[c, t, slot] = (wide(pbuf, c, t, slot) + wide(core_in, t, slot)).astype(LOW)

    def cbuf(*at):
        return pbuf.at[(c, *at)]

    def line_send(k, sub, pred):
        d = order[k]
        up = d > z
        step = jnp.where(up, 1, -1)
        index = jnp.where(z + step == d, jnp.where(up, 4, 5), d)
        send(
            cbuf(0, 2 * d + sub), zf_in.at[index, sub], zf_sem.at[index, sub],
            (dp + 2 * step, sq), pred,
        )

    def line_partial(k, sub):
        partial(2 * order[k] + sub, 0)

    def line_combine(k, sub):
        combine(2 * order[k] + sub, 0)
        if k < 3:
            line_send(k, sub, jnp.logical_not(inner))

    def line_add(slot, index, sub):
        arrived(zf_in.at[index, sub], zf_sem.at[index, sub])
        pbuf[c, 0, slot] = (wide(pbuf, c, 0, slot) + wide(zf_in, index, sub)).astype(LOW)

    def line_middle(k, sub):
        d = order[k]
        pl.when(inner)(lambda: line_add(2 * d + sub, d, sub))
        line_send(k, sub, inner)

    def line_end(sub):
        pl.when(has_down)(lambda: line_add(2 * z + sub, 4, sub))
        pl.when(has_up)(lambda: line_add(2 * z + sub, 5, sub))

    def line_out():
        send(cbuf(0, 2 * z + 1 - x), x_in.at[z, 0], x_sem.at[z, 0], dev_x)

    def far_partial(k, t):
        partial(2 * order[k] + 1 - x, t)

    def near_partial(k, t):
        partial(2 * order[k] + x, t)

    def far_combine(k, t):
        d = order[k]
        slot = 2 * d + 1 - x
        combine(slot, t)
        if k == 1:
            send(cbuf(t, slot, 1 - y), y_pair.at[t, 1], ypair_sem.at[t, 1], dev_y)
        else:
            send(cbuf(t, slot), x_in.at[d, t], x_sem.at[d, t], dev_x)

    def near_combine(k, t):
        slot = 2 * order[k] + x
        combine(slot, t)
        if k == 1:
            send(cbuf(t, slot, 1 - y), y_pair.at[t, 0], ypair_sem.at[t, 0], dev_y)

    def turn(k, t):
        d = order[k]
        near, far = 2 * d + x, 2 * d + 1 - x
        if k == 1:
            for half in range(2):
                arrived(y_pair.at[t, half], ypair_sem.at[t, half])
            pbuf[c, t, far, y] = (
                wide(pbuf, c, t, far, y) + wide(y_pair, t, 1)
            ).astype(LOW)
            send(cbuf(t, far, y), x_in.at[d, t, 0], x_sem.at[d, t], dev_x)
        else:
            arrived(x_in.at[d, t], x_sem.at[d, t])
            pbuf[c, t, near] = (wide(pbuf, c, t, near) + wide(x_in, d, t)).astype(LOW)
            send(cbuf(t, near, 1 - y), y_in.at[d, t], y_sem.at[d, t], dev_y)

    def plane_sum(k, t):
        d = order[k]
        near = 2 * d + x
        mine = wide(pbuf, c, t, near, y)
        if k == 1:
            arrived(x_in.at[d, t, 0], x_sem.at[d, t])
            return mine + wide(y_pair, t, 0) + wide(x_in, d, t, 0)
        arrived(y_in.at[d, t], y_sem.at[d, t])
        return mine + wide(y_in, d, t)

    def onward(k, t):
        d = order[k]
        tbuf[...] = plane_sum(k, t)

        @pl.when(inner)
        def _():
            arrived(z_in.at[d, t], z_sem.at[d, t])
            tbuf[...] += wide(z_in, d, t)

        ebuf[k, t] = tbuf[...].astype(LOW)
        up = d > z
        step = jnp.where(up, 1, -1)
        index = jnp.where(z + step == d, jnp.where(up, 4, 5), d)
        send(ebuf.at[k, t], z_in.at[index, t], z_sem.at[index, t], (dp + 2 * step, sq))

    squares = []

    def finish(t):
        tbuf[...] = plane_sum(3, t)
        if t > 0:
            for index, there in ((4, has_down), (5, has_up)):

                @pl.when(there)
                def _(index=index):
                    arrived(z_in.at[index, t], z_sem.at[index, t])
                    tbuf[...] += wide(z_in, index, t)

        total = tbuf[...].astype(LOW)
        tlow[t] = total
        wide_total = total.astype(WIDE)
        rows = (wide_total * wide_total).reshape(-1, 8, wide_total.shape[-1])
        squares.append(jnp.sum(rows, axis=0))
        at = own_ref.at[t, sq]
        for device in (dev_y, dev_c):
            send(tlow.at[t], at, out_sem.at[t, sq], device)
        own_moves.append(move(tlow.at[t], at))

    vbuf[0] = jnp.zeros(vbuf.shape[1:], WIDE)
    vbuf[0, 0:1] = col_sum(wide(rbuf, 0))
    vbuf[0, 1:2] = col_sum(wide(rbuf, 2))
    vbuf[0, 2:12] = sums_ref[0:10]
    vbuf[0, pl.ds(16 + 3 * y + 2 * c, 1)] = sums_ref[10:11]
    vbuf[0, pl.ds(16 + 3 * y + 1, 1)] = sums_ref[11:12]
    steps = {
        "lp": line_partial,
        "lc": line_combine,
        "lm": line_middle,
        "le": line_end,
        "lo": line_out,
        "fp": far_partial,
        "np": near_partial,
        "fc": far_combine,
        "nc": near_combine,
        "turn": turn,
        "on": onward,
        "end": finish,
        "vs": vec_send,
        "va": vec_add,
        "in": input_send,
    }
    for name, *at in REDUCE_ORDER:
        steps[name](*at)

    squares = squares[0] + squares[1] + squares[2]
    folded = squares[:, :128]
    for lane in range(1, squares.shape[-1] // 128):
        folded = folded + squares[:, 128 * lane : 128 * (lane + 1)]
    s_own[...] = folded
    for step in range(1, 4):
        send(s_own, s_seq.at[sq], seq_sem.at[sq], (dp, sq ^ step))
    s_seq[sq] = folded
    for t in (1, 0, 2):
        arrived(own_ref.at[t, sq ^ 2], out_sem.at[t, sq ^ 2])
        send(own_ref.at[t, sq ^ 2], own_ref.at[t, sq ^ 2], out_sem.at[t, sq ^ 2], dev_c)
    for step in range(1, 4):
        arrived(s_seq.at[sq ^ step], seq_sem.at[sq ^ step])
    group = s_seq[0] + s_seq[1] + s_seq[2] + s_seq[3]
    s_dp[dp] = group
    for step in range(1, 8):
        send(s_dp.at[dp], s_dp.at[dp], dp_sem.at[dp], (dp ^ step, sq))
    for step in range(1, 8):
        arrived(s_dp.at[dp ^ step], dp_sem.at[dp ^ step])
    everyone = s_dp[0]
    for index in range(1, 8):
        everyone = everyone + s_dp[index]
    sq_ref[...] = everyone
    vt_ref[0:16] = vbuf[5][0:16]
    vt_ref[16:24] = vbuf[2][16:24]

    for t in range(3):
        arrived(own_ref.at[t, sq ^ 1], out_sem.at[t, sq ^ 1])
        arrived(own_ref.at[t, sq ^ 3], out_sem.at[t, sq ^ 3])
    for step in range(1, 4):
        other = sq ^ step
        there, member = other // 2, other % 2
        arrived(gi_ref.at[3 * there + 2 * member], in_sem.at[other, 0])
        arrived(gi_ref.at[3 * there + 1, pl.ds(64 * member, 64)], in_sem.at[other, 1])
    for copy in own_moves:
        copy.wait()
    for copy, pred in remotes:
        if pred is None:
            copy.wait_send()
        else:
            pl.when(pred)(lambda copy=copy: copy.wait_send())


def reduce_all(owners, rows, out, left, grads, right, sums, grad_rows, sent_dev):
    width = rows.shape[-1]
    part = TILE // 4
    hbm = pl.BlockSpec(memory_space=pl.ANY)
    vmem = pl.BlockSpec(memory_space=pltpu.VMEM)
    smem = pl.BlockSpec(memory_space=pltpu.SMEM)
    dma = pltpu.SemaphoreType.DMA
    owned, totals, squares, input_grad = pl.pallas_call(
        reduce_body,
        out_shape=(
            jax.ShapeDtypeStruct((3, 4, part, width), LOW),
            jax.ShapeDtypeStruct((24, width), WIDE),
            jax.ShapeDtypeStruct((8, 128), WIDE),
            jax.ShapeDtypeStruct((sent_dev, 128, width), LOW),
        ),
        in_specs=[smem] + [hbm] * 8 + [vmem, hbm],
        out_specs=(hbm, vmem, vmem, hbm),
        scratch_shapes=[
            pltpu.VMEM((20, 768, TILE), LOW),
            pltpu.VMEM((6, 768, width), LOW),
            pltpu.VMEM((2, 3, 8, 2, part, width), LOW),
            pltpu.VMEM((3, 8, 2, part, width), LOW),
            pltpu.VMEM((4, 3, 2, part, width), LOW),
            pltpu.VMEM((4, 3, part, width), LOW),
            pltpu.VMEM((3, 2, part, width), LOW),
            pltpu.VMEM((6, 3, part, width), LOW),
            pltpu.VMEM((6, 2, 2, part, width), LOW),
            pltpu.VMEM((3, 3, part, width), LOW),
            pltpu.VMEM((part, width), WIDE),
            pltpu.VMEM((3, part, width), LOW),
            pltpu.VMEM((6, 24, width), WIDE),
            pltpu.VMEM((5, 24, width), WIDE),
            pltpu.VMEM((8, 128), WIDE),
            pltpu.VMEM((4, 8, 128), WIDE),
            pltpu.VMEM((8, 8, 128), WIDE),
            dma((96,)),
            dma((32,)),
            dma((3, 8)),
            dma((4, 3)),
            dma((4, 3)),
            dma((3, 2)),
            dma((6, 3)),
            dma((6, 2)),
            dma((5,)),
            dma((3, 4)),
            dma((4,)),
            dma((8,)),
            dma((4, 2)),
        ],
        compiler_params=params(collective_id=2, has_side_effects=True),
        name="reduce_gradients",
    )(owners, rows, out, left, *grads, right, sums, grad_rows)
    return owned.reshape(3 * TILE, width), totals, squares, input_grad


def optimizer_body(
    len_ref, mem_ref, g_ref, sq_ref, tot_ref, w_ref, one_ref, two_ref, vw_ref, vone_ref, vtwo_ref,
    norm_ref, emb_ref, *rest,
):
    outs, clip_ref = rest[:-1], rest[-1]
    count = vw_ref.shape[0]

    @pl.when(pl.program_id(0) == 0)
    def _():
        gradient = tot_ref[:count]
        total = jnp.sum(sq_ref[...], keepdims=True) + jnp.sum(gradient * gradient, keepdims=True)
        norm = jnp.sqrt(total)
        norm_ref[...] = norm
        clip_ref[...] = jnp.broadcast_to(MAX_NORM / jnp.maximum(norm, MAX_NORM), clip_ref.shape)

    clip = clip_ref[...]

    def update(refs, outs, gradient, rate, decay):
        new = adam_step(refs[2][...], refs[0][...], refs[1][...], gradient, rate, decay)
        for ref, value in zip(outs, new + (new[2].astype(LOW),)):
            ref[...] = value

    update(
        (one_ref, two_ref, w_ref), outs[:4], g_ref[...].astype(WIDE) * clip,
        RATE_MATRIX, WEIGHT_DECAY,
    )

    @pl.when(pl.program_id(0) == 0)
    def _():
        update((vone_ref, vtwo_ref, vw_ref), outs[4:], tot_ref[:count] * clip, RATE_VECTOR, 0.0)
        groups, most = mem_ref.shape
        sentences = len_ref.shape[0]
        first = lax.axis_index("dp") * sentences
        pooled = [
            tot_ref[16 + s : 17 + s] / len_ref[s].astype(WIDE) for s in range(sentences)
        ]
        for g in range(groups):
            listed = jnp.int32(0)
            total = jnp.zeros_like(pooled[0])
            for m in range(most):
                listed += jnp.where(mem_ref[g, m] >= 0, 1, 0)
            for s in range(sentences):
                times = jnp.int32(0)
                for m in range(most):
                    times += jnp.where(mem_ref[g, m] == first + s, 1, 0)
                total = total + pooled[s] * times.astype(WIDE)
            emb_ref[g : g + 1] = total / listed.astype(WIDE)


def optimizer(lengths, members, owned, squares, totals, matrices, vectors):
    block_rows, width = owned.shape
    steps = 4 if block_rows % 64 == 0 else 3
    smem = pl.BlockSpec(memory_space=pltpu.SMEM)
    mat = pl.BlockSpec((block_rows // steps, width), lambda i: (i, 0))

    def whole(shape):
        return pl.BlockSpec(shape, lambda i: (0, 0))

    vec = whole(vectors[0].shape)
    embeddings = (members.shape[0], width)
    return pl.pallas_call(
        optimizer_body,
        grid=(steps,),
        in_specs=[smem, smem, mat, whole(squares.shape), whole(totals.shape)]
        + [mat] * 3
        + [vec] * 3,
        out_specs=(whole((1, 1)), whole(embeddings)) + (mat,) * 4 + (vec,) * 4,
        out_shape=(
            jax.ShapeDtypeStruct((1, 1), WIDE),
            jax.ShapeDtypeStruct(embeddings, WIDE),
        )
        + tuple(
            jax.ShapeDtypeStruct(like.shape, dtype)
            for like in (owned, vectors[0])
            for dtype in (WIDE, WIDE, WIDE, LOW)
        ),
        scratch_shapes=[pltpu.VMEM((1, width), WIDE)],
        compiler_params=params(),
        name="optimizer",
    )(lengths, members, owned, squares, totals, *matrices, *vectors)


def to_positions(value):
    width = value.shape[1]
    moved = jnp.concatenate(
        [value[:512].reshape(4, 128, width), value[512:].reshape(4, 64, width)], axis=1
    )
    moved = lax.all_to_all(moved, "seq", split_axis=0, concat_axis=0, tiled=True)
    rows = []
    for y in range(2):
        rows.append(moved[2 * y, :128])
        rows.append(jnp.concatenate([moved[2 * y, 128:], moved[2 * y + 1, 128:]], axis=0))
        rows.append(moved[2 * y + 1, :128])
    return jnp.stack(rows)


def to_rows(tokens):
    width = tokens.shape[-1]
    core = lax.axis_index("seq") % 2
    pieces = []
    for j in range(4):
        y, c = j // 2, j % 2
        pieces += [tokens[3 * y + 2 * c], tokens[3 * y + 1]]
    moved = jnp.concatenate(pieces, axis=0).reshape(4, 256, width)
    moved = lax.all_to_all(moved, "seq", split_axis=0, concat_axis=0, tiled=True)
    shared = moved[:, 128:].reshape(4, 2, 64, width)
    own = lax.dynamic_index_in_dim(shared, core, 1, keepdims=False)
    other = lax.dynamic_index_in_dim(shared, 1 - core, 1, keepdims=False)
    return jnp.concatenate(
        [moved[:, :128].reshape(512, width), own.reshape(256, width), other.reshape(256, width)],
        axis=0,
    )


def local(
    tokens,
    grad_out,
    lengths,
    members,
    owners,
    mat_master,
    mat_moment1,
    mat_moment2,
    vec_master,
    vec_moment1,
    vec_moment2,
):
    sent_dev, local_len, model_width = tokens.shape
    dp_count = lax.axis_size("dp")
    block_rows = mat_master.shape[0]
    direct = dp_count == 8 and block_rows == 3 * TILE

    if direct:
        blocks = owners
        weights, rows, qkv, attended, out_grad, lse = front(
            owners, lengths, mat_master, tokens, grad_out, vec_master
        )
    else:
        gathered = lax.all_gather(mat_master.astype(LOW), "dp", axis=0, tiled=True)
        weights = gathered.reshape(dp_count, block_rows, model_width)[owners]
        weights = weights.reshape(-1, TILE, model_width)
        rows = to_rows(tokens)
        blocks = jnp.arange(weights.shape[0] // 3, dtype=jnp.int32)
        qkv = qkv_project(blocks, rows, weights, vec_master)
        attended, lse, out_grad = attend(lengths, qkv, grad_out)
    result, left, right, d_attended, d_branch, d_resid, sums = middle(
        blocks, lengths, attended, rows, out_grad, weights, vec_master
    )
    dq, dk, dv, output = attend_back(
        lengths, qkv, lse, d_attended, attended, result, sent_dev
    )
    grad_rows = grad_in(blocks, dq, dk, dv, d_resid, weights)

    if direct:
        owned, totals, squares, input_grad = reduce_all(
            owners, rows, attended, left, (dq, dk, dv, d_branch), right, sums, grad_rows, sent_dev
        )
    else:
        grads = grad_ff(blocks, left, right)
        grads, sums_qv = grad_attn(blocks, rows, dq, dk, dv, attended, d_branch, grads)
        input_grad = to_positions(grad_rows)
        inverse = jnp.argsort(owners)
        grads = grads.reshape(dp_count, block_rows, model_width)[inverse]
        grads = grads.reshape(dp_count * block_rows, model_width)
        quarter = lax.psum_scatter(grads, ("dp", "seq"), scatter_dimension=0, tiled=True)
        owned = lax.all_gather(quarter, "seq", axis=0, tiled=True)
        quarter = quarter.astype(WIDE)
        group = lax.axis_index("seq") // 2
        core = lax.axis_index("seq") % 2
        place = jnp.arange(8)[:, None]
        pooled = jnp.where(place == 3 * group + 2 * core, sums[10:11], 0.0) + jnp.where(
            place == 3 * group + 1, sums[11:12], 0.0
        )
        pooled = lax.psum(pooled, "seq")
        local_vec = jnp.concatenate([sums_qv[0:2], sums[0:14]], axis=0)
        squares, vec_total = lax.psum(
            (jnp.sum(quarter * quarter), local_vec), ("dp", "seq")
        )
        squares = jnp.full((8, 128), squares / 1024.0)
        totals = jnp.concatenate([vec_total, pooled], axis=0)

    norm, embeddings, *new = optimizer(
        lengths,
        members,
        owned,
        squares,
        totals,
        (mat_master, mat_moment1, mat_moment2),
        (vec_master, vec_moment1, vec_moment2),
    )
    return (output, input_grad, embeddings, norm.reshape(()), *new)


def solution(mesh):
    placed = (
        P("dp", "seq", None),
        P("dp", "seq", None),
        P("dp"),
        P("dp", None),
        P(),
        P("dp", None),
        P("dp", None),
        P("dp", None),
        P(),
        P(),
        P(),
    )
    return jax.shard_map(
        local,
        mesh=mesh,
        in_specs=placed,
        out_specs=(
            P("dp", "seq", None),
            P("dp", "seq", None),
            P("dp", None),
            P(),
            P("dp", None),
            P("dp", None),
            P("dp", None),
            P("dp", None),
            P(),
            P(),
            P(),
            P(),
        ),
        check_vma=False,
    )
```

```python
import functools

import jax
import jax.numpy as jnp
from jax import lax
from jax.experimental import pallas as pl
from jax.experimental.pallas import tpu as pltpu
from jax.sharding import PartitionSpec as P

HEADS = 12
HEAD_DIM = 64
FEEDFWD_UNITS = 3072
STEP = 10


NORM_EPS = 1e-06
MASK_FILL = -1e30
MAX_NORM = 1.0
ADAM_ONE = 0.9
ADAM_TWO = 0.999
ADAM_EPS = 1e-08
WEIGHT_DECAY = 0.01
RATE_MATRIX = 0.04
RATE_VECTOR = 0.5

FWD_PAIRS = 6
BACK_PAIRS = 6
NORM_ROWS = 128
TILE = 384
VMEM_LIMIT = 60 * 1024 * 1024
MESH_ID = pl.DeviceIdType.MESH
LOW = jnp.bfloat16
WIDE = jnp.float32


def adam_step(master, moment_one, moment_two, gradient, learn_rate, decay_rate):
    moment_one = ADAM_ONE * moment_one + (1.0 - ADAM_ONE) * gradient
    moment_two = ADAM_TWO * moment_two + (1.0 - ADAM_TWO) * gradient * gradient
    scaled_one = moment_one / (1.0 - ADAM_ONE**STEP)
    scaled_two = moment_two / (1.0 - ADAM_TWO**STEP)
    master = master - learn_rate * (
        scaled_one / (jnp.sqrt(scaled_two) + ADAM_EPS) + decay_rate * master
    )
    return (moment_one, moment_two, master)


def dot_nn(left, right):
    return jnp.dot(left, right, preferred_element_type=WIDE)


def dot_nt(left, right):
    return lax.dot_general(
        left, right, (((1,), (1,)), ((), ())), preferred_element_type=WIDE
    )


def dot_tn(left, right):
    return lax.dot_general(
        left, right, (((0,), (0,)), ((), ())), preferred_element_type=WIDE
    )


def tile_at(owners, tile):
    return 3 * owners[tile // 3] + tile % 3


def params(**kwargs):
    return pltpu.CompilerParams(vmem_limit_bytes=VMEM_LIMIT, **kwargs)


GATHER_HEAD = 10
GATHER_ORDER = (
    ("tk",), ("xb", 1), ("xs", 0), ("zs", 0), ("zs", 2), ("xb", 0), ("r", 1, 0), ("r", 0, 0),
    ("xs", 1), ("r", 1, 2), ("zs", 1), ("xr", 1, 0), ("r", 0, 2), ("xb", 2), ("r", 1, 1),
    ("r", 2, 0), ("r", 2, 2), ("r", 0, 1), ("xs", 2), ("xob", 2), ("r", 2, 1), ("zx", 0),
    ("xo", 0), ("zx", 1), ("yr", 1, 2), ("xr", 1, 1), ("tf",), ("zx", 2), ("xr", 2, 0), ("xo", 2),
    ("yr", 2, 1), ("e1", 0), ("xob", 1), ("xr", 2, 2), ("yx", 1, 1), ("xo", 1), ("xr", 1, 2),
    ("xr", 2, 1), ("e1", 1), ("xsr", 0), ("yx", 1, 0), ("e1", 2), ("yx", 1, 2), ("yx", 2, 2),
    ("yr", 2, 0), ("yr", 1, 0), ("e2", 2), ("yr", 1, 1), ("xsr", 1), ("xob", 0), ("e2", 1),
    ("yx", 2, 0), ("xsr", 2), ("yr", 2, 2), ("e2", 0), ("yx", 2, 1),
)


def front_body(
    own_of_ref, len_ref, w_ref, x_ref, g_ref, vec_ref,
    weights_ref, rows_ref, qkv_ref, mats_ref, o_ref, gy_ref, lse_ref,
    wide_buf, own_buf, out_ref, xo_ref, qkv_buf, mats_buf, o_buf,
    send_sem, recv_sem, tok_recv, local_sem, ex_send, ex_recv, ex_local,
):
    dp, sq = lax.axis_index("dp"), lax.axis_index("seq")
    z, x = dp // 2, dp % 2
    y, c = sq // 2, sq % 2
    q, qc, qy, qyc = sq, sq ^ 1, sq ^ 2, sq ^ 3
    dev_c, dev_y, dev_yc, dev_x = (dp, sq ^ 1), (dp, sq ^ 2), (dp, sq ^ 3), (dp ^ 1, sq)
    dev_near = (dp ^ 2, sq)
    has_up, has_down, inner = z < 3, z > 0, (z > 0) & (z < 3)
    dev_up = (jnp.minimum(dp + 2, dp % 2 + 6), sq)
    dev_down = (jnp.maximum(dp - 2, dp % 2), sq)
    sources = (z ^ 1, jnp.where(z < 2, 2, 1), jnp.where(z < 2, 3, 0))
    used = [0, 0]
    started, locals_ = [], []

    def move(src, dst):
        copy = pltpu.make_async_copy(src, dst, local_sem.at[used[1]])
        used[1] += 1
        copy.start()
        return copy

    loads = []
    for at in (q, qy, qc, qyc):
        thirds = pl.ds(3 * at, 3)
        loads.append(move(w_ref.at[thirds], wide_buf.at[thirds]))

    barrier = pltpu.get_barrier_semaphore()

    def greet(device):
        pl.semaphore_signal(barrier, inc=1, device_id=device, device_id_type=MESH_ID)

    for device in (dev_c, dev_y, dev_yc, dev_x):
        greet(device)
    pl.when(has_up)(lambda: greet(dev_up))
    pl.when(has_down)(lambda: greet(dev_down))
    pl.semaphore_wait(barrier, 4 + jnp.where(inner, 2, 1))

    def send(src, dst, recv, device, pred=None):
        copy = pltpu.make_async_remote_copy(
            src_ref=src,
            dst_ref=dst,
            send_sem=send_sem.at[used[0]],
            recv_sem=recv,
            device_id=device,
            device_id_type=MESH_ID,
        )
        used[0] += 1
        if pred is None:
            copy.start()
        else:
            pl.when(pred)(lambda: copy.start())
        started.append((copy, pred))

    def piece(slot, quarter, h, device, pred=None, own=False):
        at = out_ref.at[slot, 3 * quarter + h]
        src = own_buf.at[3 * quarter + h] if own else at
        send(src, at, recv_sem.at[slot, quarter, h], device, pred)

    def arrived(slot, quarter, h):
        at = out_ref.at[slot, 3 * quarter + h]
        pltpu.make_async_copy(at, at, recv_sem.at[slot, quarter, h]).wait()

    def taken(slot, quarter, h):
        arrived(slot, quarter, h)
        piece(slot, quarter, h, dev_c)

    def near(k):
        return 2 * sources[k] + x

    def far(k):
        return 2 * sources[k] + 1 - x

    oy = 1 - y
    full_own, full_sib = 3 * y + 2 * c, 3 * y + 2 * (1 - c)
    full_far, full_cross = 3 * oy + 2 * c, 3 * oy + 2 * (1 - c)

    def full_rows(j):
        return xo_ref.at[pl.ds(128 * j, 128)]

    def half_rows(part, j, core):
        return xo_ref.at[pl.ds(512 + 256 * (part ^ core) + 64 * j, 64)]

    def token_send():
        send(x_ref.at[full_far], full_rows(sq), tok_recv.at[sq, 0], dev_y)
        for part in range(2):
            src = x_ref.at[3 * oy + 1, pl.ds(64 * part, 64)]
            send(src, half_rows(part, sq, c), tok_recv.at[sq, 1 + part], dev_y)
        send(x_ref.at[full_cross], full_rows(sq), tok_recv.at[sq, 0], dev_yc)
        send(x_ref.at[full_sib], full_rows(sq), tok_recv.at[sq, 0], dev_c)
        locals_.append(move(x_ref.at[full_own], full_rows(sq)))
        for part in range(2):
            src = x_ref.at[3 * y + 1, pl.ds(64 * part, 64)]
            send(src, half_rows(part, sq, 1 - c), tok_recv.at[sq, 1 + part], dev_c)
            locals_.append(move(src, half_rows(part, sq, c)))

    def token_forward():
        for part in range(2):
            at = half_rows(part, sq ^ 2, c)
            pltpu.make_async_copy(at, at, tok_recv.at[sq ^ 2, 1 + part]).wait()
            send(at, half_rows(part, sq ^ 2, 1 - c), tok_recv.at[sq ^ 2, 1 + part], dev_c)

    def own_line(h):
        piece(dp, q, h, dev_up, has_up, own=True)
        piece(dp, q, h, dev_down, has_down, own=True)

    def line(k, h):
        arrived(near(k), q, h)
        onward = (jnp.where(sources[k] < z, dev_up[0], dev_down[0]), sq)
        piece(near(k), q, h, onward, inner)
        if k > 0:
            piece(near(k), q, h, dev_x)
            piece(near(k), q, h, dev_y)
        piece(near(k), q, h, dev_c)

    def from_x_own(h):
        arrived(dp ^ 1, q, h)
        piece(dp ^ 1, q, h, dev_near)
        piece(dp ^ 1, q, h, dev_c)

    def near_other_half(h):
        arrived(near(0), qy, h)
        piece(near(0), qy, h, dev_x)
        piece(near(0), qy, h, dev_c)

    def from_x(k, h):
        arrived(far(k), q, h)
        piece(far(k), q, h, dev_y)
        piece(far(k), q, h, dev_c)

    steps = {
        "tk": token_send,
        "tf": token_forward,
        "zs": own_line,
        "zx": lambda h: piece(dp, qy, h, dev_near, own=True),
        "xs": lambda h: piece(dp, q, h, dev_x, own=True),
        "xb": lambda h: piece(dp, qy, h, dev_x, own=True),
        "r": line,
        "xo": from_x_own,
        "xob": lambda h: taken(dp ^ 1, qy, h),
        "e1": near_other_half,
        "e2": lambda h: taken(far(0), q, h),
        "yr": lambda k, h: taken(near(k), qy, h),
        "xr": from_x,
        "xsr": lambda h: taken(far(0), qy, h),
        "yx": lambda k, h: taken(far(k), qy, h),
    }

    def round_own(index, quarter):
        loads[index].wait()
        thirds = pl.ds(3 * quarter, 3)
        own_buf[thirds] = wide_buf[thirds].astype(LOW)

    round_own(0, q)
    round_own(1, qy)
    for name, *at in GATHER_ORDER[:GATHER_HEAD]:
        steps[name](*at)
    round_own(2, qc)
    round_own(3, qyc)
    locals_.append(move(own_buf, out_ref.at[dp]))
    for name, *at in GATHER_ORDER[GATHER_HEAD:]:
        steps[name](*at)
    exchange = Exchange(by_sentence(g_ref, gy_ref), ex_send, ex_recv, ex_local)
    exchange.start()
    for step in range(1, 8):
        for h in range(3):
            arrived(dp ^ step, qc, h)
            arrived(dp ^ step, qyc, h)
    for other in (sq ^ 1, sq ^ 2, sq ^ 3):
        at = full_rows(other)
        pltpu.make_async_copy(at, at, tok_recv.at[other, 0]).wait()
    for other in (sq ^ 1, sq ^ 3):
        for part in range(2):
            at = half_rows(part, other, c)
            pltpu.make_async_copy(at, at, tok_recv.at[other, 1 + part]).wait()
    for copy in locals_:
        copy.wait()
    stores = [move(out_ref.at[slot], weights_ref.at[slot]) for slot in range(8)]
    stores.append(move(xo_ref, rows_ref))

    for part in range(3):
        for half in range(2):
            tile = 2 * part + half
            held = out_ref[own_of_ref[tile // 3], 4 * (tile % 3) : 4 * (tile % 3) + 4]
            rows = slice(TILE * half, TILE * (half + 1))
            mats_buf[part, rows] = held.reshape(TILE, held.shape[-1])
        stores.append(move(mats_buf.at[part], mats_ref.at[part]))
        value = dot_nn(xo_ref[...], mats_buf[part])
        if part == 0:
            value = (value + vec_ref[0:1]) * HEAD_DIM ** (-0.5)
        elif part == 2:
            value = value + vec_ref[1:2]
        qkv_buf[part] = value.astype(LOW)
        stores.append(move(qkv_buf.at[part], qkv_ref.at[part]))

    def attend_block(block, carry):
        bias = key_bias(len_ref, block == 2)
        at = pl.ds(pl.multiple_of(256 * block, 256), 256)
        keys = pl.ds(pl.multiple_of(512 * (block // 2), 512), 512)
        for pair in range(qkv_buf.shape[-1] // 128):
            lanes = slice(128 * pair, 128 * (pair + 1))
            out, logs = attend_pair(
                qkv_buf[0, at, lanes], qkv_buf[1, keys, lanes], qkv_buf[2, keys, lanes], bias
            )
            o_buf[at, lanes] = out
            for head in range(2):
                lse_ref[2 * pair + head : 2 * pair + head + 1, at] = logs[head]
        return carry

    lax.fori_loop(0, 3, attend_block, 0)
    stores.append(move(o_buf, o_ref))
    exchange.finish()
    for copy in stores:
        copy.wait()
    for copy, pred in started:
        if pred is None:
            copy.wait_send()
        else:
            pl.when(pred)(lambda copy=copy: copy.wait_send())


def front(owners, lengths, block, tokens, grad_out, vectors):
    block_rows, width = block.shape
    part = block_rows // 12
    hbm = pl.BlockSpec(memory_space=pl.ANY)
    smem = pl.BlockSpec(memory_space=pltpu.SMEM)
    vmem = pl.BlockSpec(memory_space=pltpu.VMEM)
    dma = pltpu.SemaphoreType.DMA
    flat = jax.ShapeDtypeStruct((768, width), LOW)
    weights, *rest = pl.pallas_call(
        front_body,
        out_shape=(
            jax.ShapeDtypeStruct((8, 12, part, width), LOW),
            jax.ShapeDtypeStruct((1024, width), LOW),
            jax.ShapeDtypeStruct((3, 1024, width), LOW),
            jax.ShapeDtypeStruct((3, width, width), LOW),
            flat,
            flat,
            jax.ShapeDtypeStruct((HEADS, 768), WIDE),
        ),
        in_specs=[smem] * 2 + [hbm] * 3 + [vmem],
        out_specs=(hbm,) * 6 + (vmem,),
        scratch_shapes=[
            pltpu.VMEM((12, part, width), WIDE),
            pltpu.VMEM((12, part, width), LOW),
            pltpu.VMEM((8, 12, part, width), LOW),
            pltpu.VMEM((1024, width), LOW),
            pltpu.VMEM((3, 1024, width), LOW),
            pltpu.VMEM((3, width, width), LOW),
            pltpu.VMEM((768, width), LOW),
            dma((160,)),
            dma((8, 4, 3)),
            dma((4, 3)),
            dma((24,)),
        ]
        + EXCHANGE_SEMS,
        compiler_params=params(collective_id=1, has_side_effects=True),
        name="gather_attend",
    )(owners, lengths, block.reshape(12, part, width), tokens, grad_out, vectors)
    return weights.reshape(8 * block_rows // TILE, TILE, width), *rest


def qkv_body(map_ref, x_ref, top_ref, low_ref, vec_ref, out_ref):
    part = pl.program_id(0)
    scale = jnp.where(part == 0, HEAD_DIM ** (-0.5), 1.0)
    value = dot_nn(x_ref[:, :TILE], top_ref[0]) + dot_nn(x_ref[:, TILE:], low_ref[0])
    bias = jnp.where(part == 0, vec_ref[0:1], jnp.where(part == 2, vec_ref[1:2], 0.0))
    out_ref[0] = ((value + bias) * scale).astype(LOW)


def qkv_project(owners, rows, weights, vectors):
    count, width = rows.shape
    return pl.pallas_call(
        qkv_body,
        grid_spec=pltpu.PrefetchScalarGridSpec(
            num_scalar_prefetch=1,
            grid=(3,),
            in_specs=[
                pl.BlockSpec((count, width), lambda i, m: (0, 0)),
                pl.BlockSpec((1, TILE, width), lambda i, m: (tile_at(m, 2 * i), 0, 0)),
                pl.BlockSpec((1, TILE, width), lambda i, m: (tile_at(m, 2 * i + 1), 0, 0)),
                pl.BlockSpec(vectors.shape, lambda i, m: (0, 0)),
            ],
            out_specs=pl.BlockSpec((1, count, width), lambda i, m: (i, 0, 0)),
        ),
        out_shape=jax.ShapeDtypeStruct((3, count, width), LOW),
        compiler_params=params(),
        name="qkv",
    )(owners, rows, weights, weights, vectors)


def group_barrier(dp, sq):
    barrier = pltpu.get_barrier_semaphore()
    for step in range(1, 4):
        pl.semaphore_signal(
            barrier, inc=1, device_id=(dp, sq ^ step), device_id_type=MESH_ID
        )
    pl.semaphore_wait(barrier, 3)


class Exchange:
    def __init__(self, pieces, send_sem, recv_sem, local_sem):
        self.dp, self.sq = lax.axis_index("dp"), lax.axis_index("seq")
        self.pieces = pieces
        self.sems = (send_sem, recv_sem, local_sem)

    def copies(self):
        send_sem, recv_sem, local_sem = self.sems
        out = []
        for step in (2, 3, 1):
            target = self.sq ^ step
            for kind, (src, dst) in enumerate(self.pieces(self.sq, target)):
                out.append(
                    pltpu.make_async_remote_copy(
                        src_ref=src,
                        dst_ref=dst,
                        send_sem=send_sem.at[step - 1, kind],
                        recv_sem=recv_sem.at[self.sq, kind],
                        device_id=(self.dp, target),
                        device_id_type=MESH_ID,
                    )
                )
        for kind, (src, dst) in enumerate(self.pieces(self.sq, self.sq)):
            out.append(pltpu.make_async_copy(src, dst, local_sem.at[kind]))
        return out

    def start(self):
        for copy in self.copies():
            copy.start()

    def finish(self):
        copies = self.copies()
        for copy in copies[:6]:
            copy.wait_send()
        for copy in copies[6:]:
            copy.wait()
        for step in range(1, 4):
            source = self.sq ^ step
            for kind, (_, dst) in enumerate(self.pieces(source, self.sq)):
                pltpu.make_async_copy(dst, dst, self.sems[1].at[source, kind]).wait()


EXCHANGE_SEMS = [
    pltpu.SemaphoreType.DMA((3, 2)),
    pltpu.SemaphoreType.DMA((4, 2)),
    pltpu.SemaphoreType.DMA((2,)),
]


def by_sentence(src, dst):
    def pieces(source, target):
        y, c = target // 2, target % 2
        return (
            (src.at[3 * y + 2 * c], dst.at[pl.ds(128 * source, 128)]),
            (src.at[3 * y + 1, pl.ds(64 * c, 64)], dst.at[pl.ds(512 + 64 * source, 64)]),
        )

    return pieces


def by_position(src, dst):
    def pieces(source, target):
        y, c = source // 2, source % 2
        return (
            (src.at[pl.ds(128 * target, 128)], dst.at[3 * y + 2 * c]),
            (src.at[pl.ds(512 + 64 * target, 64)], dst.at[3 * y + 1, pl.ds(64 * c, 64)]),
        )

    return pieces


def sentence_length(lengths_ref, shared):
    sq = lax.axis_index("seq")
    group, core = sq // 2, sq % 2
    return jnp.where(shared, lengths_ref[3 * group + 1], lengths_ref[3 * group + 2 * core])


def positions(shape, shared, first=0):
    row = first + lax.broadcasted_iota(jnp.int32, shape, 0)
    own = lax.axis_index("seq") % 2
    half = row // 256
    part = row - 256 * half
    core = own + half - 2 * own * half
    mixed = (part // 64) * 128 + part % 64 + 64 * core
    return jnp.where(shared, mixed, row)


def key_bias(lengths_ref, shared):
    inside = positions((512, 128), shared) < sentence_length(lengths_ref, shared)
    bias = jnp.where(inside, 0.0, MASK_FILL)
    return jnp.concatenate([bias, bias], axis=1)


def head_masks(shape):
    lane = lax.broadcasted_iota(jnp.int32, shape, 1)
    return (lane < HEAD_DIM, lane >= HEAD_DIM)


def attend_pair(queries, keys, values, bias):
    value_t = values.T
    outs, logs = [], []
    for head, mask in enumerate(head_masks(queries.shape)):
        scores = dot_nt(keys, jnp.where(mask, queries, jnp.zeros_like(queries))) + bias
        top = jnp.max(scores, axis=0, keepdims=True)
        shifted = jnp.exp(scores - top)
        total = jnp.sum(shifted, axis=0, keepdims=True)
        part = value_t[HEAD_DIM * head : HEAD_DIM * (head + 1)]
        outs.append(dot_nn(part, shifted.astype(LOW)) * (1.0 / total))
        logs.append(top + jnp.log(total))
    return jnp.concatenate(outs, axis=0).T.astype(LOW), logs


def attend_body(
    len_ref, q_ref, k_ref, v_ref, g_ref, o_ref, lse_ref, gy_ref, send_sem, recv_sem, local_sem
):
    block, group = pl.program_id(0), pl.program_id(1)
    exchange = Exchange(by_sentence(g_ref, gy_ref), send_sem, recv_sem, local_sem)

    @pl.when((block == 0) & (group == 0))
    def _():
        group_barrier(exchange.dp, exchange.sq)
        exchange.start()

    bias = key_bias(len_ref, block == 2)
    for pair in range(q_ref.shape[-1] // 128):
        lanes = slice(128 * pair, 128 * (pair + 1))
        out, logs = attend_pair(q_ref[0, :, lanes], k_ref[0, :, lanes], v_ref[0, :, lanes], bias)
        o_ref[:, lanes] = out
        for head in range(2):
            lse_ref[0, 2 * pair + head : 2 * pair + head + 1, :] = logs[head]

    @pl.when((block == 2) & (group == pl.num_programs(1) - 1))
    def _():
        exchange.finish()


def attend(lengths, qkv, grad_out):
    width = qkv.shape[-1]
    groups = width // 128 // FWD_PAIRS
    lanes = 128 * FWD_PAIRS
    hbm = pl.BlockSpec(memory_space=pl.ANY)
    return pl.pallas_call(
        attend_body,
        grid=(3, groups),
        in_specs=[
            pl.BlockSpec(memory_space=pltpu.SMEM),
            pl.BlockSpec((1, 256, lanes), lambda i, h: (0, i, h)),
            pl.BlockSpec((1, 512, lanes), lambda i, h: (1, i // 2, h)),
            pl.BlockSpec((1, 512, lanes), lambda i, h: (2, i // 2, h)),
            hbm,
        ],
        out_specs=(
            pl.BlockSpec((256, lanes), lambda i, h: (i, h)),
            pl.BlockSpec((1, 2 * FWD_PAIRS, 256), lambda i, h: (h, 0, i)),
            hbm,
        ),
        out_shape=(
            jax.ShapeDtypeStruct((768, width), LOW),
            jax.ShapeDtypeStruct((groups, 2 * FWD_PAIRS, 768), WIDE),
            jax.ShapeDtypeStruct((768, width), LOW),
        ),
        scratch_shapes=EXCHANGE_SEMS,
        compiler_params=params(collective_id=3, has_side_effects=True),
        name="attend",
    )(lengths, qkv, qkv, qkv, grad_out)


def attend_back_body(
    len_ref, q_ref, k_ref, v_ref, lse_ref, do_ref, o_ref, y_ref,
    dq_ref, dk_ref, dv_ref, out_ref,
    acc, keep, give, take, send_sem, recv_sem, local_sem, give_sem, take_sem,
):
    group, block = pl.program_id(0), pl.program_id(1)
    exchange = Exchange(by_position(y_ref, out_ref), send_sem, recv_sem, local_sem)
    dp, sq = exchange.dp, exchange.sq

    @pl.when((block == 0) & (group == 0))
    def _():
        group_barrier(dp, sq)
        exchange.start()

    bias = key_bias(len_ref, block == 0)
    d_keys, d_values = [], []
    for pair in range(q_ref.shape[-1] // 128):
        lanes = slice(128 * pair, 128 * (pair + 1))
        queries, keys, values = q_ref[0, :, lanes], k_ref[0, :, lanes], v_ref[0, :, lanes]
        grads = do_ref[:, lanes]
        keys_t = keys.T
        inner = (grads.astype(WIDE) * o_ref[:, lanes].astype(WIDE)).T
        d_query = []
        d_key = d_value = 0.0
        for head, mask in enumerate(head_masks(queries.shape)):
            query = jnp.where(mask, queries, jnp.zeros_like(queries))
            grad = jnp.where(mask, grads, jnp.zeros_like(grads))
            rows = slice(HEAD_DIM * head, HEAD_DIM * (head + 1))
            inner_sum = jnp.sum(inner[rows], axis=0, keepdims=True)
            scores = dot_nt(keys, query) + bias
            probs = jnp.exp(scores - lse_ref[0, 2 * pair + head : 2 * pair + head + 1, :])
            d_probs = dot_nt(values, grad)
            d_scores = (probs * (d_probs - inner_sum)).astype(LOW)
            d_value = d_value + dot_nn(probs.astype(LOW), grad)
            d_key = d_key + dot_nn(d_scores, query)
            d_query.append(dot_nn(keys_t[rows], d_scores))
        d_query = jnp.concatenate(d_query, axis=0) * HEAD_DIM ** (-0.5)
        dq_ref[:, lanes] = d_query.T.astype(LOW)
        d_keys.append((lanes, d_key))
        d_values.append((lanes, d_value))
    pairs = ((0, d_keys), (1, d_values))

    def swap(kind):
        return pltpu.make_async_remote_copy(
            src_ref=give.at[group, kind],
            dst_ref=take.at[group, kind],
            send_sem=give_sem.at[group, kind],
            recv_sem=take_sem.at[group, kind],
            device_id=(dp, sq ^ 1),
            device_id_type=MESH_ID,
        )

    @pl.when(block == 0)
    def _():
        for kind, parts in pairs:
            for lanes, part in parts:
                keep[kind, :, lanes] = part[:256]
                give[group, kind, :, lanes] = part[256:].astype(LOW)
            swap(kind).start()

    @pl.when(block == 1)
    def _():
        for kind, parts in pairs:
            for lanes, part in parts:
                acc[kind, :, lanes] = part

    @pl.when(block == 2)
    def _():
        for (kind, parts), ref in zip(pairs, (dk_ref, dv_ref)):
            swap(kind).wait()
            for lanes, part in parts:
                ref[:512, lanes] = (acc[kind, :, lanes] + part).astype(LOW)
                other = take[group, kind, :, lanes].astype(WIDE)
                ref[512:, lanes] = (keep[kind, :, lanes] + other).astype(LOW)

    @pl.when((block == 2) & (group == pl.num_programs(0) - 1))
    def _():
        exchange.finish()


def attend_back(lengths, qkv, lse, d_out, out, result, sent_dev):
    width = qkv.shape[-1]
    groups = width // 128 // BACK_PAIRS
    lanes = 128 * BACK_PAIRS
    hbm = pl.BlockSpec(memory_space=pl.ANY)
    query = pl.BlockSpec((256, lanes), lambda h, i: ((i + 2) % 3, h))
    keys = pl.BlockSpec((768, lanes), lambda h, i: (0, h))
    flat = jax.ShapeDtypeStruct((768, width), LOW)
    shared = lambda i: jnp.where(i == 0, 1, 0)
    return pl.pallas_call(
        attend_back_body,
        grid=(groups, 3),
        in_specs=[
            pl.BlockSpec(memory_space=pltpu.SMEM),
            pl.BlockSpec((1, 256, lanes), lambda h, i: (0, (i + 2) % 3, h)),
            pl.BlockSpec((1, 512, lanes), lambda h, i: (1, shared(i), h)),
            pl.BlockSpec((1, 512, lanes), lambda h, i: (2, shared(i), h)),
            pl.BlockSpec((1, 2 * BACK_PAIRS, 256), lambda h, i: (h, 0, (i + 2) % 3)),
            query,
            query,
            hbm,
        ],
        out_specs=(query, keys, keys, hbm),
        out_shape=(flat, flat, flat, jax.ShapeDtypeStruct((sent_dev, 128, width), LOW)),
        scratch_shapes=[
            pltpu.VMEM((2, 512, lanes), WIDE),
            pltpu.VMEM((2, 256, lanes), WIDE),
            pltpu.VMEM((groups, 2, 256, lanes), LOW),
            pltpu.VMEM((groups, 2, 256, lanes), LOW),
        ]
        + EXCHANGE_SEMS
        + [pltpu.SemaphoreType.DMA((groups, 2)), pltpu.SemaphoreType.DMA((groups, 2))],
        compiler_params=params(collective_id=4, has_side_effects=True),
        name="attend_back",
    )(lengths, qkv, qkv, qkv, lse.reshape(groups, 2 * BACK_PAIRS, 768), d_out, out, result)


def row_mean(value):
    return jnp.mean(value, axis=-1, keepdims=True)


def col_sum(value):
    return jnp.sum(value, axis=0, keepdims=True)


def middle_body(
    map_ref, len_ref, o_hbm, x_hbm, gy_hbm, w_ref, vec_ref,
    y_hbm, left_hbm, right_hbm, do_hbm, da_hbm, dh_hbm, sums_ref,
    w_buf, o_buf, x_buf, gy_buf, left, right, slope, total, hat_one, rstd_one, low_buf,
    sem, in_sem, out_sem,
):
    count, width = o_buf.shape
    tiles = w_buf.shape[0]
    chunks = FEEDFWD_UNITS // width

    def fetch(t):
        return pltpu.make_async_copy(w_ref.at[tile_at(map_ref, 6 + t)], w_buf.at[t], sem.at[t])

    inputs = [
        pltpu.make_async_copy(src, dst, in_sem.at[i])
        for i, (src, dst) in enumerate(
            (
                (o_hbm, o_buf),
                (x_hbm.at[pl.ds(0, count)], x_buf),
                (gy_hbm, gy_buf),
            )
        )
    ]
    inputs[0].start()
    for t in range(2):
        fetch(t).start()
    inputs[1].start()
    for c in range(chunks):
        for t in (2 + 2 * c, 3 + 2 * c, 10 + 2 * c, 11 + 2 * c):
            fetch(t).start()
    inputs[2].start()
    outputs = []

    def put(src, dst):
        copy = pltpu.make_async_copy(src, dst, out_sem.at[len(outputs)])
        copy.start()
        outputs.append(copy)

    def put_left(t, value):
        for u in range(2):
            left[t + u] = value[:, TILE * u : TILE * (u + 1)]
            put(left.at[t + u], left_hbm.at[t + u])

    def ready(*which):
        for t in which:
            fetch(t).wait()

    def pair(t):
        return w_buf[t : t + 2].reshape(2 * TILE, width)

    def vec(row):
        return vec_ref[row : row + 1, :]

    def fold(value):
        return jnp.sum(value.reshape(-1, 8, width), axis=0)

    def over_rows(body, carried):
        zero = (jnp.zeros((8, width), WIDE),) * carried

        def step(i, carry):
            return body(pl.ds(pl.multiple_of(i * NORM_ROWS, NORM_ROWS), NORM_ROWS), i, carry)

        return lax.fori_loop(0, count // NORM_ROWS, step, zero)

    inputs[0].wait()
    ready(0, 1)
    total[...] = dot_nn(o_buf[...], pair(0))
    inputs[1].wait()

    def norm_one(at, i, carry):
        resid = x_buf[at].astype(WIDE) + (total[at] + vec(2))
        centered = resid - row_mean(resid)
        rstd = lax.rsqrt(row_mean(centered * centered) + NORM_EPS)
        rstd_one[at] = rstd
        hat = centered * rstd
        hat_one[at] = hat
        first = hat * vec(4) + vec(5)
        total[at] = first + vec(3)
        right[0, at] = first.astype(LOW)
        return carry

    over_rows(norm_one, 0)
    put(right.at[0], right_hbm.at[0])

    first_low = right[0]
    for c in range(chunks):
        ready(2 + 2 * c, 3 + 2 * c, 10 + 2 * c, 11 + 2 * c)
        act = dot_nt(first_low, pair(2 + 2 * c)) + vec(8 + c)
        cdf = 0.5 + 0.5 * lax.erf(act * (0.5**0.5))
        pdf = jnp.exp(-0.5 * act * act) * 0.3989422804014327
        slope[c] = cdf + act * pdf
        active = (act * cdf).astype(LOW)
        put_left(8 + 2 * c, active)
        total[...] += dot_nn(active, pair(10 + 2 * c))
    inputs[2].wait()

    def norm_two(at, i, carry):
        d_gain, d_shift, d_bias, pool_full, pool_half = carry
        resid = total[at]
        centered = resid - row_mean(resid)
        rstd = lax.rsqrt(row_mean(centered * centered) + NORM_EPS)
        hat = centered * rstd
        result = hat * vec(6) + vec(7)
        low_buf[0, at] = result.astype(LOW)
        shared = i * NORM_ROWS >= 512
        row = positions((NORM_ROWS, 128), shared, i * NORM_ROWS - jnp.where(shared, 512, 0))
        valid = jnp.where(row < sentence_length(len_ref, shared), 1.0, 0.0)
        pooled = fold(result * jnp.concatenate([valid] * (width // 128), axis=1))
        part = shared.astype(WIDE)
        grad = gy_buf[at].astype(WIDE)
        d_gain = d_gain + fold(grad * hat)
        d_shift = d_shift + fold(grad)
        grad = grad * vec(6)
        d_resid = rstd * (grad - row_mean(grad) - hat * row_mean(grad * hat))
        total[at] = d_resid
        grad_low = d_resid.astype(LOW)
        right[1, at] = grad_low
        return (
            d_gain,
            d_shift,
            d_bias + fold(grad_low.astype(WIDE)),
            pool_full + pooled * (1.0 - part),
            pool_half + pooled * part,
        )

    sums_ref[...] = jnp.zeros_like(sums_ref)
    found = over_rows(norm_two, 5)
    for row, value in zip((4, 5, 1, 10, 11), found):
        sums_ref[row : row + 1, :] = col_sum(value)
    put(low_buf.at[0], y_hbm)
    put(right.at[1], right_hbm.at[1])

    grad_low = right[1]
    for c in range(chunks):
        d_active = dot_nt(grad_low, pair(10 + 2 * c))
        d_act = (d_active * slope[c]).astype(LOW)
        put_left(2 * c, d_act)
        sums_ref[6 + c : 7 + c, :] = col_sum(d_act.astype(WIDE))
        total[...] += dot_nn(d_act, pair(2 + 2 * c))

    def norm_back(at, i, carry):
        d_gain, d_shift, d_bias = carry
        grad = total[at]
        hat = hat_one[at]
        d_gain = d_gain + fold(grad * hat)
        d_shift = d_shift + fold(grad)
        grad = grad * vec(4)
        d_resid = rstd_one[at] * (grad - row_mean(grad) - hat * row_mean(grad * hat))
        total[at] = d_resid
        grad_low = d_resid.astype(LOW)
        low_buf[1, at] = grad_low
        return (d_gain, d_shift, d_bias + fold(grad_low.astype(WIDE)))

    found = over_rows(norm_back, 3)
    for row, value in zip((2, 3, 0), found):
        sums_ref[row : row + 1, :] = col_sum(value)
    put(total, dh_hbm)
    put(low_buf.at[1], da_hbm)
    low_buf[2] = dot_nt(low_buf[1], pair(0)).astype(LOW)
    put(low_buf.at[2], do_hbm)
    for copy in outputs:
        copy.wait()


def middle(owners, lengths, attended, rows, out_grad, weights, vectors):
    count, width = attended.shape
    half = FEEDFWD_UNITS // TILE
    tiles = 2 + 2 * half
    hbm = pl.BlockSpec(memory_space=pl.ANY)
    smem = pl.BlockSpec(memory_space=pltpu.SMEM)
    vmem = pl.BlockSpec(memory_space=pltpu.VMEM)
    flat = jax.ShapeDtypeStruct((count, width), LOW)
    return pl.pallas_call(
        middle_body,
        in_specs=[smem, smem] + [hbm] * 4 + [vmem],
        out_specs=(hbm,) * 6 + (vmem,),
        out_shape=(
            flat,
            jax.ShapeDtypeStruct((2 * half, count, TILE), LOW),
            jax.ShapeDtypeStruct((2, count, width), LOW),
            flat,
            flat,
            jax.ShapeDtypeStruct((count, width), WIDE),
            jax.ShapeDtypeStruct((16, width), WIDE),
        ),
        scratch_shapes=[
            pltpu.VMEM((tiles, TILE, width), LOW),
            pltpu.VMEM((count, width), LOW),
            pltpu.VMEM((count, width), LOW),
            pltpu.VMEM((count, width), LOW),
            pltpu.VMEM((2 * half, count, TILE), LOW),
            pltpu.VMEM((2, count, width), LOW),
            pltpu.VMEM((half // 2, count, width), WIDE),
            pltpu.VMEM((count, width), WIDE),
            pltpu.VMEM((count, width), WIDE),
            pltpu.VMEM((count, 1), WIDE),
            pltpu.VMEM((3, count, width), LOW),
            pltpu.SemaphoreType.DMA((tiles,)),
            pltpu.SemaphoreType.DMA((3,)),
            pltpu.SemaphoreType.DMA((2 * half + 6,)),
        ],
        compiler_params=params(),
        name="feed_forward",
    )(owners, lengths, attended, rows, out_grad, weights, vectors)


def grad_ff_body(map_ref, left_ref, right_ref, out_ref):
    out_ref[0] = dot_tn(left_ref[0], right_ref[0]).astype(LOW)


def grad_ff(owners, left, right):
    per = FEEDFWD_UNITS // TILE
    count, width = right.shape[1:]
    return pl.pallas_call(
        grad_ff_body,
        grid_spec=pltpu.PrefetchScalarGridSpec(
            num_scalar_prefetch=1,
            grid=(2 * per,),
            in_specs=[
                pl.BlockSpec((1, count, TILE), lambda i, m: (i, 0, 0)),
                pl.BlockSpec((1, count, width), lambda i, m: (i // per, 0, 0)),
            ],
            out_specs=pl.BlockSpec((1, TILE, width), lambda i, m: (tile_at(m, 8 + i), 0, 0)),
        ),
        out_shape=jax.ShapeDtypeStruct((8 + 2 * per, TILE, width), LOW),
        compiler_params=params(),
        name="grad_ff",
    )(owners, left, right)


def grad_attn_body(
    map_ref, x_ref, dq_ref, dk_ref, dv_ref, o_ref, da_ref, into_ref, out_ref, sums_ref
):
    step = pl.program_id(0)
    for part, grad_ref in enumerate((dq_ref, dk_ref, dv_ref)):

        @pl.when(step // 2 == part)
        def _(grad_ref=grad_ref):
            out_ref[0] = dot_tn(x_ref[...], grad_ref[...]).astype(LOW)

    @pl.when(step // 2 == 3)
    def _():
        out_ref[0] = dot_tn(o_ref[...], da_ref[...]).astype(LOW)

    @pl.when(step == 0)
    def _():
        sums_ref[...] = jnp.zeros_like(sums_ref)
        sums_ref[0:1, :] = col_sum(dq_ref[...].astype(WIDE))
        sums_ref[1:2, :] = col_sum(dv_ref[...].astype(WIDE))


def grad_attn(owners, rows, dq, dk, dv, attended, da, into):
    count, width = dq.shape
    whole = pl.BlockSpec((count, width), lambda i, m: (0, 0))
    return pl.pallas_call(
        grad_attn_body,
        grid_spec=pltpu.PrefetchScalarGridSpec(
            num_scalar_prefetch=1,
            grid=(8,),
            in_specs=[
                pl.BlockSpec((count, TILE), lambda i, m: (0, i % 2)),
                whole,
                whole,
                whole,
                pl.BlockSpec((768, TILE), lambda i, m: (0, i % 2)),
                pl.BlockSpec((768, width), lambda i, m: (0, 0)),
                pl.BlockSpec(memory_space=pl.ANY),
            ],
            out_specs=(
                pl.BlockSpec((1, TILE, width), lambda i, m: (tile_at(m, i), 0, 0)),
                pl.BlockSpec((8, width), lambda i, m: (0, 0)),
            ),
        ),
        out_shape=(
            jax.ShapeDtypeStruct(into.shape, LOW),
            jax.ShapeDtypeStruct((8, width), WIDE),
        ),
        input_output_aliases={7: 0},
        compiler_params=params(),
        name="grad_attn",
    )(owners, rows, dq, dk, dv, attended, da, into)


def grad_in_body(map_ref, dq_ref, dk_ref, dv_ref, dh_ref, *refs):
    w_refs, out_ref = refs[:6], refs[6]
    for half in range(2):
        cols = slice(TILE * half, TILE * (half + 1))
        value = dh_ref[:, cols]
        for part, grad_ref in enumerate((dq_ref, dk_ref, dv_ref)):
            value = value + dot_nt(grad_ref[...], w_refs[2 * part + half][0])
        out_ref[:, cols] = value.astype(LOW)


def grad_in(owners, dq, dk, dv, dh, weights):
    count, width = dq.shape
    block = pl.BlockSpec((256, width), lambda i, m: (i, 0))
    return pl.pallas_call(
        grad_in_body,
        grid_spec=pltpu.PrefetchScalarGridSpec(
            num_scalar_prefetch=1,
            grid=(count // 256,),
            in_specs=[block] * 4
            + [
                pl.BlockSpec((1, TILE, width), lambda i, m, t=t: (tile_at(m, t), 0, 0)) for t in range(6)
            ],
            out_specs=block,
        ),
        out_shape=jax.ShapeDtypeStruct((count, width), LOW),
        compiler_params=params(),
        name="grad_in",
    )(owners, dq, dk, dv, dh, *([weights] * 6))


REDUCE_MODE = (
    {"n": "z", "a": "y", "e": "x", "o": "x"},
    {"n": "z", "a": "y", "e": "x", "o": "x"},
    {"n": "x", "a": "y", "e": "x", "o": "x"},
)
REDUCE_ORDER = (
    ("part", "n", "f", 2), ("part", "a", "n", 1), ("part", "a", "n", 2), ("vs", 0),
    ("both", "n", "f", 2), ("both", "a", "n", 1), ("part", "e", "f", 1), ("both", "a", "n", 2),
    ("part", "n", "n", 1), ("part", "e", "f", 0), ("va", 0), ("part", "a", "f", 2),
    ("both", "e", "f", 1), ("vs", 1), ("part", "a", "f", 0), ("part", "e", "f", 2),
    ("part", "a", "f", 1), ("both", "a", "f", 2), ("both", "n", "n", 1), ("part", "n", "f", 1),
    ("part", "a", "n", 0), ("both", "e", "f", 0), ("part", "o", "f", 2), ("both", "a", "f", 0),
    ("both", "a", "n", 0), ("both", "n", "f", 1), ("part", "e", "n", 2), ("part", "e", "n", 1),
    ("part", "n", "f", 0), ("part", "o", "n", 1), ("turn", "n", 1), ("part", "o", "f", 1),
    ("both", "e", "f", 2), ("both", "a", "f", 1), ("part", "e", "n", 0), ("part", "o", "f", 0),
    ("both", "e", "n", 1), ("turn", "e", 1), ("both", "n", "f", 0), ("part", "n", "n", 0),
    ("both", "e", "n", 0), ("part", "o", "n", 2), ("both", "o", "f", 1), ("turn", "e", 0),
    ("both", "n", "n", 0), ("both", "o", "f", 2), ("own", "f", 1), ("both", "e", "n", 2),
    ("turn", "a", 1), ("both", "o", "f", 0), ("turn", "e", 2), ("gin",), ("in",),
    ("both", "o", "n", 1), ("turn", "a", 0), ("own", "f", 0), ("own", "n", 1), ("on", "e", 2),
    ("turn", "o", 1), ("part", "o", "n", 0), ("part", "n", "n", 2), ("turn", "a", 2), ("va", 1),
    ("on", "a", 1), ("both", "n", "n", 2), ("own", "f", 2), ("both", "o", "n", 2), ("vs", 2),
    ("on", "e", 1), ("turn", "n", 2), ("both", "o", "n", 0), ("on", "a", 0), ("own", "n", 0),
    ("turn", "o", 0), ("on", "e", 0), ("end", 1), ("on", "a", 2), ("own", "n", 2), ("on", "n", 2),
    ("turn", "o", 2), ("end", 0), ("va", 2), ("on", "n", 1), ("vs", 3), ("end", 2), ("va", 3),
    ("turn", "n", 0), ("vs", 4), ("va", 4), ("on", "n", 0),
)


def reduce_body(
    own_of_ref, x_ref, o_ref, left_ref, dq_ref, dk_ref, dv_ref, da_ref, right_ref,
    w_ref, dh_ref, sums_ref, own_ref, vt_ref, sq_ref, gi_ref,
    left_0, left_1, left_2, rbuf, wbuf, dhbuf, gbuf, pbuf, core_in, x_two, x_one, y_two, y_one,
    zf_in, mid_in, fin_in, near_in, ebuf, tbuf, tlow, vbuf, v_in, s_own, s_seq, s_dp,
    send_sem, local_sem, core_sem, xtwo_sem, xone_sem, ytwo_sem, yone_sem,
    zf_sem, mid_sem, fin_sem, near_sem, v_sem, out_sem, seq_sem, dp_sem, in_sem,
):
    dp, sq = lax.axis_index("dp"), lax.axis_index("seq")
    z, x = dp // 2, dp % 2
    y, c = sq // 2, sq % 2
    dev_c, dev_y, dev_yc, dev_x = (dp, sq ^ 1), (dp, sq ^ 2), (dp, sq ^ 3), (dp ^ 1, sq)
    dev_near = (dp ^ 2, sq)
    inner = (z > 0) & (z < 3)
    outer = jnp.logical_not(inner)
    place = {
        "n": z ^ 1,
        "a": jnp.where(z < 2, 2, 1),
        "e": jnp.where(z < 2, 3, 0),
        "o": z,
    }
    lefts = (left_0, left_1, left_2)
    used = [0, 0]
    remotes, own_moves = [], []

    def move(src, dst):
        copy = pltpu.make_async_copy(src, dst, local_sem.at[used[1]])
        used[1] += 1
        copy.start()
        return copy

    def load_right():
        copies = [move(right_ref, rbuf.at[pl.ds(4, 2)])]
        for index, ref in enumerate((dq_ref, dk_ref, dv_ref, da_ref)):
            copies.append(move(ref, rbuf.at[index]))
        return copies

    def load_left(t):
        copies = []
        for block in range(8):
            tile = 3 * block + t
            cols = pl.ds(TILE * (tile % 2), TILE)
            if tile < 6:
                src = x_ref.at[pl.ds(0, 768), cols]
            elif tile < 8:
                src = o_ref.at[:, cols]
            else:
                src = left_ref.at[tile - 8]
            copies.append(move(src, lefts[t].at[block]))
        return copies

    def load_input():
        return [move(w_ref, wbuf), move(dh_ref, dhbuf)]

    loads = {"right": load_right()}
    for name, *at in REDUCE_ORDER:
        if name == "part" and at[2] not in loads:
            loads[at[2]] = load_left(at[2])
        if name == "gin":
            loads["in"] = load_input()

    def loaded(name):
        for copy in loads.pop(name, ()):
            copy.wait()

    barrier = pltpu.get_barrier_semaphore()
    for step in range(1, 4):
        pl.semaphore_signal(
            barrier, inc=1, device_id=(dp, sq ^ step), device_id_type=MESH_ID
        )
    for step in range(1, 8):
        pl.semaphore_signal(
            barrier, inc=1, device_id=(dp ^ step, sq), device_id_type=MESH_ID
        )
    pl.semaphore_wait(barrier, 10)

    def send(src, dst, recv, device, pred=None):
        copy = pltpu.make_async_remote_copy(
            src_ref=src,
            dst_ref=dst,
            send_sem=send_sem.at[used[0]],
            recv_sem=recv,
            device_id=device,
            device_id_type=MESH_ID,
        )
        used[0] += 1
        if pred is None:
            copy.start()
        else:
            pl.when(pred)(lambda: copy.start())
        remotes.append((copy, pred))

    def arrived(at, sem):
        pltpu.make_async_copy(at, at, sem).wait()

    def wide(ref, *at):
        return ref[at].astype(WIDE)

    loaded("right")

    partners = (dev_c, dev_y, dev_x, (dp ^ 2, sq), (dp ^ 4, sq))

    def vec_send(step):
        if step == 0:
            vbuf[0] = jnp.zeros(vbuf.shape[1:], WIDE)
            vbuf[0, 0:1] = col_sum(wide(rbuf, 0))
            vbuf[0, 1:2] = col_sum(wide(rbuf, 2))
            vbuf[0, 2:12] = sums_ref[0:10]
            vbuf[0, pl.ds(16 + 3 * y + 2 * c, 1)] = sums_ref[10:11]
            vbuf[0, pl.ds(16 + 3 * y + 1, 1)] = sums_ref[11:12]
        send(vbuf.at[step], v_in.at[step], v_sem.at[step], partners[step])

    def vec_add(step):
        arrived(v_in.at[step], v_sem.at[step])
        vbuf[step + 1] = vbuf[step] + v_in[step]

    def input_grad():
        loaded("in")
        for part in range(3):
            cols = slice(256 * part, 256 * (part + 1))
            value = dhbuf[:, cols]
            for index in range(3):
                value = value + dot_nt(rbuf[index], wbuf[index, cols])
            gbuf[:, cols] = value.astype(LOW)

    def in_full(j):
        return gbuf.at[pl.ds(128 * j, 128)], gi_ref.at[3 * y + 2 * c]

    def in_half(j):
        return gbuf.at[pl.ds(512 + 64 * j, 64)], gi_ref.at[3 * y + 1, pl.ds(64 * c, 64)]

    def input_send():
        for device in (dev_y, dev_yc, dev_c):
            for kind, pair in enumerate((in_full(device[1]), in_half(device[1]))):
                send(pair[0], pair[1], in_sem.at[sq, kind], device)
        own_moves.append(move(*in_full(sq)))
        own_moves.append(move(*in_half(sq)))

    def standard_of(slot):
        found = jnp.int32(0)
        for block in range(8):
            found = jnp.maximum(found, jnp.where(own_of_ref[block] == slot, block, 0))
        return found

    def slot_of(k, p):
        return 2 * place[k] + (x if p == "n" else 1 - x)

    def partial(k, p, t):
        loaded(t)
        slot = slot_of(k, p)
        block = standard_of(slot)
        tile = 3 * block + t
        right = jnp.where(tile < 8, tile // 2, 4 + (tile - 8) // 8)
        value = dot_tn(lefts[t][block], rbuf[right]).astype(LOW)
        for quarter in range(4):
            rows = slice(96 * quarter, 96 * (quarter + 1))
            pbuf[quarter % 2, t, slot, quarter // 2] = value[rows]
        send(pbuf.at[1 - c, t, slot], core_in.at[t, slot], core_sem.at[t, slot], dev_c)

    def held(*at):
        return pbuf.at[(c, *at)]

    index_of = {"x": {}, "y": {}, "z": {}}
    for t in range(3):
        for k in "naeo":
            found = index_of[REDUCE_MODE[t][k]]
            found[k, t] = len(found)

    def first_send(k, p, t):
        slot = slot_of(k, p)
        if REDUCE_MODE[t][k] == "y":
            at, half = index_of["y"][k, t], "nf".index(p)
            send(held(t, slot, 1 - y), y_two.at[at, half], ytwo_sem.at[at, half], dev_y)
        elif p == "f":
            at = index_of["x"][k, t]
            send(held(t, slot), x_two.at[at], xtwo_sem.at[at], dev_x)

    def both_cores(k, p, t):
        slot = slot_of(k, p)
        arrived(core_in.at[t, slot], core_sem.at[t, slot])
        pbuf[c, t, slot] = (wide(pbuf, c, t, slot) + wide(core_in, t, slot)).astype(LOW)
        if REDUCE_MODE[t][k] == "z":
            half = "nf".index(p)
            send(held(t, slot), zf_in.at[t, half], zf_sem.at[t, half], dev_near)
        elif k != "o":
            first_send(k, p, t)

    def own_block(p, t):
        if REDUCE_MODE[t]["n"] == "z":
            slot, half = slot_of("o", p), "nf".index(p)
            arrived(zf_in.at[t, half], zf_sem.at[t, half])
            pbuf[c, t, slot] = (wide(pbuf, c, t, slot) + wide(zf_in, t, half)).astype(LOW)
        first_send("o", p, t)

    def turn(k, t):
        mode = REDUCE_MODE[t][k]
        if mode == "z":
            return
        at = index_of[mode][k, t]
        near, far = slot_of(k, "n"), slot_of(k, "f")
        if mode == "y":
            for half in range(2):
                arrived(y_two.at[at, half], ytwo_sem.at[at, half])
            pbuf[c, t, far, y] = (wide(pbuf, c, t, far, y) + wide(y_two, at, 1)).astype(LOW)
            send(held(t, far, y), x_one.at[at], xone_sem.at[at], dev_x)
        else:
            arrived(x_two.at[at], xtwo_sem.at[at])
            pbuf[c, t, near] = (wide(pbuf, c, t, near) + wide(x_two, at)).astype(LOW)
            send(held(t, near, 1 - y), y_one.at[at], yone_sem.at[at], dev_y)

    def plane_sum(k, t):
        mode = REDUCE_MODE[t][k]
        at = index_of[mode][k, t]
        mine = wide(pbuf, c, t, slot_of(k, "n"), y)
        if mode == "y":
            arrived(x_one.at[at], xone_sem.at[at])
            return mine + wide(y_two, at, 0) + wide(x_one, at)
        arrived(y_one.at[at], yone_sem.at[at])
        return mine + wide(y_one, at)

    def onward(k, t):
        if REDUCE_MODE[t][k] == "z":
            return
        row = "nae".index(k)
        tbuf[...] = plane_sum(k, t)
        if k == "n":
            ebuf[row, t] = tbuf[...].astype(LOW)
            send(ebuf.at[row, t], near_in.at[t], near_sem.at[t], dev_near)
            return

        @pl.when(inner)
        def _():
            arrived(mid_in.at[row, t], mid_sem.at[row, t])
            tbuf[...] += wide(mid_in, row, t)

        ebuf[row, t] = tbuf[...].astype(LOW)
        owner = (2 * place[k] + x, sq)
        send(ebuf.at[row, t], fin_in.at[t], fin_sem.at[t], owner, inner)
        send(ebuf.at[row, t], mid_in.at[row, t], mid_sem.at[row, t], dev_near, outer)

    squares = []

    def finish(t):
        value = plane_sum("o", t)
        if REDUCE_MODE[t]["n"] != "z":
            arrived(near_in.at[t], near_sem.at[t])
            value = value + wide(near_in, t)
        arrived(fin_in.at[t], fin_sem.at[t])
        total = (value + wide(fin_in, t)).astype(LOW)
        tlow[t] = total
        wide_total = total.astype(WIDE)
        rows = (wide_total * wide_total).reshape(-1, 8, wide_total.shape[-1])
        squares.append(jnp.sum(rows, axis=0))
        at = own_ref.at[t, sq]
        for device in (dev_y, dev_c):
            send(tlow.at[t], at, out_sem.at[t, sq], device)
        own_moves.append(move(tlow.at[t], at))

    steps = {
        "part": partial,
        "both": both_cores,
        "own": own_block,
        "turn": turn,
        "on": onward,
        "end": finish,
        "vs": vec_send,
        "va": vec_add,
        "gin": input_grad,
        "in": input_send,
    }
    for name, *at in REDUCE_ORDER:
        steps[name](*at)

    squares = squares[0] + squares[1] + squares[2]
    folded = squares[:, :128]
    for lane in range(1, squares.shape[-1] // 128):
        folded = folded + squares[:, 128 * lane : 128 * (lane + 1)]
    s_own[...] = folded
    for step in range(1, 4):
        send(s_own, s_seq.at[sq], seq_sem.at[sq], (dp, sq ^ step))
    s_seq[sq] = folded
    for t in [at[0] for name, *at in REDUCE_ORDER if name == "end"]:
        arrived(own_ref.at[t, sq ^ 2], out_sem.at[t, sq ^ 2])
        send(own_ref.at[t, sq ^ 2], own_ref.at[t, sq ^ 2], out_sem.at[t, sq ^ 2], dev_c)
    for step in range(1, 4):
        arrived(s_seq.at[sq ^ step], seq_sem.at[sq ^ step])
    group = s_seq[0] + s_seq[1] + s_seq[2] + s_seq[3]
    s_dp[dp] = group
    for step in range(1, 8):
        send(s_dp.at[dp], s_dp.at[dp], dp_sem.at[dp], (dp ^ step, sq))
    for step in range(1, 8):
        arrived(s_dp.at[dp ^ step], dp_sem.at[dp ^ step])
    everyone = s_dp[0]
    for index in range(1, 8):
        everyone = everyone + s_dp[index]
    sq_ref[...] = everyone
    vt_ref[0:16] = vbuf[5][0:16]
    vt_ref[16:24] = vbuf[2][16:24]

    for t in range(3):
        arrived(own_ref.at[t, sq ^ 1], out_sem.at[t, sq ^ 1])
        arrived(own_ref.at[t, sq ^ 3], out_sem.at[t, sq ^ 3])
    for step in range(1, 4):
        other = sq ^ step
        there, member = other // 2, other % 2
        arrived(gi_ref.at[3 * there + 2 * member], in_sem.at[other, 0])
        arrived(gi_ref.at[3 * there + 1, pl.ds(64 * member, 64)], in_sem.at[other, 1])
    for copy in own_moves:
        copy.wait()
    for copy, pred in remotes:
        if pred is None:
            copy.wait_send()
        else:
            pl.when(pred)(lambda copy=copy: copy.wait_send())


def reduce_all(owners, rows, out, left, grads, right, matrices, d_resid, sums, sent_dev):
    width = rows.shape[-1]
    part = TILE // 4
    hbm = pl.BlockSpec(memory_space=pl.ANY)
    vmem = pl.BlockSpec(memory_space=pltpu.VMEM)
    smem = pl.BlockSpec(memory_space=pltpu.SMEM)
    dma = pltpu.SemaphoreType.DMA
    modes = "".join(mode for modes in REDUCE_MODE for mode in modes.values())
    x_first, y_first = max(modes.count("x"), 1), max(modes.count("y"), 1)

    def low(*shape):
        return pltpu.VMEM(shape + (part, width), LOW)

    owned, totals, squares, input_grad = pl.pallas_call(
        reduce_body,
        out_shape=(
            jax.ShapeDtypeStruct((3, 4, part, width), LOW),
            jax.ShapeDtypeStruct((24, width), WIDE),
            jax.ShapeDtypeStruct((8, 128), WIDE),
            jax.ShapeDtypeStruct((sent_dev, 128, width), LOW),
        ),
        in_specs=[smem] + [hbm] * 10 + [vmem],
        out_specs=(hbm, vmem, vmem, hbm),
        scratch_shapes=[
            pltpu.VMEM((8, 768, TILE), LOW),
            pltpu.VMEM((8, 768, TILE), LOW),
            pltpu.VMEM((8, 768, TILE), LOW),
            pltpu.VMEM((6, 768, width), LOW),
            pltpu.VMEM((3, width, width), LOW),
            pltpu.VMEM((768, width), WIDE),
            pltpu.VMEM((768, width), LOW),
            low(2, 3, 8, 2),
            low(3, 8, 2),
            low(x_first, 2),
            low(y_first),
            low(y_first, 2),
            low(x_first),
            low(3, 2, 2),
            low(3, 3),
            low(3),
            low(3),
            low(3, 3),
            pltpu.VMEM((part, width), WIDE),
            low(3),
            pltpu.VMEM((6, 24, width), WIDE),
            pltpu.VMEM((5, 24, width), WIDE),
            pltpu.VMEM((8, 128), WIDE),
            pltpu.VMEM((4, 8, 128), WIDE),
            pltpu.VMEM((8, 8, 128), WIDE),
            dma((128,)),
            dma((48,)),
            dma((3, 8)),
            dma((x_first,)),
            dma((y_first,)),
            dma((y_first, 2)),
            dma((x_first,)),
            dma((3, 2)),
            dma((3, 3)),
            dma((3,)),
            dma((3,)),
            dma((5,)),
            dma((3, 4)),
            dma((4,)),
            dma((8,)),
            dma((4, 2)),
        ],
        compiler_params=params(collective_id=2, has_side_effects=True),
        name="reduce_gradients",
    )(owners, rows, out, left, *grads, right, matrices, d_resid, sums)
    return owned.reshape(3 * TILE, width), totals, squares, input_grad


def optimizer_body(
    len_ref, mem_ref, g_ref, sq_ref, tot_ref, w_ref, one_ref, two_ref, vw_ref, vone_ref, vtwo_ref,
    norm_ref, emb_ref, *rest,
):
    outs, clip_ref = rest[:-1], rest[-1]
    count = vw_ref.shape[0]

    @pl.when(pl.program_id(0) == 0)
    def _():
        gradient = tot_ref[:count]
        total = jnp.sum(sq_ref[...], keepdims=True) + jnp.sum(gradient * gradient, keepdims=True)
        norm = jnp.sqrt(total)
        norm_ref[...] = norm
        clip_ref[...] = jnp.broadcast_to(MAX_NORM / jnp.maximum(norm, MAX_NORM), clip_ref.shape)

    clip = clip_ref[...]

    def update(refs, outs, gradient, rate, decay):
        new = adam_step(refs[2][...], refs[0][...], refs[1][...], gradient, rate, decay)
        for ref, value in zip(outs, new + (new[2].astype(LOW),)):
            ref[...] = value

    update(
        (one_ref, two_ref, w_ref), outs[:4], g_ref[...].astype(WIDE) * clip,
        RATE_MATRIX, WEIGHT_DECAY,
    )

    @pl.when(pl.program_id(0) == 0)
    def _():
        update((vone_ref, vtwo_ref, vw_ref), outs[4:], tot_ref[:count] * clip, RATE_VECTOR, 0.0)
        groups, most = mem_ref.shape
        sentences = len_ref.shape[0]
        first = lax.axis_index("dp") * sentences
        pooled = [
            tot_ref[16 + s : 17 + s] / len_ref[s].astype(WIDE) for s in range(sentences)
        ]
        for g in range(groups):
            listed = jnp.int32(0)
            total = jnp.zeros_like(pooled[0])
            for m in range(most):
                listed += jnp.where(mem_ref[g, m] >= 0, 1, 0)
            for s in range(sentences):
                times = jnp.int32(0)
                for m in range(most):
                    times += jnp.where(mem_ref[g, m] == first + s, 1, 0)
                total = total + pooled[s] * times.astype(WIDE)
            emb_ref[g : g + 1] = total / listed.astype(WIDE)


def optimizer(lengths, members, owned, squares, totals, matrices, vectors):
    block_rows, width = owned.shape
    steps = 4 if block_rows % 64 == 0 else 3
    smem = pl.BlockSpec(memory_space=pltpu.SMEM)
    mat = pl.BlockSpec((block_rows // steps, width), lambda i: (i, 0))

    def whole(shape):
        return pl.BlockSpec(shape, lambda i: (0, 0))

    vec = whole(vectors[0].shape)
    embeddings = (members.shape[0], width)
    return pl.pallas_call(
        optimizer_body,
        grid=(steps,),
        in_specs=[smem, smem, mat, whole(squares.shape), whole(totals.shape)]
        + [mat] * 3
        + [vec] * 3,
        out_specs=(whole((1, 1)), whole(embeddings)) + (mat,) * 4 + (vec,) * 4,
        out_shape=(
            jax.ShapeDtypeStruct((1, 1), WIDE),
            jax.ShapeDtypeStruct(embeddings, WIDE),
        )
        + tuple(
            jax.ShapeDtypeStruct(like.shape, dtype)
            for like in (owned, vectors[0])
            for dtype in (WIDE, WIDE, WIDE, LOW)
        ),
        scratch_shapes=[pltpu.VMEM((1, width), WIDE)],
        compiler_params=params(),
        name="optimizer",
    )(lengths, members, owned, squares, totals, *matrices, *vectors)


def to_positions(value):
    width = value.shape[1]
    moved = jnp.concatenate(
        [value[:512].reshape(4, 128, width), value[512:].reshape(4, 64, width)], axis=1
    )
    moved = lax.all_to_all(moved, "seq", split_axis=0, concat_axis=0, tiled=True)
    rows = []
    for y in range(2):
        rows.append(moved[2 * y, :128])
        rows.append(jnp.concatenate([moved[2 * y, 128:], moved[2 * y + 1, 128:]], axis=0))
        rows.append(moved[2 * y + 1, :128])
    return jnp.stack(rows)


def to_rows(tokens):
    width = tokens.shape[-1]
    core = lax.axis_index("seq") % 2
    pieces = []
    for j in range(4):
        y, c = j // 2, j % 2
        pieces += [tokens[3 * y + 2 * c], tokens[3 * y + 1]]
    moved = jnp.concatenate(pieces, axis=0).reshape(4, 256, width)
    moved = lax.all_to_all(moved, "seq", split_axis=0, concat_axis=0, tiled=True)
    shared = moved[:, 128:].reshape(4, 2, 64, width)
    own = lax.dynamic_index_in_dim(shared, core, 1, keepdims=False)
    other = lax.dynamic_index_in_dim(shared, 1 - core, 1, keepdims=False)
    return jnp.concatenate(
        [moved[:, :128].reshape(512, width), own.reshape(256, width), other.reshape(256, width)],
        axis=0,
    )


def local(
    tokens,
    grad_out,
    lengths,
    members,
    owners,
    mat_master,
    mat_moment1,
    mat_moment2,
    vec_master,
    vec_moment1,
    vec_moment2,
):
    sent_dev, local_len, model_width = tokens.shape
    dp_count = lax.axis_size("dp")
    block_rows = mat_master.shape[0]
    direct = dp_count == 8 and block_rows == 3 * TILE

    if direct:
        blocks = owners
        weights, rows, qkv, matrices, attended, out_grad, lse = front(
            owners, lengths, mat_master, tokens, grad_out, vec_master
        )
    else:
        gathered = lax.all_gather(mat_master.astype(LOW), "dp", axis=0, tiled=True)
        weights = gathered.reshape(dp_count, block_rows, model_width)[owners]
        weights = weights.reshape(-1, TILE, model_width)
        rows = to_rows(tokens)
        blocks = jnp.arange(weights.shape[0] // 3, dtype=jnp.int32)
        qkv = qkv_project(blocks, rows, weights, vec_master)
        attended, lse, out_grad = attend(lengths, qkv, grad_out)
    result, left, right, d_attended, d_branch, d_resid, sums = middle(
        blocks, lengths, attended, rows, out_grad, weights, vec_master
    )
    dq, dk, dv, output = attend_back(
        lengths, qkv, lse, d_attended, attended, result, sent_dev
    )
    if direct:
        owned, totals, squares, input_grad = reduce_all(
            owners,
            rows,
            attended,
            left,
            (dq, dk, dv, d_branch),
            right,
            matrices,
            d_resid,
            sums,
            sent_dev,
        )
    else:
        grad_rows = grad_in(blocks, dq, dk, dv, d_resid, weights)
        grads = grad_ff(blocks, left, right)
        grads, sums_qv = grad_attn(blocks, rows, dq, dk, dv, attended, d_branch, grads)
        input_grad = to_positions(grad_rows)
        inverse = jnp.argsort(owners)
        grads = grads.reshape(dp_count, block_rows, model_width)[inverse]
        grads = grads.reshape(dp_count * block_rows, model_width)
        quarter = lax.psum_scatter(grads, ("dp", "seq"), scatter_dimension=0, tiled=True)
        owned = lax.all_gather(quarter, "seq", axis=0, tiled=True)
        quarter = quarter.astype(WIDE)
        group = lax.axis_index("seq") // 2
        core = lax.axis_index("seq") % 2
        place = jnp.arange(8)[:, None]
        pooled = jnp.where(place == 3 * group + 2 * core, sums[10:11], 0.0) + jnp.where(
            place == 3 * group + 1, sums[11:12], 0.0
        )
        pooled = lax.psum(pooled, "seq")
        local_vec = jnp.concatenate([sums_qv[0:2], sums[0:14]], axis=0)
        squares, vec_total = lax.psum(
            (jnp.sum(quarter * quarter), local_vec), ("dp", "seq")
        )
        squares = jnp.full((8, 128), squares / 1024.0)
        totals = jnp.concatenate([vec_total, pooled], axis=0)

    norm, embeddings, *new = optimizer(
        lengths,
        members,
        owned,
        squares,
        totals,
        (mat_master, mat_moment1, mat_moment2),
        (vec_master, vec_moment1, vec_moment2),
    )
    return (output, input_grad, embeddings, norm.reshape(()), *new)


def solution(mesh):
    placed = (
        P("dp", "seq", None),
        P("dp", "seq", None),
        P("dp"),
        P("dp", None),
        P(),
        P("dp", None),
        P("dp", None),
        P("dp", None),
        P(),
        P(),
        P(),
    )
    return jax.shard_map(
        local,
        mesh=mesh,
        in_specs=placed,
        out_specs=(
            P("dp", "seq", None),
            P("dp", "seq", None),
            P("dp", None),
            P(),
            P("dp", None),
            P("dp", None),
            P("dp", None),
            P("dp", None),
            P(),
            P(),
            P(),
            P(),
        ),
        check_vma=False,
    )
```

```python
import functools

import jax
import jax.numpy as jnp
from jax import lax
from jax.experimental import pallas as pl
from jax.experimental.pallas import tpu as pltpu
from jax.sharding import PartitionSpec as P

HEADS = 12
HEAD_DIM = 64
FEEDFWD_UNITS = 3072
STEP = 10


NORM_EPS = 1e-06
MASK_FILL = -1e30
MAX_NORM = 1.0
ADAM_ONE = 0.9
ADAM_TWO = 0.999
ADAM_EPS = 1e-08
WEIGHT_DECAY = 0.01
RATE_MATRIX = 0.04
RATE_VECTOR = 0.5

FWD_PAIRS = 6
BACK_PAIRS = 6
NORM_ROWS = 128
TILE = 384
VMEM_LIMIT = 60 * 1024 * 1024
MESH_ID = pl.DeviceIdType.MESH
LOW = jnp.bfloat16
WIDE = jnp.float32


def adam_step(master, moment_one, moment_two, gradient, learn_rate, decay_rate):
    moment_one = ADAM_ONE * moment_one + (1.0 - ADAM_ONE) * gradient
    moment_two = ADAM_TWO * moment_two + (1.0 - ADAM_TWO) * gradient * gradient
    scaled_one = moment_one / (1.0 - ADAM_ONE**STEP)
    scaled_two = moment_two / (1.0 - ADAM_TWO**STEP)
    master = master - learn_rate * (
        scaled_one / (jnp.sqrt(scaled_two) + ADAM_EPS) + decay_rate * master
    )
    return (moment_one, moment_two, master)


def dot_nn(left, right):
    return jnp.dot(left, right, preferred_element_type=WIDE)


def dot_nt(left, right):
    return lax.dot_general(
        left, right, (((1,), (1,)), ((), ())), preferred_element_type=WIDE
    )


def dot_tn(left, right):
    return lax.dot_general(
        left, right, (((0,), (0,)), ((), ())), preferred_element_type=WIDE
    )


def tile_at(owners, tile):
    return 3 * owners[tile // 3] + tile % 3


def params(**kwargs):
    return pltpu.CompilerParams(vmem_limit_bytes=VMEM_LIMIT, **kwargs)


GATHER_HEAD = 10
GATHER_ORDER = (
    ("tk",), ("xb", 1), ("xs", 0), ("zs", 0), ("zs", 2), ("xb", 0), ("r", 1, 0), ("r", 0, 0),
    ("xs", 1), ("r", 1, 2), ("zs", 1), ("xr", 1, 0), ("r", 0, 2), ("xb", 2), ("r", 1, 1),
    ("r", 2, 0), ("r", 2, 2), ("r", 0, 1), ("xs", 2), ("xob", 2), ("r", 2, 1), ("zx", 0),
    ("xo", 0), ("zx", 1), ("yr", 1, 2), ("xr", 1, 1), ("tf",), ("zx", 2), ("xr", 2, 0), ("xo", 2),
    ("yr", 2, 1), ("e1", 0), ("xob", 1), ("xr", 2, 2), ("yx", 1, 1), ("xo", 1), ("xr", 1, 2),
    ("xr", 2, 1), ("e1", 1), ("xsr", 0), ("yx", 1, 0), ("e1", 2), ("yx", 1, 2), ("yx", 2, 2),
    ("yr", 2, 0), ("yr", 1, 0), ("e2", 2), ("yr", 1, 1), ("xsr", 1), ("xob", 0), ("e2", 1),
    ("yx", 2, 0), ("xsr", 2), ("yr", 2, 2), ("e2", 0), ("yx", 2, 1),
)


def front_body(
    own_of_ref, len_ref, w_ref, x_ref, g_ref, vec_ref,
    weights_ref, rows_ref, qkv_ref, mats_ref, o_ref, gy_ref, lse_ref,
    wide_buf, own_buf, out_ref, xo_ref, qkv_buf, mats_buf, o_buf,
    send_sem, recv_sem, tok_recv, local_sem, ex_send, ex_recv, ex_local,
):
    dp, sq = lax.axis_index("dp"), lax.axis_index("seq")
    z, x = dp // 2, dp % 2
    y, c = sq // 2, sq % 2
    q, qc, qy, qyc = sq, sq ^ 1, sq ^ 2, sq ^ 3
    dev_c, dev_y, dev_yc, dev_x = (dp, sq ^ 1), (dp, sq ^ 2), (dp, sq ^ 3), (dp ^ 1, sq)
    dev_near = (dp ^ 2, sq)
    has_up, has_down, inner = z < 3, z > 0, (z > 0) & (z < 3)
    dev_up = (jnp.minimum(dp + 2, dp % 2 + 6), sq)
    dev_down = (jnp.maximum(dp - 2, dp % 2), sq)
    sources = (z ^ 1, jnp.where(z < 2, 2, 1), jnp.where(z < 2, 3, 0))
    used = [0, 0]
    started, locals_ = [], []

    def move(src, dst):
        copy = pltpu.make_async_copy(src, dst, local_sem.at[used[1]])
        used[1] += 1
        copy.start()
        return copy

    loads = []
    for at in (q, qy, qc, qyc):
        thirds = pl.ds(3 * at, 3)
        loads.append(move(w_ref.at[thirds], wide_buf.at[thirds]))

    barrier = pltpu.get_barrier_semaphore()

    def greet(device):
        pl.semaphore_signal(barrier, inc=1, device_id=device, device_id_type=MESH_ID)

    for device in (dev_c, dev_y, dev_yc, dev_x):
        greet(device)
    pl.when(has_up)(lambda: greet(dev_up))
    pl.when(has_down)(lambda: greet(dev_down))
    pl.semaphore_wait(barrier, 4 + jnp.where(inner, 2, 1))

    def send(src, dst, recv, device, pred=None):
        copy = pltpu.make_async_remote_copy(
            src_ref=src,
            dst_ref=dst,
            send_sem=send_sem.at[used[0]],
            recv_sem=recv,
            device_id=device,
            device_id_type=MESH_ID,
        )
        used[0] += 1
        if pred is None:
            copy.start()
        else:
            pl.when(pred)(lambda: copy.start())
        started.append((copy, pred))

    def piece(slot, quarter, h, device, pred=None, own=False):
        at = out_ref.at[slot, 3 * quarter + h]
        src = own_buf.at[3 * quarter + h] if own else at
        send(src, at, recv_sem.at[slot, quarter, h], device, pred)

    def arrived(slot, quarter, h):
        at = out_ref.at[slot, 3 * quarter + h]
        pltpu.make_async_copy(at, at, recv_sem.at[slot, quarter, h]).wait()

    def taken(slot, quarter, h):
        arrived(slot, quarter, h)
        piece(slot, quarter, h, dev_c)

    def near(k):
        return 2 * sources[k] + x

    def far(k):
        return 2 * sources[k] + 1 - x

    oy = 1 - y
    full_own, full_sib = 3 * y + 2 * c, 3 * y + 2 * (1 - c)
    full_far, full_cross = 3 * oy + 2 * c, 3 * oy + 2 * (1 - c)

    def full_rows(j):
        return xo_ref.at[pl.ds(128 * j, 128)]

    def half_rows(part, j, core):
        return xo_ref.at[pl.ds(512 + 256 * (part ^ core) + 64 * j, 64)]

    def token_send():
        send(x_ref.at[full_far], full_rows(sq), tok_recv.at[sq, 0], dev_y)
        for part in range(2):
            src = x_ref.at[3 * oy + 1, pl.ds(64 * part, 64)]
            send(src, half_rows(part, sq, c), tok_recv.at[sq, 1 + part], dev_y)
        send(x_ref.at[full_cross], full_rows(sq), tok_recv.at[sq, 0], dev_yc)
        send(x_ref.at[full_sib], full_rows(sq), tok_recv.at[sq, 0], dev_c)
        locals_.append(move(x_ref.at[full_own], full_rows(sq)))
        for part in range(2):
            src = x_ref.at[3 * y + 1, pl.ds(64 * part, 64)]
            send(src, half_rows(part, sq, 1 - c), tok_recv.at[sq, 1 + part], dev_c)
            locals_.append(move(src, half_rows(part, sq, c)))

    def token_forward():
        for part in range(2):
            at = half_rows(part, sq ^ 2, c)
            pltpu.make_async_copy(at, at, tok_recv.at[sq ^ 2, 1 + part]).wait()
            send(at, half_rows(part, sq ^ 2, 1 - c), tok_recv.at[sq ^ 2, 1 + part], dev_c)

    def own_line(h):
        piece(dp, q, h, dev_up, has_up, own=True)
        piece(dp, q, h, dev_down, has_down, own=True)

    def line(k, h):
        arrived(near(k), q, h)
        onward = (jnp.where(sources[k] < z, dev_up[0], dev_down[0]), sq)
        piece(near(k), q, h, onward, inner)
        if k > 0:
            piece(near(k), q, h, dev_x)
            piece(near(k), q, h, dev_y)
        piece(near(k), q, h, dev_c)

    def from_x_own(h):
        arrived(dp ^ 1, q, h)
        piece(dp ^ 1, q, h, dev_near)
        piece(dp ^ 1, q, h, dev_c)

    def near_other_half(h):
        arrived(near(0), qy, h)
        piece(near(0), qy, h, dev_x)
        piece(near(0), qy, h, dev_c)

    def from_x(k, h):
        arrived(far(k), q, h)
        piece(far(k), q, h, dev_y)
        piece(far(k), q, h, dev_c)

    steps = {
        "tk": token_send,
        "tf": token_forward,
        "zs": own_line,
        "zx": lambda h: piece(dp, qy, h, dev_near, own=True),
        "xs": lambda h: piece(dp, q, h, dev_x, own=True),
        "xb": lambda h: piece(dp, qy, h, dev_x, own=True),
        "r": line,
        "xo": from_x_own,
        "xob": lambda h: taken(dp ^ 1, qy, h),
        "e1": near_other_half,
        "e2": lambda h: taken(far(0), q, h),
        "yr": lambda k, h: taken(near(k), qy, h),
        "xr": from_x,
        "xsr": lambda h: taken(far(0), qy, h),
        "yx": lambda k, h: taken(far(k), qy, h),
    }

    def round_own(index, quarter):
        loads[index].wait()
        thirds = pl.ds(3 * quarter, 3)
        own_buf[thirds] = wide_buf[thirds].astype(LOW)

    round_own(0, q)
    round_own(1, qy)
    for name, *at in GATHER_ORDER[:GATHER_HEAD]:
        steps[name](*at)
    round_own(2, qc)
    round_own(3, qyc)
    locals_.append(move(own_buf, out_ref.at[dp]))
    for name, *at in GATHER_ORDER[GATHER_HEAD:]:
        steps[name](*at)
    exchange = Exchange(by_sentence(g_ref, gy_ref), ex_send, ex_recv, ex_local)
    exchange.start()
    for step in range(1, 8):
        for h in range(3):
            arrived(dp ^ step, qc, h)
            arrived(dp ^ step, qyc, h)
    for other in (sq ^ 1, sq ^ 2, sq ^ 3):
        at = full_rows(other)
        pltpu.make_async_copy(at, at, tok_recv.at[other, 0]).wait()
    for other in (sq ^ 1, sq ^ 3):
        for part in range(2):
            at = half_rows(part, other, c)
            pltpu.make_async_copy(at, at, tok_recv.at[other, 1 + part]).wait()
    for copy in locals_:
        copy.wait()
    stores = [move(out_ref.at[slot], weights_ref.at[slot]) for slot in range(8)]
    stores.append(move(xo_ref, rows_ref))

    for part in range(3):
        for half in range(2):
            tile = 2 * part + half
            held = out_ref[own_of_ref[tile // 3], 4 * (tile % 3) : 4 * (tile % 3) + 4]
            rows = slice(TILE * half, TILE * (half + 1))
            mats_buf[part, rows] = held.reshape(TILE, held.shape[-1])
        stores.append(move(mats_buf.at[part], mats_ref.at[part]))
        value = dot_nn(xo_ref[...], mats_buf[part])
        if part == 0:
            value = (value + vec_ref[0:1]) * HEAD_DIM ** (-0.5)
        elif part == 2:
            value = value + vec_ref[1:2]
        qkv_buf[part] = value.astype(LOW)
        stores.append(move(qkv_buf.at[part], qkv_ref.at[part]))

    def attend_block(block, carry):
        bias = key_bias(len_ref, block == 2)
        at = pl.ds(pl.multiple_of(256 * block, 256), 256)
        keys = pl.ds(pl.multiple_of(512 * (block // 2), 512), 512)
        for pair in range(qkv_buf.shape[-1] // 128):
            lanes = slice(128 * pair, 128 * (pair + 1))
            out, logs = attend_pair(
                qkv_buf[0, at, lanes], qkv_buf[1, keys, lanes], qkv_buf[2, keys, lanes], bias
            )
            o_buf[at, lanes] = out
            for head in range(2):
                lse_ref[pair, head : head + 1, at] = logs[head]
        return carry

    lax.fori_loop(0, 3, attend_block, 0)
    stores.append(move(o_buf, o_ref))
    exchange.finish()
    for copy in stores:
        copy.wait()
    for copy, pred in started:
        if pred is None:
            copy.wait_send()
        else:
            pl.when(pred)(lambda copy=copy: copy.wait_send())


def front(owners, lengths, block, tokens, grad_out, vectors):
    block_rows, width = block.shape
    part = block_rows // 12
    hbm = pl.BlockSpec(memory_space=pl.ANY)
    smem = pl.BlockSpec(memory_space=pltpu.SMEM)
    vmem = pl.BlockSpec(memory_space=pltpu.VMEM)
    dma = pltpu.SemaphoreType.DMA
    flat = jax.ShapeDtypeStruct((768, width), LOW)
    weights, *rest = pl.pallas_call(
        front_body,
        out_shape=(
            jax.ShapeDtypeStruct((8, 12, part, width), LOW),
            jax.ShapeDtypeStruct((1024, width), LOW),
            jax.ShapeDtypeStruct((3, 1024, width), LOW),
            jax.ShapeDtypeStruct((3, width, width), LOW),
            flat,
            flat,
            jax.ShapeDtypeStruct((HEADS // 2, 2, 768), WIDE),
        ),
        in_specs=[smem] * 2 + [hbm] * 3 + [vmem],
        out_specs=(hbm,) * 6 + (vmem,),
        scratch_shapes=[
            pltpu.VMEM((12, part, width), WIDE),
            pltpu.VMEM((12, part, width), LOW),
            pltpu.VMEM((8, 12, part, width), LOW),
            pltpu.VMEM((1024, width), LOW),
            pltpu.VMEM((3, 1024, width), LOW),
            pltpu.VMEM((3, width, width), LOW),
            pltpu.VMEM((768, width), LOW),
            dma((160,)),
            dma((8, 4, 3)),
            dma((4, 3)),
            dma((24,)),
        ]
        + EXCHANGE_SEMS,
        compiler_params=params(collective_id=1, has_side_effects=True),
        name="gather_attend",
    )(owners, lengths, block.reshape(12, part, width), tokens, grad_out, vectors)
    return weights.reshape(8 * block_rows // TILE, TILE, width), *rest


def qkv_body(map_ref, x_ref, top_ref, low_ref, vec_ref, out_ref):
    part = pl.program_id(0)
    scale = jnp.where(part == 0, HEAD_DIM ** (-0.5), 1.0)
    value = dot_nn(x_ref[:, :TILE], top_ref[0]) + dot_nn(x_ref[:, TILE:], low_ref[0])
    bias = jnp.where(part == 0, vec_ref[0:1], jnp.where(part == 2, vec_ref[1:2], 0.0))
    out_ref[0] = ((value + bias) * scale).astype(LOW)


def qkv_project(owners, rows, weights, vectors):
    count, width = rows.shape
    return pl.pallas_call(
        qkv_body,
        grid_spec=pltpu.PrefetchScalarGridSpec(
            num_scalar_prefetch=1,
            grid=(3,),
            in_specs=[
                pl.BlockSpec((count, width), lambda i, m: (0, 0)),
                pl.BlockSpec((1, TILE, width), lambda i, m: (tile_at(m, 2 * i), 0, 0)),
                pl.BlockSpec((1, TILE, width), lambda i, m: (tile_at(m, 2 * i + 1), 0, 0)),
                pl.BlockSpec(vectors.shape, lambda i, m: (0, 0)),
            ],
            out_specs=pl.BlockSpec((1, count, width), lambda i, m: (i, 0, 0)),
        ),
        out_shape=jax.ShapeDtypeStruct((3, count, width), LOW),
        compiler_params=params(),
        name="qkv",
    )(owners, rows, weights, weights, vectors)


def group_barrier(dp, sq):
    barrier = pltpu.get_barrier_semaphore()
    for step in range(1, 4):
        pl.semaphore_signal(
            barrier, inc=1, device_id=(dp, sq ^ step), device_id_type=MESH_ID
        )
    pl.semaphore_wait(barrier, 3)


class Exchange:
    def __init__(self, pieces, send_sem, recv_sem, local_sem):
        self.dp, self.sq = lax.axis_index("dp"), lax.axis_index("seq")
        self.pieces = pieces
        self.sems = (send_sem, recv_sem, local_sem)

    def copies(self):
        send_sem, recv_sem, local_sem = self.sems
        out = []
        for step in (2, 3, 1):
            target = self.sq ^ step
            for kind, (src, dst) in enumerate(self.pieces(self.sq, target)):
                out.append(
                    pltpu.make_async_remote_copy(
                        src_ref=src,
                        dst_ref=dst,
                        send_sem=send_sem.at[step - 1, kind],
                        recv_sem=recv_sem.at[self.sq, kind],
                        device_id=(self.dp, target),
                        device_id_type=MESH_ID,
                    )
                )
        for kind, (src, dst) in enumerate(self.pieces(self.sq, self.sq)):
            out.append(pltpu.make_async_copy(src, dst, local_sem.at[kind]))
        return out

    def start(self):
        for copy in self.copies():
            copy.start()

    def finish(self):
        copies = self.copies()
        for copy in copies[:6]:
            copy.wait_send()
        for copy in copies[6:]:
            copy.wait()
        for step in range(1, 4):
            source = self.sq ^ step
            for kind, (_, dst) in enumerate(self.pieces(source, self.sq)):
                pltpu.make_async_copy(dst, dst, self.sems[1].at[source, kind]).wait()


EXCHANGE_SEMS = [
    pltpu.SemaphoreType.DMA((3, 2)),
    pltpu.SemaphoreType.DMA((4, 2)),
    pltpu.SemaphoreType.DMA((2,)),
]


def by_sentence(src, dst):
    def pieces(source, target):
        y, c = target // 2, target % 2
        return (
            (src.at[3 * y + 2 * c], dst.at[pl.ds(128 * source, 128)]),
            (src.at[3 * y + 1, pl.ds(64 * c, 64)], dst.at[pl.ds(512 + 64 * source, 64)]),
        )

    return pieces


def by_position(src, dst):
    def pieces(source, target):
        y, c = source // 2, source % 2
        return (
            (src.at[pl.ds(128 * target, 128)], dst.at[3 * y + 2 * c]),
            (src.at[pl.ds(512 + 64 * target, 64)], dst.at[3 * y + 1, pl.ds(64 * c, 64)]),
        )

    return pieces


def sentence_length(lengths_ref, shared):
    sq = lax.axis_index("seq")
    group, core = sq // 2, sq % 2
    return jnp.where(shared, lengths_ref[3 * group + 1], lengths_ref[3 * group + 2 * core])


def positions(shape, shared, first=0):
    row = first + lax.broadcasted_iota(jnp.int32, shape, 0)
    own = lax.axis_index("seq") % 2
    half = row // 256
    part = row - 256 * half
    core = own + half - 2 * own * half
    mixed = (part // 64) * 128 + part % 64 + 64 * core
    return jnp.where(shared, mixed, row)


def key_bias(lengths_ref, shared):
    inside = positions((512, 128), shared) < sentence_length(lengths_ref, shared)
    bias = jnp.where(inside, 0.0, MASK_FILL)
    return jnp.concatenate([bias, bias], axis=1)


def head_masks(shape):
    lane = lax.broadcasted_iota(jnp.int32, shape, 1)
    return (lane < HEAD_DIM, lane >= HEAD_DIM)


def attend_pair(queries, keys, values, bias):
    value_t = values.T
    outs, logs = [], []
    for head, mask in enumerate(head_masks(queries.shape)):
        scores = dot_nt(keys, jnp.where(mask, queries, jnp.zeros_like(queries))) + bias
        top = jnp.max(scores, axis=0, keepdims=True)
        shifted = jnp.exp(scores - top)
        total = jnp.sum(shifted, axis=0, keepdims=True)
        part = value_t[HEAD_DIM * head : HEAD_DIM * (head + 1)]
        outs.append(dot_nn(part, shifted.astype(LOW)) * (1.0 / total))
        logs.append(top + jnp.log(total))
    return jnp.concatenate(outs, axis=0).T.astype(LOW), logs


def attend_body(
    len_ref, q_ref, k_ref, v_ref, g_ref, o_ref, lse_ref, gy_ref, send_sem, recv_sem, local_sem
):
    block, group = pl.program_id(0), pl.program_id(1)
    exchange = Exchange(by_sentence(g_ref, gy_ref), send_sem, recv_sem, local_sem)

    @pl.when((block == 0) & (group == 0))
    def _():
        group_barrier(exchange.dp, exchange.sq)
        exchange.start()

    bias = key_bias(len_ref, block == 2)
    for pair in range(q_ref.shape[-1] // 128):
        lanes = slice(128 * pair, 128 * (pair + 1))
        out, logs = attend_pair(q_ref[0, :, lanes], k_ref[0, :, lanes], v_ref[0, :, lanes], bias)
        o_ref[:, lanes] = out
        for head in range(2):
            lse_ref[0, 2 * pair + head : 2 * pair + head + 1, :] = logs[head]

    @pl.when((block == 2) & (group == pl.num_programs(1) - 1))
    def _():
        exchange.finish()


def attend(lengths, qkv, grad_out):
    width = qkv.shape[-1]
    groups = width // 128 // FWD_PAIRS
    lanes = 128 * FWD_PAIRS
    hbm = pl.BlockSpec(memory_space=pl.ANY)
    return pl.pallas_call(
        attend_body,
        grid=(3, groups),
        in_specs=[
            pl.BlockSpec(memory_space=pltpu.SMEM),
            pl.BlockSpec((1, 256, lanes), lambda i, h: (0, i, h)),
            pl.BlockSpec((1, 512, lanes), lambda i, h: (1, i // 2, h)),
            pl.BlockSpec((1, 512, lanes), lambda i, h: (2, i // 2, h)),
            hbm,
        ],
        out_specs=(
            pl.BlockSpec((256, lanes), lambda i, h: (i, h)),
            pl.BlockSpec((1, 2 * FWD_PAIRS, 256), lambda i, h: (h, 0, i)),
            hbm,
        ),
        out_shape=(
            jax.ShapeDtypeStruct((768, width), LOW),
            jax.ShapeDtypeStruct((groups, 2 * FWD_PAIRS, 768), WIDE),
            jax.ShapeDtypeStruct((768, width), LOW),
        ),
        scratch_shapes=EXCHANGE_SEMS,
        compiler_params=params(collective_id=3, has_side_effects=True),
        name="attend",
    )(lengths, qkv, qkv, qkv, grad_out)


def back_pair(queries, keys, values, grads, outs, logs, bias):
    keys_t = keys.T
    inner = (grads.astype(WIDE) * outs.astype(WIDE)).T
    d_query = []
    d_key = d_value = 0.0
    for head, mask in enumerate(head_masks(queries.shape)):
        query = jnp.where(mask, queries, jnp.zeros_like(queries))
        grad = jnp.where(mask, grads, jnp.zeros_like(grads))
        rows = slice(HEAD_DIM * head, HEAD_DIM * (head + 1))
        inner_sum = jnp.sum(inner[rows], axis=0, keepdims=True)
        scores = dot_nt(keys, query) + bias
        probs = jnp.exp(scores - logs[head : head + 1])
        d_probs = dot_nt(values, grad)
        d_scores = (probs * (d_probs - inner_sum)).astype(LOW)
        d_value = d_value + dot_nn(probs.astype(LOW), grad)
        d_key = d_key + dot_nn(d_scores, query)
        d_query.append(dot_nn(keys_t[rows], d_scores))
    d_query = jnp.concatenate(d_query, axis=0) * HEAD_DIM ** (-0.5)
    return d_query.T.astype(LOW), d_key, d_value


def attend_back_body(
    len_ref, q_ref, k_ref, v_ref, lse_ref, do_ref, o_ref, y_ref,
    dq_ref, dk_ref, dv_ref, out_ref,
    acc, keep, give, take, send_sem, recv_sem, local_sem, give_sem, take_sem,
):
    group, block = pl.program_id(0), pl.program_id(1)
    exchange = Exchange(by_position(y_ref, out_ref), send_sem, recv_sem, local_sem)
    dp, sq = exchange.dp, exchange.sq

    @pl.when((block == 0) & (group == 0))
    def _():
        group_barrier(dp, sq)
        exchange.start()

    bias = key_bias(len_ref, block == 0)
    d_keys, d_values = [], []
    for pair in range(q_ref.shape[-1] // 128):
        lanes = slice(128 * pair, 128 * (pair + 1))
        d_query, d_key, d_value = back_pair(
            q_ref[0, :, lanes], k_ref[0, :, lanes], v_ref[0, :, lanes], do_ref[:, lanes],
            o_ref[:, lanes], lse_ref[0, 2 * pair : 2 * pair + 2], bias,
        )
        dq_ref[:, lanes] = d_query
        d_keys.append((lanes, d_key))
        d_values.append((lanes, d_value))
    pairs = ((0, d_keys), (1, d_values))

    def swap(kind):
        return pltpu.make_async_remote_copy(
            src_ref=give.at[group, kind],
            dst_ref=take.at[group, kind],
            send_sem=give_sem.at[group, kind],
            recv_sem=take_sem.at[group, kind],
            device_id=(dp, sq ^ 1),
            device_id_type=MESH_ID,
        )

    @pl.when(block == 0)
    def _():
        for kind, parts in pairs:
            for lanes, part in parts:
                keep[kind, :, lanes] = part[:256]
                give[group, kind, :, lanes] = part[256:].astype(LOW)
            swap(kind).start()

    @pl.when(block == 1)
    def _():
        for kind, parts in pairs:
            for lanes, part in parts:
                acc[kind, :, lanes] = part

    @pl.when(block == 2)
    def _():
        for (kind, parts), ref in zip(pairs, (dk_ref, dv_ref)):
            swap(kind).wait()
            for lanes, part in parts:
                ref[:512, lanes] = (acc[kind, :, lanes] + part).astype(LOW)
                other = take[group, kind, :, lanes].astype(WIDE)
                ref[512:, lanes] = (keep[kind, :, lanes] + other).astype(LOW)

    @pl.when((block == 2) & (group == pl.num_programs(0) - 1))
    def _():
        exchange.finish()


def attend_back(lengths, qkv, lse, d_out, out, result, sent_dev):
    width = qkv.shape[-1]
    groups = width // 128 // BACK_PAIRS
    lanes = 128 * BACK_PAIRS
    hbm = pl.BlockSpec(memory_space=pl.ANY)
    query = pl.BlockSpec((256, lanes), lambda h, i: ((i + 2) % 3, h))
    keys = pl.BlockSpec((768, lanes), lambda h, i: (0, h))
    flat = jax.ShapeDtypeStruct((768, width), LOW)
    shared = lambda i: jnp.where(i == 0, 1, 0)
    return pl.pallas_call(
        attend_back_body,
        grid=(groups, 3),
        in_specs=[
            pl.BlockSpec(memory_space=pltpu.SMEM),
            pl.BlockSpec((1, 256, lanes), lambda h, i: (0, (i + 2) % 3, h)),
            pl.BlockSpec((1, 512, lanes), lambda h, i: (1, shared(i), h)),
            pl.BlockSpec((1, 512, lanes), lambda h, i: (2, shared(i), h)),
            pl.BlockSpec((1, 2 * BACK_PAIRS, 256), lambda h, i: (h, 0, (i + 2) % 3)),
            query,
            query,
            hbm,
        ],
        out_specs=(query, keys, keys, hbm),
        out_shape=(flat, flat, flat, jax.ShapeDtypeStruct((sent_dev, 128, width), LOW)),
        scratch_shapes=[
            pltpu.VMEM((2, 512, lanes), WIDE),
            pltpu.VMEM((2, 256, lanes), WIDE),
            pltpu.VMEM((groups, 2, 256, lanes), LOW),
            pltpu.VMEM((groups, 2, 256, lanes), LOW),
        ]
        + EXCHANGE_SEMS
        + [pltpu.SemaphoreType.DMA((groups, 2)), pltpu.SemaphoreType.DMA((groups, 2))],
        compiler_params=params(collective_id=4, has_side_effects=True),
        name="attend_back",
    )(lengths, qkv, qkv, qkv, lse.reshape(groups, 2 * BACK_PAIRS, 768), d_out, out, result)


def row_mean(value):
    return jnp.mean(value, axis=-1, keepdims=True)


def col_sum(value):
    return jnp.sum(value, axis=0, keepdims=True)


def middle_body(
    map_ref, len_ref, o_hbm, x_hbm, gy_hbm, w_ref, vec_ref,
    y_hbm, left_hbm, right_hbm, do_hbm, da_hbm, sums_ref,
    w_buf, o_buf, x_buf, gy_buf, left, right, slope, total, hat_one, rstd_one, low_buf,
    sem, in_sem, out_sem,
):
    count, width = o_buf.shape
    tiles = w_buf.shape[0]
    chunks = FEEDFWD_UNITS // width

    def fetch(t):
        return pltpu.make_async_copy(w_ref.at[tile_at(map_ref, 6 + t)], w_buf.at[t], sem.at[t])

    inputs = [
        pltpu.make_async_copy(src, dst, in_sem.at[i])
        for i, (src, dst) in enumerate(
            (
                (o_hbm, o_buf),
                (x_hbm.at[pl.ds(0, count)], x_buf),
                (gy_hbm, gy_buf),
            )
        )
    ]
    inputs[0].start()
    for t in range(2):
        fetch(t).start()
    inputs[1].start()
    for c in range(chunks):
        for t in (2 + 2 * c, 3 + 2 * c, 10 + 2 * c, 11 + 2 * c):
            fetch(t).start()
    inputs[2].start()
    outputs = []

    def put(src, dst):
        copy = pltpu.make_async_copy(src, dst, out_sem.at[len(outputs)])
        copy.start()
        outputs.append(copy)

    def put_left(t, value):
        for u in range(2):
            left[t + u] = value[:, TILE * u : TILE * (u + 1)]
            put(left.at[t + u], left_hbm.at[t + u])

    def ready(*which):
        for t in which:
            fetch(t).wait()

    def pair(t):
        return w_buf[t : t + 2].reshape(2 * TILE, width)

    def vec(row):
        return vec_ref[row : row + 1, :]

    def fold(value):
        return jnp.sum(value.reshape(-1, 8, width), axis=0)

    def over_rows(body, carried):
        zero = (jnp.zeros((8, width), WIDE),) * carried

        def step(i, carry):
            return body(pl.ds(pl.multiple_of(i * NORM_ROWS, NORM_ROWS), NORM_ROWS), i, carry)

        return lax.fori_loop(0, count // NORM_ROWS, step, zero)

    inputs[0].wait()
    ready(0, 1)
    total[...] = dot_nn(o_buf[...], pair(0))
    inputs[1].wait()

    def norm_one(at, i, carry):
        resid = x_buf[at].astype(WIDE) + (total[at] + vec(2))
        centered = resid - row_mean(resid)
        rstd = lax.rsqrt(row_mean(centered * centered) + NORM_EPS)
        rstd_one[at] = rstd
        hat = centered * rstd
        hat_one[at] = hat
        first = hat * vec(4) + vec(5)
        total[at] = first + vec(3)
        right[0, at] = first.astype(LOW)
        return carry

    over_rows(norm_one, 0)
    put(right.at[0], right_hbm.at[0])

    first_low = right[0]
    for c in range(chunks):
        ready(2 + 2 * c, 3 + 2 * c, 10 + 2 * c, 11 + 2 * c)
        act = dot_nt(first_low, pair(2 + 2 * c)) + vec(8 + c)
        cdf = 0.5 + 0.5 * lax.erf(act * (0.5**0.5))
        pdf = jnp.exp(-0.5 * act * act) * 0.3989422804014327
        slope[c] = cdf + act * pdf
        active = (act * cdf).astype(LOW)
        put_left(8 + 2 * c, active)
        total[...] += dot_nn(active, pair(10 + 2 * c))
    inputs[2].wait()

    def norm_two(at, i, carry):
        d_gain, d_shift, d_bias, pool_full, pool_half = carry
        resid = total[at]
        centered = resid - row_mean(resid)
        rstd = lax.rsqrt(row_mean(centered * centered) + NORM_EPS)
        hat = centered * rstd
        result = hat * vec(6) + vec(7)
        low_buf[0, at] = result.astype(LOW)
        shared = i * NORM_ROWS >= 512
        row = positions((NORM_ROWS, 128), shared, i * NORM_ROWS - jnp.where(shared, 512, 0))
        valid = jnp.where(row < sentence_length(len_ref, shared), 1.0, 0.0)
        pooled = fold(result * jnp.concatenate([valid] * (width // 128), axis=1))
        part = shared.astype(WIDE)
        grad = gy_buf[at].astype(WIDE)
        d_gain = d_gain + fold(grad * hat)
        d_shift = d_shift + fold(grad)
        grad = grad * vec(6)
        d_resid = rstd * (grad - row_mean(grad) - hat * row_mean(grad * hat))
        total[at] = d_resid
        grad_low = d_resid.astype(LOW)
        right[1, at] = grad_low
        return (
            d_gain,
            d_shift,
            d_bias + fold(grad_low.astype(WIDE)),
            pool_full + pooled * (1.0 - part),
            pool_half + pooled * part,
        )

    sums_ref[...] = jnp.zeros_like(sums_ref)
    found = over_rows(norm_two, 5)
    for row, value in zip((4, 5, 1, 10, 11), found):
        sums_ref[row : row + 1, :] = col_sum(value)
    put(low_buf.at[0], y_hbm)
    put(right.at[1], right_hbm.at[1])

    grad_low = right[1]
    for c in range(chunks):
        d_active = dot_nt(grad_low, pair(10 + 2 * c))
        d_act = (d_active * slope[c]).astype(LOW)
        put_left(2 * c, d_act)
        sums_ref[6 + c : 7 + c, :] = col_sum(d_act.astype(WIDE))
        total[...] += dot_nn(d_act, pair(2 + 2 * c))

    def norm_back(at, i, carry):
        d_gain, d_shift, d_bias = carry
        grad = total[at]
        hat = hat_one[at]
        d_gain = d_gain + fold(grad * hat)
        d_shift = d_shift + fold(grad)
        grad = grad * vec(4)
        d_resid = rstd_one[at] * (grad - row_mean(grad) - hat * row_mean(grad * hat))
        grad_low = d_resid.astype(LOW)
        low_buf[1, at] = grad_low
        return (d_gain, d_shift, d_bias + fold(grad_low.astype(WIDE)))

    found = over_rows(norm_back, 3)
    for row, value in zip((2, 3, 0), found):
        sums_ref[row : row + 1, :] = col_sum(value)
    put(low_buf.at[1], da_hbm)
    low_buf[2] = dot_nt(low_buf[1], pair(0)).astype(LOW)
    put(low_buf.at[2], do_hbm)
    for copy in outputs:
        copy.wait()


def middle(owners, lengths, attended, rows, out_grad, weights, vectors):
    count, width = attended.shape
    half = FEEDFWD_UNITS // TILE
    tiles = 2 + 2 * half
    hbm = pl.BlockSpec(memory_space=pl.ANY)
    smem = pl.BlockSpec(memory_space=pltpu.SMEM)
    vmem = pl.BlockSpec(memory_space=pltpu.VMEM)
    flat = jax.ShapeDtypeStruct((count, width), LOW)
    return pl.pallas_call(
        middle_body,
        in_specs=[smem, smem] + [hbm] * 4 + [vmem],
        out_specs=(hbm,) * 5 + (vmem,),
        out_shape=(
            flat,
            jax.ShapeDtypeStruct((2 * half, count, TILE), LOW),
            jax.ShapeDtypeStruct((2, count, width), LOW),
            flat,
            flat,
            jax.ShapeDtypeStruct((16, width), WIDE),
        ),
        scratch_shapes=[
            pltpu.VMEM((tiles, TILE, width), LOW),
            pltpu.VMEM((count, width), LOW),
            pltpu.VMEM((count, width), LOW),
            pltpu.VMEM((count, width), LOW),
            pltpu.VMEM((2 * half, count, TILE), LOW),
            pltpu.VMEM((2, count, width), LOW),
            pltpu.VMEM((half // 2, count, width), WIDE),
            pltpu.VMEM((count, width), WIDE),
            pltpu.VMEM((count, width), WIDE),
            pltpu.VMEM((count, 1), WIDE),
            pltpu.VMEM((3, count, width), LOW),
            pltpu.SemaphoreType.DMA((tiles,)),
            pltpu.SemaphoreType.DMA((3,)),
            pltpu.SemaphoreType.DMA((2 * half + 5,)),
        ],
        compiler_params=params(),
        name="feed_forward",
    )(owners, lengths, attended, rows, out_grad, weights, vectors)


def grad_ff_body(map_ref, left_ref, right_ref, out_ref):
    out_ref[0] = dot_tn(left_ref[0], right_ref[0]).astype(LOW)


def grad_ff(owners, left, right):
    per = FEEDFWD_UNITS // TILE
    count, width = right.shape[1:]
    return pl.pallas_call(
        grad_ff_body,
        grid_spec=pltpu.PrefetchScalarGridSpec(
            num_scalar_prefetch=1,
            grid=(2 * per,),
            in_specs=[
                pl.BlockSpec((1, count, TILE), lambda i, m: (i, 0, 0)),
                pl.BlockSpec((1, count, width), lambda i, m: (i // per, 0, 0)),
            ],
            out_specs=pl.BlockSpec((1, TILE, width), lambda i, m: (tile_at(m, 8 + i), 0, 0)),
        ),
        out_shape=jax.ShapeDtypeStruct((8 + 2 * per, TILE, width), LOW),
        compiler_params=params(),
        name="grad_ff",
    )(owners, left, right)


def grad_attn_body(
    map_ref, x_ref, dq_ref, dk_ref, dv_ref, o_ref, da_ref, into_ref, out_ref, sums_ref
):
    step = pl.program_id(0)
    for part, grad_ref in enumerate((dq_ref, dk_ref, dv_ref)):

        @pl.when(step // 2 == part)
        def _(grad_ref=grad_ref):
            out_ref[0] = dot_tn(x_ref[...], grad_ref[...]).astype(LOW)

    @pl.when(step // 2 == 3)
    def _():
        out_ref[0] = dot_tn(o_ref[...], da_ref[...]).astype(LOW)

    @pl.when(step == 0)
    def _():
        sums_ref[...] = jnp.zeros_like(sums_ref)
        sums_ref[0:1, :] = col_sum(dq_ref[...].astype(WIDE))
        sums_ref[1:2, :] = col_sum(dv_ref[...].astype(WIDE))


def grad_attn(owners, rows, dq, dk, dv, attended, da, into):
    count, width = dq.shape
    whole = pl.BlockSpec((count, width), lambda i, m: (0, 0))
    return pl.pallas_call(
        grad_attn_body,
        grid_spec=pltpu.PrefetchScalarGridSpec(
            num_scalar_prefetch=1,
            grid=(8,),
            in_specs=[
                pl.BlockSpec((count, TILE), lambda i, m: (0, i % 2)),
                whole,
                whole,
                whole,
                pl.BlockSpec((768, TILE), lambda i, m: (0, i % 2)),
                pl.BlockSpec((768, width), lambda i, m: (0, 0)),
                pl.BlockSpec(memory_space=pl.ANY),
            ],
            out_specs=(
                pl.BlockSpec((1, TILE, width), lambda i, m: (tile_at(m, i), 0, 0)),
                pl.BlockSpec((8, width), lambda i, m: (0, 0)),
            ),
        ),
        out_shape=(
            jax.ShapeDtypeStruct(into.shape, LOW),
            jax.ShapeDtypeStruct((8, width), WIDE),
        ),
        input_output_aliases={7: 0},
        compiler_params=params(),
        name="grad_attn",
    )(owners, rows, dq, dk, dv, attended, da, into)


def grad_in_body(map_ref, dq_ref, dk_ref, dv_ref, dh_ref, *refs):
    w_refs, out_ref = refs[:6], refs[6]
    for half in range(2):
        cols = slice(TILE * half, TILE * (half + 1))
        value = dh_ref[:, cols].astype(WIDE)
        for part, grad_ref in enumerate((dq_ref, dk_ref, dv_ref)):
            value = value + dot_nt(grad_ref[...], w_refs[2 * part + half][0])
        out_ref[:, cols] = value.astype(LOW)


def grad_in(owners, dq, dk, dv, dh, weights):
    count, width = dq.shape
    block = pl.BlockSpec((256, width), lambda i, m: (i, 0))
    return pl.pallas_call(
        grad_in_body,
        grid_spec=pltpu.PrefetchScalarGridSpec(
            num_scalar_prefetch=1,
            grid=(count // 256,),
            in_specs=[block] * 4
            + [
                pl.BlockSpec((1, TILE, width), lambda i, m, t=t: (tile_at(m, t), 0, 0)) for t in range(6)
            ],
            out_specs=block,
        ),
        out_shape=jax.ShapeDtypeStruct((count, width), LOW),
        compiler_params=params(),
        name="grad_in",
    )(owners, dq, dk, dv, dh, *([weights] * 6))


REDUCE_MODE = (
    {"n": "z", "a": "x", "e": "y", "o": "x"},
    {"n": "z", "a": "y", "e": "y", "o": "y"},
    {"n": "z", "a": "x", "e": "x", "o": "x"},
)
REDUCE_ORDER = (
    ("part", "n", "f", 1), ("part", "e", "f", 1), ("part", "e", "n", 1), ("both", "n", "f", 1),
    ("part", "a", "n", 1), ("both", "e", "f", 1), ("part", "a", "f", 0), ("vs", 0),
    ("part", "n", "f", 2), ("both", "a", "n", 1), ("both", "e", "n", 1), ("part", "n", "n", 1),
    ("both", "a", "f", 0), ("both", "n", "f", 2), ("va", 0), ("vs", 1), ("part", "a", "f", 2),
    ("part", "e", "f", 0), ("part", "n", "n", 2), ("both", "n", "n", 1), ("both", "a", "f", 2),
    ("turn", "n", 1), ("part", "o", "n", 1), ("both", "e", "f", 0), ("part", "a", "f", 1),
    ("part", "e", "n", 0), ("part", "o", "f", 1), ("both", "a", "f", 1), ("both", "n", "n", 2),
    ("part", "e", "f", 2), ("both", "o", "f", 1), ("part", "a", "n", 2), ("both", "e", "n", 0),
    ("both", "e", "f", 2), ("part", "n", "n", 0), ("turn", "e", 1), ("both", "a", "n", 2),
    ("turn", "a", 2), ("part", "n", "f", 0), ("both", "o", "n", 1), ("own", "n", 1),
    ("part", "o", "f", 2), ("own", "f", 1), ("both", "n", "f", 0), ("part", "a", "n", 0),
    ("part", "e", "n", 2), ("both", "o", "f", 2), ("own", "f", 2), ("part", "o", "n", 2),
    ("both", "e", "n", 2), ("both", "n", "n", 0), ("turn", "e", 2), ("both", "a", "n", 0),
    ("turn", "n", 2), ("gin",), ("in",), ("turn", "a", 1), ("part", "o", "f", 0),
    ("part", "o", "n", 0), ("turn", "n", 0), ("turn", "e", 0), ("turn", "a", 0), ("on", "e", 1),
    ("va", 1), ("both", "o", "n", 0), ("on", "n", 2), ("both", "o", "n", 2), ("own", "n", 0),
    ("both", "o", "f", 0), ("own", "f", 0), ("on", "a", 2), ("own", "n", 2), ("turn", "o", 2),
    ("on", "e", 2), ("on", "n", 0), ("turn", "o", 1), ("on", "a", 1), ("on", "n", 1), ("vs", 2),
    ("turn", "o", 0), ("on", "e", 0), ("end", 1), ("on", "a", 0), ("va", 2), ("vs", 3), ("end", 2),
    ("va", 3), ("vs", 4), ("end", 0), ("va", 4),
)


def reduce_body(
    own_of_ref, len_ref, x_ref, o_ref, left_ref, qkv_ref, do_ref, da_ref, right_ref,
    w_ref, y_ref, lse_ref, sums_ref, own_ref, vt_ref, sq_ref, gi_ref, out_ref,
    left_0, left_1, left_2, rbuf, wbuf, gbuf, give, take, pbuf, core_in, x_two, x_one, y_two, y_one,
    zf_in, mid_in, fin_in, near_in, ebuf, tbuf, tlow, vbuf, v_in, s_own, s_seq, s_dp,
    send_sem, local_sem, core_sem, xtwo_sem, xone_sem, ytwo_sem, yone_sem,
    zf_sem, mid_sem, fin_sem, near_sem, v_sem, out_sem, seq_sem, dp_sem, in_sem,
    give_sem, take_sem, free_sem, ex_send, ex_recv, ex_local,
):
    dp, sq = lax.axis_index("dp"), lax.axis_index("seq")
    z, x = dp // 2, dp % 2
    y, c = sq // 2, sq % 2
    dev_c, dev_y, dev_yc, dev_x = (dp, sq ^ 1), (dp, sq ^ 2), (dp, sq ^ 3), (dp ^ 1, sq)
    dev_near = (dp ^ 2, sq)
    inner = (z > 0) & (z < 3)
    outer = jnp.logical_not(inner)
    place = {
        "n": z ^ 1,
        "a": jnp.where(z < 2, 2, 1),
        "e": jnp.where(z < 2, 3, 0),
        "o": z,
    }
    lefts = (left_0, left_1, left_2)
    used = [0, 0]
    remotes, own_moves = [], []

    def move(src, dst):
        copy = pltpu.make_async_copy(src, dst, local_sem.at[used[1]])
        used[1] += 1
        copy.start()
        return copy

    first_loads = [
        move(qkv_ref.at[0, pl.ds(0, 768)], wbuf.at[0]),
        move(do_ref, wbuf.at[1]),
        move(o_ref, wbuf.at[2]),
        move(qkv_ref.at[1], core_in.at[pl.ds(0, 1024)]),
        move(qkv_ref.at[2], core_in.at[pl.ds(1024, 1024)]),
    ]

    loads = {"right": [move(right_ref, rbuf.at[pl.ds(4, 2)]), move(da_ref, rbuf.at[3])]}
    for t in range(3):
        loads[t] = []
        for block in range(8):
            tile = 3 * block + t
            cols = pl.ds(TILE * (tile % 2), TILE)
            if tile < 6:
                src = x_ref.at[pl.ds(0, 768), cols]
            elif tile < 8:
                src = o_ref.at[:, cols]
            else:
                src = left_ref.at[tile - 8]
            loads[t].append(move(src, lefts[t].at[block]))

    def loaded(name):
        for copy in loads.pop(name, ()):
            copy.wait()

    barrier = pltpu.get_barrier_semaphore()
    for step in range(1, 4):
        pl.semaphore_signal(
            barrier, inc=1, device_id=(dp, sq ^ step), device_id_type=MESH_ID
        )
    for step in range(1, 8):
        pl.semaphore_signal(
            barrier, inc=1, device_id=(dp ^ step, sq), device_id_type=MESH_ID
        )
    pl.semaphore_wait(barrier, 10)

    def send(src, dst, recv, device, pred=None):
        copy = pltpu.make_async_remote_copy(
            src_ref=src,
            dst_ref=dst,
            send_sem=send_sem.at[used[0]],
            recv_sem=recv,
            device_id=device,
            device_id_type=MESH_ID,
        )
        used[0] += 1
        if pred is None:
            copy.start()
        else:
            pl.when(pred)(lambda: copy.start())
        remotes.append((copy, pred))

    def arrived(at, sem):
        pltpu.make_async_copy(at, at, sem).wait()

    def wide(ref, *at):
        return ref[at].astype(WIDE)

    exchange = Exchange(by_position(y_ref, out_ref), ex_send, ex_recv, ex_local)
    exchange.start()
    for copy in first_loads:
        copy.wait()

    def swap(pair, kind):
        return pltpu.make_async_remote_copy(
            src_ref=give.at[pair, kind],
            dst_ref=take.at[pair, kind],
            send_sem=give_sem.at[pair, kind],
            recv_sem=take_sem.at[pair, kind],
            device_id=dev_c,
            device_id_type=MESH_ID,
        )

    def attend_heads(pair, carry):
        lanes = pl.ds(pl.multiple_of(128 * pair, 128), 128)
        sums = []
        for block in (2, 0, 1):
            rows = pl.ds(256 * block, 256)
            first = 512 * (block // 2)
            d_query, d_key, d_value = back_pair(
                wbuf[0, rows, lanes],
                core_in[first : first + 512, lanes],
                core_in[1024 + first : 1536 + first, lanes],
                wbuf[1, rows, lanes],
                wbuf[2, rows, lanes],
                lse_ref[pair, :, rows],
                key_bias(len_ref, block == 2),
            )
            rbuf[0, rows, lanes] = d_query
            if block == 2:
                for kind, part in enumerate((d_key, d_value)):
                    rbuf[1 + kind, pl.ds(512, 256), lanes] = part[:256].astype(LOW)
                    give[pair, kind] = part[256:].astype(LOW)
                    swap(pair, kind).start()
            else:
                sums.append((d_key, d_value))
        for kind in range(2):
            total = sums[0][kind] + sums[1][kind]
            rbuf[1 + kind, pl.ds(0, 512), lanes] = total.astype(LOW)
        return carry

    pairs = rbuf.shape[-1] // 128
    lax.fori_loop(0, pairs, attend_heads, 0)
    pl.semaphore_signal(free_sem, inc=1, device_id=dev_c, device_id_type=MESH_ID)
    loads["in"] = [move(w_ref, wbuf)]
    for pair in range(pairs):
        lanes = slice(128 * pair, 128 * (pair + 1))
        for kind in range(2):
            swap(pair, kind).wait()
            rows = pl.ds(512, 256)
            rbuf[1 + kind, rows, lanes] = (
                rbuf[1 + kind, rows, lanes].astype(WIDE) + take[pair, kind].astype(WIDE)
            ).astype(LOW)
    loaded("right")
    pl.semaphore_wait(free_sem, 1)

    partners = (dev_c, dev_y, dev_x, (dp ^ 2, sq), (dp ^ 4, sq))

    def vec_send(step):
        if step == 0:
            vbuf[0] = jnp.zeros(vbuf.shape[1:], WIDE)
            vbuf[0, 0:1] = col_sum(wide(rbuf, 0))
            vbuf[0, 1:2] = col_sum(wide(rbuf, 2))
            vbuf[0, 2:12] = sums_ref[0:10]
            vbuf[0, pl.ds(16 + 3 * y + 2 * c, 1)] = sums_ref[10:11]
            vbuf[0, pl.ds(16 + 3 * y + 1, 1)] = sums_ref[11:12]
        send(vbuf.at[step], v_in.at[step], v_sem.at[step], partners[step])

    def vec_add(step):
        arrived(v_in.at[step], v_sem.at[step])
        vbuf[step + 1] = vbuf[step] + v_in[step]

    def input_grad():
        loaded("in")
        for part in range(3):
            cols = slice(256 * part, 256 * (part + 1))
            value = wide(rbuf, 3, slice(None), cols)
            for index in range(3):
                value = value + dot_nt(rbuf[index], wbuf[index, cols])
            gbuf[:, cols] = value.astype(LOW)

    def in_full(j):
        return gbuf.at[pl.ds(128 * j, 128)], gi_ref.at[3 * y + 2 * c]

    def in_half(j):
        return gbuf.at[pl.ds(512 + 64 * j, 64)], gi_ref.at[3 * y + 1, pl.ds(64 * c, 64)]

    def input_send():
        for device in (dev_y, dev_yc, dev_c):
            for kind, pair in enumerate((in_full(device[1]), in_half(device[1]))):
                send(pair[0], pair[1], in_sem.at[sq, kind], device)
        own_moves.append(move(*in_full(sq)))
        own_moves.append(move(*in_half(sq)))

    def standard_of(slot):
        found = jnp.int32(0)
        for block in range(8):
            found = jnp.maximum(found, jnp.where(own_of_ref[block] == slot, block, 0))
        return found

    def slot_of(k, p):
        return 2 * place[k] + (x if p == "n" else 1 - x)

    def core_at(slot, t, half):
        first = 96 * (2 * (8 * t + slot) + half)
        return core_in.at[pl.ds(pl.multiple_of(first, 96), 96)]

    def partial(k, p, t):
        loaded(t)
        slot = slot_of(k, p)
        block = standard_of(slot)
        tile = 3 * block + t
        right = jnp.where(tile < 8, tile // 2, 4 + (tile - 8) // 8)
        value = dot_tn(lefts[t][block], rbuf[right]).astype(LOW)
        for quarter in range(4):
            rows = slice(96 * quarter, 96 * (quarter + 1))
            pbuf[quarter % 2, t, slot, quarter // 2] = value[rows]
        for half in range(2):
            src = pbuf.at[1 - c, t, slot, half]
            send(src, core_at(slot, t, half), core_sem.at[t, slot, half], dev_c)

    def held(*at):
        return pbuf.at[(c, *at)]

    index_of = {"x": {}, "y": {}, "z": {}}
    for t in range(3):
        for k in "naeo":
            found = index_of[REDUCE_MODE[t][k]]
            found[k, t] = len(found)

    def first_send(k, p, t):
        slot = slot_of(k, p)
        if REDUCE_MODE[t][k] == "y":
            at, half = index_of["y"][k, t], "nf".index(p)
            send(held(t, slot, 1 - y), y_two.at[at, half], ytwo_sem.at[at, half], dev_y)
        elif p == "f":
            at = index_of["x"][k, t]
            send(held(t, slot), x_two.at[at], xtwo_sem.at[at], dev_x)

    def both_cores(k, p, t):
        slot = slot_of(k, p)
        for half in range(2):
            arrived(core_at(slot, t, half), core_sem.at[t, slot, half])
            other = core_at(slot, t, half)[...].astype(WIDE)
            pbuf[c, t, slot, half] = (wide(pbuf, c, t, slot, half) + other).astype(LOW)
        if REDUCE_MODE[t][k] == "z":
            half = "nf".index(p)
            send(held(t, slot), zf_in.at[t, half], zf_sem.at[t, half], dev_near)
        elif k != "o":
            first_send(k, p, t)

    def own_block(p, t):
        if REDUCE_MODE[t]["n"] == "z":
            slot, half = slot_of("o", p), "nf".index(p)
            arrived(zf_in.at[t, half], zf_sem.at[t, half])
            pbuf[c, t, slot] = (wide(pbuf, c, t, slot) + wide(zf_in, t, half)).astype(LOW)
        first_send("o", p, t)

    def turn(k, t):
        mode = REDUCE_MODE[t][k]
        if mode == "z":
            return
        at = index_of[mode][k, t]
        near, far = slot_of(k, "n"), slot_of(k, "f")
        if mode == "y":
            for half in range(2):
                arrived(y_two.at[at, half], ytwo_sem.at[at, half])
            pbuf[c, t, far, y] = (wide(pbuf, c, t, far, y) + wide(y_two, at, 1)).astype(LOW)
            send(held(t, far, y), x_one.at[at], xone_sem.at[at], dev_x)
        else:
            arrived(x_two.at[at], xtwo_sem.at[at])
            pbuf[c, t, near] = (wide(pbuf, c, t, near) + wide(x_two, at)).astype(LOW)
            send(held(t, near, 1 - y), y_one.at[at], yone_sem.at[at], dev_y)

    def plane_sum(k, t):
        mode = REDUCE_MODE[t][k]
        at = index_of[mode][k, t]
        mine = wide(pbuf, c, t, slot_of(k, "n"), y)
        if mode == "y":
            arrived(x_one.at[at], xone_sem.at[at])
            return mine + wide(y_two, at, 0) + wide(x_one, at)
        arrived(y_one.at[at], yone_sem.at[at])
        return mine + wide(y_one, at)

    def onward(k, t):
        if REDUCE_MODE[t][k] == "z":
            return
        row = "nae".index(k)
        tbuf[...] = plane_sum(k, t)
        if k == "n":
            ebuf[row, t] = tbuf[...].astype(LOW)
            send(ebuf.at[row, t], near_in.at[t], near_sem.at[t], dev_near)
            return

        line = "ae".index(k)

        @pl.when(inner)
        def _():
            arrived(mid_in.at[line, t], mid_sem.at[line, t])
            tbuf[...] += wide(mid_in, line, t)

        ebuf[row, t] = tbuf[...].astype(LOW)
        owner = (2 * place[k] + x, sq)
        send(ebuf.at[row, t], fin_in.at[t], fin_sem.at[t], owner, inner)
        send(ebuf.at[row, t], mid_in.at[line, t], mid_sem.at[line, t], dev_near, outer)

    squares = []

    def finish(t):
        value = plane_sum("o", t)
        if REDUCE_MODE[t]["n"] != "z":
            arrived(near_in.at[t], near_sem.at[t])
            value = value + wide(near_in, t)
        arrived(fin_in.at[t], fin_sem.at[t])
        total = (value + wide(fin_in, t)).astype(LOW)
        tlow[t] = total
        wide_total = total.astype(WIDE)
        rows = (wide_total * wide_total).reshape(-1, 8, wide_total.shape[-1])
        squares.append(jnp.sum(rows, axis=0))
        at = own_ref.at[t, sq]
        for device in (dev_y, dev_c):
            send(tlow.at[t], at, out_sem.at[t, sq], device)
        own_moves.append(move(tlow.at[t], at))

    steps = {
        "part": partial,
        "both": both_cores,
        "own": own_block,
        "turn": turn,
        "on": onward,
        "end": finish,
        "vs": vec_send,
        "va": vec_add,
        "gin": input_grad,
        "in": input_send,
    }
    for name, *at in REDUCE_ORDER:
        steps[name](*at)

    squares = squares[0] + squares[1] + squares[2]
    folded = squares[:, :128]
    for lane in range(1, squares.shape[-1] // 128):
        folded = folded + squares[:, 128 * lane : 128 * (lane + 1)]
    s_own[...] = folded
    for step in range(1, 4):
        send(s_own, s_seq.at[sq], seq_sem.at[sq], (dp, sq ^ step))
    s_seq[sq] = folded
    for t in [at[0] for name, *at in REDUCE_ORDER if name == "end"]:
        arrived(own_ref.at[t, sq ^ 2], out_sem.at[t, sq ^ 2])
        send(own_ref.at[t, sq ^ 2], own_ref.at[t, sq ^ 2], out_sem.at[t, sq ^ 2], dev_c)
    for step in range(1, 4):
        arrived(s_seq.at[sq ^ step], seq_sem.at[sq ^ step])
    group = s_seq[0] + s_seq[1] + s_seq[2] + s_seq[3]
    s_dp[dp] = group
    for step in range(1, 8):
        send(s_dp.at[dp], s_dp.at[dp], dp_sem.at[dp], (dp ^ step, sq))
    for step in range(1, 8):
        arrived(s_dp.at[dp ^ step], dp_sem.at[dp ^ step])
    everyone = s_dp[0]
    for index in range(1, 8):
        everyone = everyone + s_dp[index]
    sq_ref[...] = everyone
    vt_ref[0:16] = vbuf[5][0:16]
    vt_ref[16:24] = vbuf[2][16:24]

    for t in range(3):
        arrived(own_ref.at[t, sq ^ 1], out_sem.at[t, sq ^ 1])
        arrived(own_ref.at[t, sq ^ 3], out_sem.at[t, sq ^ 3])
    for step in range(1, 4):
        other = sq ^ step
        there, member = other // 2, other % 2
        arrived(gi_ref.at[3 * there + 2 * member], in_sem.at[other, 0])
        arrived(gi_ref.at[3 * there + 1, pl.ds(64 * member, 64)], in_sem.at[other, 1])
    exchange.finish()
    for copy in own_moves:
        copy.wait()
    for copy, pred in remotes:
        if pred is None:
            copy.wait_send()
        else:
            pl.when(pred)(lambda copy=copy: copy.wait_send())


def reduce_all(
    owners, lengths, rows, out, left, qkv, d_out, d_branch, right, matrices, result, lse, sums,
    sent_dev,
):
    width = rows.shape[-1]
    part = TILE // 4
    hbm = pl.BlockSpec(memory_space=pl.ANY)
    vmem = pl.BlockSpec(memory_space=pltpu.VMEM)
    smem = pl.BlockSpec(memory_space=pltpu.SMEM)
    dma = pltpu.SemaphoreType.DMA
    modes = "".join(mode for modes in REDUCE_MODE for mode in modes.values())
    x_first, y_first = max(modes.count("x"), 1), max(modes.count("y"), 1)

    def low(*shape):
        return pltpu.VMEM(shape + (part, width), LOW)

    owned, totals, squares, input_grad, output = pl.pallas_call(
        reduce_body,
        out_shape=(
            jax.ShapeDtypeStruct((3, 4, part, width), LOW),
            jax.ShapeDtypeStruct((24, width), WIDE),
            jax.ShapeDtypeStruct((8, 128), WIDE),
            jax.ShapeDtypeStruct((sent_dev, 128, width), LOW),
            jax.ShapeDtypeStruct((sent_dev, 128, width), LOW),
        ),
        in_specs=[smem] * 2 + [hbm] * 9 + [vmem] * 2,
        out_specs=(hbm, vmem, vmem, hbm, hbm),
        scratch_shapes=[
            pltpu.VMEM((8, 768, TILE), LOW),
            pltpu.VMEM((8, 768, TILE), LOW),
            pltpu.VMEM((8, 768, TILE), LOW),
            pltpu.VMEM((6, 768, width), LOW),
            pltpu.VMEM((3, width, width), LOW),
            pltpu.VMEM((768, width), LOW),
            pltpu.VMEM((width // 128, 2, 256, 128), LOW),
            pltpu.VMEM((width // 128, 2, 256, 128), LOW),
            low(2, 3, 8, 2),
            pltpu.VMEM((48 * part, width), LOW),
            low(x_first, 2),
            low(y_first),
            low(y_first, 2),
            low(x_first),
            low(3, 2, 2),
            low(2, 3),
            low(3),
            low(3),
            low(3, 3),
            pltpu.VMEM((part, width), WIDE),
            low(3),
            pltpu.VMEM((6, 24, width), WIDE),
            pltpu.VMEM((5, 24, width), WIDE),
            pltpu.VMEM((8, 128), WIDE),
            pltpu.VMEM((4, 8, 128), WIDE),
            pltpu.VMEM((8, 8, 128), WIDE),
            dma((160,)),
            dma((48,)),
            dma((3, 8, 2)),
            dma((x_first,)),
            dma((y_first,)),
            dma((y_first, 2)),
            dma((x_first,)),
            dma((3, 2)),
            dma((2, 3)),
            dma((3,)),
            dma((3,)),
            dma((5,)),
            dma((3, 4)),
            dma((4,)),
            dma((8,)),
            dma((4, 2)),
            dma((width // 128, 2)),
            dma((width // 128, 2)),
            pltpu.SemaphoreType.REGULAR,
        ]
        + EXCHANGE_SEMS,
        compiler_params=params(collective_id=2, has_side_effects=True),
        name="reduce_gradients",
    )(
        owners, lengths, rows, out, left, qkv, d_out, d_branch, right, matrices, result, lse, sums
    )
    return owned.reshape(3 * TILE, width), totals, squares, input_grad, output


def optimizer_body(
    len_ref, mem_ref, g_ref, sq_ref, tot_ref, w_ref, one_ref, two_ref, vw_ref, vone_ref, vtwo_ref,
    out_from, in_from, norm_ref, emb_ref, *rest,
):
    outs, (out_to, in_to, clip_ref) = rest[:-3], rest[-3:]
    count = vw_ref.shape[0]

    out_to[...] = out_from[...]
    in_to[...] = in_from[...]

    @pl.when(pl.program_id(0) == 0)
    def _():
        gradient = tot_ref[:count]
        total = jnp.sum(sq_ref[...], keepdims=True) + jnp.sum(gradient * gradient, keepdims=True)
        norm = jnp.sqrt(total)
        norm_ref[...] = norm
        clip_ref[...] = jnp.broadcast_to(MAX_NORM / jnp.maximum(norm, MAX_NORM), clip_ref.shape)

    clip = clip_ref[...]

    def update(refs, outs, gradient, rate, decay):
        new = adam_step(refs[2][...], refs[0][...], refs[1][...], gradient, rate, decay)
        for ref, value in zip(outs, new + (new[2].astype(LOW),)):
            ref[...] = value

    update(
        (one_ref, two_ref, w_ref), outs[:4], g_ref[...].astype(WIDE) * clip,
        RATE_MATRIX, WEIGHT_DECAY,
    )

    @pl.when(pl.program_id(0) == 0)
    def _():
        update((vone_ref, vtwo_ref, vw_ref), outs[4:], tot_ref[:count] * clip, RATE_VECTOR, 0.0)
        groups, most = mem_ref.shape
        sentences = len_ref.shape[0]
        first = lax.axis_index("dp") * sentences
        pooled = [
            tot_ref[16 + s : 17 + s] / len_ref[s].astype(WIDE) for s in range(sentences)
        ]
        for g in range(groups):
            listed = jnp.int32(0)
            total = jnp.zeros_like(pooled[0])
            for m in range(most):
                listed += jnp.where(mem_ref[g, m] >= 0, 1, 0)
            for s in range(sentences):
                times = jnp.int32(0)
                for m in range(most):
                    times += jnp.where(mem_ref[g, m] == first + s, 1, 0)
                total = total + pooled[s] * times.astype(WIDE)
            emb_ref[g : g + 1] = total / listed.astype(WIDE)


def optimizer(lengths, members, owned, squares, totals, matrices, vectors, exchanged):
    block_rows, width = owned.shape
    steps = 4 if block_rows % 64 == 0 else 1
    smem = pl.BlockSpec(memory_space=pltpu.SMEM)
    mat = pl.BlockSpec((block_rows // steps, width), lambda i: (i, 0))

    def whole(shape):
        return pl.BlockSpec(shape, lambda i: (0, 0))

    sentences, positions_here = exchanged[0].shape[:2]
    passed = pl.BlockSpec((sentences, positions_here // steps, width), lambda i: (0, i, 0))
    vec = whole(vectors[0].shape)
    embeddings = (members.shape[0], width)
    return pl.pallas_call(
        optimizer_body,
        grid=(steps,),
        in_specs=[smem, smem, mat, whole(squares.shape), whole(totals.shape)]
        + [mat] * 3
        + [vec] * 3
        + [passed] * 2,
        out_specs=(whole((1, 1)), whole(embeddings)) + (mat,) * 4 + (vec,) * 4
        + (passed,) * 2,
        out_shape=(
            jax.ShapeDtypeStruct((1, 1), WIDE),
            jax.ShapeDtypeStruct(embeddings, WIDE),
        )
        + tuple(
            jax.ShapeDtypeStruct(like.shape, dtype)
            for like in (owned, vectors[0])
            for dtype in (WIDE, WIDE, WIDE, LOW)
        )
        + tuple(jax.ShapeDtypeStruct(like.shape, LOW) for like in exchanged),
        scratch_shapes=[pltpu.VMEM((1, width), WIDE)],
        compiler_params=params(),
        name="optimizer",
    )(lengths, members, owned, squares, totals, *matrices, *vectors, *exchanged)


def to_positions(value):
    width = value.shape[1]
    moved = jnp.concatenate(
        [value[:512].reshape(4, 128, width), value[512:].reshape(4, 64, width)], axis=1
    )
    moved = lax.all_to_all(moved, "seq", split_axis=0, concat_axis=0, tiled=True)
    rows = []
    for y in range(2):
        rows.append(moved[2 * y, :128])
        rows.append(jnp.concatenate([moved[2 * y, 128:], moved[2 * y + 1, 128:]], axis=0))
        rows.append(moved[2 * y + 1, :128])
    return jnp.stack(rows)


def to_rows(tokens):
    width = tokens.shape[-1]
    core = lax.axis_index("seq") % 2
    pieces = []
    for j in range(4):
        y, c = j // 2, j % 2
        pieces += [tokens[3 * y + 2 * c], tokens[3 * y + 1]]
    moved = jnp.concatenate(pieces, axis=0).reshape(4, 256, width)
    moved = lax.all_to_all(moved, "seq", split_axis=0, concat_axis=0, tiled=True)
    shared = moved[:, 128:].reshape(4, 2, 64, width)
    own = lax.dynamic_index_in_dim(shared, core, 1, keepdims=False)
    other = lax.dynamic_index_in_dim(shared, 1 - core, 1, keepdims=False)
    return jnp.concatenate(
        [moved[:, :128].reshape(512, width), own.reshape(256, width), other.reshape(256, width)],
        axis=0,
    )


def local(
    tokens,
    grad_out,
    lengths,
    members,
    owners,
    mat_master,
    mat_moment1,
    mat_moment2,
    vec_master,
    vec_moment1,
    vec_moment2,
):
    sent_dev, local_len, model_width = tokens.shape
    dp_count = lax.axis_size("dp")
    block_rows = mat_master.shape[0]
    direct = dp_count == 8 and block_rows == 3 * TILE

    if direct:
        blocks = owners
        weights, rows, qkv, matrices, attended, out_grad, lse = front(
            owners, lengths, mat_master, tokens, grad_out, vec_master
        )
    else:
        gathered = lax.all_gather(mat_master.astype(LOW), "dp", axis=0, tiled=True)
        weights = gathered.reshape(dp_count, block_rows, model_width)[owners]
        weights = weights.reshape(-1, TILE, model_width)
        rows = to_rows(tokens)
        blocks = jnp.arange(weights.shape[0] // 3, dtype=jnp.int32)
        qkv = qkv_project(blocks, rows, weights, vec_master)
        attended, lse, out_grad = attend(lengths, qkv, grad_out)
    result, left, right, d_attended, d_branch, sums = middle(
        blocks, lengths, attended, rows, out_grad, weights, vec_master
    )
    if direct:
        owned, totals, squares, input_grad, output = reduce_all(
            owners,
            lengths,
            rows,
            attended,
            left,
            qkv,
            d_attended,
            d_branch,
            right,
            matrices,
            result,
            lse,
            sums,
            sent_dev,
        )
    else:
        dq, dk, dv, output = attend_back(
            lengths, qkv, lse, d_attended, attended, result, sent_dev
        )
        grad_rows = grad_in(blocks, dq, dk, dv, d_branch, weights)
        grads = grad_ff(blocks, left, right)
        grads, sums_qv = grad_attn(blocks, rows, dq, dk, dv, attended, d_branch, grads)
        input_grad = to_positions(grad_rows)
        inverse = jnp.argsort(owners)
        grads = grads.reshape(dp_count, block_rows, model_width)[inverse]
        grads = grads.reshape(dp_count * block_rows, model_width)
        quarter = lax.psum_scatter(grads, ("dp", "seq"), scatter_dimension=0, tiled=True)
        owned = lax.all_gather(quarter, "seq", axis=0, tiled=True)
        quarter = quarter.astype(WIDE)
        group = lax.axis_index("seq") // 2
        core = lax.axis_index("seq") % 2
        place = jnp.arange(8)[:, None]
        pooled = jnp.where(place == 3 * group + 2 * core, sums[10:11], 0.0) + jnp.where(
            place == 3 * group + 1, sums[11:12], 0.0
        )
        pooled = lax.psum(pooled, "seq")
        local_vec = jnp.concatenate([sums_qv[0:2], sums[0:14]], axis=0)
        squares, vec_total = lax.psum(
            (jnp.sum(quarter * quarter), local_vec), ("dp", "seq")
        )
        squares = jnp.full((8, 128), squares / 1024.0)
        totals = jnp.concatenate([vec_total, pooled], axis=0)

    norm, embeddings, *new, output, input_grad = optimizer(
        lengths,
        members,
        owned,
        squares,
        totals,
        (mat_master, mat_moment1, mat_moment2),
        (vec_master, vec_moment1, vec_moment2),
        (output, input_grad),
    )
    return (output, input_grad, embeddings, norm.reshape(()), *new)


def solution(mesh):
    placed = (
        P("dp", "seq", None),
        P("dp", "seq", None),
        P("dp"),
        P("dp", None),
        P(),
        P("dp", None),
        P("dp", None),
        P("dp", None),
        P(),
        P(),
        P(),
    )
    return jax.shard_map(
        local,
        mesh=mesh,
        in_specs=placed,
        out_specs=(
            P("dp", "seq", None),
            P("dp", "seq", None),
            P("dp", None),
            P(),
            P("dp", None),
            P("dp", None),
            P("dp", None),
            P("dp", None),
            P(),
            P(),
            P(),
            P(),
        ),
        check_vma=False,
    )
```

```python
import functools

import jax
import jax.numpy as jnp
from jax import lax
from jax.experimental import pallas as pl
from jax.experimental.pallas import tpu as pltpu
from jax.sharding import PartitionSpec as P

HEADS = 12
HEAD_DIM = 64
FEEDFWD_UNITS = 3072
STEP = 10


NORM_EPS = 1e-06
MASK_FILL = -1e30
MAX_NORM = 1.0
ADAM_ONE = 0.9
ADAM_TWO = 0.999
ADAM_EPS = 1e-08
WEIGHT_DECAY = 0.01
RATE_MATRIX = 0.04
RATE_VECTOR = 0.5

FWD_PAIRS = 6
BACK_PAIRS = 6
NORM_ROWS = 128
TILE = 384
VMEM_LIMIT = 60 * 1024 * 1024
MESH_ID = pl.DeviceIdType.MESH
LOW = jnp.bfloat16
WIDE = jnp.float32


def adam_step(master, moment_one, moment_two, gradient, learn_rate, decay_rate):
    moment_one = ADAM_ONE * moment_one + (1.0 - ADAM_ONE) * gradient
    moment_two = ADAM_TWO * moment_two + (1.0 - ADAM_TWO) * gradient * gradient
    scaled_one = moment_one / (1.0 - ADAM_ONE**STEP)
    scaled_two = moment_two / (1.0 - ADAM_TWO**STEP)
    master = master - learn_rate * (
        scaled_one / (jnp.sqrt(scaled_two) + ADAM_EPS) + decay_rate * master
    )
    return (moment_one, moment_two, master)


def dot_nn(left, right):
    return jnp.dot(left, right, preferred_element_type=WIDE)


def dot_nt(left, right):
    return lax.dot_general(
        left, right, (((1,), (1,)), ((), ())), preferred_element_type=WIDE
    )


def dot_tn(left, right):
    return lax.dot_general(
        left, right, (((0,), (0,)), ((), ())), preferred_element_type=WIDE
    )


def tile_at(owners, tile):
    return 3 * owners[tile // 3] + tile % 3


def params(**kwargs):
    return pltpu.CompilerParams(vmem_limit_bytes=VMEM_LIMIT, **kwargs)


GATHER_HEAD = 10
GATHER_ORDER = (
    ("tk",), ("xb", 1), ("xs", 0), ("zs", 0), ("zs", 2), ("xb", 0), ("r", 1, 0), ("r", 0, 0),
    ("xs", 1), ("r", 1, 2), ("zs", 1), ("xr", 1, 0), ("r", 0, 2), ("xb", 2), ("r", 1, 1),
    ("r", 2, 0), ("r", 2, 2), ("r", 0, 1), ("xs", 2), ("xob", 2), ("r", 2, 1), ("zx", 0),
    ("xo", 0), ("zx", 1), ("yr", 1, 2), ("xr", 1, 1), ("tf",), ("zx", 2), ("xr", 2, 0), ("xo", 2),
    ("yr", 2, 1), ("e1", 0), ("xob", 1), ("xr", 2, 2), ("yx", 1, 1), ("xo", 1), ("xr", 1, 2),
    ("xr", 2, 1), ("e1", 1), ("xsr", 0), ("yx", 1, 0), ("e1", 2), ("yx", 1, 2), ("yx", 2, 2),
    ("yr", 2, 0), ("yr", 1, 0), ("e2", 2), ("yr", 1, 1), ("xsr", 1), ("xob", 0), ("e2", 1),
    ("yx", 2, 0), ("xsr", 2), ("yr", 2, 2), ("e2", 0), ("yx", 2, 1),
)


def front_body(
    own_of_ref, len_ref, w_ref, x_ref, g_ref, vec_ref,
    weights_ref, rows_ref, qkv_ref, mats_ref, o_ref, gy_ref, lse_ref,
    wide_buf, own_buf, out_ref, xo_ref, qkv_buf, mats_buf, o_buf,
    send_sem, recv_sem, tok_recv, local_sem, ex_send, ex_recv, ex_local,
):
    dp, sq = lax.axis_index("dp"), lax.axis_index("seq")
    z, x = dp // 2, dp % 2
    y, c = sq // 2, sq % 2
    q, qc, qy, qyc = sq, sq ^ 1, sq ^ 2, sq ^ 3
    dev_c, dev_y, dev_yc, dev_x = (dp, sq ^ 1), (dp, sq ^ 2), (dp, sq ^ 3), (dp ^ 1, sq)
    dev_near = (dp ^ 2, sq)
    has_up, has_down, inner = z < 3, z > 0, (z > 0) & (z < 3)
    dev_up = (jnp.minimum(dp + 2, dp % 2 + 6), sq)
    dev_down = (jnp.maximum(dp - 2, dp % 2), sq)
    sources = (z ^ 1, jnp.where(z < 2, 2, 1), jnp.where(z < 2, 3, 0))
    used = [0, 0]
    started, locals_ = [], []

    def move(src, dst):
        copy = pltpu.make_async_copy(src, dst, local_sem.at[used[1]])
        used[1] += 1
        copy.start()
        return copy

    loads = []
    for at in (q, qy, qc, qyc):
        thirds = pl.ds(3 * at, 3)
        loads.append(move(w_ref.at[thirds], wide_buf.at[thirds]))

    barrier = pltpu.get_barrier_semaphore()

    def greet(device):
        pl.semaphore_signal(barrier, inc=1, device_id=device, device_id_type=MESH_ID)

    for device in (dev_c, dev_y, dev_yc, dev_x):
        greet(device)
    pl.when(has_up)(lambda: greet(dev_up))
    pl.when(has_down)(lambda: greet(dev_down))
    pl.semaphore_wait(barrier, 4 + jnp.where(inner, 2, 1))

    def send(src, dst, recv, device, pred=None):
        copy = pltpu.make_async_remote_copy(
            src_ref=src,
            dst_ref=dst,
            send_sem=send_sem.at[used[0]],
            recv_sem=recv,
            device_id=device,
            device_id_type=MESH_ID,
        )
        used[0] += 1
        if pred is None:
            copy.start()
        else:
            pl.when(pred)(lambda: copy.start())
        started.append((copy, pred))

    def piece(slot, quarter, h, device, pred=None, own=False):
        at = out_ref.at[slot, 3 * quarter + h]
        src = own_buf.at[3 * quarter + h] if own else at
        send(src, at, recv_sem.at[slot, quarter, h], device, pred)

    def arrived(slot, quarter, h):
        at = out_ref.at[slot, 3 * quarter + h]
        pltpu.make_async_copy(at, at, recv_sem.at[slot, quarter, h]).wait()

    def taken(slot, quarter, h):
        arrived(slot, quarter, h)
        piece(slot, quarter, h, dev_c)

    def near(k):
        return 2 * sources[k] + x

    def far(k):
        return 2 * sources[k] + 1 - x

    oy = 1 - y
    full_own, full_sib = 3 * y + 2 * c, 3 * y + 2 * (1 - c)
    full_far, full_cross = 3 * oy + 2 * c, 3 * oy + 2 * (1 - c)

    def full_rows(j):
        return xo_ref.at[pl.ds(128 * j, 128)]

    def half_rows(part, j, core):
        return xo_ref.at[pl.ds(512 + 256 * (part ^ core) + 64 * j, 64)]

    def token_send():
        send(x_ref.at[full_far], full_rows(sq), tok_recv.at[sq, 0], dev_y)
        for part in range(2):
            src = x_ref.at[3 * oy + 1, pl.ds(64 * part, 64)]
            send(src, half_rows(part, sq, c), tok_recv.at[sq, 1 + part], dev_y)
        send(x_ref.at[full_cross], full_rows(sq), tok_recv.at[sq, 0], dev_yc)
        send(x_ref.at[full_sib], full_rows(sq), tok_recv.at[sq, 0], dev_c)
        locals_.append(move(x_ref.at[full_own], full_rows(sq)))
        for part in range(2):
            src = x_ref.at[3 * y + 1, pl.ds(64 * part, 64)]
            send(src, half_rows(part, sq, 1 - c), tok_recv.at[sq, 1 + part], dev_c)
            locals_.append(move(src, half_rows(part, sq, c)))

    def token_forward():
        for part in range(2):
            at = half_rows(part, sq ^ 2, c)
            pltpu.make_async_copy(at, at, tok_recv.at[sq ^ 2, 1 + part]).wait()
            send(at, half_rows(part, sq ^ 2, 1 - c), tok_recv.at[sq ^ 2, 1 + part], dev_c)

    def own_line(h):
        piece(dp, q, h, dev_up, has_up, own=True)
        piece(dp, q, h, dev_down, has_down, own=True)

    def line(k, h):
        arrived(near(k), q, h)
        onward = (jnp.where(sources[k] < z, dev_up[0], dev_down[0]), sq)
        piece(near(k), q, h, onward, inner)
        if k > 0:
            piece(near(k), q, h, dev_x)
            piece(near(k), q, h, dev_y)
        piece(near(k), q, h, dev_c)

    def from_x_own(h):
        arrived(dp ^ 1, q, h)
        piece(dp ^ 1, q, h, dev_near)
        piece(dp ^ 1, q, h, dev_c)

    def near_other_half(h):
        arrived(near(0), qy, h)
        piece(near(0), qy, h, dev_x)
        piece(near(0), qy, h, dev_c)

    def from_x(k, h):
        arrived(far(k), q, h)
        piece(far(k), q, h, dev_y)
        piece(far(k), q, h, dev_c)

    steps = {
        "tk": token_send,
        "tf": token_forward,
        "zs": own_line,
        "zx": lambda h: piece(dp, qy, h, dev_near, own=True),
        "xs": lambda h: piece(dp, q, h, dev_x, own=True),
        "xb": lambda h: piece(dp, qy, h, dev_x, own=True),
        "r": line,
        "xo": from_x_own,
        "xob": lambda h: taken(dp ^ 1, qy, h),
        "e1": near_other_half,
        "e2": lambda h: taken(far(0), q, h),
        "yr": lambda k, h: taken(near(k), qy, h),
        "xr": from_x,
        "xsr": lambda h: taken(far(0), qy, h),
        "yx": lambda k, h: taken(far(k), qy, h),
    }

    def round_own(index, quarter):
        loads[index].wait()
        thirds = pl.ds(3 * quarter, 3)
        own_buf[thirds] = wide_buf[thirds].astype(LOW)

    round_own(0, q)
    round_own(1, qy)
    for name, *at in GATHER_ORDER[:GATHER_HEAD]:
        steps[name](*at)
    round_own(2, qc)
    round_own(3, qyc)
    locals_.append(move(own_buf, out_ref.at[dp]))
    for name, *at in GATHER_ORDER[GATHER_HEAD:]:
        steps[name](*at)
    exchange = Exchange(by_sentence(g_ref, gy_ref), ex_send, ex_recv, ex_local)
    exchange.start()
    for step in range(1, 8):
        for h in range(3):
            arrived(dp ^ step, qc, h)
            arrived(dp ^ step, qyc, h)
    for other in (sq ^ 1, sq ^ 2, sq ^ 3):
        at = full_rows(other)
        pltpu.make_async_copy(at, at, tok_recv.at[other, 0]).wait()
    for other in (sq ^ 1, sq ^ 3):
        for part in range(2):
            at = half_rows(part, other, c)
            pltpu.make_async_copy(at, at, tok_recv.at[other, 1 + part]).wait()
    for copy in locals_:
        copy.wait()
    stores = [move(out_ref.at[slot], weights_ref.at[slot]) for slot in range(8)]
    stores.append(move(xo_ref, rows_ref))

    for part in range(3):
        for half in range(2):
            tile = 2 * part + half
            held = out_ref[own_of_ref[tile // 3], 4 * (tile % 3) : 4 * (tile % 3) + 4]
            rows = slice(TILE * half, TILE * (half + 1))
            mats_buf[part, rows] = held.reshape(TILE, held.shape[-1])
        stores.append(move(mats_buf.at[part], mats_ref.at[part]))
        value = dot_nn(xo_ref[...], mats_buf[part])
        if part == 0:
            value = (value + vec_ref[0:1]) * HEAD_DIM ** (-0.5)
        elif part == 2:
            value = value + vec_ref[1:2]
        qkv_buf[part] = value.astype(LOW)
        stores.append(move(qkv_buf.at[part], qkv_ref.at[part]))

    biases = (key_bias(len_ref, False), key_bias(len_ref, True))

    def scores_of(block, pair):
        at, keys = slice(256 * block, 256 * (block + 1)), slice(512 * (block // 2), 512 * (block // 2 + 1))
        lanes = slice(128 * pair, 128 * (pair + 1))
        return pair_scores(qkv_buf[0, at, lanes], qkv_buf[1, keys, lanes], biases[block // 2])

    items = [(block, pair) for block in range(3) for pair in range(qkv_buf.shape[-1] // 128)]
    ahead = scores_of(*items[0])
    for index, (block, pair) in enumerate(items):
        scores = ahead
        if index + 1 < len(items):
            ahead = scores_of(*items[index + 1])
        at, lanes = slice(256 * block, 256 * (block + 1)), slice(128 * pair, 128 * (pair + 1))
        first = 512 * (block // 2)
        out, logs = attend_pair(scores, qkv_buf[2, first : first + 512, lanes])
        o_buf[at, lanes] = out
        for head in range(2):
            lse_ref[pair, head : head + 1, at] = logs[head]

    stores.append(move(o_buf, o_ref))
    exchange.finish()
    for copy in stores:
        copy.wait()
    for copy, pred in started:
        if pred is None:
            copy.wait_send()
        else:
            pl.when(pred)(lambda copy=copy: copy.wait_send())


def front(owners, lengths, block, tokens, grad_out, vectors):
    block_rows, width = block.shape
    part = block_rows // 12
    hbm = pl.BlockSpec(memory_space=pl.ANY)
    smem = pl.BlockSpec(memory_space=pltpu.SMEM)
    vmem = pl.BlockSpec(memory_space=pltpu.VMEM)
    dma = pltpu.SemaphoreType.DMA
    flat = jax.ShapeDtypeStruct((768, width), LOW)
    weights, *rest = pl.pallas_call(
        front_body,
        out_shape=(
            jax.ShapeDtypeStruct((8, 12, part, width), LOW),
            jax.ShapeDtypeStruct((1024, width), LOW),
            jax.ShapeDtypeStruct((3, 1024, width), LOW),
            jax.ShapeDtypeStruct((3, width, width), LOW),
            flat,
            flat,
            jax.ShapeDtypeStruct((HEADS // 2, 2, 768), WIDE),
        ),
        in_specs=[smem] * 2 + [hbm] * 3 + [vmem],
        out_specs=(hbm,) * 6 + (vmem,),
        scratch_shapes=[
            pltpu.VMEM((12, part, width), WIDE),
            pltpu.VMEM((12, part, width), LOW),
            pltpu.VMEM((8, 12, part, width), LOW),
            pltpu.VMEM((1024, width), LOW),
            pltpu.VMEM((3, 1024, width), LOW),
            pltpu.VMEM((3, width, width), LOW),
            pltpu.VMEM((768, width), LOW),
            dma((160,)),
            dma((8, 4, 3)),
            dma((4, 3)),
            dma((24,)),
        ]
        + EXCHANGE_SEMS,
        compiler_params=params(collective_id=1, has_side_effects=True),
        name="gather_attend",
    )(owners, lengths, block.reshape(12, part, width), tokens, grad_out, vectors)
    return weights.reshape(8 * block_rows // TILE, TILE, width), *rest


def qkv_body(map_ref, x_ref, top_ref, low_ref, vec_ref, out_ref):
    part = pl.program_id(0)
    scale = jnp.where(part == 0, HEAD_DIM ** (-0.5), 1.0)
    value = dot_nn(x_ref[:, :TILE], top_ref[0]) + dot_nn(x_ref[:, TILE:], low_ref[0])
    bias = jnp.where(part == 0, vec_ref[0:1], jnp.where(part == 2, vec_ref[1:2], 0.0))
    out_ref[0] = ((value + bias) * scale).astype(LOW)


def qkv_project(owners, rows, weights, vectors):
    count, width = rows.shape
    return pl.pallas_call(
        qkv_body,
        grid_spec=pltpu.PrefetchScalarGridSpec(
            num_scalar_prefetch=1,
            grid=(3,),
            in_specs=[
                pl.BlockSpec((count, width), lambda i, m: (0, 0)),
                pl.BlockSpec((1, TILE, width), lambda i, m: (tile_at(m, 2 * i), 0, 0)),
                pl.BlockSpec((1, TILE, width), lambda i, m: (tile_at(m, 2 * i + 1), 0, 0)),
                pl.BlockSpec(vectors.shape, lambda i, m: (0, 0)),
            ],
            out_specs=pl.BlockSpec((1, count, width), lambda i, m: (i, 0, 0)),
        ),
        out_shape=jax.ShapeDtypeStruct((3, count, width), LOW),
        compiler_params=params(),
        name="qkv",
    )(owners, rows, weights, weights, vectors)


def group_barrier(dp, sq):
    barrier = pltpu.get_barrier_semaphore()
    for step in range(1, 4):
        pl.semaphore_signal(
            barrier, inc=1, device_id=(dp, sq ^ step), device_id_type=MESH_ID
        )
    pl.semaphore_wait(barrier, 3)


class Exchange:
    def __init__(self, pieces, send_sem, recv_sem, local_sem):
        self.dp, self.sq = lax.axis_index("dp"), lax.axis_index("seq")
        self.pieces = pieces
        self.sems = (send_sem, recv_sem, local_sem)

    def copies(self):
        send_sem, recv_sem, local_sem = self.sems
        out = []
        for step in (2, 3, 1):
            target = self.sq ^ step
            for kind, (src, dst) in enumerate(self.pieces(self.sq, target)):
                out.append(
                    pltpu.make_async_remote_copy(
                        src_ref=src,
                        dst_ref=dst,
                        send_sem=send_sem.at[step - 1, kind],
                        recv_sem=recv_sem.at[self.sq, kind],
                        device_id=(self.dp, target),
                        device_id_type=MESH_ID,
                    )
                )
        for kind, (src, dst) in enumerate(self.pieces(self.sq, self.sq)):
            out.append(pltpu.make_async_copy(src, dst, local_sem.at[kind]))
        return out

    def start(self):
        for copy in self.copies():
            copy.start()

    def finish(self):
        copies = self.copies()
        for copy in copies[:6]:
            copy.wait_send()
        for copy in copies[6:]:
            copy.wait()
        for step in range(1, 4):
            source = self.sq ^ step
            for kind, (_, dst) in enumerate(self.pieces(source, self.sq)):
                pltpu.make_async_copy(dst, dst, self.sems[1].at[source, kind]).wait()


EXCHANGE_SEMS = [
    pltpu.SemaphoreType.DMA((3, 2)),
    pltpu.SemaphoreType.DMA((4, 2)),
    pltpu.SemaphoreType.DMA((2,)),
]


def by_sentence(src, dst):
    def pieces(source, target):
        y, c = target // 2, target % 2
        return (
            (src.at[3 * y + 2 * c], dst.at[pl.ds(128 * source, 128)]),
            (src.at[3 * y + 1, pl.ds(64 * c, 64)], dst.at[pl.ds(512 + 64 * source, 64)]),
        )

    return pieces


def by_position(src, dst):
    def pieces(source, target):
        y, c = source // 2, source % 2
        return (
            (src.at[pl.ds(128 * target, 128)], dst.at[3 * y + 2 * c]),
            (src.at[pl.ds(512 + 64 * target, 64)], dst.at[3 * y + 1, pl.ds(64 * c, 64)]),
        )

    return pieces


def sentence_length(lengths_ref, shared):
    sq = lax.axis_index("seq")
    group, core = sq // 2, sq % 2
    return jnp.where(shared, lengths_ref[3 * group + 1], lengths_ref[3 * group + 2 * core])


def positions(shape, shared, first=0):
    row = first + lax.broadcasted_iota(jnp.int32, shape, 0)
    own = lax.axis_index("seq") % 2
    half = row // 256
    part = row - 256 * half
    core = own + half - 2 * own * half
    mixed = (part // 64) * 128 + part % 64 + 64 * core
    return jnp.where(shared, mixed, row)


def key_bias(lengths_ref, shared):
    inside = positions((512, 128), shared) < sentence_length(lengths_ref, shared)
    bias = jnp.where(inside, 0.0, MASK_FILL)
    return jnp.concatenate([bias, bias], axis=1)


def head_masks(shape):
    lane = lax.broadcasted_iota(jnp.int32, shape, 1)
    return (lane < HEAD_DIM, lane >= HEAD_DIM)


def pair_scores(queries, keys, bias):
    return [
        dot_nt(keys, jnp.where(mask, queries, jnp.zeros_like(queries))) + bias
        for mask in head_masks(queries.shape)
    ]


def attend_pair(pair_of_scores, values):
    value_t = values.T
    outs, logs = [], []
    for head, scores in enumerate(pair_of_scores):
        top = jnp.max(scores, axis=0, keepdims=True)
        shifted = jnp.exp(scores - top)
        total = jnp.sum(shifted, axis=0, keepdims=True)
        part = value_t[HEAD_DIM * head : HEAD_DIM * (head + 1)]
        outs.append(dot_nn(part, shifted.astype(LOW)) * (1.0 / total))
        logs.append(top + jnp.log(total))
    return jnp.concatenate(outs, axis=0).T.astype(LOW), logs


def attend_body(
    len_ref, q_ref, k_ref, v_ref, g_ref, o_ref, lse_ref, gy_ref, send_sem, recv_sem, local_sem
):
    block, group = pl.program_id(0), pl.program_id(1)
    exchange = Exchange(by_sentence(g_ref, gy_ref), send_sem, recv_sem, local_sem)

    @pl.when((block == 0) & (group == 0))
    def _():
        group_barrier(exchange.dp, exchange.sq)
        exchange.start()

    bias = key_bias(len_ref, block == 2)
    for pair in range(q_ref.shape[-1] // 128):
        lanes = slice(128 * pair, 128 * (pair + 1))
        scores = pair_scores(q_ref[0, :, lanes], k_ref[0, :, lanes], bias)
        out, logs = attend_pair(scores, v_ref[0, :, lanes])
        o_ref[:, lanes] = out
        for head in range(2):
            lse_ref[0, 2 * pair + head : 2 * pair + head + 1, :] = logs[head]

    @pl.when((block == 2) & (group == pl.num_programs(1) - 1))
    def _():
        exchange.finish()


def attend(lengths, qkv, grad_out):
    width = qkv.shape[-1]
    groups = width // 128 // FWD_PAIRS
    lanes = 128 * FWD_PAIRS
    hbm = pl.BlockSpec(memory_space=pl.ANY)
    return pl.pallas_call(
        attend_body,
        grid=(3, groups),
        in_specs=[
            pl.BlockSpec(memory_space=pltpu.SMEM),
            pl.BlockSpec((1, 256, lanes), lambda i, h: (0, i, h)),
            pl.BlockSpec((1, 512, lanes), lambda i, h: (1, i // 2, h)),
            pl.BlockSpec((1, 512, lanes), lambda i, h: (2, i // 2, h)),
            hbm,
        ],
        out_specs=(
            pl.BlockSpec((256, lanes), lambda i, h: (i, h)),
            pl.BlockSpec((1, 2 * FWD_PAIRS, 256), lambda i, h: (h, 0, i)),
            hbm,
        ),
        out_shape=(
            jax.ShapeDtypeStruct((768, width), LOW),
            jax.ShapeDtypeStruct((groups, 2 * FWD_PAIRS, 768), WIDE),
            jax.ShapeDtypeStruct((768, width), LOW),
        ),
        scratch_shapes=EXCHANGE_SEMS,
        compiler_params=params(collective_id=3, has_side_effects=True),
        name="attend",
    )(lengths, qkv, qkv, qkv, grad_out)


def back_first(head, queries, keys, values, grads, bias):
    mask = head_masks(queries.shape)[head]
    query = jnp.where(mask, queries, jnp.zeros_like(queries))
    grad = jnp.where(mask, grads, jnp.zeros_like(grads))
    return query, grad, dot_nt(keys, query) + bias, dot_nt(values, grad)


def back_second(head, first, keys_t, inner, log):
    query, grad, scores, d_probs = first
    rows = slice(HEAD_DIM * head, HEAD_DIM * (head + 1))
    inner_sum = jnp.sum(inner[rows], axis=0, keepdims=True)
    probs = jnp.exp(scores - log)
    d_scores = (probs * (d_probs - inner_sum)).astype(LOW)
    d_value = dot_nn(probs.astype(LOW), grad)
    return dot_nn(keys_t[rows], d_scores), dot_nn(d_scores, query), d_value


def back_inner(grads, outs):
    return (grads.astype(WIDE) * outs.astype(WIDE)).T


def back_query(parts):
    return (jnp.concatenate(parts, axis=0) * HEAD_DIM ** (-0.5)).T.astype(LOW)


def back_pair(queries, keys, values, grads, outs, logs, bias):
    keys_t, inner = keys.T, back_inner(grads, outs)
    found = []
    for head in range(2):
        first = back_first(head, queries, keys, values, grads, bias)
        found.append(back_second(head, first, keys_t, inner, logs[head : head + 1]))
    (query_a, key_a, value_a), (query_b, key_b, value_b) = found
    return back_query([query_a, query_b]), key_a + key_b, value_a + value_b


def attend_back_body(
    len_ref, q_ref, k_ref, v_ref, lse_ref, do_ref, o_ref, y_ref,
    dq_ref, dk_ref, dv_ref, out_ref,
    acc, keep, give, take, send_sem, recv_sem, local_sem, give_sem, take_sem,
):
    group, block = pl.program_id(0), pl.program_id(1)
    exchange = Exchange(by_position(y_ref, out_ref), send_sem, recv_sem, local_sem)
    dp, sq = exchange.dp, exchange.sq

    @pl.when((block == 0) & (group == 0))
    def _():
        group_barrier(dp, sq)
        exchange.start()

    bias = key_bias(len_ref, block == 0)
    d_keys, d_values = [], []
    for pair in range(q_ref.shape[-1] // 128):
        lanes = slice(128 * pair, 128 * (pair + 1))
        d_query, d_key, d_value = back_pair(
            q_ref[0, :, lanes], k_ref[0, :, lanes], v_ref[0, :, lanes], do_ref[:, lanes],
            o_ref[:, lanes], lse_ref[0, 2 * pair : 2 * pair + 2], bias,
        )
        dq_ref[:, lanes] = d_query
        d_keys.append((lanes, d_key))
        d_values.append((lanes, d_value))
    pairs = ((0, d_keys), (1, d_values))

    def swap(kind):
        return pltpu.make_async_remote_copy(
            src_ref=give.at[group, kind],
            dst_ref=take.at[group, kind],
            send_sem=give_sem.at[group, kind],
            recv_sem=take_sem.at[group, kind],
            device_id=(dp, sq ^ 1),
            device_id_type=MESH_ID,
        )

    @pl.when(block == 0)
    def _():
        for kind, parts in pairs:
            for lanes, part in parts:
                keep[kind, :, lanes] = part[:256]
                give[group, kind, :, lanes] = part[256:].astype(LOW)
            swap(kind).start()

    @pl.when(block == 1)
    def _():
        for kind, parts in pairs:
            for lanes, part in parts:
                acc[kind, :, lanes] = part

    @pl.when(block == 2)
    def _():
        for (kind, parts), ref in zip(pairs, (dk_ref, dv_ref)):
            swap(kind).wait()
            for lanes, part in parts:
                ref[:512, lanes] = (acc[kind, :, lanes] + part).astype(LOW)
                other = take[group, kind, :, lanes].astype(WIDE)
                ref[512:, lanes] = (keep[kind, :, lanes] + other).astype(LOW)

    @pl.when((block == 2) & (group == pl.num_programs(0) - 1))
    def _():
        exchange.finish()


def attend_back(lengths, qkv, lse, d_out, out, result, sent_dev):
    width = qkv.shape[-1]
    groups = width // 128 // BACK_PAIRS
    lanes = 128 * BACK_PAIRS
    hbm = pl.BlockSpec(memory_space=pl.ANY)
    query = pl.BlockSpec((256, lanes), lambda h, i: ((i + 2) % 3, h))
    keys = pl.BlockSpec((768, lanes), lambda h, i: (0, h))
    flat = jax.ShapeDtypeStruct((768, width), LOW)
    shared = lambda i: jnp.where(i == 0, 1, 0)
    return pl.pallas_call(
        attend_back_body,
        grid=(groups, 3),
        in_specs=[
            pl.BlockSpec(memory_space=pltpu.SMEM),
            pl.BlockSpec((1, 256, lanes), lambda h, i: (0, (i + 2) % 3, h)),
            pl.BlockSpec((1, 512, lanes), lambda h, i: (1, shared(i), h)),
            pl.BlockSpec((1, 512, lanes), lambda h, i: (2, shared(i), h)),
            pl.BlockSpec((1, 2 * BACK_PAIRS, 256), lambda h, i: (h, 0, (i + 2) % 3)),
            query,
            query,
            hbm,
        ],
        out_specs=(query, keys, keys, hbm),
        out_shape=(flat, flat, flat, jax.ShapeDtypeStruct((sent_dev, 128, width), LOW)),
        scratch_shapes=[
            pltpu.VMEM((2, 512, lanes), WIDE),
            pltpu.VMEM((2, 256, lanes), WIDE),
            pltpu.VMEM((groups, 2, 256, lanes), LOW),
            pltpu.VMEM((groups, 2, 256, lanes), LOW),
        ]
        + EXCHANGE_SEMS
        + [pltpu.SemaphoreType.DMA((groups, 2)), pltpu.SemaphoreType.DMA((groups, 2))],
        compiler_params=params(collective_id=4, has_side_effects=True),
        name="attend_back",
    )(lengths, qkv, qkv, qkv, lse.reshape(groups, 2 * BACK_PAIRS, 768), d_out, out, result)


def row_mean(value):
    return jnp.mean(value, axis=-1, keepdims=True)


def col_sum(value):
    return jnp.sum(value, axis=0, keepdims=True)


def middle_body(
    map_ref, len_ref, o_hbm, x_hbm, gy_hbm, w_ref, vec_ref,
    y_hbm, left_hbm, right_hbm, do_hbm, da_hbm, sums_ref,
    w_buf, o_buf, x_buf, gy_buf, left, right, slope, total, hat_one, rstd_one, low_buf,
    sem, in_sem, out_sem,
):
    count, width = o_buf.shape
    tiles = w_buf.shape[0]
    chunks = FEEDFWD_UNITS // width

    def fetch(t):
        return pltpu.make_async_copy(w_ref.at[tile_at(map_ref, 6 + t)], w_buf.at[t], sem.at[t])

    inputs = [
        pltpu.make_async_copy(src, dst, in_sem.at[i])
        for i, (src, dst) in enumerate(
            (
                (o_hbm, o_buf),
                (x_hbm.at[pl.ds(0, count)], x_buf),
                (gy_hbm, gy_buf),
            )
        )
    ]
    inputs[0].start()
    for t in range(2):
        fetch(t).start()
    inputs[1].start()
    for c in range(chunks):
        for t in (2 + 2 * c, 3 + 2 * c, 10 + 2 * c, 11 + 2 * c):
            fetch(t).start()
    inputs[2].start()
    outputs = []

    def put(src, dst):
        copy = pltpu.make_async_copy(src, dst, out_sem.at[len(outputs)])
        copy.start()
        outputs.append(copy)

    def put_left(t, value):
        for u in range(2):
            left[t + u] = value[:, TILE * u : TILE * (u + 1)]
            put(left.at[t + u], left_hbm.at[t + u])

    def ready(*which):
        for t in which:
            fetch(t).wait()

    def pair(t):
        return w_buf[t : t + 2].reshape(2 * TILE, width)

    def vec(row):
        return vec_ref[row : row + 1, :]

    def fold(value):
        return jnp.sum(value.reshape(-1, 8, width), axis=0)

    def over_rows(body, carried):
        zero = (jnp.zeros((8, width), WIDE),) * carried

        def step(i, carry):
            return body(pl.ds(pl.multiple_of(i * NORM_ROWS, NORM_ROWS), NORM_ROWS), i, carry)

        return lax.fori_loop(0, count // NORM_ROWS, step, zero)

    inputs[0].wait()
    ready(0, 1)
    total[...] = dot_nn(o_buf[...], pair(0))
    inputs[1].wait()

    def norm_one(at, i, carry):
        resid = x_buf[at].astype(WIDE) + (total[at] + vec(2))
        centered = resid - row_mean(resid)
        rstd = lax.rsqrt(row_mean(centered * centered) + NORM_EPS)
        rstd_one[at] = rstd
        hat = centered * rstd
        hat_one[at] = hat
        first = hat * vec(4) + vec(5)
        total[at] = first + vec(3)
        right[0, at] = first.astype(LOW)
        return carry

    over_rows(norm_one, 0)
    put(right.at[0], right_hbm.at[0])

    first_low = right[0]
    for c in range(chunks):
        ready(2 + 2 * c, 3 + 2 * c, 10 + 2 * c, 11 + 2 * c)
        act = dot_nt(first_low, pair(2 + 2 * c)) + vec(8 + c)
        cdf = 0.5 + 0.5 * lax.erf(act * (0.5**0.5))
        pdf = jnp.exp(-0.5 * act * act) * 0.3989422804014327
        slope[c] = cdf + act * pdf
        active = (act * cdf).astype(LOW)
        put_left(8 + 2 * c, active)
        total[...] += dot_nn(active, pair(10 + 2 * c))
    inputs[2].wait()

    def norm_two(at, i, carry):
        d_gain, d_shift, d_bias, pool_full, pool_half = carry
        resid = total[at]
        centered = resid - row_mean(resid)
        rstd = lax.rsqrt(row_mean(centered * centered) + NORM_EPS)
        hat = centered * rstd
        result = hat * vec(6) + vec(7)
        low_buf[0, at] = result.astype(LOW)
        shared = i * NORM_ROWS >= 512
        row = positions((NORM_ROWS, 128), shared, i * NORM_ROWS - jnp.where(shared, 512, 0))
        valid = jnp.where(row < sentence_length(len_ref, shared), 1.0, 0.0)
        pooled = fold(result * jnp.concatenate([valid] * (width // 128), axis=1))
        part = shared.astype(WIDE)
        grad = gy_buf[at].astype(WIDE)
        d_gain = d_gain + fold(grad * hat)
        d_shift = d_shift + fold(grad)
        grad = grad * vec(6)
        d_resid = rstd * (grad - row_mean(grad) - hat * row_mean(grad * hat))
        total[at] = d_resid
        grad_low = d_resid.astype(LOW)
        right[1, at] = grad_low
        return (
            d_gain,
            d_shift,
            d_bias + fold(grad_low.astype(WIDE)),
            pool_full + pooled * (1.0 - part),
            pool_half + pooled * part,
        )

    sums_ref[...] = jnp.zeros_like(sums_ref)
    found = over_rows(norm_two, 5)
    for row, value in zip((4, 5, 1, 10, 11), found):
        sums_ref[row : row + 1, :] = col_sum(value)
    put(low_buf.at[0], y_hbm)
    put(right.at[1], right_hbm.at[1])

    grad_low = right[1]
    for c in range(chunks):
        d_active = dot_nt(grad_low, pair(10 + 2 * c))
        d_act = (d_active * slope[c]).astype(LOW)
        put_left(2 * c, d_act)
        sums_ref[6 + c : 7 + c, :] = col_sum(d_act.astype(WIDE))
        total[...] += dot_nn(d_act, pair(2 + 2 * c))

    def norm_back(at, i, carry):
        d_gain, d_shift, d_bias = carry
        grad = total[at]
        hat = hat_one[at]
        d_gain = d_gain + fold(grad * hat)
        d_shift = d_shift + fold(grad)
        grad = grad * vec(4)
        d_resid = rstd_one[at] * (grad - row_mean(grad) - hat * row_mean(grad * hat))
        grad_low = d_resid.astype(LOW)
        low_buf[1, at] = grad_low
        return (d_gain, d_shift, d_bias + fold(grad_low.astype(WIDE)))

    found = over_rows(norm_back, 3)
    for row, value in zip((2, 3, 0), found):
        sums_ref[row : row + 1, :] = col_sum(value)
    put(low_buf.at[1], da_hbm)
    low_buf[2] = dot_nt(low_buf[1], pair(0)).astype(LOW)
    put(low_buf.at[2], do_hbm)
    for copy in outputs:
        copy.wait()


def middle(owners, lengths, attended, rows, out_grad, weights, vectors):
    count, width = attended.shape
    half = FEEDFWD_UNITS // TILE
    tiles = 2 + 2 * half
    hbm = pl.BlockSpec(memory_space=pl.ANY)
    smem = pl.BlockSpec(memory_space=pltpu.SMEM)
    vmem = pl.BlockSpec(memory_space=pltpu.VMEM)
    flat = jax.ShapeDtypeStruct((count, width), LOW)
    return pl.pallas_call(
        middle_body,
        in_specs=[smem, smem] + [hbm] * 4 + [vmem],
        out_specs=(hbm,) * 5 + (vmem,),
        out_shape=(
            flat,
            jax.ShapeDtypeStruct((2 * half, count, TILE), LOW),
            jax.ShapeDtypeStruct((2, count, width), LOW),
            flat,
            flat,
            jax.ShapeDtypeStruct((16, width), WIDE),
        ),
        scratch_shapes=[
            pltpu.VMEM((tiles, TILE, width), LOW),
            pltpu.VMEM((count, width), LOW),
            pltpu.VMEM((count, width), LOW),
            pltpu.VMEM((count, width), LOW),
            pltpu.VMEM((2 * half, count, TILE), LOW),
            pltpu.VMEM((2, count, width), LOW),
            pltpu.VMEM((half // 2, count, width), WIDE),
            pltpu.VMEM((count, width), WIDE),
            pltpu.VMEM((count, width), WIDE),
            pltpu.VMEM((count, 1), WIDE),
            pltpu.VMEM((3, count, width), LOW),
            pltpu.SemaphoreType.DMA((tiles,)),
            pltpu.SemaphoreType.DMA((3,)),
            pltpu.SemaphoreType.DMA((2 * half + 5,)),
        ],
        compiler_params=params(),
        name="feed_forward",
    )(owners, lengths, attended, rows, out_grad, weights, vectors)


def grad_ff_body(map_ref, left_ref, right_ref, out_ref):
    out_ref[0] = dot_tn(left_ref[0], right_ref[0]).astype(LOW)


def grad_ff(owners, left, right):
    per = FEEDFWD_UNITS // TILE
    count, width = right.shape[1:]
    return pl.pallas_call(
        grad_ff_body,
        grid_spec=pltpu.PrefetchScalarGridSpec(
            num_scalar_prefetch=1,
            grid=(2 * per,),
            in_specs=[
                pl.BlockSpec((1, count, TILE), lambda i, m: (i, 0, 0)),
                pl.BlockSpec((1, count, width), lambda i, m: (i // per, 0, 0)),
            ],
            out_specs=pl.BlockSpec((1, TILE, width), lambda i, m: (tile_at(m, 8 + i), 0, 0)),
        ),
        out_shape=jax.ShapeDtypeStruct((8 + 2 * per, TILE, width), LOW),
        compiler_params=params(),
        name="grad_ff",
    )(owners, left, right)


def grad_attn_body(
    map_ref, x_ref, dq_ref, dk_ref, dv_ref, o_ref, da_ref, into_ref, out_ref, sums_ref
):
    step = pl.program_id(0)
    for part, grad_ref in enumerate((dq_ref, dk_ref, dv_ref)):

        @pl.when(step // 2 == part)
        def _(grad_ref=grad_ref):
            out_ref[0] = dot_tn(x_ref[...], grad_ref[...]).astype(LOW)

    @pl.when(step // 2 == 3)
    def _():
        out_ref[0] = dot_tn(o_ref[...], da_ref[...]).astype(LOW)

    @pl.when(step == 0)
    def _():
        sums_ref[...] = jnp.zeros_like(sums_ref)
        sums_ref[0:1, :] = col_sum(dq_ref[...].astype(WIDE))
        sums_ref[1:2, :] = col_sum(dv_ref[...].astype(WIDE))


def grad_attn(owners, rows, dq, dk, dv, attended, da, into):
    count, width = dq.shape
    whole = pl.BlockSpec((count, width), lambda i, m: (0, 0))
    return pl.pallas_call(
        grad_attn_body,
        grid_spec=pltpu.PrefetchScalarGridSpec(
            num_scalar_prefetch=1,
            grid=(8,),
            in_specs=[
                pl.BlockSpec((count, TILE), lambda i, m: (0, i % 2)),
                whole,
                whole,
                whole,
                pl.BlockSpec((768, TILE), lambda i, m: (0, i % 2)),
                pl.BlockSpec((768, width), lambda i, m: (0, 0)),
                pl.BlockSpec(memory_space=pl.ANY),
            ],
            out_specs=(
                pl.BlockSpec((1, TILE, width), lambda i, m: (tile_at(m, i), 0, 0)),
                pl.BlockSpec((8, width), lambda i, m: (0, 0)),
            ),
        ),
        out_shape=(
            jax.ShapeDtypeStruct(into.shape, LOW),
            jax.ShapeDtypeStruct((8, width), WIDE),
        ),
        input_output_aliases={7: 0},
        compiler_params=params(),
        name="grad_attn",
    )(owners, rows, dq, dk, dv, attended, da, into)


def grad_in_body(map_ref, dq_ref, dk_ref, dv_ref, dh_ref, *refs):
    w_refs, out_ref = refs[:6], refs[6]
    for half in range(2):
        cols = slice(TILE * half, TILE * (half + 1))
        value = dh_ref[:, cols].astype(WIDE)
        for part, grad_ref in enumerate((dq_ref, dk_ref, dv_ref)):
            value = value + dot_nt(grad_ref[...], w_refs[2 * part + half][0])
        out_ref[:, cols] = value.astype(LOW)


def grad_in(owners, dq, dk, dv, dh, weights):
    count, width = dq.shape
    block = pl.BlockSpec((256, width), lambda i, m: (i, 0))
    return pl.pallas_call(
        grad_in_body,
        grid_spec=pltpu.PrefetchScalarGridSpec(
            num_scalar_prefetch=1,
            grid=(count // 256,),
            in_specs=[block] * 4
            + [
                pl.BlockSpec((1, TILE, width), lambda i, m, t=t: (tile_at(m, t), 0, 0)) for t in range(6)
            ],
            out_specs=block,
        ),
        out_shape=jax.ShapeDtypeStruct((count, width), LOW),
        compiler_params=params(),
        name="grad_in",
    )(owners, dq, dk, dv, dh, *([weights] * 6))


REDUCE_MODE = (
    {"n": "z", "a": "x", "e": "y", "o": "x"},
    {"n": "z", "a": "y", "e": "y", "o": "y"},
    {"n": "z", "a": "x", "e": "x", "o": "x"},
)
REDUCE_ORDER = (
    ("part", "n", "f", 1), ("part", "e", "f", 1), ("part", "e", "n", 1), ("both", "n", "f", 1),
    ("part", "a", "n", 1), ("both", "e", "f", 1), ("part", "a", "f", 0), ("vs", 0),
    ("part", "n", "f", 2), ("both", "a", "n", 1), ("both", "e", "n", 1), ("part", "n", "n", 1),
    ("both", "a", "f", 0), ("both", "n", "f", 2), ("va", 0), ("vs", 1), ("part", "a", "f", 2),
    ("part", "e", "f", 0), ("part", "n", "n", 2), ("both", "n", "n", 1), ("both", "a", "f", 2),
    ("turn", "n", 1), ("part", "o", "n", 1), ("both", "e", "f", 0), ("part", "a", "f", 1),
    ("part", "e", "n", 0), ("part", "o", "f", 1), ("both", "a", "f", 1), ("both", "n", "n", 2),
    ("part", "e", "f", 2), ("both", "o", "f", 1), ("part", "a", "n", 2), ("both", "e", "n", 0),
    ("both", "e", "f", 2), ("part", "n", "n", 0), ("turn", "e", 1), ("both", "a", "n", 2),
    ("turn", "a", 2), ("part", "n", "f", 0), ("both", "o", "n", 1), ("own", "n", 1),
    ("part", "o", "f", 2), ("own", "f", 1), ("both", "n", "f", 0), ("part", "a", "n", 0),
    ("part", "e", "n", 2), ("both", "o", "f", 2), ("own", "f", 2), ("part", "o", "n", 2),
    ("both", "e", "n", 2), ("both", "n", "n", 0), ("turn", "e", 2), ("both", "a", "n", 0),
    ("turn", "n", 2), ("gin",), ("in",), ("turn", "a", 1), ("part", "o", "f", 0),
    ("part", "o", "n", 0), ("turn", "n", 0), ("turn", "e", 0), ("turn", "a", 0), ("on", "e", 1),
    ("va", 1), ("both", "o", "n", 0), ("on", "n", 2), ("both", "o", "n", 2), ("own", "n", 0),
    ("both", "o", "f", 0), ("own", "f", 0), ("on", "a", 2), ("own", "n", 2), ("turn", "o", 2),
    ("on", "e", 2), ("on", "n", 0), ("turn", "o", 1), ("on", "a", 1), ("on", "n", 1), ("vs", 2),
    ("turn", "o", 0), ("on", "e", 0), ("end", 1), ("on", "a", 0), ("va", 2), ("vs", 3), ("end", 2),
    ("va", 3), ("vs", 4), ("end", 0), ("va", 4),
)


def reduce_body(
    own_of_ref, len_ref, x_ref, o_ref, left_ref, qkv_ref, do_ref, da_ref, right_ref,
    w_ref, y_ref, lse_ref, sums_ref, own_ref, vt_ref, sq_ref, gi_ref, out_ref,
    left_0, left_1, left_2, rbuf, wbuf, gbuf, give, take, pbuf, core_in, x_two, x_one, y_two, y_one,
    zf_in, mid_in, fin_in, near_in, ebuf, tbuf, tlow, vbuf, v_in, s_own, s_seq, s_dp,
    send_sem, local_sem, core_sem, xtwo_sem, xone_sem, ytwo_sem, yone_sem,
    zf_sem, mid_sem, fin_sem, near_sem, v_sem, out_sem, seq_sem, dp_sem, in_sem,
    give_sem, take_sem, free_sem, ex_send, ex_recv, ex_local,
):
    dp, sq = lax.axis_index("dp"), lax.axis_index("seq")
    z, x = dp // 2, dp % 2
    y, c = sq // 2, sq % 2
    dev_c, dev_y, dev_yc, dev_x = (dp, sq ^ 1), (dp, sq ^ 2), (dp, sq ^ 3), (dp ^ 1, sq)
    dev_near = (dp ^ 2, sq)
    inner = (z > 0) & (z < 3)
    outer = jnp.logical_not(inner)
    place = {
        "n": z ^ 1,
        "a": jnp.where(z < 2, 2, 1),
        "e": jnp.where(z < 2, 3, 0),
        "o": z,
    }
    lefts = (left_0, left_1, left_2)
    used = [0, 0]
    remotes, own_moves = [], []

    def move(src, dst):
        copy = pltpu.make_async_copy(src, dst, local_sem.at[used[1]])
        used[1] += 1
        copy.start()
        return copy

    first_loads = [
        move(qkv_ref.at[0, pl.ds(0, 768)], wbuf.at[0]),
        move(do_ref, wbuf.at[1]),
        move(o_ref, wbuf.at[2]),
        move(qkv_ref.at[1], core_in.at[pl.ds(0, 1024)]),
        move(qkv_ref.at[2], core_in.at[pl.ds(1024, 1024)]),
    ]

    loads = {"right": [move(right_ref, rbuf.at[pl.ds(4, 2)]), move(da_ref, rbuf.at[3])]}
    for t in range(3):
        loads[t] = []
        for block in range(8):
            tile = 3 * block + t
            cols = pl.ds(TILE * (tile % 2), TILE)
            if tile < 6:
                src = x_ref.at[pl.ds(0, 768), cols]
            elif tile < 8:
                src = o_ref.at[:, cols]
            else:
                src = left_ref.at[tile - 8]
            loads[t].append(move(src, lefts[t].at[block]))

    def loaded(name):
        for copy in loads.pop(name, ()):
            copy.wait()

    barrier = pltpu.get_barrier_semaphore()
    for step in range(1, 4):
        pl.semaphore_signal(
            barrier, inc=1, device_id=(dp, sq ^ step), device_id_type=MESH_ID
        )
    for step in range(1, 8):
        pl.semaphore_signal(
            barrier, inc=1, device_id=(dp ^ step, sq), device_id_type=MESH_ID
        )
    pl.semaphore_wait(barrier, 10)

    def send(src, dst, recv, device, pred=None):
        copy = pltpu.make_async_remote_copy(
            src_ref=src,
            dst_ref=dst,
            send_sem=send_sem.at[used[0]],
            recv_sem=recv,
            device_id=device,
            device_id_type=MESH_ID,
        )
        used[0] += 1
        if pred is None:
            copy.start()
        else:
            pl.when(pred)(lambda: copy.start())
        remotes.append((copy, pred))

    def arrived(at, sem):
        pltpu.make_async_copy(at, at, sem).wait()

    def wide(ref, *at):
        return ref[at].astype(WIDE)

    exchange = Exchange(by_position(y_ref, out_ref), ex_send, ex_recv, ex_local)
    exchange.start()
    for copy in first_loads:
        copy.wait()

    def swap(pair, kind):
        return pltpu.make_async_remote_copy(
            src_ref=give.at[pair, kind],
            dst_ref=take.at[pair, kind],
            send_sem=give_sem.at[pair, kind],
            recv_sem=take_sem.at[pair, kind],
            device_id=dev_c,
            device_id_type=MESH_ID,
        )

    biases = (key_bias(len_ref, False), key_bias(len_ref, True))
    pairs = rbuf.shape[-1] // 128

    def back_at(pair, block):
        lanes, rows = slice(128 * pair, 128 * (pair + 1)), slice(256 * block, 256 * (block + 1))
        first = 512 * (block // 2)
        keys = core_in[first : first + 512, lanes]
        return lanes, rows, keys, core_in[1024 + first : 1536 + first, lanes]

    def first_of(pair, block, head):
        lanes, rows, keys, values = back_at(pair, block)
        return back_first(
            head, wbuf[0, rows, lanes], keys, values, wbuf[1, rows, lanes], biases[block // 2]
        )

    items = [(p, block, head) for p in range(pairs) for block in (2, 0, 1) for head in range(2)]
    ahead = first_of(*items[0])
    parts = {}
    for index, (pair, block, head) in enumerate(items):
        this = ahead
        if index + 1 < len(items):
            ahead = first_of(*items[index + 1])
        lanes, rows, keys, _ = back_at(pair, block)
        if head == 0:
            keys_t, weighed = keys.T, back_inner(wbuf[1, rows, lanes], wbuf[2, rows, lanes])
        log = lse_ref[pair, head : head + 1, rows]
        parts[block, head] = back_second(head, this, keys_t, weighed, log)
        if head == 0:
            continue
        rbuf[0, rows, lanes] = back_query([parts[block, 0][0], parts[block, 1][0]])
        for kind in range(2):
            part = parts[block, 0][1 + kind] + parts[block, 1][1 + kind]
            if block == 2:
                rbuf[1 + kind, 512:768, lanes] = part[:256].astype(LOW)
                give[pair, kind] = part[256:].astype(LOW)
                swap(pair, kind).start()
            elif block == 0:
                parts["sum", kind] = part
            else:
                total = parts["sum", kind] + part
                rbuf[1 + kind, 0:512, lanes] = total.astype(LOW)
    pl.semaphore_signal(free_sem, inc=1, device_id=dev_c, device_id_type=MESH_ID)
    loads["in"] = [move(w_ref, wbuf)]
    for pair in range(pairs):
        lanes = slice(128 * pair, 128 * (pair + 1))
        for kind in range(2):
            swap(pair, kind).wait()
            rows = pl.ds(512, 256)
            rbuf[1 + kind, rows, lanes] = (
                rbuf[1 + kind, rows, lanes].astype(WIDE) + take[pair, kind].astype(WIDE)
            ).astype(LOW)
    loaded("right")
    pl.semaphore_wait(free_sem, 1)

    partners = (dev_c, dev_y, dev_x, (dp ^ 2, sq), (dp ^ 4, sq))

    def vec_send(step):
        if step == 0:
            vbuf[0] = jnp.zeros(vbuf.shape[1:], WIDE)
            vbuf[0, 0:1] = col_sum(wide(rbuf, 0))
            vbuf[0, 1:2] = col_sum(wide(rbuf, 2))
            vbuf[0, 2:12] = sums_ref[0:10]
            vbuf[0, pl.ds(16 + 3 * y + 2 * c, 1)] = sums_ref[10:11]
            vbuf[0, pl.ds(16 + 3 * y + 1, 1)] = sums_ref[11:12]
        send(vbuf.at[step], v_in.at[step], v_sem.at[step], partners[step])

    def vec_add(step):
        arrived(v_in.at[step], v_sem.at[step])
        vbuf[step + 1] = vbuf[step] + v_in[step]

    def input_grad():
        loaded("in")
        for part in range(3):
            cols = slice(256 * part, 256 * (part + 1))
            value = wide(rbuf, 3, slice(None), cols)
            for index in range(3):
                value = value + dot_nt(rbuf[index], wbuf[index, cols])
            gbuf[:, cols] = value.astype(LOW)

    def in_full(j):
        return gbuf.at[pl.ds(128 * j, 128)], gi_ref.at[3 * y + 2 * c]

    def in_half(j):
        return gbuf.at[pl.ds(512 + 64 * j, 64)], gi_ref.at[3 * y + 1, pl.ds(64 * c, 64)]

    def input_send():
        for device in (dev_y, dev_yc, dev_c):
            for kind, pair in enumerate((in_full(device[1]), in_half(device[1]))):
                send(pair[0], pair[1], in_sem.at[sq, kind], device)
        own_moves.append(move(*in_full(sq)))
        own_moves.append(move(*in_half(sq)))

    def standard_of(slot):
        found = jnp.int32(0)
        for block in range(8):
            found = jnp.maximum(found, jnp.where(own_of_ref[block] == slot, block, 0))
        return found

    def slot_of(k, p):
        return 2 * place[k] + (x if p == "n" else 1 - x)

    def core_at(slot, t, half):
        first = 96 * (2 * (8 * t + slot) + half)
        return core_in.at[pl.ds(pl.multiple_of(first, 96), 96)]

    def partial(k, p, t):
        loaded(t)
        slot = slot_of(k, p)
        block = standard_of(slot)
        tile = 3 * block + t
        right = jnp.where(tile < 8, tile // 2, 4 + (tile - 8) // 8)
        value = dot_tn(lefts[t][block], rbuf[right]).astype(LOW)
        for quarter in range(4):
            rows = slice(96 * quarter, 96 * (quarter + 1))
            pbuf[quarter % 2, t, slot, quarter // 2] = value[rows]
        for half in range(2):
            src = pbuf.at[1 - c, t, slot, half]
            send(src, core_at(slot, t, half), core_sem.at[t, slot, half], dev_c)

    def held(*at):
        return pbuf.at[(c, *at)]

    index_of = {"x": {}, "y": {}, "z": {}}
    for t in range(3):
        for k in "naeo":
            found = index_of[REDUCE_MODE[t][k]]
            found[k, t] = len(found)

    def first_send(k, p, t):
        slot = slot_of(k, p)
        if REDUCE_MODE[t][k] == "y":
            at, half = index_of["y"][k, t], "nf".index(p)
            send(held(t, slot, 1 - y), y_two.at[at, half], ytwo_sem.at[at, half], dev_y)
        elif p == "f":
            at = index_of["x"][k, t]
            send(held(t, slot), x_two.at[at], xtwo_sem.at[at], dev_x)

    def both_cores(k, p, t):
        slot = slot_of(k, p)
        for half in range(2):
            arrived(core_at(slot, t, half), core_sem.at[t, slot, half])
            other = core_at(slot, t, half)[...].astype(WIDE)
            pbuf[c, t, slot, half] = (wide(pbuf, c, t, slot, half) + other).astype(LOW)
        if REDUCE_MODE[t][k] == "z":
            half = "nf".index(p)
            send(held(t, slot), zf_in.at[t, half], zf_sem.at[t, half], dev_near)
        elif k != "o":
            first_send(k, p, t)

    def own_block(p, t):
        if REDUCE_MODE[t]["n"] == "z":
            slot, half = slot_of("o", p), "nf".index(p)
            arrived(zf_in.at[t, half], zf_sem.at[t, half])
            pbuf[c, t, slot] = (wide(pbuf, c, t, slot) + wide(zf_in, t, half)).astype(LOW)
        first_send("o", p, t)

    def turn(k, t):
        mode = REDUCE_MODE[t][k]
        if mode == "z":
            return
        at = index_of[mode][k, t]
        near, far = slot_of(k, "n"), slot_of(k, "f")
        if mode == "y":
            for half in range(2):
                arrived(y_two.at[at, half], ytwo_sem.at[at, half])
            pbuf[c, t, far, y] = (wide(pbuf, c, t, far, y) + wide(y_two, at, 1)).astype(LOW)
            send(held(t, far, y), x_one.at[at], xone_sem.at[at], dev_x)
        else:
            arrived(x_two.at[at], xtwo_sem.at[at])
            pbuf[c, t, near] = (wide(pbuf, c, t, near) + wide(x_two, at)).astype(LOW)
            send(held(t, near, 1 - y), y_one.at[at], yone_sem.at[at], dev_y)

    def plane_sum(k, t):
        mode = REDUCE_MODE[t][k]
        at = index_of[mode][k, t]
        mine = wide(pbuf, c, t, slot_of(k, "n"), y)
        if mode == "y":
            arrived(x_one.at[at], xone_sem.at[at])
            return mine + wide(y_two, at, 0) + wide(x_one, at)
        arrived(y_one.at[at], yone_sem.at[at])
        return mine + wide(y_one, at)

    def onward(k, t):
        if REDUCE_MODE[t][k] == "z":
            return
        row = "aen".index(k)
        tbuf[...] = plane_sum(k, t)
        if k == "n":
            ebuf[row, t] = tbuf[...].astype(LOW)
            send(ebuf.at[row, t], near_in.at[t], near_sem.at[t], dev_near)
            return

        line = "ae".index(k)

        @pl.when(inner)
        def _():
            arrived(mid_in.at[line, t], mid_sem.at[line, t])
            tbuf[...] += wide(mid_in, line, t)

        ebuf[row, t] = tbuf[...].astype(LOW)
        owner = (2 * place[k] + x, sq)
        send(ebuf.at[row, t], fin_in.at[t], fin_sem.at[t], owner, inner)
        send(ebuf.at[row, t], mid_in.at[line, t], mid_sem.at[line, t], dev_near, outer)

    squares = []

    def finish(t):
        value = plane_sum("o", t)
        if REDUCE_MODE[t]["n"] != "z":
            arrived(near_in.at[t], near_sem.at[t])
            value = value + wide(near_in, t)
        arrived(fin_in.at[t], fin_sem.at[t])
        total = (value + wide(fin_in, t)).astype(LOW)
        tlow[t] = total
        wide_total = total.astype(WIDE)
        rows = (wide_total * wide_total).reshape(-1, 8, wide_total.shape[-1])
        squares.append(jnp.sum(rows, axis=0))
        at = own_ref.at[t, sq]
        for device in (dev_y, dev_c):
            send(tlow.at[t], at, out_sem.at[t, sq], device)
        own_moves.append(move(tlow.at[t], at))

    steps = {
        "part": partial,
        "both": both_cores,
        "own": own_block,
        "turn": turn,
        "on": onward,
        "end": finish,
        "vs": vec_send,
        "va": vec_add,
        "gin": input_grad,
        "in": input_send,
    }
    for name, *at in REDUCE_ORDER:
        steps[name](*at)

    squares = squares[0] + squares[1] + squares[2]
    folded = squares[:, :128]
    for lane in range(1, squares.shape[-1] // 128):
        folded = folded + squares[:, 128 * lane : 128 * (lane + 1)]
    s_own[...] = folded
    for step in range(1, 4):
        send(s_own, s_seq.at[sq], seq_sem.at[sq], (dp, sq ^ step))
    s_seq[sq] = folded
    for t in [at[0] for name, *at in REDUCE_ORDER if name == "end"]:
        arrived(own_ref.at[t, sq ^ 2], out_sem.at[t, sq ^ 2])
        send(own_ref.at[t, sq ^ 2], own_ref.at[t, sq ^ 2], out_sem.at[t, sq ^ 2], dev_c)
    for step in range(1, 4):
        arrived(s_seq.at[sq ^ step], seq_sem.at[sq ^ step])
    group = s_seq[0] + s_seq[1] + s_seq[2] + s_seq[3]
    s_dp[dp] = group
    for step in range(1, 8):
        send(s_dp.at[dp], s_dp.at[dp], dp_sem.at[dp], (dp ^ step, sq))
    for step in range(1, 8):
        arrived(s_dp.at[dp ^ step], dp_sem.at[dp ^ step])
    everyone = s_dp[0]
    for index in range(1, 8):
        everyone = everyone + s_dp[index]
    sq_ref[...] = everyone
    vt_ref[0:16] = vbuf[5][0:16]
    vt_ref[16:24] = vbuf[2][16:24]

    for t in range(3):
        arrived(own_ref.at[t, sq ^ 1], out_sem.at[t, sq ^ 1])
        arrived(own_ref.at[t, sq ^ 3], out_sem.at[t, sq ^ 3])
    for step in range(1, 4):
        other = sq ^ step
        there, member = other // 2, other % 2
        arrived(gi_ref.at[3 * there + 2 * member], in_sem.at[other, 0])
        arrived(gi_ref.at[3 * there + 1, pl.ds(64 * member, 64)], in_sem.at[other, 1])
    exchange.finish()
    for copy in own_moves:
        copy.wait()
    for copy, pred in remotes:
        if pred is None:
            copy.wait_send()
        else:
            pl.when(pred)(lambda copy=copy: copy.wait_send())


def reduce_all(
    owners, lengths, rows, out, left, qkv, d_out, d_branch, right, matrices, result, lse, sums,
    sent_dev,
):
    width = rows.shape[-1]
    part = TILE // 4
    hbm = pl.BlockSpec(memory_space=pl.ANY)
    vmem = pl.BlockSpec(memory_space=pltpu.VMEM)
    smem = pl.BlockSpec(memory_space=pltpu.SMEM)
    dma = pltpu.SemaphoreType.DMA
    modes = "".join(mode for modes in REDUCE_MODE for mode in modes.values())
    x_first, y_first = max(modes.count("x"), 1), max(modes.count("y"), 1)
    near_over = int(any(mode["n"] != "z" for mode in REDUCE_MODE))

    def low(*shape):
        return pltpu.VMEM(shape + (part, width), LOW)

    owned, totals, squares, input_grad, output = pl.pallas_call(
        reduce_body,
        out_shape=(
            jax.ShapeDtypeStruct((3, 4, part, width), LOW),
            jax.ShapeDtypeStruct((24, width), WIDE),
            jax.ShapeDtypeStruct((8, 128), WIDE),
            jax.ShapeDtypeStruct((sent_dev, 128, width), LOW),
            jax.ShapeDtypeStruct((sent_dev, 128, width), LOW),
        ),
        in_specs=[smem] * 2 + [hbm] * 9 + [vmem] * 2,
        out_specs=(hbm, vmem, vmem, hbm, hbm),
        scratch_shapes=[
            pltpu.VMEM((8, 768, TILE), LOW),
            pltpu.VMEM((8, 768, TILE), LOW),
            pltpu.VMEM((8, 768, TILE), LOW),
            pltpu.VMEM((6, 768, width), LOW),
            pltpu.VMEM((3, width, width), LOW),
            pltpu.VMEM((768, width), LOW),
            pltpu.VMEM((width // 128, 2, 256, 128), LOW),
            pltpu.VMEM((width // 128, 2, 256, 128), LOW),
            low(2, 3, 8, 2),
            pltpu.VMEM((48 * part, width), LOW),
            low(x_first, 2),
            low(y_first),
            low(y_first, 2),
            low(x_first),
            low(3, 2, 2),
            low(2, 3),
            low(3),
            low(3 if near_over else 1),
            low(2 + near_over, 3),
            pltpu.VMEM((part, width), WIDE),
            low(3),
            pltpu.VMEM((6, 24, width), WIDE),
            pltpu.VMEM((5, 24, width), WIDE),
            pltpu.VMEM((8, 128), WIDE),
            pltpu.VMEM((4, 8, 128), WIDE),
            pltpu.VMEM((8, 8, 128), WIDE),
            dma((160,)),
            dma((48,)),
            dma((3, 8, 2)),
            dma((x_first,)),
            dma((y_first,)),
            dma((y_first, 2)),
            dma((x_first,)),
            dma((3, 2)),
            dma((2, 3)),
            dma((3,)),
            dma((3,)),
            dma((5,)),
            dma((3, 4)),
            dma((4,)),
            dma((8,)),
            dma((4, 2)),
            dma((width // 128, 2)),
            dma((width // 128, 2)),
            pltpu.SemaphoreType.REGULAR,
        ]
        + EXCHANGE_SEMS,
        compiler_params=params(collective_id=2, has_side_effects=True),
        name="reduce_gradients",
    )(
        owners, lengths, rows, out, left, qkv, d_out, d_branch, right, matrices, result, lse, sums
    )
    return owned.reshape(3 * TILE, width), totals, squares, input_grad, output


def optimizer_body(
    len_ref, mem_ref, g_ref, sq_ref, tot_ref, w_ref, one_ref, two_ref, vw_ref, vone_ref, vtwo_ref,
    out_from, in_from, norm_ref, emb_ref, *rest,
):
    outs, (out_to, in_to, clip_ref) = rest[:-3], rest[-3:]
    count = vw_ref.shape[0]

    out_to[...] = out_from[...]
    in_to[...] = in_from[...]

    @pl.when(pl.program_id(0) == 0)
    def _():
        gradient = tot_ref[:count]
        total = jnp.sum(sq_ref[...], keepdims=True) + jnp.sum(gradient * gradient, keepdims=True)
        norm = jnp.sqrt(total)
        norm_ref[...] = norm
        clip_ref[...] = jnp.broadcast_to(MAX_NORM / jnp.maximum(norm, MAX_NORM), clip_ref.shape)

    clip = clip_ref[...]

    def update(refs, outs, gradient, rate, decay):
        new = adam_step(refs[2][...], refs[0][...], refs[1][...], gradient, rate, decay)
        for ref, value in zip(outs, new + (new[2].astype(LOW),)):
            ref[...] = value

    update(
        (one_ref, two_ref, w_ref), outs[:4], g_ref[...].astype(WIDE) * clip,
        RATE_MATRIX, WEIGHT_DECAY,
    )

    @pl.when(pl.program_id(0) == 0)
    def _():
        update((vone_ref, vtwo_ref, vw_ref), outs[4:], tot_ref[:count] * clip, RATE_VECTOR, 0.0)
        groups, most = mem_ref.shape
        sentences = len_ref.shape[0]
        first = lax.axis_index("dp") * sentences
        pooled = [
            tot_ref[16 + s : 17 + s] / len_ref[s].astype(WIDE) for s in range(sentences)
        ]
        for g in range(groups):
            listed = jnp.int32(0)
            total = jnp.zeros_like(pooled[0])
            for m in range(most):
                listed += jnp.where(mem_ref[g, m] >= 0, 1, 0)
            for s in range(sentences):
                times = jnp.int32(0)
                for m in range(most):
                    times += jnp.where(mem_ref[g, m] == first + s, 1, 0)
                total = total + pooled[s] * times.astype(WIDE)
            emb_ref[g : g + 1] = total / listed.astype(WIDE)


def optimizer(lengths, members, owned, squares, totals, matrices, vectors, exchanged):
    block_rows, width = owned.shape
    steps = 4 if block_rows % 64 == 0 else 1
    smem = pl.BlockSpec(memory_space=pltpu.SMEM)
    mat = pl.BlockSpec((block_rows // steps, width), lambda i: (i, 0))

    def whole(shape):
        return pl.BlockSpec(shape, lambda i: (0, 0))

    sentences, positions_here = exchanged[0].shape[:2]
    passed = pl.BlockSpec((sentences, positions_here // steps, width), lambda i: (0, i, 0))
    vec = whole(vectors[0].shape)
    embeddings = (members.shape[0], width)
    return pl.pallas_call(
        optimizer_body,
        grid=(steps,),
        in_specs=[smem, smem, mat, whole(squares.shape), whole(totals.shape)]
        + [mat] * 3
        + [vec] * 3
        + [passed] * 2,
        out_specs=(whole((1, 1)), whole(embeddings)) + (mat,) * 4 + (vec,) * 4
        + (passed,) * 2,
        out_shape=(
            jax.ShapeDtypeStruct((1, 1), WIDE),
            jax.ShapeDtypeStruct(embeddings, WIDE),
        )
        + tuple(
            jax.ShapeDtypeStruct(like.shape, dtype)
            for like in (owned, vectors[0])
            for dtype in (WIDE, WIDE, WIDE, LOW)
        )
        + tuple(jax.ShapeDtypeStruct(like.shape, LOW) for like in exchanged),
        scratch_shapes=[pltpu.VMEM((1, width), WIDE)],
        compiler_params=params(),
        name="optimizer",
    )(lengths, members, owned, squares, totals, *matrices, *vectors, *exchanged)


def to_positions(value):
    width = value.shape[1]
    moved = jnp.concatenate(
        [value[:512].reshape(4, 128, width), value[512:].reshape(4, 64, width)], axis=1
    )
    moved = lax.all_to_all(moved, "seq", split_axis=0, concat_axis=0, tiled=True)
    rows = []
    for y in range(2):
        rows.append(moved[2 * y, :128])
        rows.append(jnp.concatenate([moved[2 * y, 128:], moved[2 * y + 1, 128:]], axis=0))
        rows.append(moved[2 * y + 1, :128])
    return jnp.stack(rows)


def to_rows(tokens):
    width = tokens.shape[-1]
    core = lax.axis_index("seq") % 2
    pieces = []
    for j in range(4):
        y, c = j // 2, j % 2
        pieces += [tokens[3 * y + 2 * c], tokens[3 * y + 1]]
    moved = jnp.concatenate(pieces, axis=0).reshape(4, 256, width)
    moved = lax.all_to_all(moved, "seq", split_axis=0, concat_axis=0, tiled=True)
    shared = moved[:, 128:].reshape(4, 2, 64, width)
    own = lax.dynamic_index_in_dim(shared, core, 1, keepdims=False)
    other = lax.dynamic_index_in_dim(shared, 1 - core, 1, keepdims=False)
    return jnp.concatenate(
        [moved[:, :128].reshape(512, width), own.reshape(256, width), other.reshape(256, width)],
        axis=0,
    )


def local(
    tokens,
    grad_out,
    lengths,
    members,
    owners,
    mat_master,
    mat_moment1,
    mat_moment2,
    vec_master,
    vec_moment1,
    vec_moment2,
):
    sent_dev, local_len, model_width = tokens.shape
    dp_count = lax.axis_size("dp")
    block_rows = mat_master.shape[0]
    direct = dp_count == 8 and block_rows == 3 * TILE

    if direct:
        blocks = owners
        weights, rows, qkv, matrices, attended, out_grad, lse = front(
            owners, lengths, mat_master, tokens, grad_out, vec_master
        )
    else:
        gathered = lax.all_gather(mat_master.astype(LOW), "dp", axis=0, tiled=True)
        weights = gathered.reshape(dp_count, block_rows, model_width)[owners]
        weights = weights.reshape(-1, TILE, model_width)
        rows = to_rows(tokens)
        blocks = jnp.arange(weights.shape[0] // 3, dtype=jnp.int32)
        qkv = qkv_project(blocks, rows, weights, vec_master)
        attended, lse, out_grad = attend(lengths, qkv, grad_out)
    result, left, right, d_attended, d_branch, sums = middle(
        blocks, lengths, attended, rows, out_grad, weights, vec_master
    )
    if direct:
        owned, totals, squares, input_grad, output = reduce_all(
            owners,
            lengths,
            rows,
            attended,
            left,
            qkv,
            d_attended,
            d_branch,
            right,
            matrices,
            result,
            lse,
            sums,
            sent_dev,
        )
    else:
        dq, dk, dv, output = attend_back(
            lengths, qkv, lse, d_attended, attended, result, sent_dev
        )
        grad_rows = grad_in(blocks, dq, dk, dv, d_branch, weights)
        grads = grad_ff(blocks, left, right)
        grads, sums_qv = grad_attn(blocks, rows, dq, dk, dv, attended, d_branch, grads)
        input_grad = to_positions(grad_rows)
        inverse = jnp.argsort(owners)
        grads = grads.reshape(dp_count, block_rows, model_width)[inverse]
        grads = grads.reshape(dp_count * block_rows, model_width)
        quarter = lax.psum_scatter(grads, ("dp", "seq"), scatter_dimension=0, tiled=True)
        owned = lax.all_gather(quarter, "seq", axis=0, tiled=True)
        quarter = quarter.astype(WIDE)
        group = lax.axis_index("seq") // 2
        core = lax.axis_index("seq") % 2
        place = jnp.arange(8)[:, None]
        pooled = jnp.where(place == 3 * group + 2 * core, sums[10:11], 0.0) + jnp.where(
            place == 3 * group + 1, sums[11:12], 0.0
        )
        pooled = lax.psum(pooled, "seq")
        local_vec = jnp.concatenate([sums_qv[0:2], sums[0:14]], axis=0)
        squares, vec_total = lax.psum(
            (jnp.sum(quarter * quarter), local_vec), ("dp", "seq")
        )
        squares = jnp.full((8, 128), squares / 1024.0)
        totals = jnp.concatenate([vec_total, pooled], axis=0)

    norm, embeddings, *new, output, input_grad = optimizer(
        lengths,
        members,
        owned,
        squares,
        totals,
        (mat_master, mat_moment1, mat_moment2),
        (vec_master, vec_moment1, vec_moment2),
        (output, input_grad),
    )
    return (output, input_grad, embeddings, norm.reshape(()), *new)


def solution(mesh):
    placed = (
        P("dp", "seq", None),
        P("dp", "seq", None),
        P("dp"),
        P("dp", None),
        P(),
        P("dp", None),
        P("dp", None),
        P("dp", None),
        P(),
        P(),
        P(),
    )
    return jax.shard_map(
        local,
        mesh=mesh,
        in_specs=placed,
        out_specs=(
            P("dp", "seq", None),
            P("dp", "seq", None),
            P("dp", None),
            P(),
            P("dp", None),
            P("dp", None),
            P("dp", None),
            P("dp", None),
            P(),
            P(),
            P(),
            P(),
        ),
        check_vma=False,
    )
```

```python
import functools

import jax
import jax.numpy as jnp
from jax import lax
from jax.experimental import pallas as pl
from jax.experimental.pallas import tpu as pltpu
from jax.sharding import PartitionSpec as P

HEADS = 12
HEAD_DIM = 64
FEEDFWD_UNITS = 3072
STEP = 10


NORM_EPS = 1e-06
MASK_FILL = -1e30
MAX_NORM = 1.0
ADAM_ONE = 0.9
ADAM_TWO = 0.999
ADAM_EPS = 1e-08
WEIGHT_DECAY = 0.01
RATE_MATRIX = 0.04
RATE_VECTOR = 0.5

FWD_PAIRS = 6
BACK_PAIRS = 6
NORM_ROWS = 128
TILE = 384
VMEM_LIMIT = 60 * 1024 * 1024
MESH_ID = pl.DeviceIdType.MESH
LOW = jnp.bfloat16
WIDE = jnp.float32


def adam_step(master, moment_one, moment_two, gradient, learn_rate, decay_rate):
    moment_one = ADAM_ONE * moment_one + (1.0 - ADAM_ONE) * gradient
    moment_two = ADAM_TWO * moment_two + (1.0 - ADAM_TWO) * gradient * gradient
    scaled_one = moment_one / (1.0 - ADAM_ONE**STEP)
    scaled_two = moment_two / (1.0 - ADAM_TWO**STEP)
    master = master - learn_rate * (
        scaled_one / (jnp.sqrt(scaled_two) + ADAM_EPS) + decay_rate * master
    )
    return (moment_one, moment_two, master)


def dot_nn(left, right):
    return jnp.dot(left, right, preferred_element_type=WIDE)


def dot_nt(left, right):
    return lax.dot_general(
        left, right, (((1,), (1,)), ((), ())), preferred_element_type=WIDE
    )


def dot_tn(left, right):
    return lax.dot_general(
        left, right, (((0,), (0,)), ((), ())), preferred_element_type=WIDE
    )


def tile_at(owners, tile):
    return 3 * owners[tile // 3] + tile % 3


def params(**kwargs):
    return pltpu.CompilerParams(vmem_limit_bytes=VMEM_LIMIT, **kwargs)


GATHER_HEAD = 10
GATHER_ORDER = (
    ("tk",), ("xb", 1), ("xs", 0), ("zs", 0), ("zs", 2), ("xb", 0), ("r", 1, 0), ("r", 0, 0),
    ("xs", 1), ("r", 1, 2), ("zs", 1), ("xr", 1, 0), ("r", 0, 2), ("xb", 2), ("r", 1, 1),
    ("r", 2, 0), ("r", 2, 2), ("r", 0, 1), ("xs", 2), ("xob", 2), ("r", 2, 1), ("zx", 0),
    ("xo", 0), ("zx", 1), ("yr", 1, 2), ("xr", 1, 1), ("tf",), ("zx", 2), ("xr", 2, 0), ("xo", 2),
    ("yr", 2, 1), ("e1", 0), ("xob", 1), ("xr", 2, 2), ("yx", 1, 1), ("xo", 1), ("xr", 1, 2),
    ("xr", 2, 1), ("e1", 1), ("xsr", 0), ("yx", 1, 0), ("e1", 2), ("yx", 1, 2), ("yx", 2, 2),
    ("yr", 2, 0), ("yr", 1, 0), ("e2", 2), ("yr", 1, 1), ("xsr", 1), ("xob", 0), ("e2", 1),
    ("yx", 2, 0), ("xsr", 2), ("yr", 2, 2), ("e2", 0), ("yx", 2, 1),
)


def front_body(
    own_of_ref, len_ref, w_ref, x_ref, g_ref, vec_ref,
    weights_ref, rows_ref, qkv_ref, mats_ref, o_ref, gy_ref, lse_ref,
    wide_buf, own_buf, out_ref, xo_ref, qkv_buf, mats_buf, o_buf,
    send_sem, recv_sem, tok_recv, local_sem, ex_send, ex_recv, ex_local,
):
    dp, sq = lax.axis_index("dp"), lax.axis_index("seq")
    z, x = dp // 2, dp % 2
    y, c = sq // 2, sq % 2
    q, qc, qy, qyc = sq, sq ^ 1, sq ^ 2, sq ^ 3
    dev_c, dev_y, dev_yc, dev_x = (dp, sq ^ 1), (dp, sq ^ 2), (dp, sq ^ 3), (dp ^ 1, sq)
    dev_near = (dp ^ 2, sq)
    has_up, has_down, inner = z < 3, z > 0, (z > 0) & (z < 3)
    dev_up = (jnp.minimum(dp + 2, dp % 2 + 6), sq)
    dev_down = (jnp.maximum(dp - 2, dp % 2), sq)
    sources = (z ^ 1, jnp.where(z < 2, 2, 1), jnp.where(z < 2, 3, 0))
    used = [0, 0]
    started, locals_ = [], []

    def move(src, dst):
        copy = pltpu.make_async_copy(src, dst, local_sem.at[used[1]])
        used[1] += 1
        copy.start()
        return copy

    loads = []
    for at in (q, qy, qc, qyc):
        thirds = pl.ds(3 * at, 3)
        loads.append(move(w_ref.at[thirds], wide_buf.at[thirds]))

    barrier = pltpu.get_barrier_semaphore()

    def greet(device):
        pl.semaphore_signal(barrier, inc=1, device_id=device, device_id_type=MESH_ID)

    for device in (dev_c, dev_y, dev_yc, dev_x):
        greet(device)
    pl.when(has_up)(lambda: greet(dev_up))
    pl.when(has_down)(lambda: greet(dev_down))
    pl.semaphore_wait(barrier, 4 + jnp.where(inner, 2, 1))

    def send(src, dst, recv, device, pred=None):
        copy = pltpu.make_async_remote_copy(
            src_ref=src,
            dst_ref=dst,
            send_sem=send_sem.at[used[0]],
            recv_sem=recv,
            device_id=device,
            device_id_type=MESH_ID,
        )
        used[0] += 1
        if pred is None:
            copy.start()
        else:
            pl.when(pred)(lambda: copy.start())
        started.append((copy, pred))

    def piece(slot, quarter, h, device, pred=None, own=False):
        at = out_ref.at[slot, 3 * quarter + h]
        src = own_buf.at[3 * quarter + h] if own else at
        send(src, at, recv_sem.at[slot, quarter, h], device, pred)

    def arrived(slot, quarter, h):
        at = out_ref.at[slot, 3 * quarter + h]
        pltpu.make_async_copy(at, at, recv_sem.at[slot, quarter, h]).wait()

    def taken(slot, quarter, h):
        arrived(slot, quarter, h)
        piece(slot, quarter, h, dev_c)

    def near(k):
        return 2 * sources[k] + x

    def far(k):
        return 2 * sources[k] + 1 - x

    oy = 1 - y
    full_own, full_sib = 3 * y + 2 * c, 3 * y + 2 * (1 - c)
    full_far, full_cross = 3 * oy + 2 * c, 3 * oy + 2 * (1 - c)

    def full_rows(j):
        return xo_ref.at[pl.ds(128 * j, 128)]

    def half_rows(part, j, core):
        return xo_ref.at[pl.ds(512 + 256 * (part ^ core) + 64 * j, 64)]

    def token_send():
        send(x_ref.at[full_far], full_rows(sq), tok_recv.at[sq, 0], dev_y)
        for part in range(2):
            src = x_ref.at[3 * oy + 1, pl.ds(64 * part, 64)]
            send(src, half_rows(part, sq, c), tok_recv.at[sq, 1 + part], dev_y)
        send(x_ref.at[full_cross], full_rows(sq), tok_recv.at[sq, 0], dev_yc)
        send(x_ref.at[full_sib], full_rows(sq), tok_recv.at[sq, 0], dev_c)
        locals_.append(move(x_ref.at[full_own], full_rows(sq)))
        for part in range(2):
            src = x_ref.at[3 * y + 1, pl.ds(64 * part, 64)]
            send(src, half_rows(part, sq, 1 - c), tok_recv.at[sq, 1 + part], dev_c)
            locals_.append(move(src, half_rows(part, sq, c)))

    def token_forward():
        for part in range(2):
            at = half_rows(part, sq ^ 2, c)
            pltpu.make_async_copy(at, at, tok_recv.at[sq ^ 2, 1 + part]).wait()
            send(at, half_rows(part, sq ^ 2, 1 - c), tok_recv.at[sq ^ 2, 1 + part], dev_c)

    def own_line(h):
        piece(dp, q, h, dev_up, has_up, own=True)
        piece(dp, q, h, dev_down, has_down, own=True)

    def line(k, h):
        arrived(near(k), q, h)
        onward = (jnp.where(sources[k] < z, dev_up[0], dev_down[0]), sq)
        piece(near(k), q, h, onward, inner)
        if k > 0:
            piece(near(k), q, h, dev_x)
            piece(near(k), q, h, dev_y)
        piece(near(k), q, h, dev_c)

    def from_x_own(h):
        arrived(dp ^ 1, q, h)
        piece(dp ^ 1, q, h, dev_near)
        piece(dp ^ 1, q, h, dev_c)

    def near_other_half(h):
        arrived(near(0), qy, h)
        piece(near(0), qy, h, dev_x)
        piece(near(0), qy, h, dev_c)

    def from_x(k, h):
        arrived(far(k), q, h)
        piece(far(k), q, h, dev_y)
        piece(far(k), q, h, dev_c)

    steps = {
        "tk": token_send,
        "tf": token_forward,
        "zs": own_line,
        "zx": lambda h: piece(dp, qy, h, dev_near, own=True),
        "xs": lambda h: piece(dp, q, h, dev_x, own=True),
        "xb": lambda h: piece(dp, qy, h, dev_x, own=True),
        "r": line,
        "xo": from_x_own,
        "xob": lambda h: taken(dp ^ 1, qy, h),
        "e1": near_other_half,
        "e2": lambda h: taken(far(0), q, h),
        "yr": lambda k, h: taken(near(k), qy, h),
        "xr": from_x,
        "xsr": lambda h: taken(far(0), qy, h),
        "yx": lambda k, h: taken(far(k), qy, h),
    }

    def round_own(index, quarter):
        loads[index].wait()
        thirds = pl.ds(3 * quarter, 3)
        own_buf[thirds] = wide_buf[thirds].astype(LOW)

    round_own(0, q)
    round_own(1, qy)
    for name, *at in GATHER_ORDER[:GATHER_HEAD]:
        steps[name](*at)
    round_own(2, qc)
    round_own(3, qyc)
    locals_.append(move(own_buf, out_ref.at[dp]))
    for name, *at in GATHER_ORDER[GATHER_HEAD:]:
        steps[name](*at)
    exchange = Exchange(by_sentence(g_ref, gy_ref), ex_send, ex_recv, ex_local)
    exchange.start()
    for step in range(1, 8):
        for h in range(3):
            arrived(dp ^ step, qc, h)
            arrived(dp ^ step, qyc, h)
    for other in (sq ^ 1, sq ^ 2, sq ^ 3):
        at = full_rows(other)
        pltpu.make_async_copy(at, at, tok_recv.at[other, 0]).wait()
    for other in (sq ^ 1, sq ^ 3):
        for part in range(2):
            at = half_rows(part, other, c)
            pltpu.make_async_copy(at, at, tok_recv.at[other, 1 + part]).wait()
    for copy in locals_:
        copy.wait()
    stores = [move(out_ref.at[slot], weights_ref.at[slot]) for slot in range(8)]
    stores.append(move(xo_ref, rows_ref))

    for part in range(3):
        for half in range(2):
            tile = 2 * part + half
            held = out_ref[own_of_ref[tile // 3], 4 * (tile % 3) : 4 * (tile % 3) + 4]
            rows = slice(TILE * half, TILE * (half + 1))
            mats_buf[part, rows] = held.reshape(TILE, held.shape[-1])
        stores.append(move(mats_buf.at[part], mats_ref.at[part]))
        value = dot_nn(xo_ref[...], mats_buf[part])
        if part == 0:
            value = (value + vec_ref[0:1]) * HEAD_DIM ** (-0.5)
        elif part == 2:
            value = value + vec_ref[1:2]
        qkv_buf[part] = value.astype(LOW)
        stores.append(move(qkv_buf.at[part], qkv_ref.at[part]))

    def attend_block(block, carry):
        bias = key_bias(len_ref, block == 2)
        at = pl.ds(pl.multiple_of(256 * block, 256), 256)
        keys = pl.ds(pl.multiple_of(512 * (block // 2), 512), 512)
        pairs = qkv_buf.shape[-1] // 128

        def scores_of(pair):
            lanes = slice(128 * pair, 128 * (pair + 1))
            return pair_scores(qkv_buf[0, at, lanes], qkv_buf[1, keys, lanes], bias)

        ahead = scores_of(0)
        for pair in range(pairs):
            scores = ahead
            if pair + 1 < pairs:
                ahead = scores_of(pair + 1)
            lanes = slice(128 * pair, 128 * (pair + 1))
            out, logs = attend_pair(scores, qkv_buf[2, keys, lanes])
            o_buf[at, lanes] = out
            for head in range(2):
                lse_ref[pair, head : head + 1, at] = logs[head]
        return carry

    lax.fori_loop(0, 3, attend_block, 0)
    stores.append(move(o_buf, o_ref))
    exchange.finish()
    for copy in stores:
        copy.wait()
    for copy, pred in started:
        if pred is None:
            copy.wait_send()
        else:
            pl.when(pred)(lambda copy=copy: copy.wait_send())


def front(owners, lengths, block, tokens, grad_out, vectors):
    block_rows, width = block.shape
    part = block_rows // 12
    hbm = pl.BlockSpec(memory_space=pl.ANY)
    smem = pl.BlockSpec(memory_space=pltpu.SMEM)
    vmem = pl.BlockSpec(memory_space=pltpu.VMEM)
    dma = pltpu.SemaphoreType.DMA
    flat = jax.ShapeDtypeStruct((768, width), LOW)
    weights, *rest = pl.pallas_call(
        front_body,
        out_shape=(
            jax.ShapeDtypeStruct((8, 12, part, width), LOW),
            jax.ShapeDtypeStruct((1024, width), LOW),
            jax.ShapeDtypeStruct((3, 1024, width), LOW),
            jax.ShapeDtypeStruct((3, width, width), LOW),
            flat,
            flat,
            jax.ShapeDtypeStruct((HEADS // 2, 2, 768), WIDE),
        ),
        in_specs=[smem] * 2 + [hbm] * 3 + [vmem],
        out_specs=(hbm,) * 6 + (vmem,),
        scratch_shapes=[
            pltpu.VMEM((12, part, width), WIDE),
            pltpu.VMEM((12, part, width), LOW),
            pltpu.VMEM((8, 12, part, width), LOW),
            pltpu.VMEM((1024, width), LOW),
            pltpu.VMEM((3, 1024, width), LOW),
            pltpu.VMEM((3, width, width), LOW),
            pltpu.VMEM((768, width), LOW),
            dma((160,)),
            dma((8, 4, 3)),
            dma((4, 3)),
            dma((24,)),
        ]
        + EXCHANGE_SEMS,
        compiler_params=params(collective_id=1, has_side_effects=True),
        name="gather_attend",
    )(owners, lengths, block.reshape(12, part, width), tokens, grad_out, vectors)
    return weights.reshape(8 * block_rows // TILE, TILE, width), *rest


def qkv_body(map_ref, x_ref, top_ref, low_ref, vec_ref, out_ref):
    part = pl.program_id(0)
    scale = jnp.where(part == 0, HEAD_DIM ** (-0.5), 1.0)
    value = dot_nn(x_ref[:, :TILE], top_ref[0]) + dot_nn(x_ref[:, TILE:], low_ref[0])
    bias = jnp.where(part == 0, vec_ref[0:1], jnp.where(part == 2, vec_ref[1:2], 0.0))
    out_ref[0] = ((value + bias) * scale).astype(LOW)


def qkv_project(owners, rows, weights, vectors):
    count, width = rows.shape
    return pl.pallas_call(
        qkv_body,
        grid_spec=pltpu.PrefetchScalarGridSpec(
            num_scalar_prefetch=1,
            grid=(3,),
            in_specs=[
                pl.BlockSpec((count, width), lambda i, m: (0, 0)),
                pl.BlockSpec((1, TILE, width), lambda i, m: (tile_at(m, 2 * i), 0, 0)),
                pl.BlockSpec((1, TILE, width), lambda i, m: (tile_at(m, 2 * i + 1), 0, 0)),
                pl.BlockSpec(vectors.shape, lambda i, m: (0, 0)),
            ],
            out_specs=pl.BlockSpec((1, count, width), lambda i, m: (i, 0, 0)),
        ),
        out_shape=jax.ShapeDtypeStruct((3, count, width), LOW),
        compiler_params=params(),
        name="qkv",
    )(owners, rows, weights, weights, vectors)


def group_barrier(dp, sq):
    barrier = pltpu.get_barrier_semaphore()
    for step in range(1, 4):
        pl.semaphore_signal(
            barrier, inc=1, device_id=(dp, sq ^ step), device_id_type=MESH_ID
        )
    pl.semaphore_wait(barrier, 3)


class Exchange:
    def __init__(self, pieces, send_sem, recv_sem, local_sem):
        self.dp, self.sq = lax.axis_index("dp"), lax.axis_index("seq")
        self.pieces = pieces
        self.sems = (send_sem, recv_sem, local_sem)

    def copies(self):
        send_sem, recv_sem, local_sem = self.sems
        out = []
        for step in (2, 3, 1):
            target = self.sq ^ step
            for kind, (src, dst) in enumerate(self.pieces(self.sq, target)):
                out.append(
                    pltpu.make_async_remote_copy(
                        src_ref=src,
                        dst_ref=dst,
                        send_sem=send_sem.at[step - 1, kind],
                        recv_sem=recv_sem.at[self.sq, kind],
                        device_id=(self.dp, target),
                        device_id_type=MESH_ID,
                    )
                )
        for kind, (src, dst) in enumerate(self.pieces(self.sq, self.sq)):
            out.append(pltpu.make_async_copy(src, dst, local_sem.at[kind]))
        return out

    def start(self):
        for copy in self.copies():
            copy.start()

    def finish(self):
        copies = self.copies()
        for copy in copies[:6]:
            copy.wait_send()
        for copy in copies[6:]:
            copy.wait()
        for step in range(1, 4):
            source = self.sq ^ step
            for kind, (_, dst) in enumerate(self.pieces(source, self.sq)):
                pltpu.make_async_copy(dst, dst, self.sems[1].at[source, kind]).wait()


EXCHANGE_SEMS = [
    pltpu.SemaphoreType.DMA((3, 2)),
    pltpu.SemaphoreType.DMA((4, 2)),
    pltpu.SemaphoreType.DMA((2,)),
]


def by_sentence(src, dst):
    def pieces(source, target):
        y, c = target // 2, target % 2
        return (
            (src.at[3 * y + 2 * c], dst.at[pl.ds(128 * source, 128)]),
            (src.at[3 * y + 1, pl.ds(64 * c, 64)], dst.at[pl.ds(512 + 64 * source, 64)]),
        )

    return pieces


def by_position(src, dst):
    def pieces(source, target):
        y, c = source // 2, source % 2
        return (
            (src.at[pl.ds(128 * target, 128)], dst.at[3 * y + 2 * c]),
            (src.at[pl.ds(512 + 64 * target, 64)], dst.at[3 * y + 1, pl.ds(64 * c, 64)]),
        )

    return pieces


def sentence_length(lengths_ref, shared):
    sq = lax.axis_index("seq")
    group, core = sq // 2, sq % 2
    return jnp.where(shared, lengths_ref[3 * group + 1], lengths_ref[3 * group + 2 * core])


def positions(shape, shared, first=0):
    row = first + lax.broadcasted_iota(jnp.int32, shape, 0)
    own = lax.axis_index("seq") % 2
    half = row // 256
    part = row - 256 * half
    core = own + half - 2 * own * half
    mixed = (part // 64) * 128 + part % 64 + 64 * core
    return jnp.where(shared, mixed, row)


def key_bias(lengths_ref, shared):
    inside = positions((512, 128), shared) < sentence_length(lengths_ref, shared)
    bias = jnp.where(inside, 0.0, MASK_FILL)
    return jnp.concatenate([bias, bias], axis=1)


def head_masks(shape):
    lane = lax.broadcasted_iota(jnp.int32, shape, 1)
    return (lane < HEAD_DIM, lane >= HEAD_DIM)


def pair_scores(queries, keys, bias):
    return [
        dot_nt(keys, jnp.where(mask, queries, jnp.zeros_like(queries))) + bias
        for mask in head_masks(queries.shape)
    ]


def attend_pair(pair_of_scores, values):
    value_t = values.T
    outs, logs = [], []
    for head, scores in enumerate(pair_of_scores):
        top = jnp.max(scores, axis=0, keepdims=True)
        shifted = jnp.exp(scores - top)
        total = jnp.sum(shifted, axis=0, keepdims=True)
        part = value_t[HEAD_DIM * head : HEAD_DIM * (head + 1)]
        outs.append(dot_nn(part, shifted.astype(LOW)) * (1.0 / total))
        logs.append(top + jnp.log(total))
    return jnp.concatenate(outs, axis=0).T.astype(LOW), logs


def attend_body(
    len_ref, q_ref, k_ref, v_ref, g_ref, o_ref, lse_ref, gy_ref, send_sem, recv_sem, local_sem
):
    block, group = pl.program_id(0), pl.program_id(1)
    exchange = Exchange(by_sentence(g_ref, gy_ref), send_sem, recv_sem, local_sem)

    @pl.when((block == 0) & (group == 0))
    def _():
        group_barrier(exchange.dp, exchange.sq)
        exchange.start()

    bias = key_bias(len_ref, block == 2)
    for pair in range(q_ref.shape[-1] // 128):
        lanes = slice(128 * pair, 128 * (pair + 1))
        scores = pair_scores(q_ref[0, :, lanes], k_ref[0, :, lanes], bias)
        out, logs = attend_pair(scores, v_ref[0, :, lanes])
        o_ref[:, lanes] = out
        for head in range(2):
            lse_ref[0, 2 * pair + head : 2 * pair + head + 1, :] = logs[head]

    @pl.when((block == 2) & (group == pl.num_programs(1) - 1))
    def _():
        exchange.finish()


def attend(lengths, qkv, grad_out):
    width = qkv.shape[-1]
    groups = width // 128 // FWD_PAIRS
    lanes = 128 * FWD_PAIRS
    hbm = pl.BlockSpec(memory_space=pl.ANY)
    return pl.pallas_call(
        attend_body,
        grid=(3, groups),
        in_specs=[
            pl.BlockSpec(memory_space=pltpu.SMEM),
            pl.BlockSpec((1, 256, lanes), lambda i, h: (0, i, h)),
            pl.BlockSpec((1, 512, lanes), lambda i, h: (1, i // 2, h)),
            pl.BlockSpec((1, 512, lanes), lambda i, h: (2, i // 2, h)),
            hbm,
        ],
        out_specs=(
            pl.BlockSpec((256, lanes), lambda i, h: (i, h)),
            pl.BlockSpec((1, 2 * FWD_PAIRS, 256), lambda i, h: (h, 0, i)),
            hbm,
        ),
        out_shape=(
            jax.ShapeDtypeStruct((768, width), LOW),
            jax.ShapeDtypeStruct((groups, 2 * FWD_PAIRS, 768), WIDE),
            jax.ShapeDtypeStruct((768, width), LOW),
        ),
        scratch_shapes=EXCHANGE_SEMS,
        compiler_params=params(collective_id=3, has_side_effects=True),
        name="attend",
    )(lengths, qkv, qkv, qkv, grad_out)


def back_first(head, queries, keys, values, grads, bias):
    mask = head_masks(queries.shape)[head]
    query = jnp.where(mask, queries, jnp.zeros_like(queries))
    grad = jnp.where(mask, grads, jnp.zeros_like(grads))
    return query, grad, dot_nt(keys, query) + bias, dot_nt(values, grad)


def back_second(head, first, keys_t, inner, log):
    query, grad, scores, d_probs = first
    rows = slice(HEAD_DIM * head, HEAD_DIM * (head + 1))
    inner_sum = jnp.sum(inner[rows], axis=0, keepdims=True)
    probs = jnp.exp(scores - log)
    d_scores = (probs * (d_probs - inner_sum)).astype(LOW)
    d_value = dot_nn(probs.astype(LOW), grad)
    return dot_nn(keys_t[rows], d_scores), dot_nn(d_scores, query), d_value


def back_inner(grads, outs):
    return (grads.astype(WIDE) * outs.astype(WIDE)).T


def back_query(parts):
    return (jnp.concatenate(parts, axis=0) * HEAD_DIM ** (-0.5)).T.astype(LOW)


def back_pair(queries, keys, values, grads, outs, logs, bias):
    keys_t, inner = keys.T, back_inner(grads, outs)
    found = []
    for head in range(2):
        first = back_first(head, queries, keys, values, grads, bias)
        found.append(back_second(head, first, keys_t, inner, logs[head : head + 1]))
    (query_a, key_a, value_a), (query_b, key_b, value_b) = found
    return back_query([query_a, query_b]), key_a + key_b, value_a + value_b


def attend_back_body(
    len_ref, q_ref, k_ref, v_ref, lse_ref, do_ref, o_ref, y_ref,
    dq_ref, dk_ref, dv_ref, out_ref,
    acc, keep, give, take, send_sem, recv_sem, local_sem, give_sem, take_sem,
):
    group, block = pl.program_id(0), pl.program_id(1)
    exchange = Exchange(by_position(y_ref, out_ref), send_sem, recv_sem, local_sem)
    dp, sq = exchange.dp, exchange.sq

    @pl.when((block == 0) & (group == 0))
    def _():
        group_barrier(dp, sq)
        exchange.start()

    bias = key_bias(len_ref, block == 0)
    d_keys, d_values = [], []
    for pair in range(q_ref.shape[-1] // 128):
        lanes = slice(128 * pair, 128 * (pair + 1))
        d_query, d_key, d_value = back_pair(
            q_ref[0, :, lanes], k_ref[0, :, lanes], v_ref[0, :, lanes], do_ref[:, lanes],
            o_ref[:, lanes], lse_ref[0, 2 * pair : 2 * pair + 2], bias,
        )
        dq_ref[:, lanes] = d_query
        d_keys.append((lanes, d_key))
        d_values.append((lanes, d_value))
    pairs = ((0, d_keys), (1, d_values))

    def swap(kind):
        return pltpu.make_async_remote_copy(
            src_ref=give.at[group, kind],
            dst_ref=take.at[group, kind],
            send_sem=give_sem.at[group, kind],
            recv_sem=take_sem.at[group, kind],
            device_id=(dp, sq ^ 1),
            device_id_type=MESH_ID,
        )

    @pl.when(block == 0)
    def _():
        for kind, parts in pairs:
            for lanes, part in parts:
                keep[kind, :, lanes] = part[:256]
                give[group, kind, :, lanes] = part[256:].astype(LOW)
            swap(kind).start()

    @pl.when(block == 1)
    def _():
        for kind, parts in pairs:
            for lanes, part in parts:
                acc[kind, :, lanes] = part

    @pl.when(block == 2)
    def _():
        for (kind, parts), ref in zip(pairs, (dk_ref, dv_ref)):
            swap(kind).wait()
            for lanes, part in parts:
                ref[:512, lanes] = (acc[kind, :, lanes] + part).astype(LOW)
                other = take[group, kind, :, lanes].astype(WIDE)
                ref[512:, lanes] = (keep[kind, :, lanes] + other).astype(LOW)

    @pl.when((block == 2) & (group == pl.num_programs(0) - 1))
    def _():
        exchange.finish()


def attend_back(lengths, qkv, lse, d_out, out, result, sent_dev):
    width = qkv.shape[-1]
    groups = width // 128 // BACK_PAIRS
    lanes = 128 * BACK_PAIRS
    hbm = pl.BlockSpec(memory_space=pl.ANY)
    query = pl.BlockSpec((256, lanes), lambda h, i: ((i + 2) % 3, h))
    keys = pl.BlockSpec((768, lanes), lambda h, i: (0, h))
    flat = jax.ShapeDtypeStruct((768, width), LOW)
    shared = lambda i: jnp.where(i == 0, 1, 0)
    return pl.pallas_call(
        attend_back_body,
        grid=(groups, 3),
        in_specs=[
            pl.BlockSpec(memory_space=pltpu.SMEM),
            pl.BlockSpec((1, 256, lanes), lambda h, i: (0, (i + 2) % 3, h)),
            pl.BlockSpec((1, 512, lanes), lambda h, i: (1, shared(i), h)),
            pl.BlockSpec((1, 512, lanes), lambda h, i: (2, shared(i), h)),
            pl.BlockSpec((1, 2 * BACK_PAIRS, 256), lambda h, i: (h, 0, (i + 2) % 3)),
            query,
            query,
            hbm,
        ],
        out_specs=(query, keys, keys, hbm),
        out_shape=(flat, flat, flat, jax.ShapeDtypeStruct((sent_dev, 128, width), LOW)),
        scratch_shapes=[
            pltpu.VMEM((2, 512, lanes), WIDE),
            pltpu.VMEM((2, 256, lanes), WIDE),
            pltpu.VMEM((groups, 2, 256, lanes), LOW),
            pltpu.VMEM((groups, 2, 256, lanes), LOW),
        ]
        + EXCHANGE_SEMS
        + [pltpu.SemaphoreType.DMA((groups, 2)), pltpu.SemaphoreType.DMA((groups, 2))],
        compiler_params=params(collective_id=4, has_side_effects=True),
        name="attend_back",
    )(lengths, qkv, qkv, qkv, lse.reshape(groups, 2 * BACK_PAIRS, 768), d_out, out, result)


def row_mean(value):
    return jnp.mean(value, axis=-1, keepdims=True)


def col_sum(value):
    return jnp.sum(value, axis=0, keepdims=True)


def middle_body(
    map_ref, len_ref, o_hbm, x_hbm, gy_hbm, w_ref, vec_ref,
    y_hbm, left_hbm, right_hbm, do_hbm, da_hbm, sums_ref,
    w_buf, o_buf, x_buf, gy_buf, left, right, slope, total, hat_one, rstd_one, low_buf,
    sem, in_sem, out_sem,
):
    count, width = o_buf.shape
    tiles = w_buf.shape[0]
    chunks = FEEDFWD_UNITS // width

    def fetch(t):
        return pltpu.make_async_copy(w_ref.at[tile_at(map_ref, 6 + t)], w_buf.at[t], sem.at[t])

    inputs = [
        pltpu.make_async_copy(src, dst, in_sem.at[i])
        for i, (src, dst) in enumerate(
            (
                (o_hbm, o_buf),
                (x_hbm.at[pl.ds(0, count)], x_buf),
                (gy_hbm, gy_buf),
            )
        )
    ]
    inputs[0].start()
    for t in range(2):
        fetch(t).start()
    inputs[1].start()
    for c in range(chunks):
        for t in (2 + 2 * c, 3 + 2 * c, 10 + 2 * c, 11 + 2 * c):
            fetch(t).start()
    inputs[2].start()
    outputs = []

    def put(src, dst):
        copy = pltpu.make_async_copy(src, dst, out_sem.at[len(outputs)])
        copy.start()
        outputs.append(copy)

    def put_left(t, value):
        for u in range(2):
            left[t + u] = value[:, TILE * u : TILE * (u + 1)]
            put(left.at[t + u], left_hbm.at[t + u])

    def ready(*which):
        for t in which:
            fetch(t).wait()

    def pair(t):
        return w_buf[t : t + 2].reshape(2 * TILE, width)

    def vec(row):
        return vec_ref[row : row + 1, :]

    def fold(value):
        return jnp.sum(value.reshape(-1, 8, width), axis=0)

    def over_rows(body, carried):
        zero = (jnp.zeros((8, width), WIDE),) * carried

        def step(i, carry):
            return body(pl.ds(pl.multiple_of(i * NORM_ROWS, NORM_ROWS), NORM_ROWS), i, carry)

        return lax.fori_loop(0, count // NORM_ROWS, step, zero)

    inputs[0].wait()
    ready(0, 1)
    total[...] = dot_nn(o_buf[...], pair(0))
    inputs[1].wait()

    def norm_one(at, i, carry):
        resid = x_buf[at].astype(WIDE) + (total[at] + vec(2))
        centered = resid - row_mean(resid)
        rstd = lax.rsqrt(row_mean(centered * centered) + NORM_EPS)
        rstd_one[at] = rstd
        hat = centered * rstd
        hat_one[at] = hat
        first = hat * vec(4) + vec(5)
        total[at] = first + vec(3)
        right[0, at] = first.astype(LOW)
        return carry

    over_rows(norm_one, 0)
    put(right.at[0], right_hbm.at[0])

    first_low = right[0]
    for c in range(chunks):
        ready(2 + 2 * c, 3 + 2 * c, 10 + 2 * c, 11 + 2 * c)
        act = dot_nt(first_low, pair(2 + 2 * c)) + vec(8 + c)
        cdf = 0.5 + 0.5 * lax.erf(act * (0.5**0.5))
        pdf = jnp.exp(-0.5 * act * act) * 0.3989422804014327
        slope[c] = cdf + act * pdf
        active = (act * cdf).astype(LOW)
        put_left(8 + 2 * c, active)
        total[...] += dot_nn(active, pair(10 + 2 * c))
    inputs[2].wait()

    def norm_two(at, i, carry):
        d_gain, d_shift, d_bias, pool_full, pool_half = carry
        resid = total[at]
        centered = resid - row_mean(resid)
        rstd = lax.rsqrt(row_mean(centered * centered) + NORM_EPS)
        hat = centered * rstd
        result = hat * vec(6) + vec(7)
        low_buf[0, at] = result.astype(LOW)
        shared = i * NORM_ROWS >= 512
        row = positions((NORM_ROWS, 128), shared, i * NORM_ROWS - jnp.where(shared, 512, 0))
        valid = jnp.where(row < sentence_length(len_ref, shared), 1.0, 0.0)
        pooled = fold(result * jnp.concatenate([valid] * (width // 128), axis=1))
        part = shared.astype(WIDE)
        grad = gy_buf[at].astype(WIDE)
        d_gain = d_gain + fold(grad * hat)
        d_shift = d_shift + fold(grad)
        grad = grad * vec(6)
        d_resid = rstd * (grad - row_mean(grad) - hat * row_mean(grad * hat))
        total[at] = d_resid
        grad_low = d_resid.astype(LOW)
        right[1, at] = grad_low
        return (
            d_gain,
            d_shift,
            d_bias + fold(grad_low.astype(WIDE)),
            pool_full + pooled * (1.0 - part),
            pool_half + pooled * part,
        )

    sums_ref[...] = jnp.zeros_like(sums_ref)
    found = over_rows(norm_two, 5)
    for row, value in zip((4, 5, 1, 10, 11), found):
        sums_ref[row : row + 1, :] = col_sum(value)
    put(low_buf.at[0], y_hbm)
    put(right.at[1], right_hbm.at[1])

    grad_low = right[1]
    for c in range(chunks):
        d_active = dot_nt(grad_low, pair(10 + 2 * c))
        d_act = (d_active * slope[c]).astype(LOW)
        put_left(2 * c, d_act)
        sums_ref[6 + c : 7 + c, :] = col_sum(d_act.astype(WIDE))
        total[...] += dot_nn(d_act, pair(2 + 2 * c))

    def norm_back(at, i, carry):
        d_gain, d_shift, d_bias = carry
        grad = total[at]
        hat = hat_one[at]
        d_gain = d_gain + fold(grad * hat)
        d_shift = d_shift + fold(grad)
        grad = grad * vec(4)
        d_resid = rstd_one[at] * (grad - row_mean(grad) - hat * row_mean(grad * hat))
        grad_low = d_resid.astype(LOW)
        low_buf[1, at] = grad_low
        return (d_gain, d_shift, d_bias + fold(grad_low.astype(WIDE)))

    found = over_rows(norm_back, 3)
    for row, value in zip((2, 3, 0), found):
        sums_ref[row : row + 1, :] = col_sum(value)
    put(low_buf.at[1], da_hbm)
    low_buf[2] = dot_nt(low_buf[1], pair(0)).astype(LOW)
    put(low_buf.at[2], do_hbm)
    for copy in outputs:
        copy.wait()


def middle(owners, lengths, attended, rows, out_grad, weights, vectors):
    count, width = attended.shape
    half = FEEDFWD_UNITS // TILE
    tiles = 2 + 2 * half
    hbm = pl.BlockSpec(memory_space=pl.ANY)
    smem = pl.BlockSpec(memory_space=pltpu.SMEM)
    vmem = pl.BlockSpec(memory_space=pltpu.VMEM)
    flat = jax.ShapeDtypeStruct((count, width), LOW)
    return pl.pallas_call(
        middle_body,
        in_specs=[smem, smem] + [hbm] * 4 + [vmem],
        out_specs=(hbm,) * 5 + (vmem,),
        out_shape=(
            flat,
            jax.ShapeDtypeStruct((2 * half, count, TILE), LOW),
            jax.ShapeDtypeStruct((2, count, width), LOW),
            flat,
            flat,
            jax.ShapeDtypeStruct((16, width), WIDE),
        ),
        scratch_shapes=[
            pltpu.VMEM((tiles, TILE, width), LOW),
            pltpu.VMEM((count, width), LOW),
            pltpu.VMEM((count, width), LOW),
            pltpu.VMEM((count, width), LOW),
            pltpu.VMEM((2 * half, count, TILE), LOW),
            pltpu.VMEM((2, count, width), LOW),
            pltpu.VMEM((half // 2, count, width), WIDE),
            pltpu.VMEM((count, width), WIDE),
            pltpu.VMEM((count, width), WIDE),
            pltpu.VMEM((count, 1), WIDE),
            pltpu.VMEM((3, count, width), LOW),
            pltpu.SemaphoreType.DMA((tiles,)),
            pltpu.SemaphoreType.DMA((3,)),
            pltpu.SemaphoreType.DMA((2 * half + 5,)),
        ],
        compiler_params=params(),
        name="feed_forward",
    )(owners, lengths, attended, rows, out_grad, weights, vectors)


def grad_ff_body(map_ref, left_ref, right_ref, out_ref):
    out_ref[0] = dot_tn(left_ref[0], right_ref[0]).astype(LOW)


def grad_ff(owners, left, right):
    per = FEEDFWD_UNITS // TILE
    count, width = right.shape[1:]
    return pl.pallas_call(
        grad_ff_body,
        grid_spec=pltpu.PrefetchScalarGridSpec(
            num_scalar_prefetch=1,
            grid=(2 * per,),
            in_specs=[
                pl.BlockSpec((1, count, TILE), lambda i, m: (i, 0, 0)),
                pl.BlockSpec((1, count, width), lambda i, m: (i // per, 0, 0)),
            ],
            out_specs=pl.BlockSpec((1, TILE, width), lambda i, m: (tile_at(m, 8 + i), 0, 0)),
        ),
        out_shape=jax.ShapeDtypeStruct((8 + 2 * per, TILE, width), LOW),
        compiler_params=params(),
        name="grad_ff",
    )(owners, left, right)


def grad_attn_body(
    map_ref, x_ref, dq_ref, dk_ref, dv_ref, o_ref, da_ref, into_ref, out_ref, sums_ref
):
    step = pl.program_id(0)
    for part, grad_ref in enumerate((dq_ref, dk_ref, dv_ref)):

        @pl.when(step // 2 == part)
        def _(grad_ref=grad_ref):
            out_ref[0] = dot_tn(x_ref[...], grad_ref[...]).astype(LOW)

    @pl.when(step // 2 == 3)
    def _():
        out_ref[0] = dot_tn(o_ref[...], da_ref[...]).astype(LOW)

    @pl.when(step == 0)
    def _():
        sums_ref[...] = jnp.zeros_like(sums_ref)
        sums_ref[0:1, :] = col_sum(dq_ref[...].astype(WIDE))
        sums_ref[1:2, :] = col_sum(dv_ref[...].astype(WIDE))


def grad_attn(owners, rows, dq, dk, dv, attended, da, into):
    count, width = dq.shape
    whole = pl.BlockSpec((count, width), lambda i, m: (0, 0))
    return pl.pallas_call(
        grad_attn_body,
        grid_spec=pltpu.PrefetchScalarGridSpec(
            num_scalar_prefetch=1,
            grid=(8,),
            in_specs=[
                pl.BlockSpec((count, TILE), lambda i, m: (0, i % 2)),
                whole,
                whole,
                whole,
                pl.BlockSpec((768, TILE), lambda i, m: (0, i % 2)),
                pl.BlockSpec((768, width), lambda i, m: (0, 0)),
                pl.BlockSpec(memory_space=pl.ANY),
            ],
            out_specs=(
                pl.BlockSpec((1, TILE, width), lambda i, m: (tile_at(m, i), 0, 0)),
                pl.BlockSpec((8, width), lambda i, m: (0, 0)),
            ),
        ),
        out_shape=(
            jax.ShapeDtypeStruct(into.shape, LOW),
            jax.ShapeDtypeStruct((8, width), WIDE),
        ),
        input_output_aliases={7: 0},
        compiler_params=params(),
        name="grad_attn",
    )(owners, rows, dq, dk, dv, attended, da, into)


def grad_in_body(map_ref, dq_ref, dk_ref, dv_ref, dh_ref, *refs):
    w_refs, out_ref = refs[:6], refs[6]
    for half in range(2):
        cols = slice(TILE * half, TILE * (half + 1))
        value = dh_ref[:, cols].astype(WIDE)
        for part, grad_ref in enumerate((dq_ref, dk_ref, dv_ref)):
            value = value + dot_nt(grad_ref[...], w_refs[2 * part + half][0])
        out_ref[:, cols] = value.astype(LOW)


def grad_in(owners, dq, dk, dv, dh, weights):
    count, width = dq.shape
    block = pl.BlockSpec((256, width), lambda i, m: (i, 0))
    return pl.pallas_call(
        grad_in_body,
        grid_spec=pltpu.PrefetchScalarGridSpec(
            num_scalar_prefetch=1,
            grid=(count // 256,),
            in_specs=[block] * 4
            + [
                pl.BlockSpec((1, TILE, width), lambda i, m, t=t: (tile_at(m, t), 0, 0)) for t in range(6)
            ],
            out_specs=block,
        ),
        out_shape=jax.ShapeDtypeStruct((count, width), LOW),
        compiler_params=params(),
        name="grad_in",
    )(owners, dq, dk, dv, dh, *([weights] * 6))


REDUCE_MODE = (
    {"n": "z", "a": "x", "e": "y", "o": "x"},
    {"n": "z", "a": "y", "e": "y", "o": "y"},
    {"n": "z", "a": "x", "e": "x", "o": "x"},
)
REDUCE_ORDER = (
    ("part", "n", "f", 1), ("part", "e", "f", 1), ("part", "e", "n", 1), ("both", "n", "f", 1),
    ("part", "a", "n", 1), ("both", "e", "f", 1), ("part", "a", "f", 0), ("vs", 0),
    ("part", "n", "f", 2), ("both", "a", "n", 1), ("both", "e", "n", 1), ("part", "n", "n", 1),
    ("both", "a", "f", 0), ("both", "n", "f", 2), ("va", 0), ("vs", 1), ("part", "a", "f", 2),
    ("part", "e", "f", 0), ("part", "n", "n", 2), ("both", "n", "n", 1), ("both", "a", "f", 2),
    ("turn", "n", 1), ("part", "o", "n", 1), ("both", "e", "f", 0), ("part", "a", "f", 1),
    ("part", "e", "n", 0), ("part", "o", "f", 1), ("both", "a", "f", 1), ("both", "n", "n", 2),
    ("part", "e", "f", 2), ("both", "o", "f", 1), ("part", "a", "n", 2), ("both", "e", "n", 0),
    ("both", "e", "f", 2), ("part", "n", "n", 0), ("turn", "e", 1), ("both", "a", "n", 2),
    ("turn", "a", 2), ("part", "n", "f", 0), ("both", "o", "n", 1), ("own", "n", 1),
    ("part", "o", "f", 2), ("own", "f", 1), ("both", "n", "f", 0), ("part", "a", "n", 0),
    ("part", "e", "n", 2), ("both", "o", "f", 2), ("own", "f", 2), ("part", "o", "n", 2),
    ("both", "e", "n", 2), ("both", "n", "n", 0), ("turn", "e", 2), ("both", "a", "n", 0),
    ("turn", "n", 2), ("gin",), ("in",), ("turn", "a", 1), ("part", "o", "f", 0),
    ("part", "o", "n", 0), ("turn", "n", 0), ("turn", "e", 0), ("turn", "a", 0), ("on", "e", 1),
    ("va", 1), ("both", "o", "n", 0), ("on", "n", 2), ("both", "o", "n", 2), ("own", "n", 0),
    ("both", "o", "f", 0), ("own", "f", 0), ("on", "a", 2), ("own", "n", 2), ("turn", "o", 2),
    ("on", "e", 2), ("on", "n", 0), ("turn", "o", 1), ("on", "a", 1), ("on", "n", 1), ("vs", 2),
    ("turn", "o", 0), ("on", "e", 0), ("end", 1), ("on", "a", 0), ("va", 2), ("vs", 3), ("end", 2),
    ("va", 3), ("vs", 4), ("end", 0), ("va", 4),
)


def reduce_body(
    own_of_ref, len_ref, x_ref, o_ref, left_ref, qkv_ref, do_ref, da_ref, right_ref,
    w_ref, y_ref, lse_ref, sums_ref, own_ref, vt_ref, sq_ref, gi_ref, out_ref,
    left_0, left_1, left_2, rbuf, wbuf, gbuf, give, take, pbuf, core_in, x_two, x_one, y_two, y_one,
    zf_in, mid_in, fin_in, near_in, ebuf, tbuf, tlow, vbuf, v_in, s_own, s_seq, s_dp,
    send_sem, local_sem, core_sem, xtwo_sem, xone_sem, ytwo_sem, yone_sem,
    zf_sem, mid_sem, fin_sem, near_sem, v_sem, out_sem, seq_sem, dp_sem, in_sem,
    give_sem, take_sem, free_sem, ex_send, ex_recv, ex_local,
):
    dp, sq = lax.axis_index("dp"), lax.axis_index("seq")
    z, x = dp // 2, dp % 2
    y, c = sq // 2, sq % 2
    dev_c, dev_y, dev_yc, dev_x = (dp, sq ^ 1), (dp, sq ^ 2), (dp, sq ^ 3), (dp ^ 1, sq)
    dev_near = (dp ^ 2, sq)
    inner = (z > 0) & (z < 3)
    outer = jnp.logical_not(inner)
    place = {
        "n": z ^ 1,
        "a": jnp.where(z < 2, 2, 1),
        "e": jnp.where(z < 2, 3, 0),
        "o": z,
    }
    lefts = (left_0, left_1, left_2)
    used = [0, 0]
    remotes, own_moves = [], []

    def move(src, dst):
        copy = pltpu.make_async_copy(src, dst, local_sem.at[used[1]])
        used[1] += 1
        copy.start()
        return copy

    first_loads = [
        move(qkv_ref.at[0, pl.ds(0, 768)], wbuf.at[0]),
        move(do_ref, wbuf.at[1]),
        move(o_ref, wbuf.at[2]),
        move(qkv_ref.at[1], core_in.at[pl.ds(0, 1024)]),
        move(qkv_ref.at[2], core_in.at[pl.ds(1024, 1024)]),
    ]

    loads = {"right": [move(right_ref, rbuf.at[pl.ds(4, 2)]), move(da_ref, rbuf.at[3])]}
    for t in range(3):
        loads[t] = []
        for block in range(8):
            tile = 3 * block + t
            cols = pl.ds(TILE * (tile % 2), TILE)
            if tile < 6:
                src = x_ref.at[pl.ds(0, 768), cols]
            elif tile < 8:
                src = o_ref.at[:, cols]
            else:
                src = left_ref.at[tile - 8]
            loads[t].append(move(src, lefts[t].at[block]))

    def loaded(name):
        for copy in loads.pop(name, ()):
            copy.wait()

    barrier = pltpu.get_barrier_semaphore()
    for step in range(1, 4):
        pl.semaphore_signal(
            barrier, inc=1, device_id=(dp, sq ^ step), device_id_type=MESH_ID
        )
    for step in range(1, 8):
        pl.semaphore_signal(
            barrier, inc=1, device_id=(dp ^ step, sq), device_id_type=MESH_ID
        )
    pl.semaphore_wait(barrier, 10)

    def send(src, dst, recv, device, pred=None):
        copy = pltpu.make_async_remote_copy(
            src_ref=src,
            dst_ref=dst,
            send_sem=send_sem.at[used[0]],
            recv_sem=recv,
            device_id=device,
            device_id_type=MESH_ID,
        )
        used[0] += 1
        if pred is None:
            copy.start()
        else:
            pl.when(pred)(lambda: copy.start())
        remotes.append((copy, pred))

    def arrived(at, sem):
        pltpu.make_async_copy(at, at, sem).wait()

    def wide(ref, *at):
        return ref[at].astype(WIDE)

    exchange = Exchange(by_position(y_ref, out_ref), ex_send, ex_recv, ex_local)
    exchange.start()
    for copy in first_loads:
        copy.wait()

    def swap(pair, kind):
        return pltpu.make_async_remote_copy(
            src_ref=give.at[pair, kind],
            dst_ref=take.at[pair, kind],
            send_sem=give_sem.at[pair, kind],
            recv_sem=take_sem.at[pair, kind],
            device_id=dev_c,
            device_id_type=MESH_ID,
        )

    biases = (key_bias(len_ref, False), key_bias(len_ref, True))
    pairs = rbuf.shape[-1] // 128

    def back_at(pair, block):
        lanes, rows = slice(128 * pair, 128 * (pair + 1)), slice(256 * block, 256 * (block + 1))
        first = 512 * (block // 2)
        keys = core_in[first : first + 512, lanes]
        return lanes, rows, keys, core_in[1024 + first : 1536 + first, lanes]

    def first_of(pair, block, head):
        lanes, rows, keys, values = back_at(pair, block)
        return back_first(
            head, wbuf[0, rows, lanes], keys, values, wbuf[1, rows, lanes], biases[block // 2]
        )

    items = [(p, block, head) for p in range(pairs) for block in (2, 0, 1) for head in range(2)]
    ahead = first_of(*items[0])
    parts = {}
    for index, (pair, block, head) in enumerate(items):
        this = ahead
        if index + 1 < len(items):
            ahead = first_of(*items[index + 1])
        lanes, rows, keys, _ = back_at(pair, block)
        if head == 0:
            keys_t, weighed = keys.T, back_inner(wbuf[1, rows, lanes], wbuf[2, rows, lanes])
        log = lse_ref[pair, head : head + 1, rows]
        parts[block, head] = back_second(head, this, keys_t, weighed, log)
        if head == 0:
            continue
        rbuf[0, rows, lanes] = back_query([parts[block, 0][0], parts[block, 1][0]])
        for kind in range(2):
            part = parts[block, 0][1 + kind] + parts[block, 1][1 + kind]
            if block == 2:
                rbuf[1 + kind, 512:768, lanes] = part[:256].astype(LOW)
                give[pair, kind] = part[256:].astype(LOW)
                swap(pair, kind).start()
            elif block == 0:
                parts["sum", kind] = part
            else:
                total = parts["sum", kind] + part
                rbuf[1 + kind, 0:512, lanes] = total.astype(LOW)
    pl.semaphore_signal(free_sem, inc=1, device_id=dev_c, device_id_type=MESH_ID)
    loads["in"] = [move(w_ref, wbuf)]
    for pair in range(pairs):
        lanes = slice(128 * pair, 128 * (pair + 1))
        for kind in range(2):
            swap(pair, kind).wait()
            rows = pl.ds(512, 256)
            rbuf[1 + kind, rows, lanes] = (
                rbuf[1 + kind, rows, lanes].astype(WIDE) + take[pair, kind].astype(WIDE)
            ).astype(LOW)
    loaded("right")
    pl.semaphore_wait(free_sem, 1)

    partners = (dev_c, dev_y, dev_x, (dp ^ 2, sq), (dp ^ 4, sq))

    def vec_send(step):
        if step == 0:
            vbuf[0] = jnp.zeros(vbuf.shape[1:], WIDE)
            vbuf[0, 0:1] = col_sum(wide(rbuf, 0))
            vbuf[0, 1:2] = col_sum(wide(rbuf, 2))
            vbuf[0, 2:12] = sums_ref[0:10]
            vbuf[0, pl.ds(16 + 3 * y + 2 * c, 1)] = sums_ref[10:11]
            vbuf[0, pl.ds(16 + 3 * y + 1, 1)] = sums_ref[11:12]
        send(vbuf.at[step], v_in.at[step], v_sem.at[step], partners[step])

    def vec_add(step):
        arrived(v_in.at[step], v_sem.at[step])
        vbuf[step + 1] = vbuf[step] + v_in[step]

    def input_grad():
        loaded("in")
        for part in range(3):
            cols = slice(256 * part, 256 * (part + 1))
            value = wide(rbuf, 3, slice(None), cols)
            for index in range(3):
                value = value + dot_nt(rbuf[index], wbuf[index, cols])
            gbuf[:, cols] = value.astype(LOW)

    def in_full(j):
        return gbuf.at[pl.ds(128 * j, 128)], gi_ref.at[3 * y + 2 * c]

    def in_half(j):
        return gbuf.at[pl.ds(512 + 64 * j, 64)], gi_ref.at[3 * y + 1, pl.ds(64 * c, 64)]

    def input_send():
        for device in (dev_y, dev_yc, dev_c):
            for kind, pair in enumerate((in_full(device[1]), in_half(device[1]))):
                send(pair[0], pair[1], in_sem.at[sq, kind], device)
        own_moves.append(move(*in_full(sq)))
        own_moves.append(move(*in_half(sq)))

    def standard_of(slot):
        found = jnp.int32(0)
        for block in range(8):
            found = jnp.maximum(found, jnp.where(own_of_ref[block] == slot, block, 0))
        return found

    def slot_of(k, p):
        return 2 * place[k] + (x if p == "n" else 1 - x)

    def core_at(slot, t, half):
        first = 96 * (2 * (8 * t + slot) + half)
        return core_in.at[pl.ds(pl.multiple_of(first, 96), 96)]

    def partial(k, p, t):
        loaded(t)
        slot = slot_of(k, p)
        block = standard_of(slot)
        tile = 3 * block + t
        right = jnp.where(tile < 8, tile // 2, 4 + (tile - 8) // 8)
        value = dot_tn(lefts[t][block], rbuf[right]).astype(LOW)
        for quarter in range(4):
            rows = slice(96 * quarter, 96 * (quarter + 1))
            pbuf[quarter % 2, t, slot, quarter // 2] = value[rows]
        for half in range(2):
            src = pbuf.at[1 - c, t, slot, half]
            send(src, core_at(slot, t, half), core_sem.at[t, slot, half], dev_c)

    def held(*at):
        return pbuf.at[(c, *at)]

    index_of = {"x": {}, "y": {}, "z": {}}
    for t in range(3):
        for k in "naeo":
            found = index_of[REDUCE_MODE[t][k]]
            found[k, t] = len(found)

    def first_send(k, p, t):
        slot = slot_of(k, p)
        if REDUCE_MODE[t][k] == "y":
            at, half = index_of["y"][k, t], "nf".index(p)
            send(held(t, slot, 1 - y), y_two.at[at, half], ytwo_sem.at[at, half], dev_y)
        elif p == "f":
            at = index_of["x"][k, t]
            send(held(t, slot), x_two.at[at], xtwo_sem.at[at], dev_x)

    def both_cores(k, p, t):
        slot = slot_of(k, p)
        for half in range(2):
            arrived(core_at(slot, t, half), core_sem.at[t, slot, half])
            other = core_at(slot, t, half)[...].astype(WIDE)
            pbuf[c, t, slot, half] = (wide(pbuf, c, t, slot, half) + other).astype(LOW)
        if REDUCE_MODE[t][k] == "z":
            half = "nf".index(p)
            send(held(t, slot), zf_in.at[t, half], zf_sem.at[t, half], dev_near)
        elif k != "o":
            first_send(k, p, t)

    def own_block(p, t):
        if REDUCE_MODE[t]["n"] == "z":
            slot, half = slot_of("o", p), "nf".index(p)
            arrived(zf_in.at[t, half], zf_sem.at[t, half])
            pbuf[c, t, slot] = (wide(pbuf, c, t, slot) + wide(zf_in, t, half)).astype(LOW)
        first_send("o", p, t)

    def turn(k, t):
        mode = REDUCE_MODE[t][k]
        if mode == "z":
            return
        at = index_of[mode][k, t]
        near, far = slot_of(k, "n"), slot_of(k, "f")
        if mode == "y":
            for half in range(2):
                arrived(y_two.at[at, half], ytwo_sem.at[at, half])
            pbuf[c, t, far, y] = (wide(pbuf, c, t, far, y) + wide(y_two, at, 1)).astype(LOW)
            send(held(t, far, y), x_one.at[at], xone_sem.at[at], dev_x)
        else:
            arrived(x_two.at[at], xtwo_sem.at[at])
            pbuf[c, t, near] = (wide(pbuf, c, t, near) + wide(x_two, at)).astype(LOW)
            send(held(t, near, 1 - y), y_one.at[at], yone_sem.at[at], dev_y)

    def plane_sum(k, t):
        mode = REDUCE_MODE[t][k]
        at = index_of[mode][k, t]
        mine = wide(pbuf, c, t, slot_of(k, "n"), y)
        if mode == "y":
            arrived(x_one.at[at], xone_sem.at[at])
            return mine + wide(y_two, at, 0) + wide(x_one, at)
        arrived(y_one.at[at], yone_sem.at[at])
        return mine + wide(y_one, at)

    def onward(k, t):
        if REDUCE_MODE[t][k] == "z":
            return
        row = "aen".index(k)
        tbuf[...] = plane_sum(k, t)
        if k == "n":
            ebuf[row, t] = tbuf[...].astype(LOW)
            send(ebuf.at[row, t], near_in.at[t], near_sem.at[t], dev_near)
            return

        line = "ae".index(k)

        @pl.when(inner)
        def _():
            arrived(mid_in.at[line, t], mid_sem.at[line, t])
            tbuf[...] += wide(mid_in, line, t)

        ebuf[row, t] = tbuf[...].astype(LOW)
        owner = (2 * place[k] + x, sq)
        send(ebuf.at[row, t], fin_in.at[t], fin_sem.at[t], owner, inner)
        send(ebuf.at[row, t], mid_in.at[line, t], mid_sem.at[line, t], dev_near, outer)

    squares = []

    def finish(t):
        value = plane_sum("o", t)
        if REDUCE_MODE[t]["n"] != "z":
            arrived(near_in.at[t], near_sem.at[t])
            value = value + wide(near_in, t)
        arrived(fin_in.at[t], fin_sem.at[t])
        total = (value + wide(fin_in, t)).astype(LOW)
        tlow[t] = total
        wide_total = total.astype(WIDE)
        rows = (wide_total * wide_total).reshape(-1, 8, wide_total.shape[-1])
        squares.append(jnp.sum(rows, axis=0))
        at = own_ref.at[t, sq]
        for device in (dev_y, dev_c):
            send(tlow.at[t], at, out_sem.at[t, sq], device)
        own_moves.append(move(tlow.at[t], at))

    steps = {
        "part": partial,
        "both": both_cores,
        "own": own_block,
        "turn": turn,
        "on": onward,
        "end": finish,
        "vs": vec_send,
        "va": vec_add,
        "gin": input_grad,
        "in": input_send,
    }
    for name, *at in REDUCE_ORDER:
        steps[name](*at)

    squares = squares[0] + squares[1] + squares[2]
    folded = squares[:, :128]
    for lane in range(1, squares.shape[-1] // 128):
        folded = folded + squares[:, 128 * lane : 128 * (lane + 1)]
    s_own[...] = folded
    for step in range(1, 4):
        send(s_own, s_seq.at[sq], seq_sem.at[sq], (dp, sq ^ step))
    s_seq[sq] = folded
    for t in [at[0] for name, *at in REDUCE_ORDER if name == "end"]:
        arrived(own_ref.at[t, sq ^ 2], out_sem.at[t, sq ^ 2])
        send(own_ref.at[t, sq ^ 2], own_ref.at[t, sq ^ 2], out_sem.at[t, sq ^ 2], dev_c)
    for step in range(1, 4):
        arrived(s_seq.at[sq ^ step], seq_sem.at[sq ^ step])
    group = s_seq[0] + s_seq[1] + s_seq[2] + s_seq[3]
    s_dp[dp] = group
    for step in range(1, 8):
        send(s_dp.at[dp], s_dp.at[dp], dp_sem.at[dp], (dp ^ step, sq))
    for step in range(1, 8):
        arrived(s_dp.at[dp ^ step], dp_sem.at[dp ^ step])
    everyone = s_dp[0]
    for index in range(1, 8):
        everyone = everyone + s_dp[index]
    sq_ref[...] = everyone
    vt_ref[0:16] = vbuf[5][0:16]
    vt_ref[16:24] = vbuf[2][16:24]

    for t in range(3):
        arrived(own_ref.at[t, sq ^ 1], out_sem.at[t, sq ^ 1])
        arrived(own_ref.at[t, sq ^ 3], out_sem.at[t, sq ^ 3])
    for step in range(1, 4):
        other = sq ^ step
        there, member = other // 2, other % 2
        arrived(gi_ref.at[3 * there + 2 * member], in_sem.at[other, 0])
        arrived(gi_ref.at[3 * there + 1, pl.ds(64 * member, 64)], in_sem.at[other, 1])
    exchange.finish()
    for copy in own_moves:
        copy.wait()
    for copy, pred in remotes:
        if pred is None:
            copy.wait_send()
        else:
            pl.when(pred)(lambda copy=copy: copy.wait_send())


def reduce_all(
    owners, lengths, rows, out, left, qkv, d_out, d_branch, right, matrices, result, lse, sums,
    sent_dev,
):
    width = rows.shape[-1]
    part = TILE // 4
    hbm = pl.BlockSpec(memory_space=pl.ANY)
    vmem = pl.BlockSpec(memory_space=pltpu.VMEM)
    smem = pl.BlockSpec(memory_space=pltpu.SMEM)
    dma = pltpu.SemaphoreType.DMA
    modes = "".join(mode for modes in REDUCE_MODE for mode in modes.values())
    x_first, y_first = max(modes.count("x"), 1), max(modes.count("y"), 1)
    near_over = int(any(mode["n"] != "z" for mode in REDUCE_MODE))

    def low(*shape):
        return pltpu.VMEM(shape + (part, width), LOW)

    owned, totals, squares, input_grad, output = pl.pallas_call(
        reduce_body,
        out_shape=(
            jax.ShapeDtypeStruct((3, 4, part, width), LOW),
            jax.ShapeDtypeStruct((24, width), WIDE),
            jax.ShapeDtypeStruct((8, 128), WIDE),
            jax.ShapeDtypeStruct((sent_dev, 128, width), LOW),
            jax.ShapeDtypeStruct((sent_dev, 128, width), LOW),
        ),
        in_specs=[smem] * 2 + [hbm] * 9 + [vmem] * 2,
        out_specs=(hbm, vmem, vmem, hbm, hbm),
        scratch_shapes=[
            pltpu.VMEM((8, 768, TILE), LOW),
            pltpu.VMEM((8, 768, TILE), LOW),
            pltpu.VMEM((8, 768, TILE), LOW),
            pltpu.VMEM((6, 768, width), LOW),
            pltpu.VMEM((3, width, width), LOW),
            pltpu.VMEM((768, width), LOW),
            pltpu.VMEM((width // 128, 2, 256, 128), LOW),
            pltpu.VMEM((width // 128, 2, 256, 128), LOW),
            low(2, 3, 8, 2),
            pltpu.VMEM((48 * part, width), LOW),
            low(x_first, 2),
            low(y_first),
            low(y_first, 2),
            low(x_first),
            low(3, 2, 2),
            low(2, 3),
            low(3),
            low(3 if near_over else 1),
            low(2 + near_over, 3),
            pltpu.VMEM((part, width), WIDE),
            low(3),
            pltpu.VMEM((6, 24, width), WIDE),
            pltpu.VMEM((5, 24, width), WIDE),
            pltpu.VMEM((8, 128), WIDE),
            pltpu.VMEM((4, 8, 128), WIDE),
            pltpu.VMEM((8, 8, 128), WIDE),
            dma((160,)),
            dma((48,)),
            dma((3, 8, 2)),
            dma((x_first,)),
            dma((y_first,)),
            dma((y_first, 2)),
            dma((x_first,)),
            dma((3, 2)),
            dma((2, 3)),
            dma((3,)),
            dma((3,)),
            dma((5,)),
            dma((3, 4)),
            dma((4,)),
            dma((8,)),
            dma((4, 2)),
            dma((width // 128, 2)),
            dma((width // 128, 2)),
            pltpu.SemaphoreType.REGULAR,
        ]
        + EXCHANGE_SEMS,
        compiler_params=params(collective_id=2, has_side_effects=True),
        name="reduce_gradients",
    )(
        owners, lengths, rows, out, left, qkv, d_out, d_branch, right, matrices, result, lse, sums
    )
    return owned.reshape(3 * TILE, width), totals, squares, input_grad, output


def optimizer_body(
    len_ref, mem_ref, g_ref, sq_ref, tot_ref, w_ref, one_ref, two_ref, vw_ref, vone_ref, vtwo_ref,
    out_from, in_from, norm_ref, emb_ref, *rest,
):
    outs, (out_to, in_to, clip_ref) = rest[:-3], rest[-3:]
    count = vw_ref.shape[0]

    out_to[...] = out_from[...]
    in_to[...] = in_from[...]

    @pl.when(pl.program_id(0) == 0)
    def _():
        gradient = tot_ref[:count]
        total = jnp.sum(sq_ref[...], keepdims=True) + jnp.sum(gradient * gradient, keepdims=True)
        norm = jnp.sqrt(total)
        norm_ref[...] = norm
        clip_ref[...] = jnp.broadcast_to(MAX_NORM / jnp.maximum(norm, MAX_NORM), clip_ref.shape)

    clip = clip_ref[...]

    def update(refs, outs, gradient, rate, decay):
        new = adam_step(refs[2][...], refs[0][...], refs[1][...], gradient, rate, decay)
        for ref, value in zip(outs, new + (new[2].astype(LOW),)):
            ref[...] = value

    update(
        (one_ref, two_ref, w_ref), outs[:4], g_ref[...].astype(WIDE) * clip,
        RATE_MATRIX, WEIGHT_DECAY,
    )

    @pl.when(pl.program_id(0) == 0)
    def _():
        update((vone_ref, vtwo_ref, vw_ref), outs[4:], tot_ref[:count] * clip, RATE_VECTOR, 0.0)
        groups, most = mem_ref.shape
        sentences = len_ref.shape[0]
        first = lax.axis_index("dp") * sentences
        pooled = [
            tot_ref[16 + s : 17 + s] / len_ref[s].astype(WIDE) for s in range(sentences)
        ]
        for g in range(groups):
            listed = jnp.int32(0)
            total = jnp.zeros_like(pooled[0])
            for m in range(most):
                listed += jnp.where(mem_ref[g, m] >= 0, 1, 0)
            for s in range(sentences):
                times = jnp.int32(0)
                for m in range(most):
                    times += jnp.where(mem_ref[g, m] == first + s, 1, 0)
                total = total + pooled[s] * times.astype(WIDE)
            emb_ref[g : g + 1] = total / listed.astype(WIDE)


def optimizer(lengths, members, owned, squares, totals, matrices, vectors, exchanged):
    block_rows, width = owned.shape
    steps = 4 if block_rows % 64 == 0 else 1
    smem = pl.BlockSpec(memory_space=pltpu.SMEM)
    mat = pl.BlockSpec((block_rows // steps, width), lambda i: (i, 0))

    def whole(shape):
        return pl.BlockSpec(shape, lambda i: (0, 0))

    sentences, positions_here = exchanged[0].shape[:2]
    passed = pl.BlockSpec((sentences, positions_here // steps, width), lambda i: (0, i, 0))
    vec = whole(vectors[0].shape)
    embeddings = (members.shape[0], width)
    return pl.pallas_call(
        optimizer_body,
        grid=(steps,),
        in_specs=[smem, smem, mat, whole(squares.shape), whole(totals.shape)]
        + [mat] * 3
        + [vec] * 3
        + [passed] * 2,
        out_specs=(whole((1, 1)), whole(embeddings)) + (mat,) * 4 + (vec,) * 4
        + (passed,) * 2,
        out_shape=(
            jax.ShapeDtypeStruct((1, 1), WIDE),
            jax.ShapeDtypeStruct(embeddings, WIDE),
        )
        + tuple(
            jax.ShapeDtypeStruct(like.shape, dtype)
            for like in (owned, vectors[0])
            for dtype in (WIDE, WIDE, WIDE, LOW)
        )
        + tuple(jax.ShapeDtypeStruct(like.shape, LOW) for like in exchanged),
        scratch_shapes=[pltpu.VMEM((1, width), WIDE)],
        compiler_params=params(),
        name="optimizer",
    )(lengths, members, owned, squares, totals, *matrices, *vectors, *exchanged)


def to_positions(value):
    width = value.shape[1]
    moved = jnp.concatenate(
        [value[:512].reshape(4, 128, width), value[512:].reshape(4, 64, width)], axis=1
    )
    moved = lax.all_to_all(moved, "seq", split_axis=0, concat_axis=0, tiled=True)
    rows = []
    for y in range(2):
        rows.append(moved[2 * y, :128])
        rows.append(jnp.concatenate([moved[2 * y, 128:], moved[2 * y + 1, 128:]], axis=0))
        rows.append(moved[2 * y + 1, :128])
    return jnp.stack(rows)


def to_rows(tokens):
    width = tokens.shape[-1]
    core = lax.axis_index("seq") % 2
    pieces = []
    for j in range(4):
        y, c = j // 2, j % 2
        pieces += [tokens[3 * y + 2 * c], tokens[3 * y + 1]]
    moved = jnp.concatenate(pieces, axis=0).reshape(4, 256, width)
    moved = lax.all_to_all(moved, "seq", split_axis=0, concat_axis=0, tiled=True)
    shared = moved[:, 128:].reshape(4, 2, 64, width)
    own = lax.dynamic_index_in_dim(shared, core, 1, keepdims=False)
    other = lax.dynamic_index_in_dim(shared, 1 - core, 1, keepdims=False)
    return jnp.concatenate(
        [moved[:, :128].reshape(512, width), own.reshape(256, width), other.reshape(256, width)],
        axis=0,
    )


def local(
    tokens,
    grad_out,
    lengths,
    members,
    owners,
    mat_master,
    mat_moment1,
    mat_moment2,
    vec_master,
    vec_moment1,
    vec_moment2,
):
    sent_dev, local_len, model_width = tokens.shape
    dp_count = lax.axis_size("dp")
    block_rows = mat_master.shape[0]
    direct = dp_count == 8 and block_rows == 3 * TILE

    if direct:
        blocks = owners
        weights, rows, qkv, matrices, attended, out_grad, lse = front(
            owners, lengths, mat_master, tokens, grad_out, vec_master
        )
    else:
        gathered = lax.all_gather(mat_master.astype(LOW), "dp", axis=0, tiled=True)
        weights = gathered.reshape(dp_count, block_rows, model_width)[owners]
        weights = weights.reshape(-1, TILE, model_width)
        rows = to_rows(tokens)
        blocks = jnp.arange(weights.shape[0] // 3, dtype=jnp.int32)
        qkv = qkv_project(blocks, rows, weights, vec_master)
        attended, lse, out_grad = attend(lengths, qkv, grad_out)
    result, left, right, d_attended, d_branch, sums = middle(
        blocks, lengths, attended, rows, out_grad, weights, vec_master
    )
    if direct:
        owned, totals, squares, input_grad, output = reduce_all(
            owners,
            lengths,
            rows,
            attended,
            left,
            qkv,
            d_attended,
            d_branch,
            right,
            matrices,
            result,
            lse,
            sums,
            sent_dev,
        )
    else:
        dq, dk, dv, output = attend_back(
            lengths, qkv, lse, d_attended, attended, result, sent_dev
        )
        grad_rows = grad_in(blocks, dq, dk, dv, d_branch, weights)
        grads = grad_ff(blocks, left, right)
        grads, sums_qv = grad_attn(blocks, rows, dq, dk, dv, attended, d_branch, grads)
        input_grad = to_positions(grad_rows)
        inverse = jnp.argsort(owners)
        grads = grads.reshape(dp_count, block_rows, model_width)[inverse]
        grads = grads.reshape(dp_count * block_rows, model_width)
        quarter = lax.psum_scatter(grads, ("dp", "seq"), scatter_dimension=0, tiled=True)
        owned = lax.all_gather(quarter, "seq", axis=0, tiled=True)
        quarter = quarter.astype(WIDE)
        group = lax.axis_index("seq") // 2
        core = lax.axis_index("seq") % 2
        place = jnp.arange(8)[:, None]
        pooled = jnp.where(place == 3 * group + 2 * core, sums[10:11], 0.0) + jnp.where(
            place == 3 * group + 1, sums[11:12], 0.0
        )
        pooled = lax.psum(pooled, "seq")
        local_vec = jnp.concatenate([sums_qv[0:2], sums[0:14]], axis=0)
        squares, vec_total = lax.psum(
            (jnp.sum(quarter * quarter), local_vec), ("dp", "seq")
        )
        squares = jnp.full((8, 128), squares / 1024.0)
        totals = jnp.concatenate([vec_total, pooled], axis=0)

    norm, embeddings, *new, output, input_grad = optimizer(
        lengths,
        members,
        owned,
        squares,
        totals,
        (mat_master, mat_moment1, mat_moment2),
        (vec_master, vec_moment1, vec_moment2),
        (output, input_grad),
    )
    return (output, input_grad, embeddings, norm.reshape(()), *new)


def solution(mesh):
    placed = (
        P("dp", "seq", None),
        P("dp", "seq", None),
        P("dp"),
        P("dp", None),
        P(),
        P("dp", None),
        P("dp", None),
        P("dp", None),
        P(),
        P(),
        P(),
    )
    return jax.shard_map(
        local,
        mesh=mesh,
        in_specs=placed,
        out_specs=(
            P("dp", "seq", None),
            P("dp", "seq", None),
            P("dp", None),
            P(),
            P("dp", None),
            P("dp", None),
            P("dp", None),
            P("dp", None),
            P(),
            P(),
            P(),
            P(),
        ),
        check_vma=False,
    )
```

```python
import functools

import jax
import jax.numpy as jnp
from jax import lax
from jax.experimental import pallas as pl
from jax.experimental.pallas import tpu as pltpu
from jax.sharding import PartitionSpec as P

HEADS = 12
HEAD_DIM = 64
FEEDFWD_UNITS = 3072
STEP = 10


NORM_EPS = 1e-06
MASK_FILL = -1e30
MAX_NORM = 1.0
ADAM_ONE = 0.9
ADAM_TWO = 0.999
ADAM_EPS = 1e-08
WEIGHT_DECAY = 0.01
RATE_MATRIX = 0.04
RATE_VECTOR = 0.5

FWD_PAIRS = 6
BACK_PAIRS = 6
NORM_ROWS = 128
TILE = 384
VMEM_LIMIT = 60 * 1024 * 1024
MESH_ID = pl.DeviceIdType.MESH
LOW = jnp.bfloat16
WIDE = jnp.float32


def adam_step(master, moment_one, moment_two, gradient, learn_rate, decay_rate):
    moment_one = ADAM_ONE * moment_one + (1.0 - ADAM_ONE) * gradient
    moment_two = ADAM_TWO * moment_two + (1.0 - ADAM_TWO) * gradient * gradient
    scaled_one = moment_one / (1.0 - ADAM_ONE**STEP)
    scaled_two = moment_two / (1.0 - ADAM_TWO**STEP)
    master = master - learn_rate * (
        scaled_one / (jnp.sqrt(scaled_two) + ADAM_EPS) + decay_rate * master
    )
    return (moment_one, moment_two, master)


def dot_nn(left, right):
    return jnp.dot(left, right, preferred_element_type=WIDE)


def dot_nt(left, right):
    return lax.dot_general(
        left, right, (((1,), (1,)), ((), ())), preferred_element_type=WIDE
    )


def dot_tn(left, right):
    return lax.dot_general(
        left, right, (((0,), (0,)), ((), ())), preferred_element_type=WIDE
    )


def tile_at(owners, tile):
    return 3 * owners[tile // 3] + tile % 3


def params(**kwargs):
    return pltpu.CompilerParams(vmem_limit_bytes=VMEM_LIMIT, **kwargs)


GATHER_HEAD = 10
GATHER_ORDER = (
    ("tk",), ("xb", 1), ("xs", 0), ("zs", 0), ("zs", 2), ("xb", 0), ("r", 1, 0), ("r", 0, 0),
    ("xs", 1), ("r", 1, 2), ("zs", 1), ("xr", 1, 0), ("r", 0, 2), ("xb", 2), ("r", 1, 1),
    ("r", 2, 0), ("r", 2, 2), ("r", 0, 1), ("xs", 2), ("xob", 2), ("r", 2, 1), ("zx", 0),
    ("xo", 0), ("zx", 1), ("yr", 1, 2), ("xr", 1, 1), ("tf",), ("zx", 2), ("xr", 2, 0), ("xo", 2),
    ("yr", 2, 1), ("e1", 0), ("xob", 1), ("xr", 2, 2), ("yx", 1, 1), ("xo", 1), ("xr", 1, 2),
    ("xr", 2, 1), ("e1", 1), ("xsr", 0), ("yx", 1, 0), ("e1", 2), ("yx", 1, 2), ("yx", 2, 2),
    ("yr", 2, 0), ("yr", 1, 0), ("e2", 2), ("yr", 1, 1), ("xsr", 1), ("xob", 0), ("e2", 1),
    ("yx", 2, 0), ("xsr", 2), ("yr", 2, 2), ("e2", 0), ("yx", 2, 1),
)


def front_body(
    own_of_ref, len_ref, w_ref, x_ref, g_ref, vec_ref,
    weights_ref, rows_ref, qkv_ref, mats_ref, o_ref, gy_ref, lse_ref,
    wide_buf, own_buf, out_ref, xo_ref, qkv_buf, mats_buf, o_buf,
    send_sem, recv_sem, tok_recv, local_sem, ex_send, ex_recv, ex_local,
):
    dp, sq = lax.axis_index("dp"), lax.axis_index("seq")
    z, x = dp // 2, dp % 2
    y, c = sq // 2, sq % 2
    q, qc, qy, qyc = sq, sq ^ 1, sq ^ 2, sq ^ 3
    dev_c, dev_y, dev_yc, dev_x = (dp, sq ^ 1), (dp, sq ^ 2), (dp, sq ^ 3), (dp ^ 1, sq)
    dev_near = (dp ^ 2, sq)
    has_up, has_down, inner = z < 3, z > 0, (z > 0) & (z < 3)
    dev_up = (jnp.minimum(dp + 2, dp % 2 + 6), sq)
    dev_down = (jnp.maximum(dp - 2, dp % 2), sq)
    sources = (z ^ 1, jnp.where(z < 2, 2, 1), jnp.where(z < 2, 3, 0))
    used = [0, 0]
    started, locals_ = [], []

    def move(src, dst):
        copy = pltpu.make_async_copy(src, dst, local_sem.at[used[1]])
        used[1] += 1
        copy.start()
        return copy

    loads = []
    for at in (q, qy, qc, qyc):
        thirds = pl.ds(3 * at, 3)
        loads.append(move(w_ref.at[thirds], wide_buf.at[thirds]))

    barrier = pltpu.get_barrier_semaphore()

    def greet(device):
        pl.semaphore_signal(barrier, inc=1, device_id=device, device_id_type=MESH_ID)

    for device in (dev_c, dev_y, dev_yc, dev_x):
        greet(device)
    pl.when(has_up)(lambda: greet(dev_up))
    pl.when(has_down)(lambda: greet(dev_down))
    pl.semaphore_wait(barrier, 4 + jnp.where(inner, 2, 1))

    def send(src, dst, recv, device, pred=None):
        copy = pltpu.make_async_remote_copy(
            src_ref=src,
            dst_ref=dst,
            send_sem=send_sem.at[used[0]],
            recv_sem=recv,
            device_id=device,
            device_id_type=MESH_ID,
        )
        used[0] += 1
        if pred is None:
            copy.start()
        else:
            pl.when(pred)(lambda: copy.start())
        started.append((copy, pred))

    def piece(slot, quarter, h, device, pred=None, own=False):
        at = out_ref.at[slot, 3 * quarter + h]
        src = own_buf.at[3 * quarter + h] if own else at
        send(src, at, recv_sem.at[slot, quarter, h], device, pred)

    def arrived(slot, quarter, h):
        at = out_ref.at[slot, 3 * quarter + h]
        pltpu.make_async_copy(at, at, recv_sem.at[slot, quarter, h]).wait()

    def taken(slot, quarter, h):
        arrived(slot, quarter, h)
        piece(slot, quarter, h, dev_c)

    def near(k):
        return 2 * sources[k] + x

    def far(k):
        return 2 * sources[k] + 1 - x

    oy = 1 - y
    full_own, full_sib = 3 * y + 2 * c, 3 * y + 2 * (1 - c)
    full_far, full_cross = 3 * oy + 2 * c, 3 * oy + 2 * (1 - c)

    def full_rows(j):
        return xo_ref.at[pl.ds(128 * j, 128)]

    def half_rows(part, j, core):
        return xo_ref.at[pl.ds(512 + 256 * (part ^ core) + 64 * j, 64)]

    def token_send():
        send(x_ref.at[full_far], full_rows(sq), tok_recv.at[sq, 0], dev_y)
        for part in range(2):
            src = x_ref.at[3 * oy + 1, pl.ds(64 * part, 64)]
            send(src, half_rows(part, sq, c), tok_recv.at[sq, 1 + part], dev_y)
        send(x_ref.at[full_cross], full_rows(sq), tok_recv.at[sq, 0], dev_yc)
        send(x_ref.at[full_sib], full_rows(sq), tok_recv.at[sq, 0], dev_c)
        locals_.append(move(x_ref.at[full_own], full_rows(sq)))
        for part in range(2):
            src = x_ref.at[3 * y + 1, pl.ds(64 * part, 64)]
            send(src, half_rows(part, sq, 1 - c), tok_recv.at[sq, 1 + part], dev_c)
            locals_.append(move(src, half_rows(part, sq, c)))

    def token_forward():
        for part in range(2):
            at = half_rows(part, sq ^ 2, c)
            pltpu.make_async_copy(at, at, tok_recv.at[sq ^ 2, 1 + part]).wait()
            send(at, half_rows(part, sq ^ 2, 1 - c), tok_recv.at[sq ^ 2, 1 + part], dev_c)

    def own_line(h):
        piece(dp, q, h, dev_up, has_up, own=True)
        piece(dp, q, h, dev_down, has_down, own=True)

    def line(k, h):
        arrived(near(k), q, h)
        onward = (jnp.where(sources[k] < z, dev_up[0], dev_down[0]), sq)
        piece(near(k), q, h, onward, inner)
        if k > 0:
            piece(near(k), q, h, dev_x)
            piece(near(k), q, h, dev_y)
        piece(near(k), q, h, dev_c)

    def from_x_own(h):
        arrived(dp ^ 1, q, h)
        piece(dp ^ 1, q, h, dev_near)
        piece(dp ^ 1, q, h, dev_c)

    def near_other_half(h):
        arrived(near(0), qy, h)
        piece(near(0), qy, h, dev_x)
        piece(near(0), qy, h, dev_c)

    def from_x(k, h):
        arrived(far(k), q, h)
        piece(far(k), q, h, dev_y)
        piece(far(k), q, h, dev_c)

    steps = {
        "tk": token_send,
        "tf": token_forward,
        "zs": own_line,
        "zx": lambda h: piece(dp, qy, h, dev_near, own=True),
        "xs": lambda h: piece(dp, q, h, dev_x, own=True),
        "xb": lambda h: piece(dp, qy, h, dev_x, own=True),
        "r": line,
        "xo": from_x_own,
        "xob": lambda h: taken(dp ^ 1, qy, h),
        "e1": near_other_half,
        "e2": lambda h: taken(far(0), q, h),
        "yr": lambda k, h: taken(near(k), qy, h),
        "xr": from_x,
        "xsr": lambda h: taken(far(0), qy, h),
        "yx": lambda k, h: taken(far(k), qy, h),
    }

    def round_own(index, quarter):
        loads[index].wait()
        thirds = pl.ds(3 * quarter, 3)
        own_buf[thirds] = wide_buf[thirds].astype(LOW)

    round_own(0, q)
    round_own(1, qy)
    for name, *at in GATHER_ORDER[:GATHER_HEAD]:
        steps[name](*at)
    round_own(2, qc)
    round_own(3, qyc)
    locals_.append(move(own_buf, out_ref.at[dp]))
    for name, *at in GATHER_ORDER[GATHER_HEAD:]:
        steps[name](*at)
    exchange = Exchange(by_sentence(g_ref, gy_ref), ex_send, ex_recv, ex_local)
    exchange.start()
    for step in range(1, 8):
        for h in range(3):
            arrived(dp ^ step, qc, h)
            arrived(dp ^ step, qyc, h)
    for other in (sq ^ 1, sq ^ 2, sq ^ 3):
        at = full_rows(other)
        pltpu.make_async_copy(at, at, tok_recv.at[other, 0]).wait()
    for other in (sq ^ 1, sq ^ 3):
        for part in range(2):
            at = half_rows(part, other, c)
            pltpu.make_async_copy(at, at, tok_recv.at[other, 1 + part]).wait()
    for copy in locals_:
        copy.wait()
    stores = [move(out_ref.at[slot], weights_ref.at[slot]) for slot in range(8)]
    stores.append(move(xo_ref, rows_ref))

    for part in range(3):
        for half in range(2):
            tile = 2 * part + half
            held = out_ref[own_of_ref[tile // 3], 4 * (tile % 3) : 4 * (tile % 3) + 4]
            rows = slice(TILE * half, TILE * (half + 1))
            mats_buf[part, rows] = held.reshape(TILE, held.shape[-1])
        stores.append(move(mats_buf.at[part], mats_ref.at[part]))
        value = dot_nn(xo_ref[...], mats_buf[part])
        if part == 0:
            value = (value + vec_ref[0:1]) * HEAD_DIM ** (-0.5)
        elif part == 2:
            value = value + vec_ref[1:2]
        qkv_buf[part] = value.astype(LOW)
        stores.append(move(qkv_buf.at[part], qkv_ref.at[part]))

    def attend_block(block, carry):
        bias = key_bias(len_ref, block == 2)
        at = pl.ds(pl.multiple_of(256 * block, 256), 256)
        keys = pl.ds(pl.multiple_of(512 * (block // 2), 512), 512)
        pairs = qkv_buf.shape[-1] // 128

        def scores_of(pair):
            lanes = slice(128 * pair, 128 * (pair + 1))
            return pair_scores(qkv_buf[0, at, lanes], qkv_buf[1, keys, lanes], bias)

        ahead = scores_of(0)
        for pair in range(pairs):
            scores = ahead
            if pair + 1 < pairs:
                ahead = scores_of(pair + 1)
            lanes = slice(128 * pair, 128 * (pair + 1))
            out, logs = attend_pair(scores, qkv_buf[2, keys, lanes])
            o_buf[at, lanes] = out
            for head in range(2):
                lse_ref[pair, head : head + 1, at] = logs[head]
        return carry

    lax.fori_loop(0, 3, attend_block, 0)
    stores.append(move(o_buf, o_ref))
    exchange.finish()
    for copy in stores:
        copy.wait()
    for copy, pred in started:
        if pred is None:
            copy.wait_send()
        else:
            pl.when(pred)(lambda copy=copy: copy.wait_send())


def front(owners, lengths, block, tokens, grad_out, vectors):
    block_rows, width = block.shape
    part = block_rows // 12
    hbm = pl.BlockSpec(memory_space=pl.ANY)
    smem = pl.BlockSpec(memory_space=pltpu.SMEM)
    vmem = pl.BlockSpec(memory_space=pltpu.VMEM)
    dma = pltpu.SemaphoreType.DMA
    flat = jax.ShapeDtypeStruct((768, width), LOW)
    weights, *rest = pl.pallas_call(
        front_body,
        out_shape=(
            jax.ShapeDtypeStruct((8, 12, part, width), LOW),
            jax.ShapeDtypeStruct((1024, width), LOW),
            jax.ShapeDtypeStruct((3, 1024, width), LOW),
            jax.ShapeDtypeStruct((3, width, width), LOW),
            flat,
            flat,
            jax.ShapeDtypeStruct((HEADS // 2, 2, 768), WIDE),
        ),
        in_specs=[smem] * 2 + [hbm] * 3 + [vmem],
        out_specs=(hbm,) * 6 + (vmem,),
        scratch_shapes=[
            pltpu.VMEM((12, part, width), WIDE),
            pltpu.VMEM((12, part, width), LOW),
            pltpu.VMEM((8, 12, part, width), LOW),
            pltpu.VMEM((1024, width), LOW),
            pltpu.VMEM((3, 1024, width), LOW),
            pltpu.VMEM((3, width, width), LOW),
            pltpu.VMEM((768, width), LOW),
            dma((160,)),
            dma((8, 4, 3)),
            dma((4, 3)),
            dma((24,)),
        ]
        + EXCHANGE_SEMS,
        compiler_params=params(collective_id=1, has_side_effects=True),
        name="gather_attend",
    )(owners, lengths, block.reshape(12, part, width), tokens, grad_out, vectors)
    return weights.reshape(8 * block_rows // TILE, TILE, width), *rest


def qkv_body(map_ref, x_ref, top_ref, low_ref, vec_ref, out_ref):
    part = pl.program_id(0)
    scale = jnp.where(part == 0, HEAD_DIM ** (-0.5), 1.0)
    value = dot_nn(x_ref[:, :TILE], top_ref[0]) + dot_nn(x_ref[:, TILE:], low_ref[0])
    bias = jnp.where(part == 0, vec_ref[0:1], jnp.where(part == 2, vec_ref[1:2], 0.0))
    out_ref[0] = ((value + bias) * scale).astype(LOW)


def qkv_project(owners, rows, weights, vectors):
    count, width = rows.shape
    return pl.pallas_call(
        qkv_body,
        grid_spec=pltpu.PrefetchScalarGridSpec(
            num_scalar_prefetch=1,
            grid=(3,),
            in_specs=[
                pl.BlockSpec((count, width), lambda i, m: (0, 0)),
                pl.BlockSpec((1, TILE, width), lambda i, m: (tile_at(m, 2 * i), 0, 0)),
                pl.BlockSpec((1, TILE, width), lambda i, m: (tile_at(m, 2 * i + 1), 0, 0)),
                pl.BlockSpec(vectors.shape, lambda i, m: (0, 0)),
            ],
            out_specs=pl.BlockSpec((1, count, width), lambda i, m: (i, 0, 0)),
        ),
        out_shape=jax.ShapeDtypeStruct((3, count, width), LOW),
        compiler_params=params(),
        name="qkv",
    )(owners, rows, weights, weights, vectors)


def group_barrier(dp, sq):
    barrier = pltpu.get_barrier_semaphore()
    for step in range(1, 4):
        pl.semaphore_signal(
            barrier, inc=1, device_id=(dp, sq ^ step), device_id_type=MESH_ID
        )
    pl.semaphore_wait(barrier, 3)


class Exchange:
    def __init__(self, pieces, send_sem, recv_sem, local_sem):
        self.dp, self.sq = lax.axis_index("dp"), lax.axis_index("seq")
        self.pieces = pieces
        self.sems = (send_sem, recv_sem, local_sem)

    def copies(self):
        send_sem, recv_sem, local_sem = self.sems
        out = []
        for step in (2, 3, 1):
            target = self.sq ^ step
            for kind, (src, dst) in enumerate(self.pieces(self.sq, target)):
                out.append(
                    pltpu.make_async_remote_copy(
                        src_ref=src,
                        dst_ref=dst,
                        send_sem=send_sem.at[step - 1, kind],
                        recv_sem=recv_sem.at[self.sq, kind],
                        device_id=(self.dp, target),
                        device_id_type=MESH_ID,
                    )
                )
        for kind, (src, dst) in enumerate(self.pieces(self.sq, self.sq)):
            out.append(pltpu.make_async_copy(src, dst, local_sem.at[kind]))
        return out

    def start(self):
        for copy in self.copies():
            copy.start()

    def finish(self):
        copies = self.copies()
        for copy in copies[:6]:
            copy.wait_send()
        for copy in copies[6:]:
            copy.wait()
        for step in range(1, 4):
            source = self.sq ^ step
            for kind, (_, dst) in enumerate(self.pieces(source, self.sq)):
                pltpu.make_async_copy(dst, dst, self.sems[1].at[source, kind]).wait()


EXCHANGE_SEMS = [
    pltpu.SemaphoreType.DMA((3, 2)),
    pltpu.SemaphoreType.DMA((4, 2)),
    pltpu.SemaphoreType.DMA((2,)),
]


def by_sentence(src, dst):
    def pieces(source, target):
        y, c = target // 2, target % 2
        return (
            (src.at[3 * y + 2 * c], dst.at[pl.ds(128 * source, 128)]),
            (src.at[3 * y + 1, pl.ds(64 * c, 64)], dst.at[pl.ds(512 + 64 * source, 64)]),
        )

    return pieces


def by_position(src, dst):
    def pieces(source, target):
        y, c = source // 2, source % 2
        return (
            (src.at[pl.ds(128 * target, 128)], dst.at[3 * y + 2 * c]),
            (src.at[pl.ds(512 + 64 * target, 64)], dst.at[3 * y + 1, pl.ds(64 * c, 64)]),
        )

    return pieces


def sentence_length(lengths_ref, shared):
    sq = lax.axis_index("seq")
    group, core = sq // 2, sq % 2
    return jnp.where(shared, lengths_ref[3 * group + 1], lengths_ref[3 * group + 2 * core])


def positions(shape, shared, first=0):
    row = first + lax.broadcasted_iota(jnp.int32, shape, 0)
    own = lax.axis_index("seq") % 2
    half = row // 256
    part = row - 256 * half
    core = own + half - 2 * own * half
    mixed = (part // 64) * 128 + part % 64 + 64 * core
    return jnp.where(shared, mixed, row)


def key_bias(lengths_ref, shared):
    inside = positions((512, 128), shared) < sentence_length(lengths_ref, shared)
    bias = jnp.where(inside, 0.0, MASK_FILL)
    return jnp.concatenate([bias, bias], axis=1)


def head_masks(shape):
    lane = lax.broadcasted_iota(jnp.int32, shape, 1)
    return (lane < HEAD_DIM, lane >= HEAD_DIM)


def pair_scores(queries, keys, bias):
    return [
        dot_nt(keys, jnp.where(mask, queries, jnp.zeros_like(queries))) + bias
        for mask in head_masks(queries.shape)
    ]


def attend_pair(pair_of_scores, values):
    value_t = values.T
    outs, logs = [], []
    for head, scores in enumerate(pair_of_scores):
        top = jnp.max(scores, axis=0, keepdims=True)
        shifted = jnp.exp(scores - top)
        total = jnp.sum(shifted, axis=0, keepdims=True)
        part = value_t[HEAD_DIM * head : HEAD_DIM * (head + 1)]
        outs.append(dot_nn(part, shifted.astype(LOW)) * (1.0 / total))
        logs.append(top + jnp.log(total))
    return jnp.concatenate(outs, axis=0).T.astype(LOW), logs


def attend_body(
    len_ref, q_ref, k_ref, v_ref, g_ref, o_ref, lse_ref, gy_ref, send_sem, recv_sem, local_sem
):
    block, group = pl.program_id(0), pl.program_id(1)
    exchange = Exchange(by_sentence(g_ref, gy_ref), send_sem, recv_sem, local_sem)

    @pl.when((block == 0) & (group == 0))
    def _():
        group_barrier(exchange.dp, exchange.sq)
        exchange.start()

    bias = key_bias(len_ref, block == 2)
    for pair in range(q_ref.shape[-1] // 128):
        lanes = slice(128 * pair, 128 * (pair + 1))
        scores = pair_scores(q_ref[0, :, lanes], k_ref[0, :, lanes], bias)
        out, logs = attend_pair(scores, v_ref[0, :, lanes])
        o_ref[:, lanes] = out
        for head in range(2):
            lse_ref[0, 2 * pair + head : 2 * pair + head + 1, :] = logs[head]

    @pl.when((block == 2) & (group == pl.num_programs(1) - 1))
    def _():
        exchange.finish()


def attend(lengths, qkv, grad_out):
    width = qkv.shape[-1]
    groups = width // 128 // FWD_PAIRS
    lanes = 128 * FWD_PAIRS
    hbm = pl.BlockSpec(memory_space=pl.ANY)
    return pl.pallas_call(
        attend_body,
        grid=(3, groups),
        in_specs=[
            pl.BlockSpec(memory_space=pltpu.SMEM),
            pl.BlockSpec((1, 256, lanes), lambda i, h: (0, i, h)),
            pl.BlockSpec((1, 512, lanes), lambda i, h: (1, i // 2, h)),
            pl.BlockSpec((1, 512, lanes), lambda i, h: (2, i // 2, h)),
            hbm,
        ],
        out_specs=(
            pl.BlockSpec((256, lanes), lambda i, h: (i, h)),
            pl.BlockSpec((1, 2 * FWD_PAIRS, 256), lambda i, h: (h, 0, i)),
            hbm,
        ),
        out_shape=(
            jax.ShapeDtypeStruct((768, width), LOW),
            jax.ShapeDtypeStruct((groups, 2 * FWD_PAIRS, 768), WIDE),
            jax.ShapeDtypeStruct((768, width), LOW),
        ),
        scratch_shapes=EXCHANGE_SEMS,
        compiler_params=params(collective_id=3, has_side_effects=True),
        name="attend",
    )(lengths, qkv, qkv, qkv, grad_out)


def back_first(head, queries, keys, values, grads, bias):
    mask = head_masks(queries.shape)[head]
    query = jnp.where(mask, queries, jnp.zeros_like(queries))
    grad = jnp.where(mask, grads, jnp.zeros_like(grads))
    return query, grad, dot_nt(keys, query) + bias, dot_nt(values, grad)


def back_second(head, first, keys_t, inner, log):
    query, grad, scores, d_probs = first
    rows = slice(HEAD_DIM * head, HEAD_DIM * (head + 1))
    inner_sum = jnp.sum(inner[rows], axis=0, keepdims=True)
    probs = jnp.exp(scores - log)
    d_scores = (probs * (d_probs - inner_sum)).astype(LOW)
    d_value = dot_nn(probs.astype(LOW), grad)
    return dot_nn(keys_t[rows], d_scores), dot_nn(d_scores, query), d_value


def back_inner(grads, outs):
    return (grads.astype(WIDE) * outs.astype(WIDE)).T


def back_query(parts):
    return (jnp.concatenate(parts, axis=0) * HEAD_DIM ** (-0.5)).T.astype(LOW)


def back_pair(queries, keys, values, grads, outs, logs, bias):
    keys_t, inner = keys.T, back_inner(grads, outs)
    found = []
    for head in range(2):
        first = back_first(head, queries, keys, values, grads, bias)
        found.append(back_second(head, first, keys_t, inner, logs[head : head + 1]))
    (query_a, key_a, value_a), (query_b, key_b, value_b) = found
    return back_query([query_a, query_b]), key_a + key_b, value_a + value_b


def attend_back_body(
    len_ref, q_ref, k_ref, v_ref, lse_ref, do_ref, o_ref, y_ref,
    dq_ref, dk_ref, dv_ref, out_ref,
    acc, keep, give, take, send_sem, recv_sem, local_sem, give_sem, take_sem,
):
    group, block = pl.program_id(0), pl.program_id(1)
    exchange = Exchange(by_position(y_ref, out_ref), send_sem, recv_sem, local_sem)
    dp, sq = exchange.dp, exchange.sq

    @pl.when((block == 0) & (group == 0))
    def _():
        group_barrier(dp, sq)
        exchange.start()

    bias = key_bias(len_ref, block == 0)
    d_keys, d_values = [], []
    for pair in range(q_ref.shape[-1] // 128):
        lanes = slice(128 * pair, 128 * (pair + 1))
        d_query, d_key, d_value = back_pair(
            q_ref[0, :, lanes], k_ref[0, :, lanes], v_ref[0, :, lanes], do_ref[:, lanes],
            o_ref[:, lanes], lse_ref[0, 2 * pair : 2 * pair + 2], bias,
        )
        dq_ref[:, lanes] = d_query
        d_keys.append((lanes, d_key))
        d_values.append((lanes, d_value))
    pairs = ((0, d_keys), (1, d_values))

    def swap(kind):
        return pltpu.make_async_remote_copy(
            src_ref=give.at[group, kind],
            dst_ref=take.at[group, kind],
            send_sem=give_sem.at[group, kind],
            recv_sem=take_sem.at[group, kind],
            device_id=(dp, sq ^ 1),
            device_id_type=MESH_ID,
        )

    @pl.when(block == 0)
    def _():
        for kind, parts in pairs:
            for lanes, part in parts:
                keep[kind, :, lanes] = part[:256]
                give[group, kind, :, lanes] = part[256:].astype(LOW)
            swap(kind).start()

    @pl.when(block == 1)
    def _():
        for kind, parts in pairs:
            for lanes, part in parts:
                acc[kind, :, lanes] = part

    @pl.when(block == 2)
    def _():
        for (kind, parts), ref in zip(pairs, (dk_ref, dv_ref)):
            swap(kind).wait()
            for lanes, part in parts:
                ref[:512, lanes] = (acc[kind, :, lanes] + part).astype(LOW)
                other = take[group, kind, :, lanes].astype(WIDE)
                ref[512:, lanes] = (keep[kind, :, lanes] + other).astype(LOW)

    @pl.when((block == 2) & (group == pl.num_programs(0) - 1))
    def _():
        exchange.finish()


def attend_back(lengths, qkv, lse, d_out, out, result, sent_dev):
    width = qkv.shape[-1]
    groups = width // 128 // BACK_PAIRS
    lanes = 128 * BACK_PAIRS
    hbm = pl.BlockSpec(memory_space=pl.ANY)
    query = pl.BlockSpec((256, lanes), lambda h, i: ((i + 2) % 3, h))
    keys = pl.BlockSpec((768, lanes), lambda h, i: (0, h))
    flat = jax.ShapeDtypeStruct((768, width), LOW)
    shared = lambda i: jnp.where(i == 0, 1, 0)
    return pl.pallas_call(
        attend_back_body,
        grid=(groups, 3),
        in_specs=[
            pl.BlockSpec(memory_space=pltpu.SMEM),
            pl.BlockSpec((1, 256, lanes), lambda h, i: (0, (i + 2) % 3, h)),
            pl.BlockSpec((1, 512, lanes), lambda h, i: (1, shared(i), h)),
            pl.BlockSpec((1, 512, lanes), lambda h, i: (2, shared(i), h)),
            pl.BlockSpec((1, 2 * BACK_PAIRS, 256), lambda h, i: (h, 0, (i + 2) % 3)),
            query,
            query,
            hbm,
        ],
        out_specs=(query, keys, keys, hbm),
        out_shape=(flat, flat, flat, jax.ShapeDtypeStruct((sent_dev, 128, width), LOW)),
        scratch_shapes=[
            pltpu.VMEM((2, 512, lanes), WIDE),
            pltpu.VMEM((2, 256, lanes), WIDE),
            pltpu.VMEM((groups, 2, 256, lanes), LOW),
            pltpu.VMEM((groups, 2, 256, lanes), LOW),
        ]
        + EXCHANGE_SEMS
        + [pltpu.SemaphoreType.DMA((groups, 2)), pltpu.SemaphoreType.DMA((groups, 2))],
        compiler_params=params(collective_id=4, has_side_effects=True),
        name="attend_back",
    )(lengths, qkv, qkv, qkv, lse.reshape(groups, 2 * BACK_PAIRS, 768), d_out, out, result)


def row_mean(value):
    return jnp.mean(value, axis=-1, keepdims=True)


def col_sum(value):
    return jnp.sum(value, axis=0, keepdims=True)


def middle_body(
    map_ref, len_ref, o_hbm, x_hbm, gy_hbm, w_ref, vec_ref,
    y_hbm, left_hbm, right_hbm, do_hbm, da_hbm, sums_ref,
    w_buf, o_buf, x_buf, gy_buf, left, right, slope, total, hat_one, rstd_one, low_buf,
    sem, in_sem, out_sem,
):
    count, width = o_buf.shape
    tiles = w_buf.shape[0]
    chunks = FEEDFWD_UNITS // width

    def fetch(t):
        return pltpu.make_async_copy(w_ref.at[tile_at(map_ref, 6 + t)], w_buf.at[t], sem.at[t])

    inputs = [
        pltpu.make_async_copy(src, dst, in_sem.at[i])
        for i, (src, dst) in enumerate(
            (
                (o_hbm, o_buf),
                (x_hbm.at[pl.ds(0, count)], x_buf),
                (gy_hbm, gy_buf),
            )
        )
    ]
    inputs[0].start()
    for t in range(2):
        fetch(t).start()
    inputs[1].start()
    for c in range(chunks):
        for t in (2 + 2 * c, 3 + 2 * c, 10 + 2 * c, 11 + 2 * c):
            fetch(t).start()
    inputs[2].start()
    outputs = []

    def put(src, dst):
        copy = pltpu.make_async_copy(src, dst, out_sem.at[len(outputs)])
        copy.start()
        outputs.append(copy)

    def put_left(t, value):
        for u in range(2):
            left[t + u] = value[:, TILE * u : TILE * (u + 1)]
            put(left.at[t + u], left_hbm.at[t + u])

    def ready(*which):
        for t in which:
            fetch(t).wait()

    def pair(t):
        return w_buf[t : t + 2].reshape(2 * TILE, width)

    def vec(row):
        return vec_ref[row : row + 1, :]

    def fold(value):
        return jnp.sum(value.reshape(-1, 8, width), axis=0)

    def over_rows(body, carried):
        zero = (jnp.zeros((8, width), WIDE),) * carried

        def step(i, carry):
            return body(pl.ds(pl.multiple_of(i * NORM_ROWS, NORM_ROWS), NORM_ROWS), i, carry)

        return lax.fori_loop(0, count // NORM_ROWS, step, zero)

    inputs[0].wait()
    ready(0, 1)
    total[...] = dot_nn(o_buf[...], pair(0))
    inputs[1].wait()

    def norm_one(at, i, carry):
        resid = x_buf[at].astype(WIDE) + (total[at] + vec(2))
        centered = resid - row_mean(resid)
        rstd = lax.rsqrt(row_mean(centered * centered) + NORM_EPS)
        rstd_one[at] = rstd
        hat = centered * rstd
        hat_one[at] = hat
        first = hat * vec(4) + vec(5)
        total[at] = first + vec(3)
        right[0, at] = first.astype(LOW)
        return carry

    over_rows(norm_one, 0)
    put(right.at[0], right_hbm.at[0])

    first_low = right[0]
    for c in range(chunks):
        ready(2 + 2 * c, 3 + 2 * c, 10 + 2 * c, 11 + 2 * c)
        act = dot_nt(first_low, pair(2 + 2 * c)) + vec(8 + c)
        cdf = 0.5 + 0.5 * lax.erf(act * (0.5**0.5))
        pdf = jnp.exp(-0.5 * act * act) * 0.3989422804014327
        slope[c] = cdf + act * pdf
        active = (act * cdf).astype(LOW)
        put_left(8 + 2 * c, active)
        total[...] += dot_nn(active, pair(10 + 2 * c))
    inputs[2].wait()

    def norm_two(at, i, carry):
        d_gain, d_shift, d_bias, pool_full, pool_half = carry
        resid = total[at]
        centered = resid - row_mean(resid)
        rstd = lax.rsqrt(row_mean(centered * centered) + NORM_EPS)
        hat = centered * rstd
        result = hat * vec(6) + vec(7)
        low_buf[0, at] = result.astype(LOW)
        shared = i * NORM_ROWS >= 512
        row = positions((NORM_ROWS, 128), shared, i * NORM_ROWS - jnp.where(shared, 512, 0))
        valid = jnp.where(row < sentence_length(len_ref, shared), 1.0, 0.0)
        pooled = fold(result * jnp.concatenate([valid] * (width // 128), axis=1))
        part = shared.astype(WIDE)
        grad = gy_buf[at].astype(WIDE)
        d_gain = d_gain + fold(grad * hat)
        d_shift = d_shift + fold(grad)
        grad = grad * vec(6)
        d_resid = rstd * (grad - row_mean(grad) - hat * row_mean(grad * hat))
        total[at] = d_resid
        grad_low = d_resid.astype(LOW)
        right[1, at] = grad_low
        return (
            d_gain,
            d_shift,
            d_bias + fold(grad_low.astype(WIDE)),
            pool_full + pooled * (1.0 - part),
            pool_half + pooled * part,
        )

    sums_ref[...] = jnp.zeros_like(sums_ref)
    found = over_rows(norm_two, 5)
    for row, value in zip((4, 5, 1, 10, 11), found):
        sums_ref[row : row + 1, :] = col_sum(value)
    put(low_buf.at[0], y_hbm)
    put(right.at[1], right_hbm.at[1])

    grad_low = right[1]
    for c in range(chunks):
        d_active = dot_nt(grad_low, pair(10 + 2 * c))
        d_act = (d_active * slope[c]).astype(LOW)
        put_left(2 * c, d_act)
        sums_ref[6 + c : 7 + c, :] = col_sum(d_act.astype(WIDE))
        total[...] += dot_nn(d_act, pair(2 + 2 * c))

    def norm_back(at, i, carry):
        d_gain, d_shift, d_bias = carry
        grad = total[at]
        hat = hat_one[at]
        d_gain = d_gain + fold(grad * hat)
        d_shift = d_shift + fold(grad)
        grad = grad * vec(4)
        d_resid = rstd_one[at] * (grad - row_mean(grad) - hat * row_mean(grad * hat))
        grad_low = d_resid.astype(LOW)
        low_buf[1, at] = grad_low
        return (d_gain, d_shift, d_bias + fold(grad_low.astype(WIDE)))

    found = over_rows(norm_back, 3)
    for row, value in zip((2, 3, 0), found):
        sums_ref[row : row + 1, :] = col_sum(value)
    put(low_buf.at[1], da_hbm)
    low_buf[2] = dot_nt(low_buf[1], pair(0)).astype(LOW)
    put(low_buf.at[2], do_hbm)
    for copy in outputs:
        copy.wait()


def middle(owners, lengths, attended, rows, out_grad, weights, vectors):
    count, width = attended.shape
    half = FEEDFWD_UNITS // TILE
    tiles = 2 + 2 * half
    hbm = pl.BlockSpec(memory_space=pl.ANY)
    smem = pl.BlockSpec(memory_space=pltpu.SMEM)
    vmem = pl.BlockSpec(memory_space=pltpu.VMEM)
    flat = jax.ShapeDtypeStruct((count, width), LOW)
    return pl.pallas_call(
        middle_body,
        in_specs=[smem, smem] + [hbm] * 4 + [vmem],
        out_specs=(hbm,) * 5 + (vmem,),
        out_shape=(
            flat,
            jax.ShapeDtypeStruct((2 * half, count, TILE), LOW),
            jax.ShapeDtypeStruct((2, count, width), LOW),
            flat,
            flat,
            jax.ShapeDtypeStruct((16, width), WIDE),
        ),
        scratch_shapes=[
            pltpu.VMEM((tiles, TILE, width), LOW),
            pltpu.VMEM((count, width), LOW),
            pltpu.VMEM((count, width), LOW),
            pltpu.VMEM((count, width), LOW),
            pltpu.VMEM((2 * half, count, TILE), LOW),
            pltpu.VMEM((2, count, width), LOW),
            pltpu.VMEM((half // 2, count, width), WIDE),
            pltpu.VMEM((count, width), WIDE),
            pltpu.VMEM((count, width), WIDE),
            pltpu.VMEM((count, 1), WIDE),
            pltpu.VMEM((3, count, width), LOW),
            pltpu.SemaphoreType.DMA((tiles,)),
            pltpu.SemaphoreType.DMA((3,)),
            pltpu.SemaphoreType.DMA((2 * half + 5,)),
        ],
        compiler_params=params(),
        name="feed_forward",
    )(owners, lengths, attended, rows, out_grad, weights, vectors)


def grad_ff_body(map_ref, left_ref, right_ref, out_ref):
    out_ref[0] = dot_tn(left_ref[0], right_ref[0]).astype(LOW)


def grad_ff(owners, left, right):
    per = FEEDFWD_UNITS // TILE
    count, width = right.shape[1:]
    return pl.pallas_call(
        grad_ff_body,
        grid_spec=pltpu.PrefetchScalarGridSpec(
            num_scalar_prefetch=1,
            grid=(2 * per,),
            in_specs=[
                pl.BlockSpec((1, count, TILE), lambda i, m: (i, 0, 0)),
                pl.BlockSpec((1, count, width), lambda i, m: (i // per, 0, 0)),
            ],
            out_specs=pl.BlockSpec((1, TILE, width), lambda i, m: (tile_at(m, 8 + i), 0, 0)),
        ),
        out_shape=jax.ShapeDtypeStruct((8 + 2 * per, TILE, width), LOW),
        compiler_params=params(),
        name="grad_ff",
    )(owners, left, right)


def grad_attn_body(
    map_ref, x_ref, dq_ref, dk_ref, dv_ref, o_ref, da_ref, into_ref, out_ref, sums_ref
):
    step = pl.program_id(0)
    for part, grad_ref in enumerate((dq_ref, dk_ref, dv_ref)):

        @pl.when(step // 2 == part)
        def _(grad_ref=grad_ref):
            out_ref[0] = dot_tn(x_ref[...], grad_ref[...]).astype(LOW)

    @pl.when(step // 2 == 3)
    def _():
        out_ref[0] = dot_tn(o_ref[...], da_ref[...]).astype(LOW)

    @pl.when(step == 0)
    def _():
        sums_ref[...] = jnp.zeros_like(sums_ref)
        sums_ref[0:1, :] = col_sum(dq_ref[...].astype(WIDE))
        sums_ref[1:2, :] = col_sum(dv_ref[...].astype(WIDE))


def grad_attn(owners, rows, dq, dk, dv, attended, da, into):
    count, width = dq.shape
    whole = pl.BlockSpec((count, width), lambda i, m: (0, 0))
    return pl.pallas_call(
        grad_attn_body,
        grid_spec=pltpu.PrefetchScalarGridSpec(
            num_scalar_prefetch=1,
            grid=(8,),
            in_specs=[
                pl.BlockSpec((count, TILE), lambda i, m: (0, i % 2)),
                whole,
                whole,
                whole,
                pl.BlockSpec((768, TILE), lambda i, m: (0, i % 2)),
                pl.BlockSpec((768, width), lambda i, m: (0, 0)),
                pl.BlockSpec(memory_space=pl.ANY),
            ],
            out_specs=(
                pl.BlockSpec((1, TILE, width), lambda i, m: (tile_at(m, i), 0, 0)),
                pl.BlockSpec((8, width), lambda i, m: (0, 0)),
            ),
        ),
        out_shape=(
            jax.ShapeDtypeStruct(into.shape, LOW),
            jax.ShapeDtypeStruct((8, width), WIDE),
        ),
        input_output_aliases={7: 0},
        compiler_params=params(),
        name="grad_attn",
    )(owners, rows, dq, dk, dv, attended, da, into)


def grad_in_body(map_ref, dq_ref, dk_ref, dv_ref, dh_ref, *refs):
    w_refs, out_ref = refs[:6], refs[6]
    for half in range(2):
        cols = slice(TILE * half, TILE * (half + 1))
        value = dh_ref[:, cols].astype(WIDE)
        for part, grad_ref in enumerate((dq_ref, dk_ref, dv_ref)):
            value = value + dot_nt(grad_ref[...], w_refs[2 * part + half][0])
        out_ref[:, cols] = value.astype(LOW)


def grad_in(owners, dq, dk, dv, dh, weights):
    count, width = dq.shape
    block = pl.BlockSpec((256, width), lambda i, m: (i, 0))
    return pl.pallas_call(
        grad_in_body,
        grid_spec=pltpu.PrefetchScalarGridSpec(
            num_scalar_prefetch=1,
            grid=(count // 256,),
            in_specs=[block] * 4
            + [
                pl.BlockSpec((1, TILE, width), lambda i, m, t=t: (tile_at(m, t), 0, 0)) for t in range(6)
            ],
            out_specs=block,
        ),
        out_shape=jax.ShapeDtypeStruct((count, width), LOW),
        compiler_params=params(),
        name="grad_in",
    )(owners, dq, dk, dv, dh, *([weights] * 6))


REDUCE_MODE = (
    {"n": "z", "a": "x", "e": "y", "o": "x"},
    {"n": "z", "a": "y", "e": "y", "o": "y"},
    {"n": "z", "a": "x", "e": "x", "o": "x"},
)
REDUCE_ORDER = (
    ("part", "n", "f", 1), ("part", "e", "f", 1), ("part", "e", "n", 1), ("both", "n", "f", 1),
    ("part", "a", "n", 1), ("both", "e", "f", 1), ("part", "a", "f", 0), ("vs", 0),
    ("part", "n", "f", 2), ("both", "a", "n", 1), ("both", "e", "n", 1), ("part", "n", "n", 1),
    ("both", "a", "f", 0), ("both", "n", "f", 2), ("va", 0), ("vs", 1), ("part", "a", "f", 2),
    ("part", "e", "f", 0), ("part", "n", "n", 2), ("both", "n", "n", 1), ("both", "a", "f", 2),
    ("turn", "n", 1), ("part", "o", "n", 1), ("both", "e", "f", 0), ("part", "a", "f", 1),
    ("part", "e", "n", 0), ("part", "o", "f", 1), ("both", "a", "f", 1), ("both", "n", "n", 2),
    ("part", "e", "f", 2), ("both", "o", "f", 1), ("part", "a", "n", 2), ("both", "e", "n", 0),
    ("both", "e", "f", 2), ("part", "n", "n", 0), ("turn", "e", 1), ("both", "a", "n", 2),
    ("turn", "a", 2), ("part", "n", "f", 0), ("both", "o", "n", 1), ("own", "n", 1),
    ("part", "o", "f", 2), ("own", "f", 1), ("both", "n", "f", 0), ("part", "a", "n", 0),
    ("part", "e", "n", 2), ("both", "o", "f", 2), ("own", "f", 2), ("part", "o", "n", 2),
    ("both", "e", "n", 2), ("both", "n", "n", 0), ("turn", "e", 2), ("both", "a", "n", 0),
    ("turn", "n", 2), ("gin",), ("in",), ("turn", "a", 1), ("part", "o", "f", 0),
    ("part", "o", "n", 0), ("turn", "n", 0), ("turn", "e", 0), ("turn", "a", 0), ("on", "e", 1),
    ("va", 1), ("both", "o", "n", 0), ("on", "n", 2), ("both", "o", "n", 2), ("own", "n", 0),
    ("both", "o", "f", 0), ("own", "f", 0), ("on", "a", 2), ("own", "n", 2), ("turn", "o", 2),
    ("on", "e", 2), ("on", "n", 0), ("turn", "o", 1), ("on", "a", 1), ("on", "n", 1), ("vs", 2),
    ("turn", "o", 0), ("on", "e", 0), ("end", 1), ("on", "a", 0), ("va", 2), ("vs", 3), ("end", 2),
    ("va", 3), ("vs", 4), ("end", 0), ("va", 4),
)


def reduce_body(
    own_of_ref, len_ref, x_ref, o_ref, left_ref, qkv_ref, do_ref, da_ref, right_ref,
    w_ref, y_ref, lse_ref, sums_ref, own_ref, vt_ref, sq_ref, gi_ref, out_ref,
    left_0, left_1, left_2, rbuf, wbuf, gbuf, give, take, pbuf, core_in, x_two, x_one, y_two, y_one,
    zf_in, mid_in, fin_in, near_in, ebuf, tbuf, tlow, vbuf, v_in, s_own, s_seq, s_dp,
    send_sem, local_sem, core_sem, xtwo_sem, xone_sem, ytwo_sem, yone_sem,
    zf_sem, mid_sem, fin_sem, near_sem, v_sem, out_sem, seq_sem, dp_sem, in_sem,
    give_sem, take_sem, free_sem, ex_send, ex_recv, ex_local,
):
    dp, sq = lax.axis_index("dp"), lax.axis_index("seq")
    z, x = dp // 2, dp % 2
    y, c = sq // 2, sq % 2
    dev_c, dev_y, dev_yc, dev_x = (dp, sq ^ 1), (dp, sq ^ 2), (dp, sq ^ 3), (dp ^ 1, sq)
    dev_near = (dp ^ 2, sq)
    inner = (z > 0) & (z < 3)
    outer = jnp.logical_not(inner)
    place = {
        "n": z ^ 1,
        "a": jnp.where(z < 2, 2, 1),
        "e": jnp.where(z < 2, 3, 0),
        "o": z,
    }
    lefts = (left_0, left_1, left_2)
    used = [0, 0]
    remotes, own_moves = [], []

    def move(src, dst):
        copy = pltpu.make_async_copy(src, dst, local_sem.at[used[1]])
        used[1] += 1
        copy.start()
        return copy

    first_loads = [
        move(qkv_ref.at[0, pl.ds(0, 768)], wbuf.at[0]),
        move(do_ref, wbuf.at[1]),
        move(o_ref, wbuf.at[2]),
        move(qkv_ref.at[1], core_in.at[pl.ds(0, 1024)]),
        move(qkv_ref.at[2], core_in.at[pl.ds(1024, 1024)]),
    ]

    def loaded(name):
        for copy in loads.pop(name, ()):
            copy.wait()

    barrier = pltpu.get_barrier_semaphore()
    for step in range(1, 4):
        pl.semaphore_signal(
            barrier, inc=1, device_id=(dp, sq ^ step), device_id_type=MESH_ID
        )
    for step in range(1, 8):
        pl.semaphore_signal(
            barrier, inc=1, device_id=(dp ^ step, sq), device_id_type=MESH_ID
        )
    pl.semaphore_wait(barrier, 10)

    def send(src, dst, recv, device, pred=None):
        copy = pltpu.make_async_remote_copy(
            src_ref=src,
            dst_ref=dst,
            send_sem=send_sem.at[used[0]],
            recv_sem=recv,
            device_id=device,
            device_id_type=MESH_ID,
        )
        used[0] += 1
        if pred is None:
            copy.start()
        else:
            pl.when(pred)(lambda: copy.start())
        remotes.append((copy, pred))

    def arrived(at, sem):
        pltpu.make_async_copy(at, at, sem).wait()

    def wide(ref, *at):
        return ref[at].astype(WIDE)

    exchange = Exchange(by_position(y_ref, out_ref), ex_send, ex_recv, ex_local)
    exchange.start()
    for copy in first_loads:
        copy.wait()

    loads = {"right": [move(right_ref, rbuf.at[pl.ds(4, 2)]), move(da_ref, rbuf.at[3])]}
    for t in range(3):
        loads[t] = []
        for block in range(8):
            tile = 3 * block + t
            cols = pl.ds(TILE * (tile % 2), TILE)
            if tile < 6:
                src = x_ref.at[pl.ds(0, 768), cols]
            elif tile < 8:
                src = o_ref.at[:, cols]
            else:
                src = left_ref.at[tile - 8]
            loads[t].append(move(src, lefts[t].at[block]))

    def swap(pair, kind):
        return pltpu.make_async_remote_copy(
            src_ref=give.at[pair, kind],
            dst_ref=take.at[pair, kind],
            send_sem=give_sem.at[pair, kind],
            recv_sem=take_sem.at[pair, kind],
            device_id=dev_c,
            device_id_type=MESH_ID,
        )

    biases = (key_bias(len_ref, False), key_bias(len_ref, True))
    pairs = rbuf.shape[-1] // 128

    def back_at(pair, block):
        lanes, rows = slice(128 * pair, 128 * (pair + 1)), slice(256 * block, 256 * (block + 1))
        first = 512 * (block // 2)
        keys = core_in[first : first + 512, lanes]
        return lanes, rows, keys, core_in[1024 + first : 1536 + first, lanes]

    def first_of(pair, block, head):
        lanes, rows, keys, values = back_at(pair, block)
        return back_first(
            head, wbuf[0, rows, lanes], keys, values, wbuf[1, rows, lanes], biases[block // 2]
        )

    items = [(p, block, head) for p in range(pairs) for block in (2, 0, 1) for head in range(2)]
    ahead = first_of(*items[0])
    parts = {}
    for index, (pair, block, head) in enumerate(items):
        this = ahead
        if index + 1 < len(items):
            ahead = first_of(*items[index + 1])
        lanes, rows, keys, _ = back_at(pair, block)
        if head == 0:
            keys_t, weighed = keys.T, back_inner(wbuf[1, rows, lanes], wbuf[2, rows, lanes])
        log = lse_ref[pair, head : head + 1, rows]
        parts[block, head] = back_second(head, this, keys_t, weighed, log)
        if head == 0:
            continue
        rbuf[0, rows, lanes] = back_query([parts[block, 0][0], parts[block, 1][0]])
        for kind in range(2):
            part = parts[block, 0][1 + kind] + parts[block, 1][1 + kind]
            if block == 2:
                rbuf[1 + kind, 512:768, lanes] = part[:256].astype(LOW)
                give[pair, kind] = part[256:].astype(LOW)
                swap(pair, kind).start()
            elif block == 0:
                parts["sum", kind] = part
            else:
                total = parts["sum", kind] + part
                rbuf[1 + kind, 0:512, lanes] = total.astype(LOW)
    pl.semaphore_signal(free_sem, inc=1, device_id=dev_c, device_id_type=MESH_ID)
    loads["in"] = [move(w_ref, wbuf)]
    for pair in range(pairs):
        lanes = slice(128 * pair, 128 * (pair + 1))
        for kind in range(2):
            swap(pair, kind).wait()
            rows = pl.ds(512, 256)
            rbuf[1 + kind, rows, lanes] = (
                rbuf[1 + kind, rows, lanes].astype(WIDE) + take[pair, kind].astype(WIDE)
            ).astype(LOW)
    loaded("right")
    pl.semaphore_wait(free_sem, 1)

    partners = (dev_c, dev_y, dev_x, (dp ^ 2, sq), (dp ^ 4, sq))

    def vec_send(step):
        if step == 0:
            vbuf[0] = jnp.zeros(vbuf.shape[1:], WIDE)
            vbuf[0, 0:1] = col_sum(wide(rbuf, 0))
            vbuf[0, 1:2] = col_sum(wide(rbuf, 2))
            vbuf[0, 2:12] = sums_ref[0:10]
            vbuf[0, pl.ds(16 + 3 * y + 2 * c, 1)] = sums_ref[10:11]
            vbuf[0, pl.ds(16 + 3 * y + 1, 1)] = sums_ref[11:12]
        send(vbuf.at[step], v_in.at[step], v_sem.at[step], partners[step])

    def vec_add(step):
        arrived(v_in.at[step], v_sem.at[step])
        vbuf[step + 1] = vbuf[step] + v_in[step]

    def input_grad():
        loaded("in")
        for part in range(3):
            cols = slice(256 * part, 256 * (part + 1))
            value = wide(rbuf, 3, slice(None), cols)
            for index in range(3):
                value = value + dot_nt(rbuf[index], wbuf[index, cols])
            gbuf[:, cols] = value.astype(LOW)

    def in_full(j):
        return gbuf.at[pl.ds(128 * j, 128)], gi_ref.at[3 * y + 2 * c]

    def in_half(j):
        return gbuf.at[pl.ds(512 + 64 * j, 64)], gi_ref.at[3 * y + 1, pl.ds(64 * c, 64)]

    def input_send():
        for device in (dev_y, dev_yc, dev_c):
            for kind, pair in enumerate((in_full(device[1]), in_half(device[1]))):
                send(pair[0], pair[1], in_sem.at[sq, kind], device)
        own_moves.append(move(*in_full(sq)))
        own_moves.append(move(*in_half(sq)))

    def standard_of(slot):
        found = jnp.int32(0)
        for block in range(8):
            found = jnp.maximum(found, jnp.where(own_of_ref[block] == slot, block, 0))
        return found

    def slot_of(k, p):
        return 2 * place[k] + (x if p == "n" else 1 - x)

    def core_at(slot, t, half):
        first = 96 * (2 * (8 * t + slot) + half)
        return core_in.at[pl.ds(pl.multiple_of(first, 96), 96)]

    def partial(k, p, t):
        loaded(t)
        slot = slot_of(k, p)
        block = standard_of(slot)
        tile = 3 * block + t
        right = jnp.where(tile < 8, tile // 2, 4 + (tile - 8) // 8)
        value = dot_tn(lefts[t][block], rbuf[right]).astype(LOW)
        for quarter in range(4):
            rows = slice(96 * quarter, 96 * (quarter + 1))
            pbuf[quarter % 2, t, slot, quarter // 2] = value[rows]
        for half in range(2):
            src = pbuf.at[1 - c, t, slot, half]
            send(src, core_at(slot, t, half), core_sem.at[t, slot, half], dev_c)

    def held(*at):
        return pbuf.at[(c, *at)]

    index_of = {"x": {}, "y": {}, "z": {}}
    for t in range(3):
        for k in "naeo":
            found = index_of[REDUCE_MODE[t][k]]
            found[k, t] = len(found)

    def first_send(k, p, t):
        slot = slot_of(k, p)
        if REDUCE_MODE[t][k] == "y":
            at, half = index_of["y"][k, t], "nf".index(p)
            send(held(t, slot, 1 - y), y_two.at[at, half], ytwo_sem.at[at, half], dev_y)
        elif p == "f":
            at = index_of["x"][k, t]
            send(held(t, slot), x_two.at[at], xtwo_sem.at[at], dev_x)

    def both_cores(k, p, t):
        slot = slot_of(k, p)
        for half in range(2):
            arrived(core_at(slot, t, half), core_sem.at[t, slot, half])
            other = core_at(slot, t, half)[...].astype(WIDE)
            pbuf[c, t, slot, half] = (wide(pbuf, c, t, slot, half) + other).astype(LOW)
        if REDUCE_MODE[t][k] == "z":
            half = "nf".index(p)
            send(held(t, slot), zf_in.at[t, half], zf_sem.at[t, half], dev_near)
        elif k != "o":
            first_send(k, p, t)

    def own_block(p, t):
        if REDUCE_MODE[t]["n"] == "z":
            slot, half = slot_of("o", p), "nf".index(p)
            arrived(zf_in.at[t, half], zf_sem.at[t, half])
            pbuf[c, t, slot] = (wide(pbuf, c, t, slot) + wide(zf_in, t, half)).astype(LOW)
        first_send("o", p, t)

    def turn(k, t):
        mode = REDUCE_MODE[t][k]
        if mode == "z":
            return
        at = index_of[mode][k, t]
        near, far = slot_of(k, "n"), slot_of(k, "f")
        if mode == "y":
            for half in range(2):
                arrived(y_two.at[at, half], ytwo_sem.at[at, half])
            pbuf[c, t, far, y] = (wide(pbuf, c, t, far, y) + wide(y_two, at, 1)).astype(LOW)
            send(held(t, far, y), x_one.at[at], xone_sem.at[at], dev_x)
        else:
            arrived(x_two.at[at], xtwo_sem.at[at])
            pbuf[c, t, near] = (wide(pbuf, c, t, near) + wide(x_two, at)).astype(LOW)
            send(held(t, near, 1 - y), y_one.at[at], yone_sem.at[at], dev_y)

    def plane_sum(k, t):
        mode = REDUCE_MODE[t][k]
        at = index_of[mode][k, t]
        mine = wide(pbuf, c, t, slot_of(k, "n"), y)
        if mode == "y":
            arrived(x_one.at[at], xone_sem.at[at])
            return mine + wide(y_two, at, 0) + wide(x_one, at)
        arrived(y_one.at[at], yone_sem.at[at])
        return mine + wide(y_one, at)

    def onward(k, t):
        if REDUCE_MODE[t][k] == "z":
            return
        row = "aen".index(k)
        tbuf[...] = plane_sum(k, t)
        if k == "n":
            ebuf[row, t] = tbuf[...].astype(LOW)
            send(ebuf.at[row, t], near_in.at[t], near_sem.at[t], dev_near)
            return

        line = "ae".index(k)

        @pl.when(inner)
        def _():
            arrived(mid_in.at[line, t], mid_sem.at[line, t])
            tbuf[...] += wide(mid_in, line, t)

        ebuf[row, t] = tbuf[...].astype(LOW)
        owner = (2 * place[k] + x, sq)
        send(ebuf.at[row, t], fin_in.at[t], fin_sem.at[t], owner, inner)
        send(ebuf.at[row, t], mid_in.at[line, t], mid_sem.at[line, t], dev_near, outer)

    squares = []

    def finish(t):
        value = plane_sum("o", t)
        if REDUCE_MODE[t]["n"] != "z":
            arrived(near_in.at[t], near_sem.at[t])
            value = value + wide(near_in, t)
        arrived(fin_in.at[t], fin_sem.at[t])
        total = (value + wide(fin_in, t)).astype(LOW)
        tlow[t] = total
        wide_total = total.astype(WIDE)
        rows = (wide_total * wide_total).reshape(-1, 8, wide_total.shape[-1])
        squares.append(jnp.sum(rows, axis=0))
        at = own_ref.at[t, sq]
        for device in (dev_y, dev_c):
            send(tlow.at[t], at, out_sem.at[t, sq], device)
        own_moves.append(move(tlow.at[t], at))

    steps = {
        "part": partial,
        "both": both_cores,
        "own": own_block,
        "turn": turn,
        "on": onward,
        "end": finish,
        "vs": vec_send,
        "va": vec_add,
        "gin": input_grad,
        "in": input_send,
    }
    for name, *at in REDUCE_ORDER:
        steps[name](*at)

    squares = squares[0] + squares[1] + squares[2]
    folded = squares[:, :128]
    for lane in range(1, squares.shape[-1] // 128):
        folded = folded + squares[:, 128 * lane : 128 * (lane + 1)]
    s_own[...] = folded
    for step in range(1, 4):
        send(s_own, s_seq.at[sq], seq_sem.at[sq], (dp, sq ^ step))
    s_seq[sq] = folded
    for t in [at[0] for name, *at in REDUCE_ORDER if name == "end"]:
        arrived(own_ref.at[t, sq ^ 2], out_sem.at[t, sq ^ 2])
        send(own_ref.at[t, sq ^ 2], own_ref.at[t, sq ^ 2], out_sem.at[t, sq ^ 2], dev_c)
    for step in range(1, 4):
        arrived(s_seq.at[sq ^ step], seq_sem.at[sq ^ step])
    group = s_seq[0] + s_seq[1] + s_seq[2] + s_seq[3]
    s_dp[dp] = group
    for step in range(1, 8):
        send(s_dp.at[dp], s_dp.at[dp], dp_sem.at[dp], (dp ^ step, sq))
    for step in range(1, 8):
        arrived(s_dp.at[dp ^ step], dp_sem.at[dp ^ step])
    everyone = s_dp[0]
    for index in range(1, 8):
        everyone = everyone + s_dp[index]
    sq_ref[...] = everyone
    vt_ref[0:16] = vbuf[5][0:16]
    vt_ref[16:24] = vbuf[2][16:24]

    for t in range(3):
        arrived(own_ref.at[t, sq ^ 1], out_sem.at[t, sq ^ 1])
        arrived(own_ref.at[t, sq ^ 3], out_sem.at[t, sq ^ 3])
    for step in range(1, 4):
        other = sq ^ step
        there, member = other // 2, other % 2
        arrived(gi_ref.at[3 * there + 2 * member], in_sem.at[other, 0])
        arrived(gi_ref.at[3 * there + 1, pl.ds(64 * member, 64)], in_sem.at[other, 1])
    exchange.finish()
    for copy in own_moves:
        copy.wait()
    for copy, pred in remotes:
        if pred is None:
            copy.wait_send()
        else:
            pl.when(pred)(lambda copy=copy: copy.wait_send())


def reduce_all(
    owners, lengths, rows, out, left, qkv, d_out, d_branch, right, matrices, result, lse, sums,
    sent_dev,
):
    width = rows.shape[-1]
    part = TILE // 4
    hbm = pl.BlockSpec(memory_space=pl.ANY)
    vmem = pl.BlockSpec(memory_space=pltpu.VMEM)
    smem = pl.BlockSpec(memory_space=pltpu.SMEM)
    dma = pltpu.SemaphoreType.DMA
    modes = "".join(mode for modes in REDUCE_MODE for mode in modes.values())
    x_first, y_first = max(modes.count("x"), 1), max(modes.count("y"), 1)
    near_over = int(any(mode["n"] != "z" for mode in REDUCE_MODE))

    def low(*shape):
        return pltpu.VMEM(shape + (part, width), LOW)

    owned, totals, squares, input_grad, output = pl.pallas_call(
        reduce_body,
        out_shape=(
            jax.ShapeDtypeStruct((3, 4, part, width), LOW),
            jax.ShapeDtypeStruct((24, width), WIDE),
            jax.ShapeDtypeStruct((8, 128), WIDE),
            jax.ShapeDtypeStruct((sent_dev, 128, width), LOW),
            jax.ShapeDtypeStruct((sent_dev, 128, width), LOW),
        ),
        in_specs=[smem] * 2 + [hbm] * 9 + [vmem] * 2,
        out_specs=(hbm, vmem, vmem, hbm, hbm),
        scratch_shapes=[
            pltpu.VMEM((8, 768, TILE), LOW),
            pltpu.VMEM((8, 768, TILE), LOW),
            pltpu.VMEM((8, 768, TILE), LOW),
            pltpu.VMEM((6, 768, width), LOW),
            pltpu.VMEM((3, width, width), LOW),
            pltpu.VMEM((768, width), LOW),
            pltpu.VMEM((width // 128, 2, 256, 128), LOW),
            pltpu.VMEM((width // 128, 2, 256, 128), LOW),
            low(2, 3, 8, 2),
            pltpu.VMEM((48 * part, width), LOW),
            low(x_first, 2),
            low(y_first),
            low(y_first, 2),
            low(x_first),
            low(3, 2, 2),
            low(2, 3),
            low(3),
            low(3 if near_over else 1),
            low(2 + near_over, 3),
            pltpu.VMEM((part, width), WIDE),
            low(3),
            pltpu.VMEM((6, 24, width), WIDE),
            pltpu.VMEM((5, 24, width), WIDE),
            pltpu.VMEM((8, 128), WIDE),
            pltpu.VMEM((4, 8, 128), WIDE),
            pltpu.VMEM((8, 8, 128), WIDE),
            dma((160,)),
            dma((48,)),
            dma((3, 8, 2)),
            dma((x_first,)),
            dma((y_first,)),
            dma((y_first, 2)),
            dma((x_first,)),
            dma((3, 2)),
            dma((2, 3)),
            dma((3,)),
            dma((3,)),
            dma((5,)),
            dma((3, 4)),
            dma((4,)),
            dma((8,)),
            dma((4, 2)),
            dma((width // 128, 2)),
            dma((width // 128, 2)),
            pltpu.SemaphoreType.REGULAR,
        ]
        + EXCHANGE_SEMS,
        compiler_params=params(collective_id=2, has_side_effects=True),
        name="reduce_gradients",
    )(
        owners, lengths, rows, out, left, qkv, d_out, d_branch, right, matrices, result, lse, sums
    )
    return owned.reshape(3 * TILE, width), totals, squares, input_grad, output


def optimizer_body(
    len_ref, mem_ref, g_ref, sq_ref, tot_ref, w_ref, one_ref, two_ref, vw_ref, vone_ref, vtwo_ref,
    out_from, in_from, norm_ref, emb_ref, *rest,
):
    outs, (out_to, in_to, clip_ref) = rest[:-3], rest[-3:]
    count = vw_ref.shape[0]

    out_to[...] = out_from[...]
    in_to[...] = in_from[...]

    @pl.when(pl.program_id(0) == 0)
    def _():
        gradient = tot_ref[:count]
        total = jnp.sum(sq_ref[...], keepdims=True) + jnp.sum(gradient * gradient, keepdims=True)
        norm = jnp.sqrt(total)
        norm_ref[...] = norm
        clip_ref[...] = jnp.broadcast_to(MAX_NORM / jnp.maximum(norm, MAX_NORM), clip_ref.shape)

    clip = clip_ref[...]

    def update(refs, outs, gradient, rate, decay):
        new = adam_step(refs[2][...], refs[0][...], refs[1][...], gradient, rate, decay)
        for ref, value in zip(outs, new + (new[2].astype(LOW),)):
            ref[...] = value

    update(
        (one_ref, two_ref, w_ref), outs[:4], g_ref[...].astype(WIDE) * clip,
        RATE_MATRIX, WEIGHT_DECAY,
    )

    @pl.when(pl.program_id(0) == 0)
    def _():
        update((vone_ref, vtwo_ref, vw_ref), outs[4:], tot_ref[:count] * clip, RATE_VECTOR, 0.0)
        groups, most = mem_ref.shape
        sentences = len_ref.shape[0]
        first = lax.axis_index("dp") * sentences
        pooled = [
            tot_ref[16 + s : 17 + s] / len_ref[s].astype(WIDE) for s in range(sentences)
        ]
        for g in range(groups):
            listed = jnp.int32(0)
            total = jnp.zeros_like(pooled[0])
            for m in range(most):
                listed += jnp.where(mem_ref[g, m] >= 0, 1, 0)
            for s in range(sentences):
                times = jnp.int32(0)
                for m in range(most):
                    times += jnp.where(mem_ref[g, m] == first + s, 1, 0)
                total = total + pooled[s] * times.astype(WIDE)
            emb_ref[g : g + 1] = total / listed.astype(WIDE)


def optimizer(lengths, members, owned, squares, totals, matrices, vectors, exchanged):
    block_rows, width = owned.shape
    steps = 4 if block_rows % 64 == 0 else 1
    smem = pl.BlockSpec(memory_space=pltpu.SMEM)
    mat = pl.BlockSpec((block_rows // steps, width), lambda i: (i, 0))

    def whole(shape):
        return pl.BlockSpec(shape, lambda i: (0, 0))

    sentences, positions_here = exchanged[0].shape[:2]
    passed = pl.BlockSpec((sentences, positions_here // steps, width), lambda i: (0, i, 0))
    vec = whole(vectors[0].shape)
    embeddings = (members.shape[0], width)
    return pl.pallas_call(
        optimizer_body,
        grid=(steps,),
        in_specs=[smem, smem, mat, whole(squares.shape), whole(totals.shape)]
        + [mat] * 3
        + [vec] * 3
        + [passed] * 2,
        out_specs=(whole((1, 1)), whole(embeddings)) + (mat,) * 4 + (vec,) * 4
        + (passed,) * 2,
        out_shape=(
            jax.ShapeDtypeStruct((1, 1), WIDE),
            jax.ShapeDtypeStruct(embeddings, WIDE),
        )
        + tuple(
            jax.ShapeDtypeStruct(like.shape, dtype)
            for like in (owned, vectors[0])
            for dtype in (WIDE, WIDE, WIDE, LOW)
        )
        + tuple(jax.ShapeDtypeStruct(like.shape, LOW) for like in exchanged),
        scratch_shapes=[pltpu.VMEM((1, width), WIDE)],
        compiler_params=params(),
        name="optimizer",
    )(lengths, members, owned, squares, totals, *matrices, *vectors, *exchanged)


def to_positions(value):
    width = value.shape[1]
    moved = jnp.concatenate(
        [value[:512].reshape(4, 128, width), value[512:].reshape(4, 64, width)], axis=1
    )
    moved = lax.all_to_all(moved, "seq", split_axis=0, concat_axis=0, tiled=True)
    rows = []
    for y in range(2):
        rows.append(moved[2 * y, :128])
        rows.append(jnp.concatenate([moved[2 * y, 128:], moved[2 * y + 1, 128:]], axis=0))
        rows.append(moved[2 * y + 1, :128])
    return jnp.stack(rows)


def to_rows(tokens):
    width = tokens.shape[-1]
    core = lax.axis_index("seq") % 2
    pieces = []
    for j in range(4):
        y, c = j // 2, j % 2
        pieces += [tokens[3 * y + 2 * c], tokens[3 * y + 1]]
    moved = jnp.concatenate(pieces, axis=0).reshape(4, 256, width)
    moved = lax.all_to_all(moved, "seq", split_axis=0, concat_axis=0, tiled=True)
    shared = moved[:, 128:].reshape(4, 2, 64, width)
    own = lax.dynamic_index_in_dim(shared, core, 1, keepdims=False)
    other = lax.dynamic_index_in_dim(shared, 1 - core, 1, keepdims=False)
    return jnp.concatenate(
        [moved[:, :128].reshape(512, width), own.reshape(256, width), other.reshape(256, width)],
        axis=0,
    )


def local(
    tokens,
    grad_out,
    lengths,
    members,
    owners,
    mat_master,
    mat_moment1,
    mat_moment2,
    vec_master,
    vec_moment1,
    vec_moment2,
):
    sent_dev, local_len, model_width = tokens.shape
    dp_count = lax.axis_size("dp")
    block_rows = mat_master.shape[0]
    direct = dp_count == 8 and block_rows == 3 * TILE

    if direct:
        blocks = owners
        weights, rows, qkv, matrices, attended, out_grad, lse = front(
            owners, lengths, mat_master, tokens, grad_out, vec_master
        )
    else:
        gathered = lax.all_gather(mat_master.astype(LOW), "dp", axis=0, tiled=True)
        weights = gathered.reshape(dp_count, block_rows, model_width)[owners]
        weights = weights.reshape(-1, TILE, model_width)
        rows = to_rows(tokens)
        blocks = jnp.arange(weights.shape[0] // 3, dtype=jnp.int32)
        qkv = qkv_project(blocks, rows, weights, vec_master)
        attended, lse, out_grad = attend(lengths, qkv, grad_out)
    result, left, right, d_attended, d_branch, sums = middle(
        blocks, lengths, attended, rows, out_grad, weights, vec_master
    )
    if direct:
        owned, totals, squares, input_grad, output = reduce_all(
            owners,
            lengths,
            rows,
            attended,
            left,
            qkv,
            d_attended,
            d_branch,
            right,
            matrices,
            result,
            lse,
            sums,
            sent_dev,
        )
    else:
        dq, dk, dv, output = attend_back(
            lengths, qkv, lse, d_attended, attended, result, sent_dev
        )
        grad_rows = grad_in(blocks, dq, dk, dv, d_branch, weights)
        grads = grad_ff(blocks, left, right)
        grads, sums_qv = grad_attn(blocks, rows, dq, dk, dv, attended, d_branch, grads)
        input_grad = to_positions(grad_rows)
        inverse = jnp.argsort(owners)
        grads = grads.reshape(dp_count, block_rows, model_width)[inverse]
        grads = grads.reshape(dp_count * block_rows, model_width)
        quarter = lax.psum_scatter(grads, ("dp", "seq"), scatter_dimension=0, tiled=True)
        owned = lax.all_gather(quarter, "seq", axis=0, tiled=True)
        quarter = quarter.astype(WIDE)
        group = lax.axis_index("seq") // 2
        core = lax.axis_index("seq") % 2
        place = jnp.arange(8)[:, None]
        pooled = jnp.where(place == 3 * group + 2 * core, sums[10:11], 0.0) + jnp.where(
            place == 3 * group + 1, sums[11:12], 0.0
        )
        pooled = lax.psum(pooled, "seq")
        local_vec = jnp.concatenate([sums_qv[0:2], sums[0:14]], axis=0)
        squares, vec_total = lax.psum(
            (jnp.sum(quarter * quarter), local_vec), ("dp", "seq")
        )
        squares = jnp.full((8, 128), squares / 1024.0)
        totals = jnp.concatenate([vec_total, pooled], axis=0)

    norm, embeddings, *new, output, input_grad = optimizer(
        lengths,
        members,
        owned,
        squares,
        totals,
        (mat_master, mat_moment1, mat_moment2),
        (vec_master, vec_moment1, vec_moment2),
        (output, input_grad),
    )
    return (output, input_grad, embeddings, norm.reshape(()), *new)


def solution(mesh):
    placed = (
        P("dp", "seq", None),
        P("dp", "seq", None),
        P("dp"),
        P("dp", None),
        P(),
        P("dp", None),
        P("dp", None),
        P("dp", None),
        P(),
        P(),
        P(),
    )
    return jax.shard_map(
        local,
        mesh=mesh,
        in_specs=placed,
        out_specs=(
            P("dp", "seq", None),
            P("dp", "seq", None),
            P("dp", None),
            P(),
            P("dp", None),
            P("dp", None),
            P("dp", None),
            P("dp", None),
            P(),
            P(),
            P(),
            P(),
        ),
        check_vma=False,
    )
```
